256 devices in a mesh: section: 16 (over z, y_lo), dp: 16 (over y_hi, x, core).
Axes of the slice: x: 4, y: 4 (y_hi: 2, y_lo: 2; y = y_hi * 2 + y_lo), z: 8, core: 2. Of those that a mesh axis runs over, the one named last changes fastest.
Arguments:
- inputs: bfloat16 [4, 512, 7168], P(None, 'dp'), may hold values from -6 to 6
- cotangent: bfloat16 [4, 512, 7168], P(None, 'dp'), may hold values from -0.3125 to 0.3125
- w_down: bfloat16 [16, 7168, 128], P('section'), may hold values from -0.0625 to 0.0625
- w_up: bfloat16 [16, 128, 7168], P('section'), may hold values from -0.5 to 0.5
Outputs:
- grad_down: bfloat16 [16, 7168, 128], P('section')
- grad_up: bfloat16 [16, 128, 7168], P('section')
- advance: bfloat16 [16, 4, 512, 7168], P('section', None, 'dp')
The draws below stay inside these ranges and needn't reach their ends.
All inputs are finite; a program needn't handle non-finite values.
Results may differ from the reference program's by a relative error of at most 0.035.
Values may be sent and summed in bfloat16 or wider, within the bound.
A program may use at most 128 MiB of HBM per device.

```python
import jax
import jax.numpy as jnp
from jax import lax

D = 7168
RANK = 128
MICRO = 4
MB = 32
LAYERS = 16
ROWS = 512
N_DP = 16


def block_levels(key, extent, pieces, low, largest):
    def one(position, blocks):
        draws = jax.random.uniform(jax.random.fold_in(jax.random.fold_in(key, 6), position), (blocks,), jnp.float32, low / len(pieces), largest / len(pieces))
        return jnp.repeat(jnp.exp(draws), extent[position] // blocks).reshape((-1,) + (1,) * (len(extent) - position - 1))

    level = one(*pieces[0])
    for cut in pieces[1:]:
        level = level * one(*cut)
    return level


def bell_draw(stream_key, extent, scale, most, shards=(), held_as=jnp.bfloat16):
    array = scale * jax.random.normal(stream_key, extent, jnp.float32)
    if shards:
        array = array * block_levels(stream_key, extent, shards, -0.22, 0.18)
    return jnp.clip(array, -most, most).astype(held_as)


def setup_inputs(seed: int = 0) -> dict:
    key_of = jax.random.split(jax.random.key(seed), 5)
    return {
        "inputs": bell_draw(key_of[0], (MICRO, ROWS, D), 1.0, 6.0, ((1, 16),)),
        "cotangent": bell_draw(key_of[1], (MICRO, ROWS, D), (1.0 / (MICRO * MB * N_DP) ** 0.5), 0.3125, ((1, 16),)),
        "w_down": bell_draw(key_of[2], (LAYERS, D, RANK), D ** -0.5, 0.0625, ((0, 16),)),
        "w_up": bell_draw(key_of[3], (LAYERS, RANK, D), RANK ** -0.5, 0.5, ((0, 16),)),
    }


eps = 1e-05
learn_rate = 0.05

def normalize(hidden):
    values = hidden.astype(jnp.float32)
    scaled = lax.rsqrt(lax.optimization_barrier(jnp.mean(values * values, axis=-1, keepdims=True)) + eps)
    return (values, values * scaled, scaled)

def gelu_slope(pre_act):
    return jax.grad(lambda entries: jnp.sum(jax.nn.gelu(entries)))(pre_act)

def layer_apply(hidden, down, upward):
    values, unit, scaled = normalize(hidden)
    pre_act = jnp.dot(unit.astype(jnp.bfloat16), down, preferred_element_type=jnp.float32)
    active = jax.nn.gelu(pre_act).astype(jnp.bfloat16)
    output = (values + jnp.dot(active, upward, preferred_element_type=jnp.float32)).astype(jnp.bfloat16)
    return (output, pre_act)

def layer_back(hidden, pre_act, incoming, down, upward):
    values, unit, scaled = normalize(hidden)
    back_act = jnp.dot(incoming, upward.T, preferred_element_type=jnp.float32)
    back_pre = (back_act * gelu_slope(pre_act)).astype(jnp.bfloat16)
    back_unit = jnp.dot(back_pre, down.T, preferred_element_type=jnp.float32)
    mixing = lax.optimization_barrier(jnp.mean(back_unit * unit, axis=-1, keepdims=True))
    outgoing = (incoming.astype(jnp.float32) + scaled * (back_unit - unit * mixing)).astype(jnp.bfloat16)
    return (outgoing, back_pre)

def weight_terms(hidden, pre_act, incoming, back_pre):
    values, unit, scaled = normalize(hidden)
    unit_low = unit.astype(jnp.bfloat16)
    active = jax.nn.gelu(pre_act).astype(jnp.bfloat16)
    contract = (((0,), (0,)), ((), ()))
    term_down = lax.dot_general(unit_low, back_pre, contract, preferred_element_type=jnp.float32)
    term_up = lax.dot_general(active, incoming, contract, preferred_element_type=jnp.float32)
    return (term_down, term_up)

def reference(inputs, cotangent, w_down, w_up):
    width = inputs.shape[-1]
    hidden = inputs.reshape(-1, width)
    saved_in = []
    saved_pre = []
    saved_out = []
    for layer in range(LAYERS):
        output, pre_act = layer_apply(hidden, w_down[layer], w_up[layer])
        saved_in.append(hidden)
        saved_pre.append(pre_act)
        saved_out.append(output)
        hidden = output
    incoming = cotangent.reshape(-1, width)
    downs = [None] * LAYERS
    ups = [None] * LAYERS
    for layer in reversed(range(LAYERS)):
        outgoing, back_pre = layer_back(saved_in[layer], saved_pre[layer], incoming, w_down[layer], w_up[layer])
        term_down, term_up = weight_terms(saved_in[layer], saved_pre[layer], incoming, back_pre)
        downs[layer] = term_down
        ups[layer] = term_up
        incoming = outgoing
    total_down = jnp.stack(downs)
    total_up = jnp.stack(ups)
    new_down = (w_down.astype(jnp.float32) - learn_rate * total_down).astype(jnp.bfloat16)
    new_up = (w_up.astype(jnp.float32) - learn_rate * total_up).astype(jnp.bfloat16)
    ahead = []
    for layer in range(LAYERS):
        if layer + 1 < LAYERS:
            result, unused = layer_apply(saved_out[layer], new_down[layer + 1], new_up[layer + 1])
        else:
            result = saved_out[layer]
        ahead.append(result)
    advance = jnp.stack(ahead).reshape(LAYERS, MICRO, ROWS, width)
    return (total_down.astype(jnp.bfloat16), total_up.astype(jnp.bfloat16), advance)
```

```python
import functools

import jax
import jax.numpy as jnp
from jax import lax
from jax.experimental import pallas as pl
from jax.experimental.pallas import tpu as pltpu
from jax.sharding import PartitionSpec as P

MESH = pl.DeviceIdType.MESH
eps = 1e-05
learn_rate = 0.05
f32 = jnp.float32
bf16 = jnp.bfloat16


def dot_nn(a, b):
    return jnp.dot(a, b, preferred_element_type=f32)


def dot_tn(a, b):
    return lax.dot_general(a, b, (((0,), (0,)), ((), ())), preferred_element_type=f32)


def dot_nt(a, b):
    return lax.dot_general(a, b, (((1,), (1,)), ((), ())), preferred_element_type=f32)


def gelu_pair(a):
    c = 0.7978845608028654
    inner = c * (a + 0.044715 * a * a * a)
    th = jnp.tanh(inner)
    value = 0.5 * a * (1.0 + th)
    slope = 0.5 * (1.0 + th) + 0.5 * a * (1.0 - th * th) * c * (1.0 + 3 * 0.044715 * a * a)
    return value, slope


def recurrence_kernel(sections, chunks, pyh, n0, mm, gu, x0, up, xout, u_out, q_out, cc, e_out,
                      ul, ql, mb, ys, nl, nsend, pacc, yacc, hacc, slope, act, rinv, ecol,
                      upart, xin, xkeep, xgive,
                      u_send, u_recv, q_send, q_recv, m_send, m_recv, n_sem, w_sem, c_send, c_recv,
                      g_send, g_recv):
    s = lax.axis_index("section")
    rows, width = x0.shape
    rank = up.shape[0]
    half = width // 2
    piece = half // chunks
    z = s // 2
    ylo = lax.rem(s, 2)
    partner = s + 1 - 2 * ylo

    def peer(offset):
        return lax.rem(s + offset, sections)

    barrier = pltpu.get_barrier_semaphore()

    def greet(o, carry):
        pl.semaphore_signal(barrier, inc=1, device_id={"section": peer(o)}, device_id_type=MESH)
        return carry

    lax.fori_loop(1, sections, greet, 0)
    pl.semaphore_wait(barrier, sections - 1)

    eye = (lax.broadcasted_iota(jnp.int32, (rows, rows), 0)
           == lax.broadcasted_iota(jnp.int32, (rows, rows), 1)).astype(f32)

    def to_row(col):
        return jnp.sum(eye * col, axis=0, keepdims=True)

    def to_col(row):
        return jnp.sum(eye * row, axis=1, keepdims=True)

    def columns(base, c):
        return pl.ds(pl.multiple_of(base + c * piece, 128), piece)

    def w_copy():
        return pltpu.make_async_remote_copy(
            src_ref=up.at[:, pl.ds(pl.multiple_of((1 - ylo) * half, 128), half)],
            dst_ref=upart, send_sem=w_sem.at[0], recv_sem=w_sem.at[1],
            device_id={"section": partner}, device_id_type=MESH)

    def u_copy(o):
        return pltpu.make_async_remote_copy(
            src_ref=ul.at[s], dst_ref=ul.at[s], send_sem=u_send.at[o], recv_sem=u_recv.at[s],
            device_id={"section": peer(o)}, device_id_type=MESH)

    def u_arrived(k):
        return pltpu.make_async_remote_copy(
            src_ref=ul.at[k], dst_ref=ul.at[k], send_sem=u_send.at[0], recv_sem=u_recv.at[k],
            device_id={"section": partner}, device_id_type=MESH)

    def q_copy(j):
        return pltpu.make_async_remote_copy(
            src_ref=ql.at[s], dst_ref=ql.at[s], send_sem=q_send.at[j], recv_sem=q_recv.at[s],
            device_id={"section": j}, device_id_type=MESH)

    def q_arrived(k):
        return pltpu.make_async_remote_copy(
            src_ref=ql.at[k], dst_ref=ql.at[k], send_sem=q_send.at[0], recv_sem=q_recv.at[k],
            device_id={"section": partner}, device_id_type=MESH)

    def m_copy(j):
        return pltpu.make_async_remote_copy(
            src_ref=mm.at[j], dst_ref=mb.at[s], send_sem=m_send.at[j], recv_sem=m_recv.at[s],
            device_id={"section": j}, device_id_type=MESH)

    def m_arrived(k):
        return pltpu.make_async_remote_copy(
            src_ref=mb.at[k], dst_ref=mb.at[k], send_sem=m_send.at[0], recv_sem=m_recv.at[k],
            device_id={"section": partner}, device_id_type=MESH)

    def n_copy():
        return pltpu.make_async_remote_copy(
            src_ref=nsend, dst_ref=nl, send_sem=n_sem.at[0], recv_sem=n_sem.at[1],
            device_id={"section": peer(1)}, device_id_type=MESH)

    def x_copy(c):
        return pltpu.make_async_remote_copy(
            src_ref=xkeep.at[:, columns(0, c)], dst_ref=xin.at[:, columns(0, c)],
            send_sem=c_send.at[c], recv_sem=c_recv.at[c],
            device_id={"section": peer(2)}, device_id_type=MESH)

    def give_copy(c):
        return pltpu.make_async_remote_copy(
            src_ref=xgive.at[:, columns(0, c)], dst_ref=xout.at[:, columns(ylo * half, c)],
            send_sem=g_send.at[c], recv_sem=g_recv.at[c],
            device_id={"section": partner}, device_id_type=MESH)

    def give_arrived(c):
        return pltpu.make_async_remote_copy(
            src_ref=xgive.at[:, columns(0, c)], dst_ref=xout.at[:, columns((1 - ylo) * half, c)],
            send_sem=g_send.at[c], recv_sem=g_recv.at[c],
            device_id={"section": partner}, device_id_type=MESH)

    def start_m(j, carry):
        @pl.when(j < s)
        def _():
            m_copy(j).start()
        return carry

    pacc[...] = pyh[0]
    yacc[...] = pyh[1]
    hacc[...] = pyh[2]
    ecol[...] = jnp.zeros_like(ecol)

    def chain(t):
        c = t - (2 * z + 3)

        @pl.when((c >= 0) & (c < chunks))
        def _():
            @pl.when(z > 0)
            def _():
                x_copy(c).wait_recv()

            @pl.when(c == 0)
            def _():
                w_copy().wait_recv()

            here = columns(ylo * half, c)
            start = jnp.where(z > 0, xin[:, columns(0, c)], x0[:, here]).astype(f32)
            mine = up[:, here]
            other = upart[:, columns(0, c)]
            first = ylo == 0
            u_a = ul[2 * z]
            u_b = ul[2 * z + 1]
            x_a = (start + dot_nn(u_a, jnp.where(first, mine, other))).astype(bf16)
            x_b = (x_a.astype(f32) + dot_nn(u_b, jnp.where(first, other, mine))).astype(bf16)
            xkeep[:, columns(0, c)] = x_b

            @pl.when(z < sections // 2 - 1)
            def _():
                x_copy(c).start()

            xgive[:, columns(0, c)] = jnp.where(first, x_b, x_a)
            give_copy(c).start()
            xout[:, here] = jnp.where(first, x_a, x_b)

    def forward_tick(t, carry):
        k = t - 1

        @pl.when((t > 0) & (k != s))
        def _():
            u_arrived(k).wait_recv()

        @pl.when((t > 0) & (k < s))
        def _():
            pacc[...] += dot_nn(ul[k], mm[k])

        @pl.when(t == s)
        def _():
            @pl.when(s > 0)
            def _():
                n_copy().wait_recv()

            norm = jnp.where(s > 0, to_col(nl[0:1, :]), n0[:, 0:1])
            scale = lax.rsqrt(norm * (1.0 / width) + eps)
            pre = pacc[...] * scale
            value, grad = gelu_pair(pre)
            ul[s] = value.astype(bf16)

            def send(o, carry):
                u_copy(o).start()
                return carry

            lax.fori_loop(1, sections, send, 0)
            act[...] = pre
            slope[...] = grad
            rinv[...] = jnp.broadcast_to(scale, rinv.shape)

        @pl.when((t > 0) & (k > s))
        def _():
            ys[k] = yacc[...]

        @pl.when(t > 0)
        def _():
            yacc[...] += dot_nn(ul[k], gu[k])

        @pl.when((t == s) & (s < sections - 1))
        def _():
            mine = ul[s]
            norm = jnp.where(s > 0, to_col(nl[0:1, :]), n0[:, 0:1])
            grown = norm + jnp.sum(
                mine.astype(f32) * (2.0 * yacc[...] + dot_nn(mine, gu[s])), axis=1, keepdims=True)
            nsend[...] = jnp.broadcast_to(to_row(grown), nsend.shape)
            n_copy().start()

        @pl.when(t == 0)
        def _():
            w_copy().start()
            lax.fori_loop(0, sections, start_m, 0)

        chain(t)
        return carry

    lax.fori_loop(0, sections, forward_tick, 0)

    @pl.when(s != sections - 1)
    def _():
        u_arrived(sections - 1).wait_recv()

    def c_of(k):
        return to_col(ql[k, rows:rows + 1, :].astype(f32) + ql[k, rows + 1:rows + 2, :].astype(f32))

    def cross(k, head):
        sum_col = ecol[...]
        cc[k, :, 0:rank] = head.astype(bf16)
        mine = ul[s].astype(f32) * sum_col
        cc[k, :, rank:2 * rank] = (-dot_tn(ul[k], mine.astype(bf16))).astype(bf16)

    def backward_tick(t, carry):
        j = 2 * sections - 1 - t
        k = j + 1
        behind = (k < sections) & (k > s)

        @pl.when(behind)
        def _():
            m_arrived(k).wait_recv()
            q_arrived(k).wait_recv()
            hacc[...] += dot_nt(ql[k, 0:rows, :], mb[k]) - c_of(k) * ys[k]

        @pl.when(s == j)
        def _():
            q = hacc[...] * slope[...]
            scale = rinv[...]
            ql[s, 0:rows, :] = (q * scale).astype(bf16)
            mix = jnp.sum(q * act[...], axis=1, keepdims=True) * (1.0 / width)
            line = to_row(mix * scale[:, 0:1] * scale[:, 0:1])
            high = line.astype(bf16)
            low = (line - high.astype(f32)).astype(bf16)
            spot = lax.broadcasted_iota(jnp.int32, (16, rows), 0)
            ql[s, rows:rows + 16, :] = jnp.where(
                spot == 0, high.astype(f32), jnp.where(spot == 1, low.astype(f32), 0.0)).astype(bf16)

            def send(i, carry):
                q_copy(s - 1 - i).start()
                return carry

            lax.fori_loop(0, s, send, 0)

        @pl.when(behind)
        def _():
            cross(k, dot_tn(ql[k, 0:rows, :], ul[s]))
            ecol[...] += jnp.broadcast_to(c_of(k), ecol.shape)

        chain(t)
        return carry

    lax.fori_loop(sections, 2 * sections, backward_tick, 0)

    def tail(k, carry):
        @pl.when(k <= s)
        def _():
            keep = jnp.where(k < s, 1.0, 0.0)
            cross(k, dot_tn(ul[k], ql[s, 0:rows, :]) * keep)
        return carry

    lax.fori_loop(0, sections, tail, 0)
    u_out[...] = ul[s]
    q_out[...] = ql[s, 0:rows, :]
    e_out[...] = ecol[...]

    def finish(c, carry):
        @pl.when(z < sections // 2 - 1)
        def _():
            x_copy(c).wait_send()
        give_copy(c).wait_send()
        give_arrived(c).wait_recv()
        return carry

    lax.fori_loop(0, chunks, finish, 0)

    def settle(o, carry):
        u_copy(o).wait_send()

        @pl.when(o - 1 < s)
        def _():
            q_copy(o - 1).wait_send()
            m_copy(o - 1).wait_send()
        return carry

    lax.fori_loop(1, sections, settle, 0)
    w_copy().wait_send()

    @pl.when(s < sections - 1)
    def _():
        n_copy().wait_send()


def recurrence(sections, pyh, n0, mm, gu, x0, up):
    rows, width = x0.shape
    rank = up.shape[0]
    half = width // 2
    chunks = 14
    vm = pl.BlockSpec(memory_space=pltpu.VMEM)
    dma = pltpu.SemaphoreType.DMA
    block = (sections, rank, rank)
    sq = (rows, rank)
    return pl.pallas_call(
        functools.partial(recurrence_kernel, sections, chunks),
        out_shape=(
            jax.ShapeDtypeStruct((rows, width), bf16),
            jax.ShapeDtypeStruct(sq, bf16),
            jax.ShapeDtypeStruct(sq, bf16),
            jax.ShapeDtypeStruct((sections, rank, 2 * rank), bf16),
            jax.ShapeDtypeStruct(sq, f32),
        ),
        in_specs=[vm] * 6,
        out_specs=(vm,) * 5,
        scratch_shapes=[
            pltpu.VMEM((sections, rows, rank), bf16),
            pltpu.VMEM((sections, rows + 16, rank), bf16),
            pltpu.VMEM(block, bf16),
            pltpu.VMEM((sections, rows, rank), f32),
            pltpu.VMEM((8, rows), f32),
            pltpu.VMEM((8, rows), f32),
            pltpu.VMEM(sq, f32), pltpu.VMEM(sq, f32), pltpu.VMEM(sq, f32),
            pltpu.VMEM(sq, f32), pltpu.VMEM(sq, f32), pltpu.VMEM(sq, f32), pltpu.VMEM(sq, f32),
            pltpu.VMEM((rank, half), bf16),
            pltpu.VMEM((rows, half), bf16),
            pltpu.VMEM((rows, half), bf16),
            pltpu.VMEM((rows, half), bf16),
            dma((sections,)), dma((sections,)), dma((sections,)), dma((sections,)),
            dma((sections,)), dma((sections,)), dma((2,)), dma((2,)),
            dma((chunks,)), dma((chunks,)), dma((chunks,)), dma((chunks,)),
        ],
        compiler_params=pltpu.CompilerParams(
            collective_id=1, has_side_effects=True, vmem_limit_bytes=40 * 1024 * 1024),
    )(pyh, n0, mm, gu, x0, up)


def per_device(inputs, cotangent, w_down, w_up):
    down = w_down[0]
    upward = w_up[0]
    micro, batch_rows, width = inputs.shape
    rank = down.shape[1]
    rows = micro * batch_rows
    sections = lax.axis_size("section")
    shards = lax.axis_size("dp")
    part = width // shards
    d = lax.axis_index("dp")
    x0 = inputs.reshape(rows, width)
    g16 = cotangent.reshape(rows, width)
    up_t = upward.T

    mine_u = lax.dynamic_slice_in_dim(up_t, d * part, part, 0)
    mine_w = lax.dynamic_slice_in_dim(down, d * part, part, 0)
    all_u = lax.all_gather(mine_u, "section")
    all_w = lax.all_gather(mine_w, "section")
    grams = jnp.einsum("kfr,fc->krc", all_u, jnp.concatenate([mine_w, mine_u], axis=1),
                       preferred_element_type=f32).astype(bf16)
    grams = lax.psum(grams, "dp")
    mm = grams[:, :, :rank]
    gu = grams[:, :, rank:]

    pyh = jnp.stack([dot_nn(x0, down), dot_nt(x0, upward), dot_nt(g16, upward)])
    values = x0.astype(f32)
    n0 = jnp.broadcast_to(jnp.sum(values * values, axis=1, keepdims=True), (rows, rank))

    ahead_in, u_s, q_s, cc, e_s = recurrence(sections, pyh, n0, mm, gu, x0, upward)

    mixed = (g16.astype(f32) - e_s[:, 0:1] * values).astype(bf16)
    g_part = jnp.concatenate([dot_tn(x0, q_s), dot_tn(mixed, u_s)], axis=1).astype(bf16)
    packed = jnp.concatenate([g_part.reshape(shards, part, 2 * rank), cc], axis=1)
    mine = lax.psum_scatter(packed, "dp", scatter_dimension=0, tiled=False)
    all_cc = lax.all_gather(mine[part:], "dp")
    order = lax.broadcasted_iota(jnp.int32, (sections, 1, 1), 0)
    s = lax.axis_index("section")
    head = all_cc[:, :, :rank]
    zero = jnp.zeros_like(head)
    for_u = jnp.concatenate([jnp.where(order < s, head, zero), all_cc[:, :, rank:]], axis=2)
    for_w = jnp.where(order > s, head, zero)
    fix_u = jnp.einsum("kfr,krc->fc", all_u, for_u, preferred_element_type=f32)
    fix_w = jnp.einsum("kfr,krc->fc", all_w, for_w, preferred_element_type=f32)
    g_mine = (mine[:part].astype(f32) + fix_u
              + jnp.pad(fix_w, ((0, 0), (rank, 0)))).astype(bf16)
    pairs = [(i, i - 1) for i in range(1, sections)]
    g_next = lax.ppermute(g_mine, "section", pairs)
    g_own = lax.all_gather(g_mine, "dp").reshape(width, 2 * rank)
    g_nxt = lax.all_gather(g_next, "dp").reshape(width, 2 * rank)
    grad_down = g_own[:, :rank]
    grad_up = g_own[:, rank:].T
    down_next, up_next = lax.ppermute((down, upward), "section", pairs)
    new_down = (down_next.astype(f32) - learn_rate * g_nxt[:, :rank].astype(f32)).astype(bf16)
    new_up = (up_next.astype(f32) - learn_rate * g_nxt[:, rank:].T.astype(f32)).astype(bf16)

    hidden = ahead_in.astype(f32)
    unit = hidden * lax.rsqrt(jnp.mean(hidden * hidden, axis=-1, keepdims=True) + eps)
    pre = dot_nn(unit.astype(bf16), new_down)
    last = s == sections - 1
    bump = dot_nn(jax.nn.gelu(pre).astype(bf16), new_up)
    advance = jnp.where(last, hidden, hidden + bump).astype(bf16)
    return (grad_down[None], grad_up[None], advance.reshape(1, micro, batch_rows, width))


def solution(mesh):
    in_specs = (
        P(None, "dp", None),
        P(None, "dp", None),
        P("section", None, None),
        P("section", None, None),
    )
    out_specs = (P("section", None, None), P("section", None, None), P("section", None, "dp", None))
    return jax.shard_map(
        per_device, mesh=mesh, in_specs=in_specs, out_specs=out_specs, check_vma=False
    )
```

```python
import functools

import jax
import jax.numpy as jnp
from jax import lax
from jax.experimental import pallas as pl
from jax.experimental.pallas import tpu as pltpu
from jax.sharding import PartitionSpec as P

MESH = pl.DeviceIdType.MESH
eps = 1e-05
learn_rate = 0.05
f32 = jnp.float32
bf16 = jnp.bfloat16


def dot_nn(a, b):
    return jnp.dot(a, b, preferred_element_type=f32)


def dot_tn(a, b):
    return lax.dot_general(a, b, (((0,), (0,)), ((), ())), preferred_element_type=f32)


def dot_nt(a, b):
    return lax.dot_general(a, b, (((1,), (1,)), ((), ())), preferred_element_type=f32)


def gelu_pair(a):
    c = 0.7978845608028654
    inner = c * (a + 0.044715 * a * a * a)
    th = jnp.tanh(inner)
    value = 0.5 * a * (1.0 + th)
    slope = 0.5 * (1.0 + th) + 0.5 * a * (1.0 - th * th) * c * (1.0 + 3 * 0.044715 * a * a)
    return value, slope


def recurrence_kernel(sections, chunks, pyh, n0, mm, gu, x0, g16, up, wd,
                      xout, gout, u_out, q_out,
                      ul, ql, mb, ys, nl, nsend, pacc, yacc, hacc, slope, act, rinv, cpair,
                      upart, wpart, xin, xkeep, xgive, gin, gkeep, ggive,
                      u_send, u_recv, q_send, q_recv, m_send, m_recv, n_sem,
                      up_send, up_recv, wp_send, wp_recv, c_send, c_recv, g_send, g_recv,
                      b_send, b_recv, h_send, h_recv):
    s = lax.axis_index("section")
    rows, width = x0.shape
    rank = up.shape[0]
    half = width // 2
    piece = half // chunks
    z = s // 2
    ylo = lax.rem(s, 2)
    partner = s + 1 - 2 * ylo

    def peer(offset):
        return lax.rem(s + offset, sections)

    barrier = pltpu.get_barrier_semaphore()

    def greet(o, carry):
        pl.semaphore_signal(barrier, inc=1, device_id={"section": peer(o)}, device_id_type=MESH)
        return carry

    lax.fori_loop(1, sections, greet, 0)
    pl.semaphore_wait(barrier, sections - 1)

    eye = (lax.broadcasted_iota(jnp.int32, (rows, rows), 0)
           == lax.broadcasted_iota(jnp.int32, (rows, rows), 1)).astype(f32)

    def to_row(col):
        return jnp.sum(eye * col, axis=0, keepdims=True)

    def to_col(row):
        return jnp.sum(eye * row, axis=1, keepdims=True)

    def columns(base, c):
        return pl.ds(pl.multiple_of(base + c * piece, 128), piece)

    def up_copy(c):
        return pltpu.make_async_remote_copy(
            src_ref=up.at[:, columns((1 - ylo) * half, c)], dst_ref=upart.at[:, columns(0, c)],
            send_sem=up_send.at[c], recv_sem=up_recv.at[c],
            device_id={"section": partner}, device_id_type=MESH)

    def wp_copy(c):
        return pltpu.make_async_remote_copy(
            src_ref=wd.at[columns((1 - ylo) * half, c), :], dst_ref=wpart.at[columns(0, c), :],
            send_sem=wp_send.at[c], recv_sem=wp_recv.at[c],
            device_id={"section": partner}, device_id_type=MESH)

    def b_copy(c):
        return pltpu.make_async_remote_copy(
            src_ref=gkeep.at[:, columns(0, c)], dst_ref=gin.at[:, columns(0, c)],
            send_sem=b_send.at[c], recv_sem=b_recv.at[c],
            device_id={"section": peer(sections - 2)}, device_id_type=MESH)

    def h_copy(c):
        return pltpu.make_async_remote_copy(
            src_ref=ggive.at[:, columns(0, c)], dst_ref=gout.at[:, columns(ylo * half, c)],
            send_sem=h_send.at[c], recv_sem=h_recv.at[c],
            device_id={"section": partner}, device_id_type=MESH)

    def h_arrived(c):
        return pltpu.make_async_remote_copy(
            src_ref=ggive.at[:, columns(0, c)], dst_ref=gout.at[:, columns((1 - ylo) * half, c)],
            send_sem=h_send.at[c], recv_sem=h_recv.at[c],
            device_id={"section": partner}, device_id_type=MESH)

    def u_copy(o):
        return pltpu.make_async_remote_copy(
            src_ref=ul.at[s], dst_ref=ul.at[s], send_sem=u_send.at[o], recv_sem=u_recv.at[s],
            device_id={"section": peer(o)}, device_id_type=MESH)

    def u_arrived(k):
        return pltpu.make_async_remote_copy(
            src_ref=ul.at[k], dst_ref=ul.at[k], send_sem=u_send.at[0], recv_sem=u_recv.at[k],
            device_id={"section": partner}, device_id_type=MESH)

    def q_copy(j):
        return pltpu.make_async_remote_copy(
            src_ref=ql.at[s], dst_ref=ql.at[s], send_sem=q_send.at[j], recv_sem=q_recv.at[s],
            device_id={"section": j}, device_id_type=MESH)

    def q_arrived(k):
        return pltpu.make_async_remote_copy(
            src_ref=ql.at[k], dst_ref=ql.at[k], send_sem=q_send.at[0], recv_sem=q_recv.at[k],
            device_id={"section": partner}, device_id_type=MESH)

    def m_copy(j):
        return pltpu.make_async_remote_copy(
            src_ref=mm.at[j], dst_ref=mb.at[s], send_sem=m_send.at[j], recv_sem=m_recv.at[s],
            device_id={"section": j}, device_id_type=MESH)

    def m_arrived(k):
        return pltpu.make_async_remote_copy(
            src_ref=mb.at[k], dst_ref=mb.at[k], send_sem=m_send.at[0], recv_sem=m_recv.at[k],
            device_id={"section": partner}, device_id_type=MESH)

    def n_copy():
        return pltpu.make_async_remote_copy(
            src_ref=nsend, dst_ref=nl, send_sem=n_sem.at[0], recv_sem=n_sem.at[1],
            device_id={"section": peer(1)}, device_id_type=MESH)

    def x_copy(c):
        return pltpu.make_async_remote_copy(
            src_ref=xkeep.at[:, columns(0, c)], dst_ref=xin.at[:, columns(0, c)],
            send_sem=c_send.at[c], recv_sem=c_recv.at[c],
            device_id={"section": peer(2)}, device_id_type=MESH)

    def give_copy(c):
        return pltpu.make_async_remote_copy(
            src_ref=xgive.at[:, columns(0, c)], dst_ref=xout.at[:, columns(ylo * half, c)],
            send_sem=g_send.at[c], recv_sem=g_recv.at[c],
            device_id={"section": partner}, device_id_type=MESH)

    def give_arrived(c):
        return pltpu.make_async_remote_copy(
            src_ref=xgive.at[:, columns(0, c)], dst_ref=xout.at[:, columns((1 - ylo) * half, c)],
            send_sem=g_send.at[c], recv_sem=g_recv.at[c],
            device_id={"section": partner}, device_id_type=MESH)

    def start_m(j, carry):
        @pl.when(j < s)
        def _():
            m_copy(j).start()
        return carry

    pacc[...] = pyh[0]
    yacc[...] = pyh[1]
    hacc[...] = pyh[2]

    def chain(t):
        c = t - (2 * z + 3)

        @pl.when((c >= 0) & (c < chunks))
        def _():
            @pl.when(z > 0)
            def _():
                x_copy(c).wait_recv()

            up_copy(c).wait_recv()
            here = columns(ylo * half, c)
            start = jnp.where(z > 0, xin[:, columns(0, c)], x0[:, here]).astype(f32)
            mine = up[:, here]
            other = upart[:, columns(0, c)]
            first = ylo == 0
            u_a = ul[2 * z]
            u_b = ul[2 * z + 1]
            x_a = (start + dot_nn(u_a, jnp.where(first, mine, other))).astype(bf16)
            x_b = (x_a.astype(f32) + dot_nn(u_b, jnp.where(first, other, mine))).astype(bf16)
            xkeep[:, columns(0, c)] = x_b

            @pl.when(z < sections // 2 - 1)
            def _():
                x_copy(c).start()

            xgive[:, columns(0, c)] = jnp.where(first, x_b, x_a)
            give_copy(c).start()
            xout[:, here] = jnp.where(first, x_a, x_b)

    def c_of(k):
        return to_col(ql[k, rows:rows + 1, :].astype(f32) + ql[k, rows + 1:rows + 2, :].astype(f32))

    def chain_back(t):
        c = t - (sections + 2 + 2 * (sections // 2 - 1 - z))

        @pl.when((c >= 0) & (c < chunks))
        def _():
            @pl.when(z < sections // 2 - 1)
            def _():
                b_copy(c).wait_recv()

            @pl.when(c == 0)
            def _():
                @pl.when(ylo == 1)
                def _():
                    q_arrived(2 * z).wait_recv()
                cpair[0] = jnp.broadcast_to(c_of(2 * z), (rows, rank))
                cpair[1] = jnp.broadcast_to(c_of(2 * z + 1), (rows, rank))

            wp_copy(c).wait_recv()
            here = columns(ylo * half, c)
            there = columns(0, c)
            first = ylo == 0
            mine = wd[here, :]
            other = wpart[there, :]
            g_b = jnp.where(z < sections // 2 - 1, gin[:, there], g16[:, here])
            x_a = jnp.where(z > 0, xin[:, there], x0[:, here]).astype(f32)
            x_b = jnp.where(first, xout[:, here], xgive[:, there]).astype(f32)
            q_a = ql[2 * z, 0:rows, :]
            q_b = ql[2 * z + 1, 0:rows, :]
            g_a = (g_b.astype(f32) + dot_nt(q_b, jnp.where(first, other, mine))
                   - cpair[1, :, 0:1] * x_b).astype(bf16)
            g_0 = (g_a.astype(f32) + dot_nt(q_a, jnp.where(first, mine, other))
                   - cpair[0, :, 0:1] * x_a).astype(bf16)

            @pl.when(z > 0)
            def _():
                gkeep[:, there] = g_0
                b_copy(c).start()

            ggive[:, there] = jnp.where(first, g_b, g_a)
            h_copy(c).start()
            gout[:, here] = jnp.where(first, g_a, g_b)

    def forward_tick(t, carry):
        k = t - 1

        @pl.when((t > 0) & (k != s))
        def _():
            u_arrived(k).wait_recv()

        @pl.when((t > 0) & (k < s))
        def _():
            pacc[...] += dot_nn(ul[k], mm[k])

        @pl.when(t == s)
        def _():
            @pl.when(s > 0)
            def _():
                n_copy().wait_recv()

            norm = jnp.where(s > 0, to_col(nl[0:1, :]), n0[:, 0:1])
            scale = lax.rsqrt(norm * (1.0 / width) + eps)
            pre = pacc[...] * scale
            value, grad = gelu_pair(pre)
            ul[s] = value.astype(bf16)

            def send(o, carry):
                u_copy(o).start()
                return carry

            lax.fori_loop(1, sections, send, 0)
            act[...] = pre
            slope[...] = grad
            rinv[...] = jnp.broadcast_to(scale, rinv.shape)

        @pl.when((t > 0) & (k > s))
        def _():
            ys[k] = yacc[...]

        @pl.when(t > 0)
        def _():
            yacc[...] += dot_nn(ul[k], gu[k])

        @pl.when((t == s) & (s < sections - 1))
        def _():
            mine = ul[s]
            norm = jnp.where(s > 0, to_col(nl[0:1, :]), n0[:, 0:1])
            grown = norm + jnp.sum(
                mine.astype(f32) * (2.0 * yacc[...] + dot_nn(mine, gu[s])), axis=1, keepdims=True)
            nsend[...] = jnp.broadcast_to(to_row(grown), nsend.shape)
            n_copy().start()

        @pl.when(t == 0)
        def _():
            lax.fori_loop(0, sections, start_m, 0)

        @pl.when(t < chunks)
        def _():
            up_copy(t).start()

        @pl.when((t >= 2) & (t < chunks + 2))
        def _():
            wp_copy(t - 2).start()

        chain(t)
        return carry

    lax.fori_loop(0, sections, forward_tick, 0)

    @pl.when(s != sections - 1)
    def _():
        u_arrived(sections - 1).wait_recv()

    def backward_tick(t, carry):
        j = 2 * sections - 1 - t
        k = j + 1
        behind = (k < sections) & (k > s)

        @pl.when(behind)
        def _():
            m_arrived(k).wait_recv()
            q_arrived(k).wait_recv()
            hacc[...] += dot_nt(ql[k, 0:rows, :], mb[k]) - c_of(k) * ys[k]

        @pl.when(s == j)
        def _():
            q = hacc[...] * slope[...]
            scale = rinv[...]
            ql[s, 0:rows, :] = (q * scale).astype(bf16)
            mix = jnp.sum(q * act[...], axis=1, keepdims=True) * (1.0 / width)
            line = to_row(mix * scale[:, 0:1] * scale[:, 0:1])
            high = line.astype(bf16)
            low = (line - high.astype(f32)).astype(bf16)
            spot = lax.broadcasted_iota(jnp.int32, (16, rows), 0)
            ql[s, rows:rows + 16, :] = jnp.where(
                spot == 0, high.astype(f32), jnp.where(spot == 1, low.astype(f32), 0.0)).astype(bf16)

            def send(i, carry):
                q_copy(s - 1 - i).start()
                return carry

            @pl.when(s > 0)
            def _():
                q_copy(s - 1).start()

            @pl.when(ylo == 0)
            def _():
                q_copy(s + 1).start()

            lax.fori_loop(1, s, send, 0)

        chain(t)
        chain_back(t)
        return carry

    lax.fori_loop(sections, 2 * sections, backward_tick, 0)

    def drain_tick(t, carry):
        chain_back(t)
        return carry

    lax.fori_loop(2 * sections, 2 * sections + chunks, drain_tick, 0)
    u_out[...] = ul[s]
    q_out[...] = ql[s, 0:rows, :]

    def finish(c, carry):
        @pl.when(z < sections // 2 - 1)
        def _():
            x_copy(c).wait_send()
        give_copy(c).wait_send()
        give_arrived(c).wait_recv()

        @pl.when(z > 0)
        def _():
            b_copy(c).wait_send()
        h_copy(c).wait_send()
        h_arrived(c).wait_recv()
        up_copy(c).wait_send()
        wp_copy(c).wait_send()
        return carry

    lax.fori_loop(0, chunks, finish, 0)

    def settle(o, carry):
        u_copy(o).wait_send()

        @pl.when(o - 1 < s)
        def _():
            q_copy(o - 1).wait_send()
            m_copy(o - 1).wait_send()
        return carry

    lax.fori_loop(1, sections, settle, 0)

    @pl.when(ylo == 0)
    def _():
        q_copy(s + 1).wait_send()

    @pl.when(s < sections - 1)
    def _():
        n_copy().wait_send()


def recurrence(sections, pyh, n0, mm, gu, x0, g16, up, wd):
    rows, width = x0.shape
    rank = up.shape[0]
    half = width // 2
    chunks = 14
    vm = pl.BlockSpec(memory_space=pltpu.VMEM)
    dma = pltpu.SemaphoreType.DMA
    sq = (rows, rank)
    wide = jax.ShapeDtypeStruct((rows, width), bf16)
    strip = pltpu.VMEM((rows, half), bf16)
    return pl.pallas_call(
        functools.partial(recurrence_kernel, sections, chunks),
        out_shape=(wide, wide, jax.ShapeDtypeStruct(sq, bf16), jax.ShapeDtypeStruct(sq, bf16)),
        in_specs=[vm] * 8,
        out_specs=(vm,) * 4,
        scratch_shapes=[
            pltpu.VMEM((sections, rows, rank), bf16),
            pltpu.VMEM((sections, rows + 16, rank), bf16),
            pltpu.VMEM((sections, rank, rank), bf16),
            pltpu.VMEM((sections, rows, rank), f32),
            pltpu.VMEM((8, rows), f32),
            pltpu.VMEM((8, rows), f32),
            pltpu.VMEM(sq, f32), pltpu.VMEM(sq, f32), pltpu.VMEM(sq, f32),
            pltpu.VMEM(sq, f32), pltpu.VMEM(sq, f32), pltpu.VMEM(sq, f32),
            pltpu.VMEM((2,) + sq, f32),
            pltpu.VMEM((rank, half), bf16),
            pltpu.VMEM((half, rank), bf16),
            strip, strip, strip, strip, strip, strip,
        ] + [dma((sections,))] * 6 + [dma((2,))] + [dma((chunks,))] * 12,
        compiler_params=pltpu.CompilerParams(
            collective_id=1, has_side_effects=True, vmem_limit_bytes=48 * 1024 * 1024),
    )(pyh, n0, mm, gu, x0, g16, up, wd)


def reduce_kernel(yh_n, x_n, sections, x1, g1, u_s, q_s, up, base, own, nxt,
                  part, rc, sums, rax, rby, sa, ray, sb, rbx, gs, nw,
                  c_send, c_recv, ax_send, ax_recv, s_sem, bx_send, bx_recv,
                  own_send, own_recv, oc_send, oc_recv, nx_send, nx_recv, ny_send, ny_recv,
                  nc_send, nc_recv):
    d = lax.axis_index("dp")
    s = lax.axis_index("section")
    yh = d // (2 * x_n)
    x = lax.rem(d // 2, x_n)
    core = lax.rem(d, 2)
    rows = base.shape[0]
    cut = rows // 2

    def place(y_, x_, c_):
        return {"dp": (y_ * x_n + x_) * 2 + c_}

    def xp(i):
        return lax.rem(x + i, x_n)

    other_core = place(yh, x, 1 - core)
    other_y = place(1 - yh, x, core)
    up_section = lax.rem(s + 1, sections)
    down_section = lax.rem(s + sections - 1, sections)

    def copy(src, dst, send, recv, where):
        return pltpu.make_async_remote_copy(src_ref=src, dst_ref=dst, send_sem=send, recv_sem=recv,
                                            device_id=where, device_id_type=MESH)

    barrier = pltpu.get_barrier_semaphore()
    peers = [other_core, other_y, {"section": up_section}, {"section": down_section}]
    peers += [place(yh, xp(i), core) for i in range(1, x_n)]
    for where in peers:
        pl.semaphore_signal(barrier, inc=1, device_id=where, device_id_type=MESH)
    pl.semaphore_wait(barrier, len(peers))

    def core_copy(b):
        return copy(part.at[b, 1 - core], rc.at[b], c_send.at[b], c_recv.at[b], other_core)

    def terms(b, carry):
        cols = pl.ds(pl.multiple_of(b * 2 * rows, 128), 2 * rows)
        u = u_s[...]
        before = (x1[:, cols].astype(f32) - dot_nn(u, up[:, cols])).astype(bf16)
        g_down = dot_tn(before, q_s[...]).astype(bf16)
        g_up = dot_tn(g1[:, cols], u).astype(bf16)
        rank = u.shape[1]
        for half in range(2):
            part[b, half, :, 0:rank] = g_down[half * rows:(half + 1) * rows]
            part[b, half, :, rank:2 * rank] = g_up[half * rows:(half + 1) * rows]
        core_copy(b).start()
        return carry

    blocks = yh_n * x_n
    lax.fori_loop(0, blocks, terms, 0)

    def first_sum(b, carry):
        core_copy(b).wait_recv()
        y_ = b // x_n
        x_ = lax.rem(b, x_n)
        sums[y_, x_] = (part[b, core].astype(f32) + rc[b].astype(f32)).astype(bf16)
        return carry

    lax.fori_loop(0, blocks, first_sum, 0)

    def ax_copy(i):
        return copy(sums.at[:, xp(i), 0:cut], rax.at[i - 1], ax_send.at[i - 1], ax_recv.at[i - 1],
                    place(yh, xp(i), core))

    by_copy = copy(sums.at[1 - yh, :, cut:rows], rby, s_sem.at[0], s_sem.at[1], other_y)
    ay_copy = copy(sa.at[1 - yh], ray, s_sem.at[2], s_sem.at[3], other_y)

    def bx_copy(i):
        return copy(sb.at[xp(i)], rbx.at[i - 1], bx_send.at[i - 1], bx_recv.at[i - 1],
                    place(yh, xp(i), core))

    by_copy.start()
    for i in range(1, x_n):
        ax_copy(i).start()
    for i in range(1, x_n):
        ax_copy(i).wait_recv()
    for y_ in range(yh_n):
        total = sums[y_, x, 0:cut].astype(f32)
        for i in range(1, x_n):
            total = total + rax[i - 1, y_].astype(f32)
        sa[y_] = total.astype(bf16)
    ay_copy.start()
    by_copy.wait_recv()
    for x_ in range(x_n):
        sb[x_] = (sums[yh, x_, cut:rows].astype(f32) + rby[x_].astype(f32)).astype(bf16)
    for i in range(1, x_n):
        bx_copy(i).start()
    ay_copy.wait_recv()
    total_a = sa[yh].astype(f32) + ray[...].astype(f32)
    for i in range(1, x_n):
        bx_copy(i).wait_recv()
    total_b = sb[x].astype(f32)
    for i in range(1, x_n):
        total_b = total_b + rbx[i - 1].astype(f32)
    gs[0:cut] = total_a.astype(bf16)
    gs[cut:rows] = total_b.astype(bf16)
    nw[...] = (base[...].astype(f32) - learn_rate * gs[...].astype(f32)).astype(bf16)

    has_next = s < sections - 1
    next_copy = copy(nw, nxt.at[yh, x, core], s_sem.at[4], s_sem.at[5], {"section": down_section})
    own_y = copy(gs, own.at[yh, x, core], s_sem.at[6], s_sem.at[7], other_y)
    own_y.start()

    @pl.when(s > 0)
    def _():
        next_copy.start()

    own[yh, x, core] = gs[...]

    def own_x(i):
        return copy(own.at[:, x, core], own.at[:, x, core], own_send.at[i - 1], own_recv.at[i - 1],
                    place(yh, xp(i), core))

    def own_c(i):
        spot = own.at[:, xp(i), core]
        return copy(spot, spot, oc_send.at[i], oc_recv.at[i], other_core)

    own_y.wait_recv()
    for i in range(1, x_n):
        own_x(i).start()
    own_c(0).start()

    def nxt_x(i):
        spot = nxt.at[yh, x, core]
        return copy(spot, spot, nx_send.at[i - 1], nx_recv.at[i - 1], place(yh, xp(i), core))

    def nxt_y(i):
        spot = nxt.at[yh, xp(i), core]
        return copy(spot, spot, ny_send.at[i], ny_recv.at[i], other_y)

    def nxt_c(i):
        spot = nxt.at[:, xp(i), core]
        return copy(spot, spot, nc_send.at[i], nc_recv.at[i], other_core)

    @pl.when(has_next)
    def _():
        next_copy.wait_recv()
        for i in range(1, x_n):
            nxt_x(i).start()
        nxt_y(0).start()

    for i in range(1, x_n):
        own_x(x_n - i).wait_recv()
        own_c(i).start()

    @pl.when(has_next)
    def _():
        for i in range(1, x_n):
            nxt_x(x_n - i).wait_recv()
            nxt_y(i).start()
        for i in range(x_n):
            nxt_y(i).wait_recv()
            nxt_c(i).start()
        for i in range(x_n):
            nxt_c(i).wait()
            nxt_y(i).wait_send()
        for i in range(1, x_n):
            nxt_x(i).wait_send()

    for i in range(x_n):
        own_c(i).wait()
    for i in range(1, x_n):
        own_x(i).wait_send()
        ax_copy(i).wait_send()
        bx_copy(i).wait_send()
    by_copy.wait_send()
    ay_copy.wait_send()
    own_y.wait_send()

    @pl.when(s > 0)
    def _():
        next_copy.wait_send()

    def settle(b, carry):
        core_copy(b).wait_send()
        return carry

    lax.fori_loop(0, blocks, settle, 0)


def reduce_gather(sections, shards, x1, g1, u_s, q_s, up, base):
    x_n = 4
    yh_n = shards // (2 * x_n)
    rows, cols = base.shape
    cut = rows // 2
    vm = pl.BlockSpec(memory_space=pltpu.VMEM)
    dma = pltpu.SemaphoreType.DMA
    full = jax.ShapeDtypeStruct((yh_n, x_n, 2, rows, cols), bf16)

    def buf(*lead):
        return pltpu.VMEM(lead + (cols,), bf16)

    return pl.pallas_call(
        functools.partial(reduce_kernel, yh_n, x_n, sections),
        out_shape=(full, full),
        in_specs=[vm] * 6,
        out_specs=(vm, vm),
        scratch_shapes=[
            buf(yh_n * x_n, 2, rows), buf(yh_n * x_n, rows), buf(yh_n, x_n, rows),
            buf(x_n - 1, yh_n, cut), buf(x_n, cut), buf(yh_n, cut), buf(cut),
            buf(x_n, cut), buf(x_n - 1, cut), buf(rows), buf(rows),
            dma((yh_n * x_n,)), dma((yh_n * x_n,)), dma((x_n - 1,)), dma((x_n - 1,)), dma((8,)),
            dma((x_n - 1,)), dma((x_n - 1,)), dma((x_n - 1,)), dma((x_n - 1,)),
            dma((x_n,)), dma((x_n,)), dma((x_n - 1,)), dma((x_n - 1,)), dma((x_n,)), dma((x_n,)),
            dma((x_n,)), dma((x_n,)),
        ],
        compiler_params=pltpu.CompilerParams(
            collective_id=2, has_side_effects=True, vmem_limit_bytes=52 * 1024 * 1024),
    )(x1, g1, u_s, q_s, up, base)


def finish_kernel(sections, own, nxt, x1, grad_down, grad_up, advance):
    last = lax.axis_index("section") == sections - 1
    rows, width = x1.shape
    rank = grad_down.shape[1]
    step = 896
    count = width // step

    def first(b, carry):
        pre, norm = carry
        here = pl.ds(pl.multiple_of(b * step, 128), step)
        block = own[here, :]
        grad_down[here, :] = block[:, 0:rank]
        grad_up[:, here] = block[:, rank:2 * rank].astype(f32).T.astype(bf16)
        x = x1[:, here]
        values = x.astype(f32)
        pre = pre + dot_nn(x, nxt[here, 0:rank])
        return pre, norm + jnp.sum(values * values, axis=1, keepdims=True)

    pre, norm = lax.fori_loop(
        0, count, first, (jnp.zeros((rows, rank), f32), jnp.zeros((rows, 1), f32)))
    value, unused = gelu_pair(pre * lax.rsqrt(norm * (1.0 / width) + eps))
    value = value.astype(bf16)

    def second(b, carry):
        here = pl.ds(pl.multiple_of(b * step, 128), step)
        bump = dot_nt(value, nxt[here, rank:2 * rank])
        advance[:, here] = (x1[:, here].astype(f32) + jnp.where(last, 0.0, bump)).astype(bf16)
        return carry

    lax.fori_loop(0, count, second, 0)


def finish(sections, own, nxt, x1):
    rows, width = x1.shape
    rank = own.shape[1] // 2
    vm = pl.BlockSpec(memory_space=pltpu.VMEM)
    return pl.pallas_call(
        functools.partial(finish_kernel, sections),
        out_shape=(
            jax.ShapeDtypeStruct((width, rank), bf16),
            jax.ShapeDtypeStruct((rank, width), bf16),
            jax.ShapeDtypeStruct((rows, width), bf16),
        ),
        in_specs=[vm] * 3,
        out_specs=(vm,) * 3,
        compiler_params=pltpu.CompilerParams(vmem_limit_bytes=48 * 1024 * 1024),
    )(own, nxt, x1)


def per_device(inputs, cotangent, w_down, w_up):
    down = w_down[0]
    upward = w_up[0]
    micro, batch_rows, width = inputs.shape
    rank = down.shape[1]
    rows = micro * batch_rows
    sections = lax.axis_size("section")
    shards = lax.axis_size("dp")
    part = width // shards
    d = lax.axis_index("dp")
    x0 = inputs.reshape(rows, width)
    g16 = cotangent.reshape(rows, width)
    up_t = upward.T

    mine_u = lax.dynamic_slice_in_dim(up_t, d * part, part, 0)
    mine_w = lax.dynamic_slice_in_dim(down, d * part, part, 0)
    all_u = lax.all_gather(mine_u, "section")
    base = jnp.concatenate([mine_w, mine_u], axis=1)
    grams = jnp.einsum("kfr,fc->krc", all_u, base,
                       preferred_element_type=f32).astype(bf16)
    grams = lax.psum(grams, "dp")
    mm = grams[:, :, :rank]
    gu = grams[:, :, rank:]

    pyh = jnp.stack([dot_nn(x0, down), dot_nt(x0, upward), dot_nt(g16, upward)])
    values = x0.astype(f32)
    n0 = jnp.broadcast_to(jnp.sum(values * values, axis=1, keepdims=True), (rows, rank))

    x1, g1, u_s, q_s = recurrence(sections, pyh, n0, mm, gu, x0, g16, upward, down)
    own, nxt = reduce_gather(sections, shards, x1, g1, u_s, q_s, upward, base)
    wide = (width, 2 * rank)
    grad_down, grad_up, advance = finish(sections, own.reshape(wide), nxt.reshape(wide), x1)
    return (grad_down[None], grad_up[None], advance.reshape(1, micro, batch_rows, width))


def solution(mesh):
    in_specs = (
        P(None, "dp", None),
        P(None, "dp", None),
        P("section", None, None),
        P("section", None, None),
    )
    out_specs = (P("section", None, None), P("section", None, None), P("section", None, "dp", None))
    return jax.shard_map(
        per_device, mesh=mesh, in_specs=in_specs, out_specs=out_specs, check_vma=False
    )
```

```python
import functools

import jax
import jax.numpy as jnp
from jax import lax
from jax.experimental import pallas as pl
from jax.experimental.pallas import tpu as pltpu
from jax.sharding import PartitionSpec as P

MESH = pl.DeviceIdType.MESH
eps = 1e-05
learn_rate = 0.05
f32 = jnp.float32
bf16 = jnp.bfloat16


def dot_nn(a, b):
    return jnp.dot(a, b, preferred_element_type=f32)


def dot_tn(a, b):
    return lax.dot_general(a, b, (((0,), (0,)), ((), ())), preferred_element_type=f32)


def dot_nt(a, b):
    return lax.dot_general(a, b, (((1,), (1,)), ((), ())), preferred_element_type=f32)


def gelu_pair(a):
    c = 0.7978845608028654
    inner = c * (a + 0.044715 * a * a * a)
    th = jnp.tanh(inner)
    value = 0.5 * a * (1.0 + th)
    slope = 0.5 * (1.0 + th) + 0.5 * a * (1.0 - th * th) * c * (1.0 + 3 * 0.044715 * a * a)
    return value, slope


def recurrence_kernel(sections, chunks, pyh, n0, mm, gu, x0, g16, up, wd,
                      xout, gout, u_out, q_out,
                      ul, ql, mb, ys, nl, nsend, pacc, yacc, hacc, slope, act, rinv, cpair,
                      upart, wpart, xin, xkeep, xgive, gin, gkeep, ggive,
                      u_send, u_recv, q_send, q_recv, m_send, m_recv, n_sem,
                      up_send, up_recv, wp_send, wp_recv, c_send, c_recv, g_send, g_recv,
                      b_send, b_recv, h_send, h_recv):
    s = lax.axis_index("section")
    rows, width = x0.shape
    rank = up.shape[0]
    half = width // 2
    piece = half // chunks
    z = s // 2
    ylo = lax.rem(s, 2)
    partner = s + 1 - 2 * ylo

    def peer(offset):
        return lax.rem(s + offset, sections)

    barrier = pltpu.get_barrier_semaphore()

    def greet(o, carry):
        pl.semaphore_signal(barrier, inc=1, device_id={"section": peer(o)}, device_id_type=MESH)
        return carry

    lax.fori_loop(1, sections, greet, 0)
    pl.semaphore_wait(barrier, sections - 1)

    eye = (lax.broadcasted_iota(jnp.int32, (rows, rows), 0)
           == lax.broadcasted_iota(jnp.int32, (rows, rows), 1)).astype(f32)

    def to_row(col):
        return jnp.sum(eye * col, axis=0, keepdims=True)

    def to_col(row):
        return jnp.sum(eye * row, axis=1, keepdims=True)

    def columns(base, c):
        return pl.ds(pl.multiple_of(base + c * piece, 128), piece)

    def up_copy(c):
        return pltpu.make_async_remote_copy(
            src_ref=up.at[:, columns((1 - ylo) * half, c)], dst_ref=upart.at[:, columns(0, c)],
            send_sem=up_send.at[c], recv_sem=up_recv.at[c],
            device_id={"section": partner}, device_id_type=MESH)

    def wp_copy(c):
        return pltpu.make_async_remote_copy(
            src_ref=wd.at[columns((1 - ylo) * half, c), :], dst_ref=wpart.at[columns(0, c), :],
            send_sem=wp_send.at[c], recv_sem=wp_recv.at[c],
            device_id={"section": partner}, device_id_type=MESH)

    def b_copy(c):
        return pltpu.make_async_remote_copy(
            src_ref=gkeep.at[:, columns(0, c)], dst_ref=gin.at[:, columns(0, c)],
            send_sem=b_send.at[c], recv_sem=b_recv.at[c],
            device_id={"section": peer(sections - 2)}, device_id_type=MESH)

    def h_copy(c):
        return pltpu.make_async_remote_copy(
            src_ref=ggive.at[:, columns(0, c)], dst_ref=gout.at[:, columns(ylo * half, c)],
            send_sem=h_send.at[c], recv_sem=h_recv.at[c],
            device_id={"section": partner}, device_id_type=MESH)

    def h_arrived(c):
        return pltpu.make_async_remote_copy(
            src_ref=ggive.at[:, columns(0, c)], dst_ref=gout.at[:, columns((1 - ylo) * half, c)],
            send_sem=h_send.at[c], recv_sem=h_recv.at[c],
            device_id={"section": partner}, device_id_type=MESH)

    def u_copy(o):
        return pltpu.make_async_remote_copy(
            src_ref=ul.at[s], dst_ref=ul.at[s], send_sem=u_send.at[o], recv_sem=u_recv.at[s],
            device_id={"section": peer(o)}, device_id_type=MESH)

    def u_arrived(k):
        return pltpu.make_async_remote_copy(
            src_ref=ul.at[k], dst_ref=ul.at[k], send_sem=u_send.at[0], recv_sem=u_recv.at[k],
            device_id={"section": partner}, device_id_type=MESH)

    def q_copy(j):
        return pltpu.make_async_remote_copy(
            src_ref=ql.at[s], dst_ref=ql.at[s], send_sem=q_send.at[j], recv_sem=q_recv.at[s],
            device_id={"section": j}, device_id_type=MESH)

    def q_arrived(k):
        return pltpu.make_async_remote_copy(
            src_ref=ql.at[k], dst_ref=ql.at[k], send_sem=q_send.at[0], recv_sem=q_recv.at[k],
            device_id={"section": partner}, device_id_type=MESH)

    def m_copy(j):
        return pltpu.make_async_remote_copy(
            src_ref=mm.at[j], dst_ref=mb.at[s], send_sem=m_send.at[j], recv_sem=m_recv.at[s],
            device_id={"section": j}, device_id_type=MESH)

    def m_arrived(k):
        return pltpu.make_async_remote_copy(
            src_ref=mb.at[k], dst_ref=mb.at[k], send_sem=m_send.at[0], recv_sem=m_recv.at[k],
            device_id={"section": partner}, device_id_type=MESH)

    def n_copy():
        return pltpu.make_async_remote_copy(
            src_ref=nsend, dst_ref=nl, send_sem=n_sem.at[0], recv_sem=n_sem.at[1],
            device_id={"section": peer(1)}, device_id_type=MESH)

    def x_copy(c):
        return pltpu.make_async_remote_copy(
            src_ref=xkeep.at[:, columns(0, c)], dst_ref=xin.at[:, columns(0, c)],
            send_sem=c_send.at[c], recv_sem=c_recv.at[c],
            device_id={"section": peer(2)}, device_id_type=MESH)

    def give_copy(c):
        return pltpu.make_async_remote_copy(
            src_ref=xgive.at[:, columns(0, c)], dst_ref=xout.at[:, columns(ylo * half, c)],
            send_sem=g_send.at[c], recv_sem=g_recv.at[c],
            device_id={"section": partner}, device_id_type=MESH)

    def give_arrived(c):
        return pltpu.make_async_remote_copy(
            src_ref=xgive.at[:, columns(0, c)], dst_ref=xout.at[:, columns((1 - ylo) * half, c)],
            send_sem=g_send.at[c], recv_sem=g_recv.at[c],
            device_id={"section": partner}, device_id_type=MESH)

    def start_m(j, carry):
        @pl.when(j < s)
        def _():
            m_copy(j).start()
        return carry

    pacc[...] = pyh[0]
    yacc[...] = pyh[1]
    hacc[...] = pyh[2]

    def chain(t):
        c = t - (2 * z + 3)

        @pl.when((c >= 0) & (c < chunks))
        def _():
            @pl.when(z > 0)
            def _():
                x_copy(c).wait_recv()

            up_copy(c).wait_recv()
            here = columns(ylo * half, c)
            start = jnp.where(z > 0, xin[:, columns(0, c)], x0[:, here]).astype(f32)
            mine = up[:, here]
            other = upart[:, columns(0, c)]
            first = ylo == 0
            u_a = ul[2 * z]
            u_b = ul[2 * z + 1]
            x_a = (start + dot_nn(u_a, jnp.where(first, mine, other))).astype(bf16)
            x_b = (x_a.astype(f32) + dot_nn(u_b, jnp.where(first, other, mine))).astype(bf16)
            xkeep[:, columns(0, c)] = x_b

            @pl.when(z < sections // 2 - 1)
            def _():
                x_copy(c).start()

            xgive[:, columns(0, c)] = jnp.where(first, x_b, x_a)
            give_copy(c).start()
            xout[:, here] = jnp.where(first, x_a, x_b)

    def c_of(k):
        return to_col(ql[k, rows:rows + 1, :].astype(f32) + ql[k, rows + 1:rows + 2, :].astype(f32))

    def chain_back(t):
        c = t - (sections + 2 + 2 * (sections // 2 - 1 - z))

        @pl.when((c >= 0) & (c < chunks))
        def _():
            @pl.when(z < sections // 2 - 1)
            def _():
                b_copy(c).wait_recv()

            @pl.when(c == 0)
            def _():
                @pl.when(ylo == 1)
                def _():
                    q_arrived(2 * z).wait_recv()
                cpair[0] = jnp.broadcast_to(c_of(2 * z), (rows, rank))
                cpair[1] = jnp.broadcast_to(c_of(2 * z + 1), (rows, rank))

            wp_copy(c).wait_recv()
            here = columns(ylo * half, c)
            there = columns(0, c)
            first = ylo == 0
            mine = wd[here, :]
            other = wpart[there, :]
            g_b = jnp.where(z < sections // 2 - 1, gin[:, there], g16[:, here])
            x_a = jnp.where(z > 0, xin[:, there], x0[:, here]).astype(f32)
            x_b = jnp.where(first, xout[:, here], xgive[:, there]).astype(f32)
            q_a = ql[2 * z, 0:rows, :]
            q_b = ql[2 * z + 1, 0:rows, :]
            g_a = (g_b.astype(f32) + dot_nt(q_b, jnp.where(first, other, mine))
                   - cpair[1, :, 0:1] * x_b).astype(bf16)
            g_0 = (g_a.astype(f32) + dot_nt(q_a, jnp.where(first, mine, other))
                   - cpair[0, :, 0:1] * x_a).astype(bf16)

            @pl.when(z > 0)
            def _():
                gkeep[:, there] = g_0
                b_copy(c).start()

            ggive[:, there] = jnp.where(first, g_b, g_a)
            h_copy(c).start()
            gout[:, here] = jnp.where(first, g_a, g_b)

    def forward_tick(t, carry):
        k = t - 1

        @pl.when((t > 0) & (k != s))
        def _():
            u_arrived(k).wait_recv()

        @pl.when((t > 0) & (k < s))
        def _():
            pacc[...] += dot_nn(ul[k], mm[k])

        @pl.when(t == s)
        def _():
            @pl.when(s > 0)
            def _():
                n_copy().wait_recv()

            norm = jnp.where(s > 0, to_col(nl[0:1, :]), n0[:, 0:1])
            scale = lax.rsqrt(norm * (1.0 / width) + eps)
            pre = pacc[...] * scale
            value, grad = gelu_pair(pre)
            ul[s] = value.astype(bf16)

            def send(o, carry):
                u_copy(o).start()
                return carry

            lax.fori_loop(1, sections, send, 0)
            act[...] = pre
            slope[...] = grad
            rinv[...] = jnp.broadcast_to(scale, rinv.shape)

        @pl.when((t > 0) & (k > s))
        def _():
            ys[k] = yacc[...]

        @pl.when(t > 0)
        def _():
            yacc[...] += dot_nn(ul[k], gu[k])

        @pl.when((t == s) & (s < sections - 1))
        def _():
            mine = ul[s]
            norm = jnp.where(s > 0, to_col(nl[0:1, :]), n0[:, 0:1])
            grown = norm + jnp.sum(
                mine.astype(f32) * (2.0 * yacc[...] + dot_nn(mine, gu[s])), axis=1, keepdims=True)
            nsend[...] = jnp.broadcast_to(to_row(grown), nsend.shape)
            n_copy().start()

        @pl.when(t == 0)
        def _():
            lax.fori_loop(0, sections, start_m, 0)

        @pl.when(t < chunks)
        def _():
            up_copy(t).start()

        @pl.when((t >= 2) & (t < chunks + 2))
        def _():
            wp_copy(t - 2).start()

        chain(t)
        return carry

    lax.fori_loop(0, sections, forward_tick, 0)

    @pl.when(s != sections - 1)
    def _():
        u_arrived(sections - 1).wait_recv()

    def backward_tick(t, carry):
        j = 2 * sections - 1 - t
        k = j + 1
        behind = (k < sections) & (k > s)

        @pl.when(behind)
        def _():
            m_arrived(k).wait_recv()
            q_arrived(k).wait_recv()
            hacc[...] += dot_nt(ql[k, 0:rows, :], mb[k]) - c_of(k) * ys[k]

        @pl.when(s == j)
        def _():
            q = hacc[...] * slope[...]
            scale = rinv[...]
            ql[s, 0:rows, :] = (q * scale).astype(bf16)
            mix = jnp.sum(q * act[...], axis=1, keepdims=True) * (1.0 / width)
            line = to_row(mix * scale[:, 0:1] * scale[:, 0:1])
            high = line.astype(bf16)
            low = (line - high.astype(f32)).astype(bf16)
            spot = lax.broadcasted_iota(jnp.int32, (16, rows), 0)
            ql[s, rows:rows + 16, :] = jnp.where(
                spot == 0, high.astype(f32), jnp.where(spot == 1, low.astype(f32), 0.0)).astype(bf16)

            def send(i, carry):
                q_copy(s - 1 - i).start()
                return carry

            @pl.when(s > 0)
            def _():
                q_copy(s - 1).start()

            @pl.when(ylo == 0)
            def _():
                q_copy(s + 1).start()

            lax.fori_loop(1, s, send, 0)

        chain(t)
        chain_back(t)
        return carry

    lax.fori_loop(sections, 2 * sections, backward_tick, 0)

    def drain_tick(t, carry):
        chain_back(t)
        return carry

    lax.fori_loop(2 * sections, 2 * sections + chunks, drain_tick, 0)
    u_out[...] = ul[s]
    q_out[...] = ql[s, 0:rows, :]

    def finish(c, carry):
        @pl.when(z < sections // 2 - 1)
        def _():
            x_copy(c).wait_send()
        give_copy(c).wait_send()
        give_arrived(c).wait_recv()

        @pl.when(z > 0)
        def _():
            b_copy(c).wait_send()
        h_copy(c).wait_send()
        h_arrived(c).wait_recv()
        up_copy(c).wait_send()
        wp_copy(c).wait_send()
        return carry

    lax.fori_loop(0, chunks, finish, 0)

    def settle(o, carry):
        u_copy(o).wait_send()

        @pl.when(o - 1 < s)
        def _():
            q_copy(o - 1).wait_send()
            m_copy(o - 1).wait_send()
        return carry

    lax.fori_loop(1, sections, settle, 0)

    @pl.when(ylo == 0)
    def _():
        q_copy(s + 1).wait_send()

    @pl.when(s < sections - 1)
    def _():
        n_copy().wait_send()


def recurrence(sections, pyh, n0, mm, gu, x0, g16, up, wd):
    rows, width = x0.shape
    rank = up.shape[0]
    half = width // 2
    chunks = 14
    vm = pl.BlockSpec(memory_space=pltpu.VMEM)
    dma = pltpu.SemaphoreType.DMA
    sq = (rows, rank)
    wide = jax.ShapeDtypeStruct((rows, width), bf16)
    strip = pltpu.VMEM((rows, half), bf16)
    return pl.pallas_call(
        functools.partial(recurrence_kernel, sections, chunks),
        out_shape=(wide, wide, jax.ShapeDtypeStruct(sq, bf16), jax.ShapeDtypeStruct(sq, bf16)),
        in_specs=[vm] * 8,
        out_specs=(vm,) * 4,
        scratch_shapes=[
            pltpu.VMEM((sections, rows, rank), bf16),
            pltpu.VMEM((sections, rows + 16, rank), bf16),
            pltpu.VMEM((sections, rank, rank), bf16),
            pltpu.VMEM((sections, rows, rank), f32),
            pltpu.VMEM((8, rows), f32),
            pltpu.VMEM((8, rows), f32),
            pltpu.VMEM(sq, f32), pltpu.VMEM(sq, f32), pltpu.VMEM(sq, f32),
            pltpu.VMEM(sq, f32), pltpu.VMEM(sq, f32), pltpu.VMEM(sq, f32),
            pltpu.VMEM((2,) + sq, f32),
            pltpu.VMEM((rank, half), bf16),
            pltpu.VMEM((half, rank), bf16),
            strip, strip, strip, strip, strip, strip,
        ] + [dma((sections,))] * 6 + [dma((2,))] + [dma((chunks,))] * 12,
        compiler_params=pltpu.CompilerParams(
            collective_id=1, has_side_effects=True, vmem_limit_bytes=48 * 1024 * 1024),
    )(pyh, n0, mm, gu, x0, g16, up, wd)


def dp_place(x_n):
    d = lax.axis_index("dp")
    return d // (2 * x_n), lax.rem(d // 2, x_n), lax.rem(d, 2)


def remote(src, dst, send, recv, where):
    return pltpu.make_async_remote_copy(src_ref=src, dst_ref=dst, send_sem=send, recv_sem=recv,
                                        device_id=where, device_id_type=MESH)


def scatter_sum(yh_n, x_n, core_copy, part, rc, sums, rax, rby, sa, ray, sb, rbx,
                ax_send, ax_recv, s_sem, bx_send, bx_recv):
    yh, x, core = dp_place(x_n)
    rows = sums.shape[2]
    cut = rows // 2
    blocks = yh_n * x_n

    def place(y_, x_, c_):
        return {"dp": (y_ * x_n + x_) * 2 + c_}

    def xp(i):
        return lax.rem(x + i, x_n)

    other_y = place(1 - yh, x, core)
    copy = remote

    def first_sum(b, carry):
        core_copy(b).wait_recv()
        y_ = b // x_n
        x_ = lax.rem(b, x_n)
        sums[y_, x_] = (part[b, core].astype(f32) + rc[b].astype(f32)).astype(bf16)
        return carry

    lax.fori_loop(0, blocks, first_sum, 0)

    def ax_copy(i):
        return copy(sums.at[:, xp(i), 0:cut], rax.at[i - 1], ax_send.at[i - 1], ax_recv.at[i - 1],
                    place(yh, xp(i), core))

    by_copy = copy(sums.at[1 - yh, :, cut:rows], rby, s_sem.at[0], s_sem.at[1], other_y)
    ay_copy = copy(sa.at[1 - yh], ray, s_sem.at[2], s_sem.at[3], other_y)

    def bx_copy(i):
        return copy(sb.at[xp(i)], rbx.at[i - 1], bx_send.at[i - 1], bx_recv.at[i - 1],
                    place(yh, xp(i), core))

    by_copy.start()
    for i in range(1, x_n):
        ax_copy(i).start()
    for i in range(1, x_n):
        ax_copy(i).wait_recv()
    for y_ in range(yh_n):
        total = sums[y_, x, 0:cut].astype(f32)
        for i in range(1, x_n):
            total = total + rax[i - 1, y_].astype(f32)
        sa[y_] = total.astype(bf16)
    ay_copy.start()
    by_copy.wait_recv()
    for x_ in range(x_n):
        sb[x_] = (sums[yh, x_, cut:rows].astype(f32) + rby[x_].astype(f32)).astype(bf16)
    for i in range(1, x_n):
        bx_copy(i).start()
    ay_copy.wait_recv()
    total_a = sa[yh].astype(f32) + ray[...].astype(f32)
    for i in range(1, x_n):
        bx_copy(i).wait_recv()
    total_b = sb[x].astype(f32)
    for i in range(1, x_n):
        total_b = total_b + rbx[i - 1].astype(f32)
    for i in range(1, x_n):
        ax_copy(i).wait_send()
        bx_copy(i).wait_send()
    by_copy.wait_send()
    ay_copy.wait_send()
    return total_a, total_b


def gram_kernel(yh_n, x_n, sections, x0, g16, down, up, mine_u, base, pyh, n0, out,
                allu, part, rc, sums, rax, rby, sa, ray, sb, rbx, gs,
                z_sem, f_send, f_recv, r_send, r_recv,
                c_send, c_recv, ax_send, ax_recv, s_sem, bx_send, bx_recv,
                ga_send, ga_recv, gb_send, gb_recv, gc_send, gc_recv):
    yh, x, core = dp_place(x_n)
    s = lax.axis_index("section")
    z_n = sections // 2
    z = s // 2
    ylo = lax.rem(s, 2)
    rank = up.shape[0]
    rows = rank
    cut = rows // 2

    def place(y_, x_, c_):
        return {"dp": (y_ * x_n + x_) * 2 + c_}

    def xp(i):
        return lax.rem(x + i, x_n)

    def zp(i):
        return lax.rem(z + i, z_n)

    other_core = place(yh, x, 1 - core)
    other_y = place(1 - yh, x, core)
    partner = {"section": s + 1 - 2 * ylo}
    after = {"section": 2 * zp(1) + ylo}
    before = {"section": 2 * zp(z_n - 1) + ylo}

    barrier = pltpu.get_barrier_semaphore()
    peers = [other_core, other_y, partner, after, before]
    peers += [place(yh, xp(i), core) for i in range(1, x_n)]
    for where in peers:
        pl.semaphore_signal(barrier, inc=1, device_id=where, device_id_type=MESH)
    pl.semaphore_wait(barrier, len(peers))

    pair = remote(mine_u, allu.at[z, ylo], z_sem.at[0], z_sem.at[1], partner)
    pair.start()
    allu[z, ylo] = mine_u[...]

    def products(z_):
        for y_ in range(2):
            part[z_, y_] = dot_tn(allu[z_, y_], base[...]).astype(bf16)

    def core_copy(b):
        return remote(part.at[b, 1 - core], rc.at[b], c_send.at[b], c_recv.at[b], other_core)

    hops = z_n // 2

    def ring_f(i):
        if i < hops:
            spot = allu.at[zp(z_n + 1 - i)]
        else:
            spot = allu.at[zp(z_n + 1 - i), 0]
        return remote(spot, spot, f_send.at[i - 1], f_recv.at[i - 1], after)

    def ring_r(i):
        if i < hops:
            spot = allu.at[zp(i - 1)]
        else:
            spot = allu.at[zp(i - 1), 1]
        return remote(spot, spot, r_send.at[i - 1], r_recv.at[i - 1], before)

    pair.wait_recv()
    ring_f(1).start()
    ring_r(1).start()

    u = up[...]
    w = down[...]
    values = x0[...]
    pyh[0] = dot_nn(values, w)
    pyh[1] = dot_nt(values, u)
    pyh[2] = dot_nt(g16[...], u)
    wide = values.astype(f32)
    n0[...] = jnp.broadcast_to(jnp.sum(wide * wide, axis=1, keepdims=True), n0.shape)
    products(z)
    core_copy(z).start()
    for i in range(1, hops + 1):
        ring_f(i).wait_recv()
        if i < hops:
            ring_f(i + 1).start()
        ring_r(i).wait_recv()
        if i < hops:
            ring_r(i + 1).start()
        products(zp(z_n - i))
        core_copy(zp(z_n - i)).start()
        if i < hops:
            products(zp(i))
            core_copy(zp(i)).start()

    total_a, total_b = scatter_sum(yh_n, x_n, core_copy, part, rc, sums, rax, rby, sa, ray, sb, rbx,
                                   ax_send, ax_recv, s_sem, bx_send, bx_recv)
    gs[0:cut] = total_a.astype(bf16)
    gs[cut:rows] = total_b.astype(bf16)
    out[yh, x, core] = gs[...]

    low = pl.ds(0, cut)
    high = pl.ds(cut, cut)

    def spread(src, spot, sems, i, where):
        return remote(src, spot, sems[0].at[i], sems[1].at[i], where)

    ga = (ga_send, ga_recv)
    gb = (gb_send, gb_recv)
    a_y = spread(gs.at[low], out.at[yh, x, core, low], ga, 0, other_y)

    def a_x(i):
        spot = out.at[:, x, core, low]
        return spread(spot, spot, ga, i, place(yh, xp(i), core))

    def b_x(i):
        return spread(gs.at[high], out.at[yh, x, core, high], gb, i - 1, place(yh, xp(i), core))

    def b_y(i):
        spot = out.at[yh, xp(i), core, high]
        return spread(spot, spot, gb, x_n - 1 + i, other_y)

    def all_c(i):
        spot = out.at[:, xp(i), core]
        return remote(spot, spot, gc_send.at[i], gc_recv.at[i], other_core)

    a_y.start()
    for i in range(1, x_n):
        b_x(i).start()
    b_y(0).start()
    a_y.wait_recv()
    for i in range(1, x_n):
        a_x(i).start()
    for i in range(1, x_n):
        b_x(x_n - i).wait_recv()
        b_y(i).start()
    b_y(0).wait_recv()
    all_c(0).start()
    for i in range(1, x_n):
        a_x(x_n - i).wait_recv()
        b_y(i).wait_recv()
        all_c(i).start()
    for i in range(x_n):
        all_c(i).wait()
        b_y(i).wait_send()
    for i in range(1, x_n):
        a_x(i).wait_send()
        b_x(i).wait_send()
    a_y.wait_send()
    pair.wait_send()
    for i in range(1, hops + 1):
        ring_f(i).wait_send()
        ring_r(i).wait_send()

    def settle(b, carry):
        core_copy(b).wait_send()
        return carry

    lax.fori_loop(0, yh_n * x_n, settle, 0)


def grams_of(sections, shards, x0, g16, down, up, mine_u, base):
    x_n = 4
    yh_n = shards // (2 * x_n)
    rows, width = x0.shape
    rank = up.shape[0]
    height = mine_u.shape[0]
    cut = rank // 2
    vm = pl.BlockSpec(memory_space=pltpu.VMEM)
    dma = pltpu.SemaphoreType.DMA

    def buf(*lead):
        return pltpu.VMEM(lead + (2 * rank,), bf16)

    return pl.pallas_call(
        functools.partial(gram_kernel, yh_n, x_n, sections),
        out_shape=(
            jax.ShapeDtypeStruct((3, rows, rank), f32),
            jax.ShapeDtypeStruct((rows, rank), f32),
            jax.ShapeDtypeStruct((yh_n, x_n, 2, rank, 2 * rank), bf16),
        ),
        in_specs=[vm] * 6,
        out_specs=(vm, vm, vm),
        scratch_shapes=[
            pltpu.VMEM((sections // 2, 2, height, rank), bf16),
            buf(yh_n * x_n, 2, rank), buf(yh_n * x_n, rank), buf(yh_n, x_n, rank),
            buf(x_n - 1, yh_n, cut), buf(x_n, cut), buf(yh_n, cut), buf(cut),
            buf(x_n, cut), buf(x_n - 1, cut), buf(rank),
            dma((2,)), dma((sections // 4,)), dma((sections // 4,)),
            dma((sections // 4,)), dma((sections // 4,)),
            dma((yh_n * x_n,)), dma((yh_n * x_n,)), dma((x_n - 1,)), dma((x_n - 1,)), dma((4,)),
            dma((x_n - 1,)), dma((x_n - 1,)),
            dma((x_n,)), dma((x_n,)), dma((2 * x_n,)), dma((2 * x_n,)), dma((x_n,)), dma((x_n,)),
        ],
        compiler_params=pltpu.CompilerParams(
            collective_id=3, has_side_effects=True, vmem_limit_bytes=48 * 1024 * 1024),
    )(x0, g16, down, up, mine_u, base)


def reduce_kernel(yh_n, x_n, sections, x1, g1, u_s, q_s, up, base, own, nxt,
                  part, rc, sums, rax, rby, sa, ray, sb, rbx, gs, nw,
                  c_send, c_recv, ax_send, ax_recv, s_sem, bx_send, bx_recv,
                  own_send, own_recv, oc_send, oc_recv, nx_send, nx_recv, ny_send, ny_recv,
                  nc_send, nc_recv):
    d = lax.axis_index("dp")
    s = lax.axis_index("section")
    yh = d // (2 * x_n)
    x = lax.rem(d // 2, x_n)
    core = lax.rem(d, 2)
    rows = base.shape[0]
    cut = rows // 2

    def place(y_, x_, c_):
        return {"dp": (y_ * x_n + x_) * 2 + c_}

    def xp(i):
        return lax.rem(x + i, x_n)

    other_core = place(yh, x, 1 - core)
    other_y = place(1 - yh, x, core)
    up_section = lax.rem(s + 1, sections)
    down_section = lax.rem(s + sections - 1, sections)

    def copy(src, dst, send, recv, where):
        return pltpu.make_async_remote_copy(src_ref=src, dst_ref=dst, send_sem=send, recv_sem=recv,
                                            device_id=where, device_id_type=MESH)

    barrier = pltpu.get_barrier_semaphore()
    peers = [other_core, other_y, {"section": up_section}, {"section": down_section}]
    peers += [place(yh, xp(i), core) for i in range(1, x_n)]
    for where in peers:
        pl.semaphore_signal(barrier, inc=1, device_id=where, device_id_type=MESH)
    pl.semaphore_wait(barrier, len(peers))

    def core_copy(b):
        return copy(part.at[b, 1 - core], rc.at[b], c_send.at[b], c_recv.at[b], other_core)

    def terms(b, carry):
        cols = pl.ds(pl.multiple_of(b * 2 * rows, 128), 2 * rows)
        u = u_s[...]
        before = (x1[:, cols].astype(f32) - dot_nn(u, up[:, cols])).astype(bf16)
        g_down = dot_tn(before, q_s[...]).astype(bf16)
        g_up = dot_tn(g1[:, cols], u).astype(bf16)
        rank = u.shape[1]
        for half in range(2):
            part[b, half, :, 0:rank] = g_down[half * rows:(half + 1) * rows]
            part[b, half, :, rank:2 * rank] = g_up[half * rows:(half + 1) * rows]
        core_copy(b).start()
        return carry

    blocks = yh_n * x_n
    lax.fori_loop(0, blocks, terms, 0)

    total_a, total_b = scatter_sum(yh_n, x_n, core_copy, part, rc, sums, rax, rby, sa, ray, sb, rbx,
                                   ax_send, ax_recv, s_sem, bx_send, bx_recv)
    gs[0:cut] = total_a.astype(bf16)
    gs[cut:rows] = total_b.astype(bf16)
    nw[...] = (base[...].astype(f32) - learn_rate * gs[...].astype(f32)).astype(bf16)

    has_next = s < sections - 1
    next_copy = copy(nw, nxt.at[yh, x, core], s_sem.at[4], s_sem.at[5], {"section": down_section})
    own_y = copy(gs, own.at[yh, x, core], s_sem.at[6], s_sem.at[7], other_y)
    own_y.start()

    @pl.when(s > 0)
    def _():
        next_copy.start()

    own[yh, x, core] = gs[...]

    def own_x(i):
        return copy(own.at[:, x, core], own.at[:, x, core], own_send.at[i - 1], own_recv.at[i - 1],
                    place(yh, xp(i), core))

    def own_c(i):
        spot = own.at[:, xp(i), core]
        return copy(spot, spot, oc_send.at[i], oc_recv.at[i], other_core)

    own_y.wait_recv()
    for i in range(1, x_n):
        own_x(i).start()
    own_c(0).start()

    def nxt_x(i):
        spot = nxt.at[yh, x, core]
        return copy(spot, spot, nx_send.at[i - 1], nx_recv.at[i - 1], place(yh, xp(i), core))

    def nxt_y(i):
        spot = nxt.at[yh, xp(i), core]
        return copy(spot, spot, ny_send.at[i], ny_recv.at[i], other_y)

    def nxt_c(i):
        spot = nxt.at[:, xp(i), core]
        return copy(spot, spot, nc_send.at[i], nc_recv.at[i], other_core)

    @pl.when(has_next)
    def _():
        next_copy.wait_recv()
        for i in range(1, x_n):
            nxt_x(i).start()
        nxt_y(0).start()

    for i in range(1, x_n):
        own_x(x_n - i).wait_recv()
        own_c(i).start()

    @pl.when(has_next)
    def _():
        for i in range(1, x_n):
            nxt_x(x_n - i).wait_recv()
            nxt_y(i).start()
        for i in range(x_n):
            nxt_y(i).wait_recv()
            nxt_c(i).start()
        for i in range(x_n):
            nxt_c(i).wait()
            nxt_y(i).wait_send()
        for i in range(1, x_n):
            nxt_x(i).wait_send()

    for i in range(x_n):
        own_c(i).wait()
    for i in range(1, x_n):
        own_x(i).wait_send()
    own_y.wait_send()

    @pl.when(s > 0)
    def _():
        next_copy.wait_send()

    def settle(b, carry):
        core_copy(b).wait_send()
        return carry

    lax.fori_loop(0, blocks, settle, 0)


def reduce_gather(sections, shards, x1, g1, u_s, q_s, up, base):
    x_n = 4
    yh_n = shards // (2 * x_n)
    rows, cols = base.shape
    cut = rows // 2
    vm = pl.BlockSpec(memory_space=pltpu.VMEM)
    dma = pltpu.SemaphoreType.DMA
    full = jax.ShapeDtypeStruct((yh_n, x_n, 2, rows, cols), bf16)

    def buf(*lead):
        return pltpu.VMEM(lead + (cols,), bf16)

    return pl.pallas_call(
        functools.partial(reduce_kernel, yh_n, x_n, sections),
        out_shape=(full, full),
        in_specs=[vm] * 6,
        out_specs=(vm, vm),
        scratch_shapes=[
            buf(yh_n * x_n, 2, rows), buf(yh_n * x_n, rows), buf(yh_n, x_n, rows),
            buf(x_n - 1, yh_n, cut), buf(x_n, cut), buf(yh_n, cut), buf(cut),
            buf(x_n, cut), buf(x_n - 1, cut), buf(rows), buf(rows),
            dma((yh_n * x_n,)), dma((yh_n * x_n,)), dma((x_n - 1,)), dma((x_n - 1,)), dma((8,)),
            dma((x_n - 1,)), dma((x_n - 1,)), dma((x_n - 1,)), dma((x_n - 1,)),
            dma((x_n,)), dma((x_n,)), dma((x_n - 1,)), dma((x_n - 1,)), dma((x_n,)), dma((x_n,)),
            dma((x_n,)), dma((x_n,)),
        ],
        compiler_params=pltpu.CompilerParams(
            collective_id=2, has_side_effects=True, vmem_limit_bytes=52 * 1024 * 1024),
    )(x1, g1, u_s, q_s, up, base)


def finish_kernel(sections, own, nxt, x1, grad_down, grad_up, advance):
    last = lax.axis_index("section") == sections - 1
    rows, width = x1.shape
    rank = grad_down.shape[1]
    step = 896
    count = width // step

    def first(b, carry):
        pre, norm = carry
        here = pl.ds(pl.multiple_of(b * step, 128), step)
        block = own[here, :]
        grad_down[here, :] = block[:, 0:rank]
        grad_up[:, here] = block[:, rank:2 * rank].astype(f32).T.astype(bf16)
        x = x1[:, here]
        values = x.astype(f32)
        pre = pre + dot_nn(x, nxt[here, 0:rank])
        return pre, norm + jnp.sum(values * values, axis=1, keepdims=True)

    pre, norm = lax.fori_loop(
        0, count, first, (jnp.zeros((rows, rank), f32), jnp.zeros((rows, 1), f32)))
    value, unused = gelu_pair(pre * lax.rsqrt(norm * (1.0 / width) + eps))
    value = value.astype(bf16)

    def second(b, carry):
        here = pl.ds(pl.multiple_of(b * step, 128), step)
        bump = dot_nt(value, nxt[here, rank:2 * rank])
        advance[:, here] = (x1[:, here].astype(f32) + jnp.where(last, 0.0, bump)).astype(bf16)
        return carry

    lax.fori_loop(0, count, second, 0)


def finish(sections, own, nxt, x1):
    rows, width = x1.shape
    rank = own.shape[1] // 2
    vm = pl.BlockSpec(memory_space=pltpu.VMEM)
    return pl.pallas_call(
        functools.partial(finish_kernel, sections),
        out_shape=(
            jax.ShapeDtypeStruct((width, rank), bf16),
            jax.ShapeDtypeStruct((rank, width), bf16),
            jax.ShapeDtypeStruct((rows, width), bf16),
        ),
        in_specs=[vm] * 3,
        out_specs=(vm,) * 3,
        compiler_params=pltpu.CompilerParams(vmem_limit_bytes=48 * 1024 * 1024),
    )(own, nxt, x1)


def per_device(inputs, cotangent, w_down, w_up):
    down = w_down[0]
    upward = w_up[0]
    micro, batch_rows, width = inputs.shape
    rank = down.shape[1]
    rows = micro * batch_rows
    sections = lax.axis_size("section")
    shards = lax.axis_size("dp")
    part = width // shards
    d = lax.axis_index("dp")
    x0 = inputs.reshape(rows, width)
    g16 = cotangent.reshape(rows, width)
    up_t = upward.T

    mine_u = lax.dynamic_slice_in_dim(up_t, d * part, part, 0)
    mine_w = lax.dynamic_slice_in_dim(down, d * part, part, 0)
    base = jnp.concatenate([mine_w, mine_u], axis=1)
    pyh, n0, grams = grams_of(sections, shards, x0, g16, down, upward, mine_u, base)
    grams = grams.reshape(sections, rank, 2 * rank)
    mm = grams[:, :, :rank]
    gu = grams[:, :, rank:]

    x1, g1, u_s, q_s = recurrence(sections, pyh, n0, mm, gu, x0, g16, upward, down)
    own, nxt = reduce_gather(sections, shards, x1, g1, u_s, q_s, upward, base)
    wide = (width, 2 * rank)
    grad_down, grad_up, advance = finish(sections, own.reshape(wide), nxt.reshape(wide), x1)
    return (grad_down[None], grad_up[None], advance.reshape(1, micro, batch_rows, width))


def solution(mesh):
    in_specs = (
        P(None, "dp", None),
        P(None, "dp", None),
        P("section", None, None),
        P("section", None, None),
    )
    out_specs = (P("section", None, None), P("section", None, None), P("section", None, "dp", None))
    return jax.shard_map(
        per_device, mesh=mesh, in_specs=in_specs, out_specs=out_specs, check_vma=False
    )
```

```python
import functools

import jax
import jax.numpy as jnp
from jax import lax
from jax.experimental import pallas as pl
from jax.experimental.pallas import tpu as pltpu
from jax.sharding import PartitionSpec as P

MESH = pl.DeviceIdType.MESH
eps = 1e-05
learn_rate = 0.05
f32 = jnp.float32
bf16 = jnp.bfloat16


def dot_nn(a, b):
    return jnp.dot(a, b, preferred_element_type=f32)


def dot_tn(a, b):
    return lax.dot_general(a, b, (((0,), (0,)), ((), ())), preferred_element_type=f32)


def dot_nt(a, b):
    return lax.dot_general(a, b, (((1,), (1,)), ((), ())), preferred_element_type=f32)


def gelu_pair(a):
    c = 0.7978845608028654
    inner = c * (a + 0.044715 * a * a * a)
    th = jnp.tanh(inner)
    value = 0.5 * a * (1.0 + th)
    slope = 0.5 * (1.0 + th) + 0.5 * a * (1.0 - th * th) * c * (1.0 + 3 * 0.044715 * a * a)
    return value, slope


def recurrence_kernel(sections, chunks, pyh, n0, nn, x0, g16, up, wd,
                      xout, gout, u_out, q_out,
                      ul, ql, qp, mb, ys, nl, nsend, acc, hacc, slope, act, rinv, uf, qs, cpair,
                      upart, wpart, xin, xkeep, xgive, gin, gkeep, ggive,
                      u_send, u_recv, q_send, q_recv, m_send, m_recv, e_sem,
                      up_send, up_recv, wp_send, wp_recv, c_send, c_recv, g_send, g_recv,
                      b_send, b_recv, h_send, h_recv):
    s = lax.axis_index("section")
    planes = sections // 2
    rows, width = x0.shape
    some = rows // 2
    rank = up.shape[0]
    half = width // 2
    piece = half // chunks
    z = s // 2
    ylo = lax.rem(s, 2)
    first = ylo == 0
    partner = {"section": s + 1 - 2 * ylo}
    head = slice(0, rank)
    tail = slice(rank, 2 * rank)
    mine = pl.ds(ylo * some, some)
    theirs = pl.ds((1 - ylo) * some, some)

    def plane(i):
        return {"section": 2 * i + ylo}

    def peer(offset):
        return lax.rem(z + offset, planes)

    barrier = pltpu.get_barrier_semaphore()
    for o in range(1, planes):
        pl.semaphore_signal(barrier, inc=1, device_id=plane(peer(o)), device_id_type=MESH)
    pl.semaphore_signal(barrier, inc=1, device_id=partner, device_id_type=MESH)
    pl.semaphore_wait(barrier, planes)

    eye = (lax.broadcasted_iota(jnp.int32, (some, rank), 0)
           == lax.broadcasted_iota(jnp.int32, (some, rank), 1)).astype(f32)

    def to_row(col):
        return jnp.sum(eye * col, axis=0, keepdims=True)

    def to_col(row):
        return jnp.sum(eye * row, axis=1, keepdims=True)

    def columns(base, c):
        return pl.ds(pl.multiple_of(base + c * piece, 128), piece)

    def up_copy(c):
        return remote(up.at[:, columns((1 - ylo) * half, c)], upart.at[:, columns(0, c)],
                      up_send.at[c], up_recv.at[c], partner)

    def wp_copy(c):
        return remote(wd.at[columns((1 - ylo) * half, c), :], wpart.at[columns(0, c), :],
                      wp_send.at[c], wp_recv.at[c], partner)

    def x_copy(c):
        return remote(xkeep.at[:, columns(0, c)], xin.at[:, columns(0, c)],
                      c_send.at[c], c_recv.at[c], plane(peer(1)))

    def b_copy(c):
        return remote(gkeep.at[:, columns(0, c)], gin.at[:, columns(0, c)],
                      b_send.at[c], b_recv.at[c], plane(peer(planes - 1)))

    def give_copy(c):
        return remote(xgive.at[:, columns(0, c)], xout.at[:, columns(ylo * half, c)],
                      g_send.at[c], g_recv.at[c], partner)

    def give_arrived(c):
        return remote(xgive.at[:, columns(0, c)], xout.at[:, columns((1 - ylo) * half, c)],
                      g_send.at[c], g_recv.at[c], partner)

    def h_copy(c):
        return remote(ggive.at[:, columns(0, c)], gout.at[:, columns(ylo * half, c)],
                      h_send.at[c], h_recv.at[c], partner)

    def h_arrived(c):
        return remote(ggive.at[:, columns(0, c)], gout.at[:, columns((1 - ylo) * half, c)],
                      h_send.at[c], h_recv.at[c], partner)

    def near_copy(k, part, sem):
        spot = ul.at[k, :, part]
        return remote(spot, spot, e_sem.at[2 * sem], e_sem.at[2 * sem + 1], plane(peer(1)))

    def n_copy():
        return remote(nsend, nl, e_sem.at[4], e_sem.at[5], plane(peer(1)))

    def uf_copy():
        return remote(ul.at[z], uf.at[mine], e_sem.at[6], e_sem.at[7], partner)

    def uf_arrived():
        return remote(ul.at[z], uf.at[theirs], e_sem.at[6], e_sem.at[7], partner)

    def qp_copy():
        return remote(ql.at[z], qp, e_sem.at[8], e_sem.at[9], partner)

    def u_copy(o):
        return remote(ul.at[z], ul.at[z], u_send.at[o], u_recv.at[z], plane(peer(o)))

    def u_arrived(k):
        return remote(ul.at[k], ul.at[k], u_send.at[0], u_recv.at[k], plane(peer(1)))

    def q_copy(j):
        return remote(ql.at[z], ql.at[z], q_send.at[j], q_recv.at[z], plane(j))

    def q_arrived(k):
        return remote(ql.at[k], ql.at[k], q_send.at[0], q_recv.at[k], plane(peer(1)))

    def m_copy(j):
        return remote(nn.at[j, :, 0:2 * rank], mb.at[z], m_send.at[j], m_recv.at[z], plane(j))

    def m_arrived(k):
        return remote(mb.at[k], mb.at[k], m_send.at[0], m_recv.at[k], plane(peer(1)))

    acc[:, 0:2 * rank] = pyh[0]
    acc[:, 2 * rank:4 * rank] = pyh[1]
    hacc[...] = pyh[2]

    def start_up(c, carry):
        up_copy(c).start()
        return carry

    lax.fori_loop(0, chunks, start_up, 0)

    def start_m(j, carry):
        m_copy(j).start()
        return carry

    lax.fori_loop(0, z, start_m, 0)

    def chain(c):
        @pl.when(z > 0)
        def _():
            x_copy(c).wait_recv()

        up_copy(c).wait_recv()
        here = columns(ylo * half, c)
        there = columns(0, c)
        start = jnp.where(z > 0, xin[:, there], x0[:, here]).astype(f32)
        ours = up[:, here]
        other = upart[:, there]
        x_a = (start + dot_nn(uf[:, head], jnp.where(first, ours, other))).astype(bf16)
        x_b = (x_a.astype(f32) + dot_nn(uf[:, tail], jnp.where(first, other, ours))).astype(bf16)
        xkeep[:, there] = x_b

        @pl.when(z < planes - 1)
        def _():
            x_copy(c).start()

        xgive[:, there] = jnp.where(first, x_b, x_a)
        give_copy(c).start()
        xout[:, here] = jnp.where(first, x_a, x_b)

    def chain_back(c):
        @pl.when(z < planes - 1)
        def _():
            b_copy(c).wait_recv()

        wp_copy(c).wait_recv()
        here = columns(ylo * half, c)
        there = columns(0, c)
        ours = wd[here, :]
        other = wpart[there, :]
        g_b = jnp.where(z < planes - 1, gin[:, there], g16[:, here])
        x_a = jnp.where(z > 0, xin[:, there], x0[:, here]).astype(f32)
        x_b = jnp.where(first, xout[:, here], xgive[:, there]).astype(f32)
        g_a = (g_b.astype(f32) + dot_nt(qs[:, tail], jnp.where(first, other, ours))
               - cpair[1, :, 0:1] * x_b).astype(bf16)
        g_0 = (g_a.astype(f32) + dot_nt(qs[:, head], jnp.where(first, ours, other))
               - cpair[0, :, 0:1] * x_a).astype(bf16)

        @pl.when(z > 0)
        def _():
            gkeep[:, there] = g_0
            b_copy(c).start()

        ggive[:, there] = jnp.where(first, g_b, g_a)
        h_copy(c).start()
        gout[:, here] = jnp.where(first, g_a, g_b)

    def forward_own():
        @pl.when(z > 0)
        def _():
            n_copy().wait_recv()

        norm_a = jnp.where(z > 0, to_col(nl[0:1, :]), n0[:, 0:1])
        scale_a = lax.rsqrt(norm_a * (1.0 / width) + eps)
        pre_a = acc[:, 0:rank] * scale_a
        value_a, slope_a = gelu_pair(pre_a)
        u_a = value_a.astype(bf16)
        ul[z, :, head] = u_a

        @pl.when(z < planes - 1)
        def _():
            near_copy(z, head, 0).start()

        step = dot_nn(u_a, nn[z, 0:rank, rank:4 * rank])
        y_a = acc[:, 2 * rank:3 * rank]
        norm_b = norm_a + jnp.sum(u_a.astype(f32) * (2.0 * y_a + step[:, rank:2 * rank]),
                                  axis=1, keepdims=True)
        scale_b = lax.rsqrt(norm_b * (1.0 / width) + eps)
        pre_b = (acc[:, rank:2 * rank] + step[:, 0:rank]) * scale_b
        value_b, slope_b = gelu_pair(pre_b)
        u_b = value_b.astype(bf16)
        ul[z, :, tail] = u_b

        @pl.when(z < planes - 1)
        def _():
            near_copy(z, tail, 1).start()

        y_b = acc[:, 2 * rank:4 * rank] + step[:, rank:3 * rank]
        more = dot_nn(u_b, nn[z, rank:2 * rank, 2 * rank:4 * rank])
        norm_c = norm_b + jnp.sum(
            u_b.astype(f32) * (2.0 * y_b[:, rank:2 * rank] + more[:, rank:2 * rank]),
            axis=1, keepdims=True)

        @pl.when(z < planes - 1)
        def _():
            nsend[...] = jnp.broadcast_to(to_row(norm_c), nsend.shape)
            n_copy().start()

        uf_copy().start()
        for o in range(2, planes):
            u_copy(o).start()

        @pl.when(z == planes - 1)
        def _():
            u_copy(1).start()

        uf[mine, :] = ul[z]
        ys[2 * z + 1] = y_b
        acc[:, 2 * rank:4 * rank] = y_b + more
        act[:, head] = pre_a
        act[:, tail] = pre_b
        slope[:, head] = slope_a
        slope[:, tail] = slope_b
        rinv[0] = jnp.broadcast_to(scale_a, (some, rank))
        rinv[1] = jnp.broadcast_to(scale_b, (some, rank))

    def c_of(stat):
        line = stat[0:1, :].astype(f32) + stat[1:2, :].astype(f32)
        return to_col(line[:, head]), to_col(line[:, tail])

    def backward_own():
        scale_b = rinv[1]
        q_b = hacc[:, tail] * slope[:, tail]
        low_b = (q_b * scale_b).astype(bf16)
        mix_b = jnp.sum(q_b * act[:, tail], axis=1, keepdims=True) * (1.0 / width)
        c_b = mix_b * scale_b[:, 0:1] * scale_b[:, 0:1]
        h_a = hacc[:, head] + dot_nt(low_b, nn[z, 0:rank, rank:2 * rank]) - c_b * ys[2 * z + 1, :, head]
        scale_a = rinv[0]
        q_a = h_a * slope[:, head]
        mix_a = jnp.sum(q_a * act[:, head], axis=1, keepdims=True) * (1.0 / width)
        c_a = mix_a * scale_a[:, 0:1] * scale_a[:, 0:1]
        ql[z, 0:some, head] = (q_a * scale_a).astype(bf16)
        ql[z, 0:some, tail] = low_b
        spot = lax.broadcasted_iota(jnp.int32, (16, rank), 0)
        for part, col in ((head, c_a), (tail, c_b)):
            line = to_row(col)
            high = line.astype(bf16).astype(f32)
            ql[z, some:some + 16, part] = jnp.where(
                spot == 0, high, jnp.where(spot == 1, line - high, 0.0)).astype(bf16)

        def send(i, carry):
            q_copy(z - 1 - i).start()
            return carry

        lax.fori_loop(0, z, send, 0)
        qp_copy().start()

    def tick(t, carry):
        k = t - 1
        sent = (k >= 0) & (k < planes)
        near = sent & (k == z - 1)

        @pl.when(sent & (k != z) & (k != z - 1))
        def _():
            u_arrived(k).wait_recv()

        @pl.when(near)
        def _():
            near_copy(k, head, 0).wait_recv()
            acc[...] += dot_nn(ul[k, :, head], nn[k, 0:rank, :])
            near_copy(k, tail, 1).wait_recv()
            acc[...] += dot_nn(ul[k, :, tail], nn[k, rank:2 * rank, :])

        @pl.when(sent & (k < z - 1))
        def _():
            acc[...] += dot_nn(ul[k], nn[k])

        @pl.when(t == z)
        def _():
            forward_own()

        @pl.when(sent & (k > z))
        def _():
            before = acc[:, 2 * rank:4 * rank]
            ys[2 * k] = before
            between = before + dot_nn(ul[k, :, head], nn[k, 0:rank, 2 * rank:4 * rank])
            ys[2 * k + 1] = between
            acc[:, 2 * rank:4 * rank] = between + dot_nn(
                ul[k, :, tail], nn[k, rank:2 * rank, 2 * rank:4 * rank])

        r = 2 * planes - t

        @pl.when((r < planes) & (r > z))
        def _():
            m_arrived(r).wait_recv()
            q_arrived(r).wait_recv()
            c_a, c_b = c_of(ql[r, some:some + 16, :])
            hacc[...] += (dot_nt(ql[r, 0:some, :], mb[r]) - c_a * ys[2 * r] - c_b * ys[2 * r + 1])

        @pl.when(t == 2 * planes - 1 - z)
        def _():
            backward_own()

        p = t - (z + 1)

        @pl.when((p >= 0) & (p < chunks // 2))
        def _():
            @pl.when(p == 0)
            def _():
                uf_arrived().wait_recv()
            for j in range(2):
                chain(2 * p + j)

        @pl.when((t >= 2) & (t < 2 + chunks // 2))
        def _():
            for j in range(2):
                wp_copy(2 * (t - 2) + j).start()

        b = t - (2 * planes - z)

        @pl.when((b >= 0) & (b < chunks // 2))
        def _():
            @pl.when(b == 0)
            def _():
                qp_copy().wait_recv()
                qs[mine, :] = ql[z, 0:some, :]
                qs[theirs, :] = qp[0:some, :]
                for where, stat in ((mine, ql[z, some:some + 16, :]), (theirs, qp[some:some + 16, :])):
                    c_a, c_b = c_of(stat)
                    cpair[0, where, :] = jnp.broadcast_to(c_a, (some, rank))
                    cpair[1, where, :] = jnp.broadcast_to(c_b, (some, rank))
            for j in range(2):
                chain_back(2 * b + j)

        return carry

    lax.fori_loop(0, 2 * planes + chunks // 2, tick, 0)
    u_out[...] = jnp.where(first, uf[:, head], uf[:, tail])
    q_out[...] = jnp.where(first, qs[:, head], qs[:, tail])

    def finish(c, carry):
        @pl.when(z < planes - 1)
        def _():
            x_copy(c).wait_send()
        give_copy(c).wait_send()
        give_arrived(c).wait_recv()

        @pl.when(z > 0)
        def _():
            b_copy(c).wait_send()
        h_copy(c).wait_send()
        h_arrived(c).wait_recv()
        up_copy(c).wait_send()
        wp_copy(c).wait_send()
        return carry

    lax.fori_loop(0, chunks, finish, 0)
    for o in range(2, planes):
        u_copy(o).wait_send()

    @pl.when(z == planes - 1)
    def _():
        u_copy(1).wait_send()

    @pl.when(z < planes - 1)
    def _():
        near_copy(z, head, 0).wait_send()
        near_copy(z, tail, 1).wait_send()
        n_copy().wait_send()

    def settle(j, carry):
        q_copy(j).wait_send()
        m_copy(j).wait_send()
        return carry

    lax.fori_loop(0, z, settle, 0)
    uf_copy().wait_send()
    qp_copy().wait_send()


def recurrence(sections, pyh, n0, nn, x0, g16, up, wd):
    rows, width = x0.shape
    rank = up.shape[0]
    half = width // 2
    some = rows // 2
    planes = sections // 2
    chunks = 14
    vm = pl.BlockSpec(memory_space=pltpu.VMEM)
    dma = pltpu.SemaphoreType.DMA
    sq = (rows, rank)
    two = (some, 2 * rank)
    wide = jax.ShapeDtypeStruct((rows, width), bf16)
    strip = pltpu.VMEM((rows, half), bf16)
    return pl.pallas_call(
        functools.partial(recurrence_kernel, sections, chunks),
        out_shape=(wide, wide, jax.ShapeDtypeStruct(sq, bf16), jax.ShapeDtypeStruct(sq, bf16)),
        in_specs=[vm] * 7,
        out_specs=(vm,) * 4,
        scratch_shapes=[
            pltpu.VMEM((planes,) + two, bf16),
            pltpu.VMEM((planes, some + 16, 2 * rank), bf16),
            pltpu.VMEM((some + 16, 2 * rank), bf16),
            pltpu.VMEM((planes, 2 * rank, 2 * rank), bf16),
            pltpu.VMEM((sections,) + two, f32),
            pltpu.VMEM((8, rank), f32),
            pltpu.VMEM((8, rank), f32),
            pltpu.VMEM((some, 4 * rank), f32),
            pltpu.VMEM(two, f32), pltpu.VMEM(two, f32), pltpu.VMEM(two, f32),
            pltpu.VMEM((2, some, rank), f32),
            pltpu.VMEM((rows, 2 * rank), bf16),
            pltpu.VMEM((rows, 2 * rank), bf16),
            pltpu.VMEM((2,) + sq, f32),
            pltpu.VMEM((rank, half), bf16),
            pltpu.VMEM((half, rank), bf16),
            strip, strip, strip, strip, strip, strip,
        ] + [dma((planes,))] * 6 + [dma((10,))] + [dma((chunks,))] * 12,
        compiler_params=pltpu.CompilerParams(
            collective_id=1, has_side_effects=True, vmem_limit_bytes=48 * 1024 * 1024),
    )(pyh, n0, nn, x0, g16, up, wd)


def dp_place(x_n):
    d = lax.axis_index("dp")
    return d // (2 * x_n), lax.rem(d // 2, x_n), lax.rem(d, 2)


def remote(src, dst, send, recv, where):
    return pltpu.make_async_remote_copy(src_ref=src, dst_ref=dst, send_sem=send, recv_sem=recv,
                                        device_id=where, device_id_type=MESH)


def scatter_sum(yh_n, x_n, core_copy, part, rc, sums, rax, rby, sa, ray, sb, rbx,
                ax_send, ax_recv, s_sem, bx_send, bx_recv):
    yh, x, core = dp_place(x_n)
    rows = sums.shape[2]
    cut = rows // 2
    blocks = yh_n * x_n

    def place(y_, x_, c_):
        return {"dp": (y_ * x_n + x_) * 2 + c_}

    def xp(i):
        return lax.rem(x + i, x_n)

    other_y = place(1 - yh, x, core)
    copy = remote

    def first_sum(b, carry):
        core_copy(b).wait_recv()
        y_ = b // x_n
        x_ = lax.rem(b, x_n)
        sums[y_, x_] = (part[b, core].astype(f32) + rc[b].astype(f32)).astype(bf16)
        return carry

    lax.fori_loop(0, blocks, first_sum, 0)

    def ax_copy(i):
        return copy(sums.at[:, xp(i), 0:cut], rax.at[i - 1], ax_send.at[i - 1], ax_recv.at[i - 1],
                    place(yh, xp(i), core))

    by_copy = copy(sums.at[1 - yh, :, cut:rows], rby, s_sem.at[0], s_sem.at[1], other_y)
    ay_copy = copy(sa.at[1 - yh], ray, s_sem.at[2], s_sem.at[3], other_y)

    def bx_copy(i):
        return copy(sb.at[xp(i)], rbx.at[i - 1], bx_send.at[i - 1], bx_recv.at[i - 1],
                    place(yh, xp(i), core))

    by_copy.start()
    for i in range(1, x_n):
        ax_copy(i).start()
    for i in range(1, x_n):
        ax_copy(i).wait_recv()
    for y_ in range(yh_n):
        total = sums[y_, x, 0:cut].astype(f32)
        for i in range(1, x_n):
            total = total + rax[i - 1, y_].astype(f32)
        sa[y_] = total.astype(bf16)
    ay_copy.start()
    by_copy.wait_recv()
    for x_ in range(x_n):
        sb[x_] = (sums[yh, x_, cut:rows].astype(f32) + rby[x_].astype(f32)).astype(bf16)
    for i in range(1, x_n):
        bx_copy(i).start()
    ay_copy.wait_recv()
    total_a = sa[yh].astype(f32) + ray[...].astype(f32)
    for i in range(1, x_n):
        bx_copy(i).wait_recv()
    total_b = sb[x].astype(f32)
    for i in range(1, x_n):
        total_b = total_b + rbx[i - 1].astype(f32)
    for i in range(1, x_n):
        ax_copy(i).wait_send()
        bx_copy(i).wait_send()
    by_copy.wait_send()
    ay_copy.wait_send()
    return total_a, total_b


def gram_kernel(yh_n, x_n, sections, x0, g16, down, up, mine_u, base, pyh, n0, out,
                allu, part, rc, sums, rax, rby, sa, ray, sb, rbx, gs, gp, two, mine3, theirs3,
                z_sem, f_send, f_recv, r_send, r_recv,
                c_send, c_recv, ax_send, ax_recv, s_sem, bx_send, bx_recv,
                ga_send, ga_recv, gb_send, gb_recv, gc_send, gc_recv):
    yh, x, core = dp_place(x_n)
    s = lax.axis_index("section")
    z_n = sections // 2
    z = s // 2
    ylo = lax.rem(s, 2)
    rank = up.shape[0]
    rows = rank
    cut = rows // 2

    def place(y_, x_, c_):
        return {"dp": (y_ * x_n + x_) * 2 + c_}

    def xp(i):
        return lax.rem(x + i, x_n)

    def zp(i):
        return lax.rem(z + i, z_n)

    other_core = place(yh, x, 1 - core)
    other_y = place(1 - yh, x, core)
    partner = {"section": s + 1 - 2 * ylo}
    after = {"section": 2 * zp(1) + ylo}
    before = {"section": 2 * zp(z_n - 1) + ylo}

    barrier = pltpu.get_barrier_semaphore()
    peers = [other_core, other_y, partner, after, before]
    peers += [place(yh, xp(i), core) for i in range(1, x_n)]
    for where in peers:
        pl.semaphore_signal(barrier, inc=1, device_id=where, device_id_type=MESH)
    pl.semaphore_wait(barrier, len(peers))

    pair = remote(mine_u, allu.at[z, ylo], z_sem.at[0], z_sem.at[1], partner)
    pair.start()
    allu[z, ylo] = mine_u[...]

    def products(z_):
        for y_ in range(2):
            part[z_, y_] = dot_tn(allu[z_, y_], base[...]).astype(bf16)

    def core_copy(b):
        return remote(part.at[b, 1 - core], rc.at[b], c_send.at[b], c_recv.at[b], other_core)

    hops = z_n // 2

    def ring_f(i):
        if i < hops:
            spot = allu.at[zp(z_n + 1 - i)]
        else:
            spot = allu.at[zp(z_n + 1 - i), 0]
        return remote(spot, spot, f_send.at[i - 1], f_recv.at[i - 1], after)

    def ring_r(i):
        if i < hops:
            spot = allu.at[zp(i - 1)]
        else:
            spot = allu.at[zp(i - 1), 1]
        return remote(spot, spot, r_send.at[i - 1], r_recv.at[i - 1], before)

    pair.wait_recv()
    ring_f(1).start()
    ring_r(1).start()

    u = up[...]
    w = down[...]
    values = x0[...]
    token_half = x0.shape[0] // 2
    keep = pl.ds(ylo * token_half, token_half)
    give = pl.ds((1 - ylo) * token_half, token_half)
    mine3[0] = dot_nn(values, w)
    mine3[1] = dot_nt(values, u)
    mine3[2] = dot_nt(g16[...], u)
    swap3 = remote(mine3.at[:, give], theirs3, z_sem.at[2], z_sem.at[3], partner)
    swap3.start()
    wide = x0[keep, :].astype(f32)
    n0[...] = jnp.broadcast_to(jnp.sum(wide * wide, axis=1, keepdims=True), n0.shape)
    products(z)
    core_copy(z).start()
    for i in range(1, hops + 1):
        ring_f(i).wait_recv()
        if i < hops:
            ring_f(i + 1).start()
        ring_r(i).wait_recv()
        if i < hops:
            ring_r(i + 1).start()
        products(zp(z_n - i))
        core_copy(zp(z_n - i)).start()
        if i < hops:
            products(zp(i))
            core_copy(zp(i)).start()

    total_a, total_b = scatter_sum(yh_n, x_n, core_copy, part, rc, sums, rax, rby, sa, ray, sb, rbx,
                                   ax_send, ax_recv, s_sem, bx_send, bx_recv)
    gs[0:cut] = total_a.astype(bf16)
    gs[cut:rows] = total_b.astype(bf16)
    swap = remote(gs, gp, z_sem.at[4], z_sem.at[5], partner)
    swap.start()

    def lanes(base, which):
        return pl.ds(pl.multiple_of(base + which * rank, 128), rank)

    swap3.wait_recv()
    pyh[:, :, lanes(0, ylo)] = mine3[:, keep]
    pyh[:, :, lanes(0, 1 - ylo)] = theirs3[...]
    two[:, lanes(0, ylo)] = gs[:, 0:rank]
    two[:, lanes(2 * rank, ylo)] = gs[:, rank:2 * rank]
    swap.wait_recv()
    two[:, lanes(0, 1 - ylo)] = gp[:, 0:rank]
    two[:, lanes(2 * rank, 1 - ylo)] = gp[:, rank:2 * rank]
    out[yh, x, core] = two[...]

    low = pl.ds(0, cut)
    high = pl.ds(cut, cut)

    def spread(src, spot, sems, i, where):
        return remote(src, spot, sems[0].at[i], sems[1].at[i], where)

    ga = (ga_send, ga_recv)
    gb = (gb_send, gb_recv)
    a_y = spread(two.at[low], out.at[yh, x, core, low], ga, 0, other_y)

    def a_x(i):
        spot = out.at[:, x, core, low]
        return spread(spot, spot, ga, i, place(yh, xp(i), core))

    def b_x(i):
        return spread(two.at[high], out.at[yh, x, core, high], gb, i - 1, place(yh, xp(i), core))

    def b_y(i):
        spot = out.at[yh, xp(i), core, high]
        return spread(spot, spot, gb, x_n - 1 + i, other_y)

    def all_c(i):
        spot = out.at[:, xp(i), core]
        return remote(spot, spot, gc_send.at[i], gc_recv.at[i], other_core)

    a_y.start()
    for i in range(1, x_n):
        b_x(i).start()
    b_y(0).start()
    a_y.wait_recv()
    for i in range(1, x_n):
        a_x(i).start()
    for i in range(1, x_n):
        b_x(x_n - i).wait_recv()
        b_y(i).start()
    b_y(0).wait_recv()
    all_c(0).start()
    for i in range(1, x_n):
        a_x(x_n - i).wait_recv()
        b_y(i).wait_recv()
        all_c(i).start()
    for i in range(x_n):
        all_c(i).wait()
        b_y(i).wait_send()
    for i in range(1, x_n):
        a_x(i).wait_send()
        b_x(i).wait_send()
    a_y.wait_send()
    pair.wait_send()
    swap.wait_send()
    swap3.wait_send()
    for i in range(1, hops + 1):
        ring_f(i).wait_send()
        ring_r(i).wait_send()

    def settle(b, carry):
        core_copy(b).wait_send()
        return carry

    lax.fori_loop(0, yh_n * x_n, settle, 0)


def grams_of(sections, shards, x0, g16, down, up, mine_u, base):
    x_n = 4
    yh_n = shards // (2 * x_n)
    rows, width = x0.shape
    rank = up.shape[0]
    height = mine_u.shape[0]
    cut = rank // 2
    vm = pl.BlockSpec(memory_space=pltpu.VMEM)
    dma = pltpu.SemaphoreType.DMA

    def buf(*lead):
        return pltpu.VMEM(lead + (2 * rank,), bf16)

    return pl.pallas_call(
        functools.partial(gram_kernel, yh_n, x_n, sections),
        out_shape=(
            jax.ShapeDtypeStruct((3, rows // 2, 2 * rank), f32),
            jax.ShapeDtypeStruct((rows // 2, rank), f32),
            jax.ShapeDtypeStruct((yh_n, x_n, 2, rank, 4 * rank), bf16),
        ),
        in_specs=[vm] * 6,
        out_specs=(vm, vm, vm),
        scratch_shapes=[
            pltpu.VMEM((sections // 2, 2, height, rank), bf16),
            buf(yh_n * x_n, 2, rank), buf(yh_n * x_n, rank), buf(yh_n, x_n, rank),
            buf(x_n - 1, yh_n, cut), buf(x_n, cut), buf(yh_n, cut), buf(cut),
            buf(x_n, cut), buf(x_n - 1, cut), buf(rank), buf(rank),
            pltpu.VMEM((rank, 4 * rank), bf16),
            pltpu.VMEM((3, rows, rank), f32), pltpu.VMEM((3, rows // 2, rank), f32),
            dma((6,)), dma((sections // 4,)), dma((sections // 4,)),
            dma((sections // 4,)), dma((sections // 4,)),
            dma((yh_n * x_n,)), dma((yh_n * x_n,)), dma((x_n - 1,)), dma((x_n - 1,)), dma((4,)),
            dma((x_n - 1,)), dma((x_n - 1,)),
            dma((x_n,)), dma((x_n,)), dma((2 * x_n,)), dma((2 * x_n,)), dma((x_n,)), dma((x_n,)),
        ],
        compiler_params=pltpu.CompilerParams(
            collective_id=3, has_side_effects=True, vmem_limit_bytes=48 * 1024 * 1024),
    )(x0, g16, down, up, mine_u, base)


def reduce_kernel(yh_n, x_n, sections, x1, g1, u_s, q_s, up, base, own, nxt,
                  part, rc, sums, rax, rby, sa, ray, sb, rbx, gs, nw,
                  c_send, c_recv, ax_send, ax_recv, s_sem, bx_send, bx_recv,
                  own_send, own_recv, oc_send, oc_recv, nx_send, nx_recv, ny_send, ny_recv,
                  nc_send, nc_recv):
    d = lax.axis_index("dp")
    s = lax.axis_index("section")
    yh = d // (2 * x_n)
    x = lax.rem(d // 2, x_n)
    core = lax.rem(d, 2)
    rows = base.shape[0]
    cut = rows // 2

    def place(y_, x_, c_):
        return {"dp": (y_ * x_n + x_) * 2 + c_}

    def xp(i):
        return lax.rem(x + i, x_n)

    other_core = place(yh, x, 1 - core)
    other_y = place(1 - yh, x, core)
    up_section = lax.rem(s + 1, sections)
    down_section = lax.rem(s + sections - 1, sections)

    def copy(src, dst, send, recv, where):
        return pltpu.make_async_remote_copy(src_ref=src, dst_ref=dst, send_sem=send, recv_sem=recv,
                                            device_id=where, device_id_type=MESH)

    barrier = pltpu.get_barrier_semaphore()
    peers = [other_core, other_y, {"section": up_section}, {"section": down_section}]
    peers += [place(yh, xp(i), core) for i in range(1, x_n)]
    for where in peers:
        pl.semaphore_signal(barrier, inc=1, device_id=where, device_id_type=MESH)
    pl.semaphore_wait(barrier, len(peers))

    def core_copy(b):
        return copy(part.at[b, 1 - core], rc.at[b], c_send.at[b], c_recv.at[b], other_core)

    def terms(b, carry):
        cols = pl.ds(pl.multiple_of(b * 2 * rows, 128), 2 * rows)
        u = u_s[...]
        before = (x1[:, cols].astype(f32) - dot_nn(u, up[:, cols])).astype(bf16)
        g_down = dot_tn(before, q_s[...]).astype(bf16)
        g_up = dot_tn(g1[:, cols], u).astype(bf16)
        rank = u.shape[1]
        for half in range(2):
            part[b, half, :, 0:rank] = g_down[half * rows:(half + 1) * rows]
            part[b, half, :, rank:2 * rank] = g_up[half * rows:(half + 1) * rows]
        core_copy(b).start()
        return carry

    blocks = yh_n * x_n
    lax.fori_loop(0, blocks, terms, 0)

    total_a, total_b = scatter_sum(yh_n, x_n, core_copy, part, rc, sums, rax, rby, sa, ray, sb, rbx,
                                   ax_send, ax_recv, s_sem, bx_send, bx_recv)
    gs[0:cut] = total_a.astype(bf16)
    gs[cut:rows] = total_b.astype(bf16)
    nw[...] = (base[...].astype(f32) - learn_rate * gs[...].astype(f32)).astype(bf16)

    has_next = s < sections - 1
    next_copy = copy(nw, nxt.at[yh, x, core], s_sem.at[4], s_sem.at[5], {"section": down_section})
    own_y = copy(gs, own.at[yh, x, core], s_sem.at[6], s_sem.at[7], other_y)
    own_y.start()

    @pl.when(s > 0)
    def _():
        next_copy.start()

    own[yh, x, core] = gs[...]

    def own_x(i):
        return copy(own.at[:, x, core], own.at[:, x, core], own_send.at[i - 1], own_recv.at[i - 1],
                    place(yh, xp(i), core))

    def own_c(i):
        spot = own.at[:, xp(i), core]
        return copy(spot, spot, oc_send.at[i], oc_recv.at[i], other_core)

    own_y.wait_recv()
    for i in range(1, x_n):
        own_x(i).start()
    own_c(0).start()

    def nxt_x(i):
        spot = nxt.at[yh, x, core]
        return copy(spot, spot, nx_send.at[i - 1], nx_recv.at[i - 1], place(yh, xp(i), core))

    def nxt_y(i):
        spot = nxt.at[yh, xp(i), core]
        return copy(spot, spot, ny_send.at[i], ny_recv.at[i], other_y)

    def nxt_c(i):
        spot = nxt.at[:, xp(i), core]
        return copy(spot, spot, nc_send.at[i], nc_recv.at[i], other_core)

    @pl.when(has_next)
    def _():
        next_copy.wait_recv()
        for i in range(1, x_n):
            nxt_x(i).start()
        nxt_y(0).start()

    for i in range(1, x_n):
        own_x(x_n - i).wait_recv()
        own_c(i).start()

    @pl.when(has_next)
    def _():
        for i in range(1, x_n):
            nxt_x(x_n - i).wait_recv()
            nxt_y(i).start()
        for i in range(x_n):
            nxt_y(i).wait_recv()
            nxt_c(i).start()
        for i in range(x_n):
            nxt_c(i).wait()
            nxt_y(i).wait_send()
        for i in range(1, x_n):
            nxt_x(i).wait_send()

    for i in range(x_n):
        own_c(i).wait()
    for i in range(1, x_n):
        own_x(i).wait_send()
    own_y.wait_send()

    @pl.when(s > 0)
    def _():
        next_copy.wait_send()

    def settle(b, carry):
        core_copy(b).wait_send()
        return carry

    lax.fori_loop(0, blocks, settle, 0)


def reduce_gather(sections, shards, x1, g1, u_s, q_s, up, base):
    x_n = 4
    yh_n = shards // (2 * x_n)
    rows, cols = base.shape
    cut = rows // 2
    vm = pl.BlockSpec(memory_space=pltpu.VMEM)
    dma = pltpu.SemaphoreType.DMA
    full = jax.ShapeDtypeStruct((yh_n, x_n, 2, rows, cols), bf16)

    def buf(*lead):
        return pltpu.VMEM(lead + (cols,), bf16)

    return pl.pallas_call(
        functools.partial(reduce_kernel, yh_n, x_n, sections),
        out_shape=(full, full),
        in_specs=[vm] * 6,
        out_specs=(vm, vm),
        scratch_shapes=[
            buf(yh_n * x_n, 2, rows), buf(yh_n * x_n, rows), buf(yh_n, x_n, rows),
            buf(x_n - 1, yh_n, cut), buf(x_n, cut), buf(yh_n, cut), buf(cut),
            buf(x_n, cut), buf(x_n - 1, cut), buf(rows), buf(rows),
            dma((yh_n * x_n,)), dma((yh_n * x_n,)), dma((x_n - 1,)), dma((x_n - 1,)), dma((8,)),
            dma((x_n - 1,)), dma((x_n - 1,)), dma((x_n - 1,)), dma((x_n - 1,)),
            dma((x_n,)), dma((x_n,)), dma((x_n - 1,)), dma((x_n - 1,)), dma((x_n,)), dma((x_n,)),
            dma((x_n,)), dma((x_n,)),
        ],
        compiler_params=pltpu.CompilerParams(
            collective_id=2, has_side_effects=True, vmem_limit_bytes=52 * 1024 * 1024),
    )(x1, g1, u_s, q_s, up, base)


def finish_kernel(sections, own, nxt, x1, grad_down, grad_up, advance):
    last = lax.axis_index("section") == sections - 1
    rows, width = x1.shape
    rank = grad_down.shape[1]
    step = 896
    count = width // step

    def first(b, carry):
        pre, norm = carry
        here = pl.ds(pl.multiple_of(b * step, 128), step)
        block = own[here, :]
        grad_down[here, :] = block[:, 0:rank]
        grad_up[:, here] = block[:, rank:2 * rank].astype(f32).T.astype(bf16)
        x = x1[:, here]
        values = x.astype(f32)
        pre = pre + dot_nn(x, nxt[here, 0:rank])
        return pre, norm + jnp.sum(values * values, axis=1, keepdims=True)

    pre, norm = lax.fori_loop(
        0, count, first, (jnp.zeros((rows, rank), f32), jnp.zeros((rows, 1), f32)))
    value, unused = gelu_pair(pre * lax.rsqrt(norm * (1.0 / width) + eps))
    value = value.astype(bf16)

    def second(b, carry):
        here = pl.ds(pl.multiple_of(b * step, 128), step)
        bump = dot_nt(value, nxt[here, rank:2 * rank])
        advance[:, here] = (x1[:, here].astype(f32) + jnp.where(last, 0.0, bump)).astype(bf16)
        return carry

    lax.fori_loop(0, count, second, 0)


def finish(sections, own, nxt, x1):
    rows, width = x1.shape
    rank = own.shape[1] // 2
    vm = pl.BlockSpec(memory_space=pltpu.VMEM)
    return pl.pallas_call(
        functools.partial(finish_kernel, sections),
        out_shape=(
            jax.ShapeDtypeStruct((width, rank), bf16),
            jax.ShapeDtypeStruct((rank, width), bf16),
            jax.ShapeDtypeStruct((rows, width), bf16),
        ),
        in_specs=[vm] * 3,
        out_specs=(vm,) * 3,
        compiler_params=pltpu.CompilerParams(vmem_limit_bytes=48 * 1024 * 1024),
    )(own, nxt, x1)


def per_device(inputs, cotangent, w_down, w_up):
    down = w_down[0]
    upward = w_up[0]
    micro, batch_rows, width = inputs.shape
    rank = down.shape[1]
    rows = micro * batch_rows
    sections = lax.axis_size("section")
    shards = lax.axis_size("dp")
    part = width // shards
    d = lax.axis_index("dp")
    x0 = inputs.reshape(rows, width)
    g16 = cotangent.reshape(rows, width)
    up_t = upward.T

    mine_u = lax.dynamic_slice_in_dim(up_t, d * part, part, 0)
    mine_w = lax.dynamic_slice_in_dim(down, d * part, part, 0)
    base = jnp.concatenate([mine_w, mine_u], axis=1)
    pyh, n0, grams = grams_of(sections, shards, x0, g16, down, upward, mine_u, base)
    grams = grams.reshape(sections // 2, 2 * rank, 4 * rank)
    x1, g1, u_s, q_s = recurrence(sections, pyh, n0, grams, x0, g16, upward, down)
    own, nxt = reduce_gather(sections, shards, x1, g1, u_s, q_s, upward, base)
    wide = (width, 2 * rank)
    grad_down, grad_up, advance = finish(sections, own.reshape(wide), nxt.reshape(wide), x1)
    return (grad_down[None], grad_up[None], advance.reshape(1, micro, batch_rows, width))


def solution(mesh):
    in_specs = (
        P(None, "dp", None),
        P(None, "dp", None),
        P("section", None, None),
        P("section", None, None),
    )
    out_specs = (P("section", None, None), P("section", None, None), P("section", None, "dp", None))
    return jax.shard_map(
        per_device, mesh=mesh, in_specs=in_specs, out_specs=out_specs, check_vma=False
    )
```

```python
import functools

import jax
import jax.numpy as jnp
from jax import lax
from jax.experimental import pallas as pl
from jax.experimental.pallas import tpu as pltpu
from jax.sharding import PartitionSpec as P

MESH = pl.DeviceIdType.MESH
eps = 1e-05
learn_rate = 0.05
f32 = jnp.float32
bf16 = jnp.bfloat16


def dot_nn(a, b):
    return jnp.dot(a, b, preferred_element_type=f32)


def dot_tn(a, b):
    return lax.dot_general(a, b, (((0,), (0,)), ((), ())), preferred_element_type=f32)


def dot_nt(a, b):
    return lax.dot_general(a, b, (((1,), (1,)), ((), ())), preferred_element_type=f32)


def gelu_pair(a):
    c = 0.7978845608028654
    inner = c * (a + 0.044715 * a * a * a)
    th = jnp.tanh(inner)
    value = 0.5 * a * (1.0 + th)
    slope = 0.5 * (1.0 + th) + 0.5 * a * (1.0 - th * th) * c * (1.0 + 3 * 0.044715 * a * a)
    return value, slope


def recurrence_kernel(sections, chunks, per, pyh, n0, nn, x0, g16, up, wd, upart, wpart,
                      xout, gout, u_out, q_out,
                      ul, ql, qp, mb, ys, nl, nsend, acc, hacc, slope, act, rinv, uf, qs, cpair,
                      xin, xkeep, xgive, gin, gkeep, ggive,
                      u_send, u_recv, q_send, q_recv, m_send, m_recv, e_sem,
                      c_send, c_recv, g_send, g_recv,
                      b_send, b_recv, h_send, h_recv):
    s = lax.axis_index("section")
    planes = sections // 2
    rows, width = x0.shape
    some = rows // 2
    rank = up.shape[0]
    half = width // 2
    piece = half // chunks
    trips = chunks // per
    z = s // 2
    ylo = lax.rem(s, 2)
    first = ylo == 0
    partner = {"section": s + 1 - 2 * ylo}
    head = slice(0, rank)
    tail = slice(rank, 2 * rank)
    mine = pl.ds(ylo * some, some)
    theirs = pl.ds((1 - ylo) * some, some)

    def plane(i):
        return {"section": 2 * i + ylo}

    def peer(offset):
        return lax.rem(z + offset, planes)

    barrier = pltpu.get_barrier_semaphore()
    for o in range(1, planes):
        pl.semaphore_signal(barrier, inc=1, device_id=plane(peer(o)), device_id_type=MESH)
    pl.semaphore_signal(barrier, inc=1, device_id=partner, device_id_type=MESH)
    pl.semaphore_wait(barrier, planes)

    eye = (lax.broadcasted_iota(jnp.int32, (some, rank), 0)
           == lax.broadcasted_iota(jnp.int32, (some, rank), 1)).astype(f32)

    def to_row(col):
        return jnp.sum(eye * col, axis=0, keepdims=True)

    def to_col(row):
        return jnp.sum(eye * row, axis=1, keepdims=True)

    def columns(base, c):
        return pl.ds(pl.multiple_of(base + c * piece, 128), piece)

    def x_copy(c):
        return remote(xkeep.at[:, columns(0, c)], xin.at[:, columns(0, c)],
                      c_send.at[c], c_recv.at[c], plane(peer(1)))

    def b_copy(c):
        return remote(gkeep.at[:, columns(0, c)], gin.at[:, columns(0, c)],
                      b_send.at[c], b_recv.at[c], plane(peer(planes - 1)))

    def give_copy(c):
        return remote(xgive.at[:, columns(0, c)], xout.at[:, columns(ylo * half, c)],
                      g_send.at[c], g_recv.at[c], partner)

    def give_arrived(c):
        return remote(xgive.at[:, columns(0, c)], xout.at[:, columns((1 - ylo) * half, c)],
                      g_send.at[c], g_recv.at[c], partner)

    def h_copy(c):
        return remote(ggive.at[:, columns(0, c)], gout.at[:, columns(ylo * half, c)],
                      h_send.at[c], h_recv.at[c], partner)

    def h_arrived(c):
        return remote(ggive.at[:, columns(0, c)], gout.at[:, columns((1 - ylo) * half, c)],
                      h_send.at[c], h_recv.at[c], partner)

    def near_copy(k, part, sem):
        spot = ul.at[k, :, part]
        return remote(spot, spot, e_sem.at[2 * sem], e_sem.at[2 * sem + 1], plane(peer(1)))

    def n_copy():
        return remote(nsend, nl, e_sem.at[4], e_sem.at[5], plane(peer(1)))

    def uf_copy():
        return remote(ul.at[z], uf.at[mine], e_sem.at[6], e_sem.at[7], partner)

    def uf_arrived():
        return remote(ul.at[z], uf.at[theirs], e_sem.at[6], e_sem.at[7], partner)

    def qp_copy():
        return remote(ql.at[z], qp, e_sem.at[8], e_sem.at[9], partner)

    def u_copy(o):
        return remote(ul.at[z], ul.at[z], u_send.at[o], u_recv.at[z], plane(peer(o)))

    def u_arrived(k):
        return remote(ul.at[k], ul.at[k], u_send.at[0], u_recv.at[k], plane(peer(1)))

    def q_copy(j):
        return remote(ql.at[z], ql.at[z], q_send.at[j], q_recv.at[z], plane(j))

    def q_arrived(k):
        return remote(ql.at[k], ql.at[k], q_send.at[0], q_recv.at[k], plane(peer(1)))

    def m_copy(j):
        return remote(nn.at[j, :, 0:2 * rank], mb.at[z], m_send.at[j], m_recv.at[z], plane(j))

    def m_arrived(k):
        return remote(mb.at[k], mb.at[k], m_send.at[0], m_recv.at[k], plane(peer(1)))

    acc[:, 0:2 * rank] = pyh[0]
    acc[:, 2 * rank:4 * rank] = pyh[1]
    hacc[...] = pyh[2]

    def start_m(j, carry):
        m_copy(j).start()
        return carry

    lax.fori_loop(0, z, start_m, 0)

    def chain(c):
        @pl.when(z > 0)
        def _():
            x_copy(c).wait_recv()

        here = columns(ylo * half, c)
        there = columns(0, c)
        start = jnp.where(z > 0, xin[:, there], x0[:, here]).astype(f32)
        ours = up[:, here]
        other = upart[:, there]
        x_a = (start + dot_nn(uf[:, head], jnp.where(first, ours, other))).astype(bf16)
        x_b = (x_a.astype(f32) + dot_nn(uf[:, tail], jnp.where(first, other, ours))).astype(bf16)
        xkeep[:, there] = x_b

        @pl.when(z < planes - 1)
        def _():
            x_copy(c).start()

        xgive[:, there] = jnp.where(first, x_b, x_a)
        give_copy(c).start()
        xout[:, here] = jnp.where(first, x_a, x_b)

    def chain_back(c):
        @pl.when(z < planes - 1)
        def _():
            b_copy(c).wait_recv()

        here = columns(ylo * half, c)
        there = columns(0, c)
        ours = wd[here, :]
        other = wpart[there, :]
        g_b = jnp.where(z < planes - 1, gin[:, there], g16[:, here])
        x_a = jnp.where(z > 0, xin[:, there], x0[:, here]).astype(f32)
        x_b = jnp.where(first, xout[:, here], xgive[:, there]).astype(f32)
        g_a = (g_b.astype(f32) + dot_nt(qs[:, tail], jnp.where(first, other, ours))
               - cpair[1, :, 0:1] * x_b).astype(bf16)
        g_0 = (g_a.astype(f32) + dot_nt(qs[:, head], jnp.where(first, ours, other))
               - cpair[0, :, 0:1] * x_a).astype(bf16)

        @pl.when(z > 0)
        def _():
            gkeep[:, there] = g_0
            b_copy(c).start()

        ggive[:, there] = jnp.where(first, g_b, g_a)
        h_copy(c).start()
        gout[:, here] = jnp.where(first, g_a, g_b)

    def forward_own():
        @pl.when(z > 0)
        def _():
            n_copy().wait_recv()

        norm_a = jnp.where(z > 0, to_col(nl[0:1, :]), n0[:, 0:1])
        scale_a = lax.rsqrt(norm_a * (1.0 / width) + eps)
        pre_a = acc[:, 0:rank] * scale_a
        value_a, slope_a = gelu_pair(pre_a)
        u_a = value_a.astype(bf16)
        ul[z, :, head] = u_a

        @pl.when(z < planes - 1)
        def _():
            near_copy(z, head, 0).start()

        step = dot_nn(u_a, nn[z, 0:rank, rank:4 * rank])
        y_a = acc[:, 2 * rank:3 * rank]
        norm_b = norm_a + jnp.sum(u_a.astype(f32) * (2.0 * y_a + step[:, rank:2 * rank]),
                                  axis=1, keepdims=True)
        scale_b = lax.rsqrt(norm_b * (1.0 / width) + eps)
        pre_b = (acc[:, rank:2 * rank] + step[:, 0:rank]) * scale_b
        value_b, slope_b = gelu_pair(pre_b)
        u_b = value_b.astype(bf16)
        ul[z, :, tail] = u_b

        @pl.when(z < planes - 1)
        def _():
            near_copy(z, tail, 1).start()

        y_b = acc[:, 2 * rank:4 * rank] + step[:, rank:3 * rank]
        more = dot_nn(u_b, nn[z, rank:2 * rank, 2 * rank:4 * rank])
        norm_c = norm_b + jnp.sum(
            u_b.astype(f32) * (2.0 * y_b[:, rank:2 * rank] + more[:, rank:2 * rank]),
            axis=1, keepdims=True)

        @pl.when(z < planes - 1)
        def _():
            nsend[...] = jnp.broadcast_to(to_row(norm_c), nsend.shape)
            n_copy().start()

        uf_copy().start()
        for o in range(2, planes):
            u_copy(o).start()

        @pl.when(z == planes - 1)
        def _():
            u_copy(1).start()

        uf[mine, :] = ul[z]
        ys[2 * z + 1] = y_b
        acc[:, 2 * rank:4 * rank] = y_b + more
        act[:, head] = pre_a
        act[:, tail] = pre_b
        slope[:, head] = slope_a
        slope[:, tail] = slope_b
        rinv[0] = jnp.broadcast_to(scale_a, (some, rank))
        rinv[1] = jnp.broadcast_to(scale_b, (some, rank))

    def c_of(stat):
        line = stat[0:1, :].astype(f32) + stat[1:2, :].astype(f32)
        return to_col(line[:, head]), to_col(line[:, tail])

    def backward_own():
        scale_b = rinv[1]
        q_b = hacc[:, tail] * slope[:, tail]
        low_b = (q_b * scale_b).astype(bf16)
        mix_b = jnp.sum(q_b * act[:, tail], axis=1, keepdims=True) * (1.0 / width)
        c_b = mix_b * scale_b[:, 0:1] * scale_b[:, 0:1]
        h_a = hacc[:, head] + dot_nt(low_b, nn[z, 0:rank, rank:2 * rank]) - c_b * ys[2 * z + 1, :, head]
        scale_a = rinv[0]
        q_a = h_a * slope[:, head]
        mix_a = jnp.sum(q_a * act[:, head], axis=1, keepdims=True) * (1.0 / width)
        c_a = mix_a * scale_a[:, 0:1] * scale_a[:, 0:1]
        ql[z, 0:some, head] = (q_a * scale_a).astype(bf16)
        ql[z, 0:some, tail] = low_b
        spot = lax.broadcasted_iota(jnp.int32, (16, rank), 0)
        for part, col in ((head, c_a), (tail, c_b)):
            line = to_row(col)
            high = line.astype(bf16).astype(f32)
            ql[z, some:some + 16, part] = jnp.where(
                spot == 0, high, jnp.where(spot == 1, line - high, 0.0)).astype(bf16)

        def send(i, carry):
            q_copy(z - 1 - i).start()
            return carry

        lax.fori_loop(0, z, send, 0)
        qp_copy().start()

    def tick(t, carry):
        k = t - 1
        sent = (k >= 0) & (k < planes)
        near = sent & (k == z - 1)

        @pl.when(sent & (k != z) & (k != z - 1))
        def _():
            u_arrived(k).wait_recv()

        @pl.when(near)
        def _():
            near_copy(k, head, 0).wait_recv()
            acc[...] += dot_nn(ul[k, :, head], nn[k, 0:rank, :])
            near_copy(k, tail, 1).wait_recv()
            acc[...] += dot_nn(ul[k, :, tail], nn[k, rank:2 * rank, :])

        @pl.when(sent & (k < z - 1))
        def _():
            acc[...] += dot_nn(ul[k], nn[k])

        @pl.when(t == z)
        def _():
            forward_own()

        @pl.when(sent & (k > z))
        def _():
            before = acc[:, 2 * rank:4 * rank]
            ys[2 * k] = before
            between = before + dot_nn(ul[k, :, head], nn[k, 0:rank, 2 * rank:4 * rank])
            ys[2 * k + 1] = between
            acc[:, 2 * rank:4 * rank] = between + dot_nn(
                ul[k, :, tail], nn[k, rank:2 * rank, 2 * rank:4 * rank])

        r = 2 * planes - t

        @pl.when((r < planes) & (r > z))
        def _():
            m_arrived(r).wait_recv()
            q_arrived(r).wait_recv()
            c_a, c_b = c_of(ql[r, some:some + 16, :])
            hacc[...] += (dot_nt(ql[r, 0:some, :], mb[r]) - c_a * ys[2 * r] - c_b * ys[2 * r + 1])

        @pl.when(t == 2 * planes - 1 - z)
        def _():
            backward_own()

        p = t - (z + 1)

        @pl.when((p >= 0) & (p < trips))
        def _():
            @pl.when(p == 0)
            def _():
                uf_arrived().wait_recv()
            for j in range(per):
                chain(per * p + j)

        b = t - (2 * planes - z)

        @pl.when((b >= 0) & (b < trips))
        def _():
            @pl.when(b == 0)
            def _():
                qp_copy().wait_recv()
                qs[mine, :] = ql[z, 0:some, :]
                qs[theirs, :] = qp[0:some, :]
                for where, stat in ((mine, ql[z, some:some + 16, :]), (theirs, qp[some:some + 16, :])):
                    c_a, c_b = c_of(stat)
                    cpair[0, where, :] = jnp.broadcast_to(c_a, (some, rank))
                    cpair[1, where, :] = jnp.broadcast_to(c_b, (some, rank))
            for j in range(per):
                chain_back(per * b + j)

        return carry

    lax.fori_loop(0, 2 * planes + trips, tick, 0)
    u_out[...] = jnp.where(first, uf[:, head], uf[:, tail])
    q_out[...] = jnp.where(first, qs[:, head], qs[:, tail])

    def finish(c, carry):
        @pl.when(z < planes - 1)
        def _():
            x_copy(c).wait_send()
        give_copy(c).wait_send()
        give_arrived(c).wait_recv()

        @pl.when(z > 0)
        def _():
            b_copy(c).wait_send()
        h_copy(c).wait_send()
        h_arrived(c).wait_recv()
        return carry

    lax.fori_loop(0, chunks, finish, 0)
    for o in range(2, planes):
        u_copy(o).wait_send()

    @pl.when(z == planes - 1)
    def _():
        u_copy(1).wait_send()

    @pl.when(z < planes - 1)
    def _():
        near_copy(z, head, 0).wait_send()
        near_copy(z, tail, 1).wait_send()
        n_copy().wait_send()

    def settle(j, carry):
        q_copy(j).wait_send()
        m_copy(j).wait_send()
        return carry

    lax.fori_loop(0, z, settle, 0)
    uf_copy().wait_send()
    qp_copy().wait_send()


def recurrence(sections, pyh, n0, nn, x0, g16, up, wd, upart, wpart):
    rows, width = x0.shape
    rank = up.shape[0]
    half = width // 2
    some = rows // 2
    planes = sections // 2
    chunks = 28
    per = 4
    vm = pl.BlockSpec(memory_space=pltpu.VMEM)
    dma = pltpu.SemaphoreType.DMA
    sq = (rows, rank)
    two = (some, 2 * rank)
    wide = jax.ShapeDtypeStruct((rows, width), bf16)
    strip = pltpu.VMEM((rows, half), bf16)
    return pl.pallas_call(
        functools.partial(recurrence_kernel, sections, chunks, per),
        out_shape=(wide, wide, jax.ShapeDtypeStruct(sq, bf16), jax.ShapeDtypeStruct(sq, bf16)),
        in_specs=[vm] * 9,
        out_specs=(vm,) * 4,
        scratch_shapes=[
            pltpu.VMEM((planes,) + two, bf16),
            pltpu.VMEM((planes, some + 16, 2 * rank), bf16),
            pltpu.VMEM((some + 16, 2 * rank), bf16),
            pltpu.VMEM((planes, 2 * rank, 2 * rank), bf16),
            pltpu.VMEM((sections,) + two, f32),
            pltpu.VMEM((8, rank), f32),
            pltpu.VMEM((8, rank), f32),
            pltpu.VMEM((some, 4 * rank), f32),
            pltpu.VMEM(two, f32), pltpu.VMEM(two, f32), pltpu.VMEM(two, f32),
            pltpu.VMEM((2, some, rank), f32),
            pltpu.VMEM((rows, 2 * rank), bf16),
            pltpu.VMEM((rows, 2 * rank), bf16),
            pltpu.VMEM((2,) + sq, f32),
            strip, strip, strip, strip, strip, strip,
        ] + [dma((planes,))] * 6 + [dma((10,))] + [dma((chunks,))] * 8,
        compiler_params=pltpu.CompilerParams(
            collective_id=1, has_side_effects=True, vmem_limit_bytes=48 * 1024 * 1024),
    )(pyh, n0, nn, x0, g16, up, wd, upart, wpart)


def dp_place(x_n):
    d = lax.axis_index("dp")
    return d // (2 * x_n), lax.rem(d // 2, x_n), lax.rem(d, 2)


def remote(src, dst, send, recv, where):
    return pltpu.make_async_remote_copy(src_ref=src, dst_ref=dst, send_sem=send, recv_sem=recv,
                                        device_id=where, device_id_type=MESH)


def block_sum(b, yh_n, x_n, core_copy, part, rc, sums, rax, rby, ax_send, ax_recv, by_send, by_recv):
    yh, x, core = dp_place(x_n)
    cut = sums.shape[2] // 2
    y_ = b // x_n
    x_ = lax.rem(b, x_n)
    core_copy(b).wait_recv()
    sums[y_, x_] = (part[b, core].astype(f32) + rc[b].astype(f32)).astype(bf16)
    turn = lax.rem(x_ - x + x_n, x_n)

    @pl.when(turn != 0)
    def _():
        sem = (turn - 1) * yh_n + y_
        remote(sums.at[y_, x_, 0:cut], rax.at[turn - 1, y_], ax_send.at[sem], ax_recv.at[sem],
               {"dp": (yh * x_n + x_) * 2 + core}).start()

    @pl.when(y_ != yh)
    def _():
        remote(sums.at[y_, x_, cut:2 * cut], rby.at[x_], by_send.at[x_], by_recv.at[x_],
               {"dp": (y_ * x_n + x) * 2 + core}).start()


def scatter_sum(yh_n, x_n, sums, rax, rby, sa, ray, sb, rbx,
                ax_send, ax_recv, by_send, by_recv, s_sem, bx_send, bx_recv):
    yh, x, core = dp_place(x_n)
    rows = sums.shape[2]
    cut = rows // 2

    def place(y_, x_, c_):
        return {"dp": (y_ * x_n + x_) * 2 + c_}

    def xp(i):
        return lax.rem(x + i, x_n)

    other_y = place(1 - yh, x, core)

    def ax_copy(i, y_):
        sem = (i - 1) * yh_n + y_
        return remote(sums.at[y_, xp(i), 0:cut], rax.at[i - 1, y_], ax_send.at[sem], ax_recv.at[sem],
                      place(yh, xp(i), core))

    def by_copy(x_):
        return remote(sums.at[1 - yh, x_, cut:rows], rby.at[x_], by_send.at[x_], by_recv.at[x_], other_y)

    def bx_copy(i):
        return remote(sb.at[xp(i)], rbx.at[i - 1], bx_send.at[i - 1], bx_recv.at[i - 1],
                      place(yh, xp(i), core))

    ay_copy = remote(sa.at[1 - yh], ray, s_sem.at[0], s_sem.at[1], other_y)

    for i in range(x_n):
        x_ = xp(i)
        by_copy(x_).wait_recv()
        sb[x_] = (sums[yh, x_, cut:rows].astype(f32) + rby[x_].astype(f32)).astype(bf16)
        if i > 0:
            bx_copy(i).start()
    for y_ in range(yh_n):
        total = sums[y_, x, 0:cut].astype(f32)
        for i in range(1, x_n):
            ax_copy(i, y_).wait_recv()
            total = total + rax[i - 1, y_].astype(f32)
        sa[y_] = total.astype(bf16)
    ay_copy.start()
    total_b = sb[x].astype(f32)
    for i in range(1, x_n):
        bx_copy(i).wait_recv()
        total_b = total_b + rbx[i - 1].astype(f32)
    ay_copy.wait_recv()
    total_a = sa[yh].astype(f32) + ray[...].astype(f32)
    for i in range(1, x_n):
        for y_ in range(yh_n):
            ax_copy(i, y_).wait_send()
        bx_copy(i).wait_send()
    for x_ in range(x_n):
        by_copy(x_).wait_send()
    ay_copy.wait_send()
    return total_a, total_b


def gram_kernel(yh_n, x_n, sections, x0, g16, down, up, mine_u, base, pyh, n0, out, upart, wpart,
                allu, part, rc, sums, rax, rby, sa, ray, sb, rbx, gs, gp, two, mine3, theirs3,
                z_sem, f_send, f_recv, r_send, r_recv,
                c_send, c_recv, ax_send, ax_recv, by_send, by_recv, s_sem, bx_send, bx_recv,
                ga_send, ga_recv, gb_send, gb_recv, gc_send, gc_recv):
    yh, x, core = dp_place(x_n)
    s = lax.axis_index("section")
    z_n = sections // 2
    z = s // 2
    ylo = lax.rem(s, 2)
    rank = up.shape[0]
    rows = rank
    cut = rows // 2

    def place(y_, x_, c_):
        return {"dp": (y_ * x_n + x_) * 2 + c_}

    def xp(i):
        return lax.rem(x + i, x_n)

    def zp(i):
        return lax.rem(z + i, z_n)

    other_core = place(yh, x, 1 - core)
    other_y = place(1 - yh, x, core)
    partner = {"section": s + 1 - 2 * ylo}
    after = {"section": 2 * zp(1) + ylo}
    before = {"section": 2 * zp(z_n - 1) + ylo}

    barrier = pltpu.get_barrier_semaphore()
    peers = [other_core, other_y, partner, after, before]
    peers += [place(yh, xp(i), core) for i in range(1, x_n)]
    for where in peers:
        pl.semaphore_signal(barrier, inc=1, device_id=where, device_id_type=MESH)
    pl.semaphore_wait(barrier, len(peers))

    pair = remote(mine_u, allu.at[z, ylo], z_sem.at[0], z_sem.at[1], partner)
    pair.start()
    allu[z, ylo] = mine_u[...]

    def products(z_):
        for y_ in range(2):
            part[z_, y_] = dot_tn(allu[z_, y_], base[...]).astype(bf16)

    def core_copy(b):
        return remote(part.at[b, 1 - core], rc.at[b], c_send.at[b], c_recv.at[b], other_core)

    hops = z_n // 2

    def ring_f(i):
        if i < hops:
            spot = allu.at[zp(z_n + 1 - i)]
        else:
            spot = allu.at[zp(z_n + 1 - i), 0]
        return remote(spot, spot, f_send.at[i - 1], f_recv.at[i - 1], after)

    def ring_r(i):
        if i < hops:
            spot = allu.at[zp(i - 1)]
        else:
            spot = allu.at[zp(i - 1), 1]
        return remote(spot, spot, r_send.at[i - 1], r_recv.at[i - 1], before)

    pair.wait_recv()
    ring_f(1).start()
    ring_r(1).start()

    u = up[...]
    w = down[...]
    values = x0[...]
    token_half = x0.shape[0] // 2
    keep = pl.ds(ylo * token_half, token_half)
    give = pl.ds((1 - ylo) * token_half, token_half)
    mine3[0] = dot_nn(values, w)
    mine3[1] = dot_nt(values, u)
    mine3[2] = dot_nt(g16[...], u)
    swap3 = remote(mine3.at[:, give], theirs3, z_sem.at[2], z_sem.at[3], partner)
    swap3.start()
    wide = x0[keep, :].astype(f32)
    n0[...] = jnp.broadcast_to(jnp.sum(wide * wide, axis=1, keepdims=True), n0.shape)
    half = x0.shape[1] // 2
    far = pl.ds(pl.multiple_of((1 - ylo) * half, 128), half)
    swap_u = remote(up.at[:, far], upart, z_sem.at[6], z_sem.at[7], partner)
    swap_w = remote(down.at[far, :], wpart, z_sem.at[8], z_sem.at[9], partner)
    swap_u.start()
    swap_w.start()

    def collect(b):
        block_sum(b, yh_n, x_n, core_copy, part, rc, sums, rax, rby,
                  ax_send, ax_recv, by_send, by_recv)

    products(z)
    core_copy(z).start()
    for i in range(1, hops + 1):
        ring_f(i).wait_recv()
        if i < hops:
            ring_f(i + 1).start()
        ring_r(i).wait_recv()
        if i < hops:
            ring_r(i + 1).start()
        products(zp(z_n - i))
        core_copy(zp(z_n - i)).start()
        if i == 1:
            collect(z)
        else:
            collect(zp(i - 1))
        if i < hops:
            products(zp(i))
            core_copy(zp(i)).start()
        collect(zp(z_n - i))

    total_a, total_b = scatter_sum(yh_n, x_n, sums, rax, rby, sa, ray, sb, rbx,
                                   ax_send, ax_recv, by_send, by_recv, s_sem, bx_send, bx_recv)
    gs[0:cut] = total_a.astype(bf16)
    gs[cut:rows] = total_b.astype(bf16)
    swap = remote(gs, gp, z_sem.at[4], z_sem.at[5], partner)
    swap.start()

    def lanes(base, which):
        return pl.ds(pl.multiple_of(base + which * rank, 128), rank)

    swap3.wait_recv()
    pyh[:, :, lanes(0, ylo)] = mine3[:, keep]
    pyh[:, :, lanes(0, 1 - ylo)] = theirs3[...]
    two[:, lanes(0, ylo)] = gs[:, 0:rank]
    two[:, lanes(2 * rank, ylo)] = gs[:, rank:2 * rank]
    swap.wait_recv()
    two[:, lanes(0, 1 - ylo)] = gp[:, 0:rank]
    two[:, lanes(2 * rank, 1 - ylo)] = gp[:, rank:2 * rank]
    out[yh, x, core] = two[...]

    low = pl.ds(0, cut)
    high = pl.ds(cut, cut)

    def spread(src, spot, sems, i, where):
        return remote(src, spot, sems[0].at[i], sems[1].at[i], where)

    ga = (ga_send, ga_recv)
    gb = (gb_send, gb_recv)
    a_y = spread(two.at[low], out.at[yh, x, core, low], ga, 0, other_y)

    def a_x(i):
        spot = out.at[:, x, core, low]
        return spread(spot, spot, ga, i, place(yh, xp(i), core))

    def b_x(i):
        return spread(two.at[high], out.at[yh, x, core, high], gb, i - 1, place(yh, xp(i), core))

    def b_y(i):
        spot = out.at[yh, xp(i), core, high]
        return spread(spot, spot, gb, x_n - 1 + i, other_y)

    def all_c(i):
        spot = out.at[:, xp(i), core]
        return remote(spot, spot, gc_send.at[i], gc_recv.at[i], other_core)

    a_y.start()
    for i in range(1, x_n):
        b_x(i).start()
    b_y(0).start()
    a_y.wait_recv()
    for i in range(1, x_n):
        a_x(i).start()
    for i in range(1, x_n):
        b_x(x_n - i).wait_recv()
        b_y(i).start()
    b_y(0).wait_recv()
    all_c(0).start()
    for i in range(1, x_n):
        a_x(x_n - i).wait_recv()
        b_y(i).wait_recv()
        all_c(i).start()
    for i in range(x_n):
        all_c(i).wait()
        b_y(i).wait_send()
    for i in range(1, x_n):
        a_x(i).wait_send()
        b_x(i).wait_send()
    a_y.wait_send()
    pair.wait_send()
    swap.wait_send()
    swap3.wait_send()
    swap_u.wait()
    swap_w.wait()
    for i in range(1, hops + 1):
        ring_f(i).wait_send()
        ring_r(i).wait_send()

    def settle(b, carry):
        core_copy(b).wait_send()
        return carry

    lax.fori_loop(0, yh_n * x_n, settle, 0)


def grams_of(sections, shards, x0, g16, down, up, mine_u, base):
    x_n = 4
    yh_n = shards // (2 * x_n)
    rows, width = x0.shape
    rank = up.shape[0]
    height = mine_u.shape[0]
    cut = rank // 2
    vm = pl.BlockSpec(memory_space=pltpu.VMEM)
    dma = pltpu.SemaphoreType.DMA

    def buf(*lead):
        return pltpu.VMEM(lead + (2 * rank,), bf16)

    return pl.pallas_call(
        functools.partial(gram_kernel, yh_n, x_n, sections),
        out_shape=(
            jax.ShapeDtypeStruct((3, rows // 2, 2 * rank), f32),
            jax.ShapeDtypeStruct((rows // 2, rank), f32),
            jax.ShapeDtypeStruct((yh_n, x_n, 2, rank, 4 * rank), bf16),
            jax.ShapeDtypeStruct((rank, width // 2), bf16),
            jax.ShapeDtypeStruct((width // 2, rank), bf16),
        ),
        in_specs=[vm] * 6,
        out_specs=(vm,) * 5,
        scratch_shapes=[
            pltpu.VMEM((sections // 2, 2, height, rank), bf16),
            buf(yh_n * x_n, 2, rank), buf(yh_n * x_n, rank), buf(yh_n, x_n, rank),
            buf(x_n - 1, yh_n, cut), buf(x_n, cut), buf(yh_n, cut), buf(cut),
            buf(x_n, cut), buf(x_n - 1, cut), buf(rank), buf(rank),
            pltpu.VMEM((rank, 4 * rank), bf16),
            pltpu.VMEM((3, rows, rank), f32), pltpu.VMEM((3, rows // 2, rank), f32),
            dma((10,)), dma((sections // 4,)), dma((sections // 4,)),
            dma((sections // 4,)), dma((sections // 4,)),
            dma((yh_n * x_n,)), dma((yh_n * x_n,)),
            dma((yh_n * (x_n - 1),)), dma((yh_n * (x_n - 1),)), dma((x_n,)), dma((x_n,)), dma((4,)),
            dma((x_n - 1,)), dma((x_n - 1,)),
            dma((x_n,)), dma((x_n,)), dma((2 * x_n,)), dma((2 * x_n,)), dma((x_n,)), dma((x_n,)),
        ],
        compiler_params=pltpu.CompilerParams(
            collective_id=3, has_side_effects=True, vmem_limit_bytes=48 * 1024 * 1024),
    )(x0, g16, down, up, mine_u, base)


def reduce_kernel(yh_n, x_n, sections, x1, g1, u_s, q_s, up, base, own, nxt,
                  part, rc, sums, rax, rby, sa, ray, sb, rbx, gs, nw,
                  c_send, c_recv, ax_send, ax_recv, by_send, by_recv, s_sem, bx_send, bx_recv,
                  own_send, own_recv, oc_send, oc_recv, nx_send, nx_recv, ny_send, ny_recv,
                  nc_send, nc_recv):
    d = lax.axis_index("dp")
    s = lax.axis_index("section")
    yh = d // (2 * x_n)
    x = lax.rem(d // 2, x_n)
    core = lax.rem(d, 2)
    rows = base.shape[0]
    cut = rows // 2

    def place(y_, x_, c_):
        return {"dp": (y_ * x_n + x_) * 2 + c_}

    def xp(i):
        return lax.rem(x + i, x_n)

    other_core = place(yh, x, 1 - core)
    other_y = place(1 - yh, x, core)
    up_section = lax.rem(s + 1, sections)
    down_section = lax.rem(s + sections - 1, sections)

    def copy(src, dst, send, recv, where):
        return pltpu.make_async_remote_copy(src_ref=src, dst_ref=dst, send_sem=send, recv_sem=recv,
                                            device_id=where, device_id_type=MESH)

    barrier = pltpu.get_barrier_semaphore()
    peers = [other_core, other_y, {"section": up_section}, {"section": down_section}]
    peers += [place(yh, xp(i), core) for i in range(1, x_n)]
    for where in peers:
        pl.semaphore_signal(barrier, inc=1, device_id=where, device_id_type=MESH)
    pl.semaphore_wait(barrier, len(peers))

    def core_copy(b):
        return copy(part.at[b, 1 - core], rc.at[b], c_send.at[b], c_recv.at[b], other_core)

    def terms(b, carry):
        cols = pl.ds(pl.multiple_of(b * 2 * rows, 128), 2 * rows)
        u = u_s[...]
        before = (x1[:, cols].astype(f32) - dot_nn(u, up[:, cols])).astype(bf16)
        g_down = dot_tn(before, q_s[...]).astype(bf16)
        g_up = dot_tn(g1[:, cols], u).astype(bf16)
        rank = u.shape[1]
        for half in range(2):
            part[b, half, :, 0:rank] = g_down[half * rows:(half + 1) * rows]
            part[b, half, :, rank:2 * rank] = g_up[half * rows:(half + 1) * rows]
        core_copy(b).start()

        @pl.when(b > 0)
        def _():
            collect(b - 1)
        return carry

    def collect(b):
        block_sum(b, yh_n, x_n, core_copy, part, rc, sums, rax, rby,
                  ax_send, ax_recv, by_send, by_recv)

    blocks = yh_n * x_n
    lax.fori_loop(0, blocks, terms, 0)
    collect(blocks - 1)

    total_a, total_b = scatter_sum(yh_n, x_n, sums, rax, rby, sa, ray, sb, rbx,
                                   ax_send, ax_recv, by_send, by_recv, s_sem, bx_send, bx_recv)
    gs[0:cut] = total_a.astype(bf16)
    gs[cut:rows] = total_b.astype(bf16)
    nw[...] = (base[...].astype(f32) - learn_rate * gs[...].astype(f32)).astype(bf16)

    has_next = s < sections - 1
    next_copy = copy(nw, nxt.at[yh, x, core], s_sem.at[4], s_sem.at[5], {"section": down_section})
    own_y = copy(gs, own.at[yh, x, core], s_sem.at[6], s_sem.at[7], other_y)
    own_y.start()

    @pl.when(s > 0)
    def _():
        next_copy.start()

    own[yh, x, core] = gs[...]

    def own_x(i):
        return copy(own.at[:, x, core], own.at[:, x, core], own_send.at[i - 1], own_recv.at[i - 1],
                    place(yh, xp(i), core))

    def own_c(i):
        spot = own.at[:, xp(i), core]
        return copy(spot, spot, oc_send.at[i], oc_recv.at[i], other_core)

    def nxt_x(i):
        spot = nxt.at[yh, x, core]
        return copy(spot, spot, nx_send.at[i - 1], nx_recv.at[i - 1], place(yh, xp(i), core))

    def nxt_y(i):
        spot = nxt.at[yh, xp(i), core]
        return copy(spot, spot, ny_send.at[i], ny_recv.at[i], other_y)

    def nxt_c(i):
        spot = nxt.at[:, xp(i), core]
        return copy(spot, spot, nc_send.at[i], nc_recv.at[i], other_core)

    @pl.when(has_next)
    def _():
        next_copy.wait_recv()
        for i in range(1, x_n):
            nxt_x(i).start()
        nxt_y(0).start()

    own_y.wait_recv()

    @pl.when(has_next)
    def _():
        for i in range(1, x_n):
            nxt_x(i).wait_send()

    for i in range(1, x_n):
        own_x(i).start()
    own_c(0).start()

    @pl.when(has_next)
    def _():
        for i in range(1, x_n):
            nxt_x(x_n - i).wait_recv()
            nxt_y(i).start()

    for i in range(1, x_n):
        own_x(x_n - i).wait_recv()
        own_c(i).start()

    @pl.when(has_next)
    def _():
        for i in range(x_n):
            nxt_y(i).wait_recv()
            nxt_c(i).start()
        for i in range(x_n):
            nxt_c(i).wait()
            nxt_y(i).wait_send()

    for i in range(x_n):
        own_c(i).wait()
    for i in range(1, x_n):
        own_x(i).wait_send()
    own_y.wait_send()

    @pl.when(s > 0)
    def _():
        next_copy.wait_send()

    def settle(b, carry):
        core_copy(b).wait_send()
        return carry

    lax.fori_loop(0, blocks, settle, 0)


def reduce_gather(sections, shards, x1, g1, u_s, q_s, up, base):
    x_n = 4
    yh_n = shards // (2 * x_n)
    rows, cols = base.shape
    cut = rows // 2
    vm = pl.BlockSpec(memory_space=pltpu.VMEM)
    dma = pltpu.SemaphoreType.DMA
    full = jax.ShapeDtypeStruct((yh_n, x_n, 2, rows, cols), bf16)

    def buf(*lead):
        return pltpu.VMEM(lead + (cols,), bf16)

    return pl.pallas_call(
        functools.partial(reduce_kernel, yh_n, x_n, sections),
        out_shape=(full, full),
        in_specs=[vm] * 6,
        out_specs=(vm, vm),
        scratch_shapes=[
            buf(yh_n * x_n, 2, rows), buf(yh_n * x_n, rows), buf(yh_n, x_n, rows),
            buf(x_n - 1, yh_n, cut), buf(x_n, cut), buf(yh_n, cut), buf(cut),
            buf(x_n, cut), buf(x_n - 1, cut), buf(rows), buf(rows),
            dma((yh_n * x_n,)), dma((yh_n * x_n,)),
            dma((yh_n * (x_n - 1),)), dma((yh_n * (x_n - 1),)), dma((x_n,)), dma((x_n,)), dma((8,)),
            dma((x_n - 1,)), dma((x_n - 1,)), dma((x_n - 1,)), dma((x_n - 1,)),
            dma((x_n,)), dma((x_n,)), dma((x_n - 1,)), dma((x_n - 1,)), dma((x_n,)), dma((x_n,)),
            dma((x_n,)), dma((x_n,)),
        ],
        compiler_params=pltpu.CompilerParams(
            collective_id=2, has_side_effects=True, vmem_limit_bytes=52 * 1024 * 1024),
    )(x1, g1, u_s, q_s, up, base)


def finish_kernel(sections, own, nxt, x1, grad_down, grad_up, advance):
    last = lax.axis_index("section") == sections - 1
    rows, width = x1.shape
    rank = grad_down.shape[1]
    step = 896
    count = width // step

    def first(b, carry):
        pre, norm = carry
        here = pl.ds(pl.multiple_of(b * step, 128), step)
        block = own[here, :]
        grad_down[here, :] = block[:, 0:rank]
        grad_up[:, here] = block[:, rank:2 * rank].astype(f32).T.astype(bf16)
        x = x1[:, here]
        values = x.astype(f32)
        pre = pre + dot_nn(x, nxt[here, 0:rank])
        return pre, norm + jnp.sum(values * values, axis=1, keepdims=True)

    pre, norm = lax.fori_loop(
        0, count, first, (jnp.zeros((rows, rank), f32), jnp.zeros((rows, 1), f32)))
    value, unused = gelu_pair(pre * lax.rsqrt(norm * (1.0 / width) + eps))
    value = value.astype(bf16)

    def second(b, carry):
        here = pl.ds(pl.multiple_of(b * step, 128), step)
        bump = dot_nt(value, nxt[here, rank:2 * rank])
        advance[:, here] = (x1[:, here].astype(f32) + jnp.where(last, 0.0, bump)).astype(bf16)
        return carry

    lax.fori_loop(0, count, second, 0)


def finish(sections, own, nxt, x1):
    rows, width = x1.shape
    rank = own.shape[1] // 2
    vm = pl.BlockSpec(memory_space=pltpu.VMEM)
    return pl.pallas_call(
        functools.partial(finish_kernel, sections),
        out_shape=(
            jax.ShapeDtypeStruct((width, rank), bf16),
            jax.ShapeDtypeStruct((rank, width), bf16),
            jax.ShapeDtypeStruct((rows, width), bf16),
        ),
        in_specs=[vm] * 3,
        out_specs=(vm,) * 3,
        compiler_params=pltpu.CompilerParams(vmem_limit_bytes=48 * 1024 * 1024),
    )(own, nxt, x1)


def per_device(inputs, cotangent, w_down, w_up):
    down = w_down[0]
    upward = w_up[0]
    micro, batch_rows, width = inputs.shape
    rank = down.shape[1]
    rows = micro * batch_rows
    sections = lax.axis_size("section")
    shards = lax.axis_size("dp")
    part = width // shards
    d = lax.axis_index("dp")
    x0 = inputs.reshape(rows, width)
    g16 = cotangent.reshape(rows, width)
    up_t = upward.T

    mine_u = lax.dynamic_slice_in_dim(up_t, d * part, part, 0)
    mine_w = lax.dynamic_slice_in_dim(down, d * part, part, 0)
    base = jnp.concatenate([mine_w, mine_u], axis=1)
    pyh, n0, grams, upart, wpart = grams_of(sections, shards, x0, g16, down, upward, mine_u, base)
    grams = grams.reshape(sections // 2, 2 * rank, 4 * rank)
    x1, g1, u_s, q_s = recurrence(sections, pyh, n0, grams, x0, g16, upward, down, upart, wpart)
    own, nxt = reduce_gather(sections, shards, x1, g1, u_s, q_s, upward, base)
    wide = (width, 2 * rank)
    grad_down, grad_up, advance = finish(sections, own.reshape(wide), nxt.reshape(wide), x1)
    return (grad_down[None], grad_up[None], advance.reshape(1, micro, batch_rows, width))


def solution(mesh):
    in_specs = (
        P(None, "dp", None),
        P(None, "dp", None),
        P("section", None, None),
        P("section", None, None),
    )
    out_specs = (P("section", None, None), P("section", None, None), P("section", None, "dp", None))
    return jax.shard_map(
        per_device, mesh=mesh, in_specs=in_specs, out_specs=out_specs, check_vma=False
    )
```

```python
import functools

import jax
import jax.numpy as jnp
from jax import lax
from jax.experimental import pallas as pl
from jax.experimental.pallas import tpu as pltpu
from jax.sharding import PartitionSpec as P

MESH = pl.DeviceIdType.MESH
eps = 1e-05
learn_rate = 0.05
f32 = jnp.float32
bf16 = jnp.bfloat16


def dot_nn(a, b):
    return jnp.dot(a, b, preferred_element_type=f32)


def dot_tn(a, b):
    return lax.dot_general(a, b, (((0,), (0,)), ((), ())), preferred_element_type=f32)


def dot_nt(a, b):
    return lax.dot_general(a, b, (((1,), (1,)), ((), ())), preferred_element_type=f32)


def gelu_pair(a):
    c = 0.7978845608028654
    inner = c * (a + 0.044715 * a * a * a)
    th = jnp.tanh(inner)
    value = 0.5 * a * (1.0 + th)
    slope = 0.5 * (1.0 + th) + 0.5 * a * (1.0 - th * th) * c * (1.0 + 3 * 0.044715 * a * a)
    return value, slope


def recurrence_kernel(sections, chunks, per, pyh, n0, nn, x0, g16, up, wd, upart, wpart,
                      xout, gout, u_out, q_out,
                      ul, ql, qp, mb, ys, nl, nsend, acc, hacc, slope, act, rinv, uf, qs, cpair,
                      xin, xkeep, xgive, gin, gkeep, ggive,
                      u_send, u_recv, q_send, q_recv, m_send, m_recv, e_sem,
                      c_send, c_recv, g_send, g_recv,
                      b_send, b_recv, h_send, h_recv):
    s = lax.axis_index("section")
    planes = sections // 2
    rows, width = x0.shape
    some = rows // 2
    rank = up.shape[0]
    half = width // 2
    piece = half // chunks
    trips = chunks // per
    z = s // 2
    ylo = lax.rem(s, 2)
    first = ylo == 0
    partner = {"section": s + 1 - 2 * ylo}
    head = slice(0, rank)
    tail = slice(rank, 2 * rank)
    mine = pl.ds(ylo * some, some)
    theirs = pl.ds((1 - ylo) * some, some)

    def plane(i):
        return {"section": 2 * i + ylo}

    def peer(offset):
        return lax.rem(z + offset, planes)

    barrier = pltpu.get_barrier_semaphore()
    for o in range(1, planes):
        pl.semaphore_signal(barrier, inc=1, device_id=plane(peer(o)), device_id_type=MESH)
    pl.semaphore_signal(barrier, inc=1, device_id=partner, device_id_type=MESH)
    pl.semaphore_wait(barrier, planes)

    eye = (lax.broadcasted_iota(jnp.int32, (some, rank), 0)
           == lax.broadcasted_iota(jnp.int32, (some, rank), 1)).astype(f32)

    def to_row(col):
        return jnp.sum(eye * col, axis=0, keepdims=True)

    def to_col(row):
        return jnp.sum(eye * row, axis=1, keepdims=True)

    def columns(base, c):
        return pl.ds(pl.multiple_of(base + c * piece, 128), piece)

    def x_copy(c):
        return remote(xkeep.at[:, columns(0, c)], xin.at[:, columns(0, c)],
                      c_send.at[c], c_recv.at[c], plane(peer(1)))

    def b_copy(c):
        return remote(gkeep.at[:, columns(0, c)], gin.at[:, columns(0, c)],
                      b_send.at[c], b_recv.at[c], plane(peer(planes - 1)))

    def give_copy(c):
        return remote(xgive.at[:, columns(0, c)], xout.at[:, columns(ylo * half, c)],
                      g_send.at[c], g_recv.at[c], partner)

    def give_arrived(c):
        return remote(xgive.at[:, columns(0, c)], xout.at[:, columns((1 - ylo) * half, c)],
                      g_send.at[c], g_recv.at[c], partner)

    def h_copy(c):
        return remote(ggive.at[:, columns(0, c)], gout.at[:, columns(ylo * half, c)],
                      h_send.at[c], h_recv.at[c], partner)

    def h_arrived(c):
        return remote(ggive.at[:, columns(0, c)], gout.at[:, columns((1 - ylo) * half, c)],
                      h_send.at[c], h_recv.at[c], partner)

    def near_copy(k, part, sem):
        spot = ul.at[k, :, part]
        return remote(spot, spot, e_sem.at[2 * sem], e_sem.at[2 * sem + 1], plane(peer(1)))

    def n_copy():
        return remote(nsend, nl, e_sem.at[4], e_sem.at[5], plane(peer(1)))

    def uf_copy():
        return remote(ul.at[z], uf.at[mine], e_sem.at[6], e_sem.at[7], partner)

    def uf_arrived():
        return remote(ul.at[z], uf.at[theirs], e_sem.at[6], e_sem.at[7], partner)

    def qp_copy():
        return remote(ql.at[z], qp, e_sem.at[8], e_sem.at[9], partner)

    def u_copy(o):
        return remote(ul.at[z], ul.at[z], u_send.at[o], u_recv.at[z], plane(peer(o)))

    def u_arrived(k):
        return remote(ul.at[k], ul.at[k], u_send.at[0], u_recv.at[k], plane(peer(1)))

    def q_copy(j):
        return remote(ql.at[z], ql.at[z], q_send.at[j], q_recv.at[z], plane(j))

    def q_arrived(k):
        return remote(ql.at[k], ql.at[k], q_send.at[0], q_recv.at[k], plane(peer(1)))

    def m_copy(j):
        return remote(nn.at[j, :, 0:2 * rank], mb.at[z], m_send.at[j], m_recv.at[z], plane(j))

    def m_arrived(k):
        return remote(mb.at[k], mb.at[k], m_send.at[0], m_recv.at[k], plane(peer(1)))

    acc[:, 0:2 * rank] = pyh[0]
    acc[:, 2 * rank:4 * rank] = pyh[1]
    hacc[...] = pyh[2]

    def start_m(j, carry):
        m_copy(j).start()
        return carry

    lax.fori_loop(0, z, start_m, 0)

    def chain(c):
        @pl.when(z > 0)
        def _():
            x_copy(c).wait_recv()

        here = columns(ylo * half, c)
        there = columns(0, c)
        start = jnp.where(z > 0, xin[:, there], x0[:, here]).astype(f32)
        ours = up[:, here]
        other = upart[:, there]
        x_a = (start + dot_nn(uf[:, head], jnp.where(first, ours, other))).astype(bf16)
        x_b = (x_a.astype(f32) + dot_nn(uf[:, tail], jnp.where(first, other, ours))).astype(bf16)
        xkeep[:, there] = x_b

        @pl.when(z < planes - 1)
        def _():
            x_copy(c).start()

        xgive[:, there] = jnp.where(first, x_b, x_a)
        give_copy(c).start()
        xout[:, here] = jnp.where(first, x_a, x_b)

    def chain_back(c):
        @pl.when(z < planes - 1)
        def _():
            b_copy(c).wait_recv()

        here = columns(ylo * half, c)
        there = columns(0, c)
        ours = wd[here, :]
        other = wpart[there, :]
        g_b = jnp.where(z < planes - 1, gin[:, there], g16[:, here])
        x_a = jnp.where(z > 0, xin[:, there], x0[:, here]).astype(f32)
        x_b = jnp.where(first, xout[:, here], xgive[:, there]).astype(f32)
        g_a = (g_b.astype(f32) + dot_nt(qs[:, tail], jnp.where(first, other, ours))
               - cpair[1, :, 0:1] * x_b).astype(bf16)
        g_0 = (g_a.astype(f32) + dot_nt(qs[:, head], jnp.where(first, ours, other))
               - cpair[0, :, 0:1] * x_a).astype(bf16)

        @pl.when(z > 0)
        def _():
            gkeep[:, there] = g_0
            b_copy(c).start()

        ggive[:, there] = jnp.where(first, g_b, g_a)
        h_copy(c).start()
        gout[:, here] = jnp.where(first, g_a, g_b)

    def forward_own():
        @pl.when(z > 0)
        def _():
            n_copy().wait_recv()

        norm_a = jnp.where(z > 0, to_col(nl[0:1, :]), n0[:, 0:1])
        scale_a = lax.rsqrt(norm_a * (1.0 / width) + eps)
        pre_a = acc[:, 0:rank] * scale_a
        value_a, slope_a = gelu_pair(pre_a)
        u_a = value_a.astype(bf16)
        ul[z, :, head] = u_a

        @pl.when(z < planes - 1)
        def _():
            near_copy(z, head, 0).start()

        step = dot_nn(u_a, nn[z, 0:rank, rank:4 * rank])
        y_a = acc[:, 2 * rank:3 * rank]
        norm_b = norm_a + jnp.sum(u_a.astype(f32) * (2.0 * y_a + step[:, rank:2 * rank]),
                                  axis=1, keepdims=True)
        scale_b = lax.rsqrt(norm_b * (1.0 / width) + eps)
        pre_b = (acc[:, rank:2 * rank] + step[:, 0:rank]) * scale_b
        value_b, slope_b = gelu_pair(pre_b)
        u_b = value_b.astype(bf16)
        ul[z, :, tail] = u_b

        @pl.when(z < planes - 1)
        def _():
            near_copy(z, tail, 1).start()

        y_b = acc[:, 2 * rank:4 * rank] + step[:, rank:3 * rank]
        more = dot_nn(u_b, nn[z, rank:2 * rank, 2 * rank:4 * rank])
        norm_c = norm_b + jnp.sum(
            u_b.astype(f32) * (2.0 * y_b[:, rank:2 * rank] + more[:, rank:2 * rank]),
            axis=1, keepdims=True)

        @pl.when(z < planes - 1)
        def _():
            nsend[...] = jnp.broadcast_to(to_row(norm_c), nsend.shape)
            n_copy().start()

        uf_copy().start()
        for o in range(2, planes):
            u_copy(o).start()

        @pl.when(z == planes - 1)
        def _():
            u_copy(1).start()

        uf[mine, :] = ul[z]
        ys[2 * z + 1] = y_b
        acc[:, 2 * rank:4 * rank] = y_b + more
        act[:, head] = pre_a
        act[:, tail] = pre_b
        slope[:, head] = slope_a
        slope[:, tail] = slope_b
        rinv[0] = jnp.broadcast_to(scale_a, (some, rank))
        rinv[1] = jnp.broadcast_to(scale_b, (some, rank))

    def c_of(stat):
        line = stat[0:1, :].astype(f32) + stat[1:2, :].astype(f32)
        return to_col(line[:, head]), to_col(line[:, tail])

    def backward_own():
        scale_b = rinv[1]
        q_b = hacc[:, tail] * slope[:, tail]
        low_b = (q_b * scale_b).astype(bf16)
        mix_b = jnp.sum(q_b * act[:, tail], axis=1, keepdims=True) * (1.0 / width)
        c_b = mix_b * scale_b[:, 0:1] * scale_b[:, 0:1]
        h_a = hacc[:, head] + dot_nt(low_b, nn[z, 0:rank, rank:2 * rank]) - c_b * ys[2 * z + 1, :, head]
        scale_a = rinv[0]
        q_a = h_a * slope[:, head]
        mix_a = jnp.sum(q_a * act[:, head], axis=1, keepdims=True) * (1.0 / width)
        c_a = mix_a * scale_a[:, 0:1] * scale_a[:, 0:1]
        ql[z, 0:some, head] = (q_a * scale_a).astype(bf16)
        ql[z, 0:some, tail] = low_b
        spot = lax.broadcasted_iota(jnp.int32, (16, rank), 0)
        for part, col in ((head, c_a), (tail, c_b)):
            line = to_row(col)
            high = line.astype(bf16).astype(f32)
            ql[z, some:some + 16, part] = jnp.where(
                spot == 0, high, jnp.where(spot == 1, line - high, 0.0)).astype(bf16)

        def send(i, carry):
            q_copy(z - 1 - i).start()
            return carry

        lax.fori_loop(0, z, send, 0)
        qp_copy().start()

    def tick(t, carry):
        k = t - 1
        sent = (k >= 0) & (k < planes)
        near = sent & (k == z - 1)

        @pl.when(sent & (k != z) & (k != z - 1))
        def _():
            u_arrived(k).wait_recv()

        @pl.when(near)
        def _():
            near_copy(k, head, 0).wait_recv()
            acc[...] += dot_nn(ul[k, :, head], nn[k, 0:rank, :])
            near_copy(k, tail, 1).wait_recv()
            acc[...] += dot_nn(ul[k, :, tail], nn[k, rank:2 * rank, :])

        @pl.when(sent & (k < z - 1))
        def _():
            acc[...] += dot_nn(ul[k], nn[k])

        @pl.when(t == z)
        def _():
            forward_own()

        @pl.when(sent & (k > z))
        def _():
            before = acc[:, 2 * rank:4 * rank]
            ys[2 * k] = before
            between = before + dot_nn(ul[k, :, head], nn[k, 0:rank, 2 * rank:4 * rank])
            ys[2 * k + 1] = between
            acc[:, 2 * rank:4 * rank] = between + dot_nn(
                ul[k, :, tail], nn[k, rank:2 * rank, 2 * rank:4 * rank])

        r = 2 * planes - t

        @pl.when((r < planes) & (r > z))
        def _():
            m_arrived(r).wait_recv()
            q_arrived(r).wait_recv()
            c_a, c_b = c_of(ql[r, some:some + 16, :])
            hacc[...] += (dot_nt(ql[r, 0:some, :], mb[r]) - c_a * ys[2 * r] - c_b * ys[2 * r + 1])

        @pl.when(t == 2 * planes - 1 - z)
        def _():
            backward_own()

        p = t - (z + 1)

        @pl.when((p >= 0) & (p < trips))
        def _():
            @pl.when(p == 0)
            def _():
                uf_arrived().wait_recv()
            for j in range(per):
                chain(per * p + j)

        b = t - (2 * planes - z)

        @pl.when((b >= 0) & (b < trips))
        def _():
            @pl.when(b == 0)
            def _():
                qp_copy().wait_recv()
                qs[mine, :] = ql[z, 0:some, :]
                qs[theirs, :] = qp[0:some, :]
                for where, stat in ((mine, ql[z, some:some + 16, :]), (theirs, qp[some:some + 16, :])):
                    c_a, c_b = c_of(stat)
                    cpair[0, where, :] = jnp.broadcast_to(c_a, (some, rank))
                    cpair[1, where, :] = jnp.broadcast_to(c_b, (some, rank))
            for j in range(per):
                chain_back(per * b + j)

        return carry

    lax.fori_loop(0, 2 * planes + trips, tick, 0)
    u_out[...] = jnp.where(first, uf[:, head], uf[:, tail])
    q_out[...] = jnp.where(first, qs[:, head], qs[:, tail])

    def finish(c, carry):
        @pl.when(z < planes - 1)
        def _():
            x_copy(c).wait_send()
        give_copy(c).wait_send()
        give_arrived(c).wait_recv()

        @pl.when(z > 0)
        def _():
            b_copy(c).wait_send()
        h_copy(c).wait_send()
        h_arrived(c).wait_recv()
        return carry

    lax.fori_loop(0, chunks, finish, 0)
    for o in range(2, planes):
        u_copy(o).wait_send()

    @pl.when(z == planes - 1)
    def _():
        u_copy(1).wait_send()

    @pl.when(z < planes - 1)
    def _():
        near_copy(z, head, 0).wait_send()
        near_copy(z, tail, 1).wait_send()
        n_copy().wait_send()

    def settle(j, carry):
        q_copy(j).wait_send()
        m_copy(j).wait_send()
        return carry

    lax.fori_loop(0, z, settle, 0)
    uf_copy().wait_send()
    qp_copy().wait_send()


def recurrence(sections, pyh, n0, nn, x0, g16, up, wd, upart, wpart):
    rows, width = x0.shape
    rank = up.shape[0]
    half = width // 2
    some = rows // 2
    planes = sections // 2
    chunks = 28
    per = 4
    vm = pl.BlockSpec(memory_space=pltpu.VMEM)
    dma = pltpu.SemaphoreType.DMA
    sq = (rows, rank)
    two = (some, 2 * rank)
    wide = jax.ShapeDtypeStruct((rows, width), bf16)
    strip = pltpu.VMEM((rows, half), bf16)
    return pl.pallas_call(
        functools.partial(recurrence_kernel, sections, chunks, per),
        out_shape=(wide, wide, jax.ShapeDtypeStruct(sq, bf16), jax.ShapeDtypeStruct(sq, bf16)),
        in_specs=[vm] * 9,
        out_specs=(vm,) * 4,
        scratch_shapes=[
            pltpu.VMEM((planes,) + two, bf16),
            pltpu.VMEM((planes, some + 16, 2 * rank), bf16),
            pltpu.VMEM((some + 16, 2 * rank), bf16),
            pltpu.VMEM((planes, 2 * rank, 2 * rank), bf16),
            pltpu.VMEM((sections,) + two, f32),
            pltpu.VMEM((8, rank), f32),
            pltpu.VMEM((8, rank), f32),
            pltpu.VMEM((some, 4 * rank), f32),
            pltpu.VMEM(two, f32), pltpu.VMEM(two, f32), pltpu.VMEM(two, f32),
            pltpu.VMEM((2, some, rank), f32),
            pltpu.VMEM((rows, 2 * rank), bf16),
            pltpu.VMEM((rows, 2 * rank), bf16),
            pltpu.VMEM((2,) + sq, f32),
            strip, strip, strip, strip, strip, strip,
        ] + [dma((planes,))] * 6 + [dma((10,))] + [dma((chunks,))] * 8,
        compiler_params=pltpu.CompilerParams(
            collective_id=1, has_side_effects=True, vmem_limit_bytes=48 * 1024 * 1024),
    )(pyh, n0, nn, x0, g16, up, wd, upart, wpart)


def dp_place(x_n):
    d = lax.axis_index("dp")
    return d // (2 * x_n), lax.rem(d // 2, x_n), lax.rem(d, 2)


def remote(src, dst, send, recv, where):
    return pltpu.make_async_remote_copy(src_ref=src, dst_ref=dst, send_sem=send, recv_sem=recv,
                                        device_id=where, device_id_type=MESH)


def block_sum(b, yh_n, x_n, core_copy, part, rc, sums, rax, rby, ax_send, ax_recv, by_send, by_recv):
    yh, x, core = dp_place(x_n)
    cut = sums.shape[2] // 2
    y_ = b // x_n
    x_ = lax.rem(b, x_n)
    core_copy(b).wait_recv()
    sums[y_, x_] = (part[b, core].astype(f32) + rc[b].astype(f32)).astype(bf16)
    turn = lax.rem(x_ - x + x_n, x_n)

    @pl.when(turn != 0)
    def _():
        sem = (turn - 1) * yh_n + y_
        remote(sums.at[y_, x_, 0:cut], rax.at[turn - 1, y_], ax_send.at[sem], ax_recv.at[sem],
               {"dp": (yh * x_n + x_) * 2 + core}).start()

    @pl.when(y_ != yh)
    def _():
        remote(sums.at[y_, x_, cut:2 * cut], rby.at[x_], by_send.at[x_], by_recv.at[x_],
               {"dp": (y_ * x_n + x) * 2 + core}).start()


def scatter_sum(yh_n, x_n, sums, rax, rby, sa, ray, sb, rbx,
                ax_send, ax_recv, by_send, by_recv, s_sem, bx_send, bx_recv):
    yh, x, core = dp_place(x_n)
    rows = sums.shape[2]
    cut = rows // 2

    def place(y_, x_, c_):
        return {"dp": (y_ * x_n + x_) * 2 + c_}

    def xp(i):
        return lax.rem(x + i, x_n)

    other_y = place(1 - yh, x, core)

    def ax_copy(i, y_):
        sem = (i - 1) * yh_n + y_
        return remote(sums.at[y_, xp(i), 0:cut], rax.at[i - 1, y_], ax_send.at[sem], ax_recv.at[sem],
                      place(yh, xp(i), core))

    def by_copy(x_):
        return remote(sums.at[1 - yh, x_, cut:rows], rby.at[x_], by_send.at[x_], by_recv.at[x_], other_y)

    def bx_copy(i):
        return remote(sb.at[xp(i)], rbx.at[i - 1], bx_send.at[i - 1], bx_recv.at[i - 1],
                      place(yh, xp(i), core))

    ay_copy = remote(sa.at[1 - yh], ray, s_sem.at[0], s_sem.at[1], other_y)

    for i in range(x_n):
        x_ = xp(i)
        by_copy(x_).wait_recv()
        sb[x_] = (sums[yh, x_, cut:rows].astype(f32) + rby[x_].astype(f32)).astype(bf16)
        if i > 0:
            bx_copy(i).start()
    for y_ in range(yh_n):
        total = sums[y_, x, 0:cut].astype(f32)
        for i in range(1, x_n):
            ax_copy(i, y_).wait_recv()
            total = total + rax[i - 1, y_].astype(f32)
        sa[y_] = total.astype(bf16)
    ay_copy.start()
    total_b = sb[x].astype(f32)
    for i in range(1, x_n):
        bx_copy(i).wait_recv()
        total_b = total_b + rbx[i - 1].astype(f32)
    ay_copy.wait_recv()
    total_a = sa[yh].astype(f32) + ray[...].astype(f32)
    for i in range(1, x_n):
        for y_ in range(yh_n):
            ax_copy(i, y_).wait_send()
        bx_copy(i).wait_send()
    for x_ in range(x_n):
        by_copy(x_).wait_send()
    ay_copy.wait_send()
    return total_a, total_b


def gram_kernel(yh_n, x_n, sections, x0, g16, down, up, mine_u, base, pyh, n0, out, upart, wpart,
                allu, part, rc, sums, rax, rby, sa, ray, sb, rbx, gs, gp, two, mine3, theirs3,
                z_sem, f_send, f_recv, r_send, r_recv,
                c_send, c_recv, ax_send, ax_recv, by_send, by_recv, s_sem, bx_send, bx_recv,
                ga_send, ga_recv, gb_send, gb_recv, gc_send, gc_recv):
    yh, x, core = dp_place(x_n)
    s = lax.axis_index("section")
    z_n = sections // 2
    z = s // 2
    ylo = lax.rem(s, 2)
    rank = up.shape[0]
    rows = rank
    cut = rows // 2

    def place(y_, x_, c_):
        return {"dp": (y_ * x_n + x_) * 2 + c_}

    def xp(i):
        return lax.rem(x + i, x_n)

    def zp(i):
        return lax.rem(z + i, z_n)

    other_core = place(yh, x, 1 - core)
    other_y = place(1 - yh, x, core)
    partner = {"section": s + 1 - 2 * ylo}
    after = {"section": 2 * zp(1) + ylo}
    before = {"section": 2 * zp(z_n - 1) + ylo}

    barrier = pltpu.get_barrier_semaphore()
    peers = [other_core, other_y, partner, after, before]
    peers += [place(yh, xp(i), core) for i in range(1, x_n)]
    for where in peers:
        pl.semaphore_signal(barrier, inc=1, device_id=where, device_id_type=MESH)
    pl.semaphore_wait(barrier, len(peers))

    pair = remote(mine_u, allu.at[z, ylo], z_sem.at[0], z_sem.at[1], partner)

    def products(z_):
        for y_ in range(2):
            part[z_, y_] = dot_tn(allu[z_, y_], base[...]).astype(bf16)

    def core_copy(b):
        return remote(part.at[b, 1 - core], rc.at[b], c_send.at[b], c_recv.at[b], other_core)

    hops = z_n // 2

    def column(j):
        return ylo if j == 0 else 1 - ylo

    def ring_f(i, j):
        spot = allu.at[zp(z_n + 1 - i), column(j)]
        src = mine_u if (i == 1 and j == 0) else spot
        sem = 2 * (i - 1) + j
        return remote(src, spot, f_send.at[sem], f_recv.at[sem], after)

    def ring_r(i, j):
        spot = allu.at[zp(i - 1), column(j)]
        src = mine_u if (i == 1 and j == 0) else spot
        sem = 2 * (i - 1) + j
        return remote(src, spot, r_send.at[sem], r_recv.at[sem], before)

    used_f = [(i, j) for i in range(1, hops + 1) for j in range(2) if i < hops or j == 0]
    used_r = [(i, j) for i in range(1, hops + 1) for j in range(2) if i < hops or j == 1]

    pair.start()
    ring_f(1, 0).start()
    ring_r(1, 0).start()
    allu[z, ylo] = mine_u[...]
    pair.wait_recv()
    ring_f(1, 1).start()
    ring_r(1, 1).start()

    half = x0.shape[1] // 2
    quarter = half // 2
    far = pl.ds(pl.multiple_of((1 - ylo) * half + core * quarter, 128), quarter)
    near = pl.ds(pl.multiple_of(core * quarter, 128), quarter)
    swap_u = remote(up.at[:, far], upart.at[:, near], z_sem.at[6], z_sem.at[7], partner)
    swap_w = remote(down.at[far, :], wpart.at[near, :], z_sem.at[8], z_sem.at[9], partner)
    share_u = remote(upart.at[:, near], upart.at[:, near], z_sem.at[10], z_sem.at[11], other_core)
    share_w = remote(wpart.at[near, :], wpart.at[near, :], z_sem.at[12], z_sem.at[13], other_core)
    swap_u.start()
    swap_w.start()

    u = up[...]
    w = down[...]
    values = x0[...]
    token_half = x0.shape[0] // 2
    keep = pl.ds(ylo * token_half, token_half)
    give = pl.ds((1 - ylo) * token_half, token_half)
    mine3[0] = dot_nn(values, w)
    mine3[1] = dot_nt(values, u)
    mine3[2] = dot_nt(g16[...], u)
    swap3 = remote(mine3.at[:, give], theirs3, z_sem.at[2], z_sem.at[3], partner)
    swap3.start()
    wide = x0[keep, :].astype(f32)
    n0[...] = jnp.broadcast_to(jnp.sum(wide * wide, axis=1, keepdims=True), n0.shape)

    def collect(b):
        block_sum(b, yh_n, x_n, core_copy, part, rc, sums, rax, rby,
                  ax_send, ax_recv, by_send, by_recv)

    products(z)
    core_copy(z).start()
    for i in range(1, hops + 1):
        for j in range(2):
            if (i, j) in used_f:
                ring_f(i, j).wait_recv()
                if (i + 1, j) in used_f:
                    ring_f(i + 1, j).start()
            if (i, j) in used_r:
                ring_r(i, j).wait_recv()
                if (i + 1, j) in used_r:
                    ring_r(i + 1, j).start()
        products(zp(z_n - i))
        core_copy(zp(z_n - i)).start()
        if i == 1:
            collect(z)
        else:
            collect(zp(i - 1))
        if i < hops:
            products(zp(i))
            core_copy(zp(i)).start()
        collect(zp(z_n - i))

    swap_u.wait_recv()
    share_u.start()
    swap_w.wait_recv()
    share_w.start()
    total_a, total_b = scatter_sum(yh_n, x_n, sums, rax, rby, sa, ray, sb, rbx,
                                   ax_send, ax_recv, by_send, by_recv, s_sem, bx_send, bx_recv)
    gs[0:cut] = total_a.astype(bf16)
    gs[cut:rows] = total_b.astype(bf16)
    swap = remote(gs, gp, z_sem.at[4], z_sem.at[5], partner)
    swap.start()

    def lanes(base, which):
        return pl.ds(pl.multiple_of(base + which * rank, 128), rank)

    swap3.wait_recv()
    pyh[:, :, lanes(0, ylo)] = mine3[:, keep]
    pyh[:, :, lanes(0, 1 - ylo)] = theirs3[...]
    two[:, lanes(0, ylo)] = gs[:, 0:rank]
    two[:, lanes(2 * rank, ylo)] = gs[:, rank:2 * rank]
    swap.wait_recv()
    two[:, lanes(0, 1 - ylo)] = gp[:, 0:rank]
    two[:, lanes(2 * rank, 1 - ylo)] = gp[:, rank:2 * rank]
    out[yh, x, core] = two[...]

    low = pl.ds(0, cut)
    high = pl.ds(cut, cut)

    def spread(src, spot, sems, i, where):
        return remote(src, spot, sems[0].at[i], sems[1].at[i], where)

    ga = (ga_send, ga_recv)
    gb = (gb_send, gb_recv)
    a_y = spread(two.at[low], out.at[yh, x, core, low], ga, 0, other_y)

    def a_x(i):
        spot = out.at[:, x, core, low]
        return spread(spot, spot, ga, i, place(yh, xp(i), core))

    def b_x(i):
        return spread(two.at[high], out.at[yh, x, core, high], gb, i - 1, place(yh, xp(i), core))

    def b_y(i):
        spot = out.at[yh, xp(i), core, high]
        return spread(spot, spot, gb, x_n - 1 + i, other_y)

    def all_c(i):
        spot = out.at[:, xp(i), core]
        return remote(spot, spot, gc_send.at[i], gc_recv.at[i], other_core)

    a_y.start()
    for i in range(1, x_n):
        b_x(i).start()
    b_y(0).start()
    a_y.wait_recv()
    for i in range(1, x_n):
        a_x(i).start()
    for i in range(1, x_n):
        b_x(x_n - i).wait_recv()
        b_y(i).start()
    b_y(0).wait_recv()
    all_c(0).start()
    for i in range(1, x_n):
        a_x(x_n - i).wait_recv()
        b_y(i).wait_recv()
        all_c(i).start()
    for i in range(x_n):
        all_c(i).wait()
        b_y(i).wait_send()
    for i in range(1, x_n):
        a_x(i).wait_send()
        b_x(i).wait_send()
    a_y.wait_send()
    pair.wait_send()
    swap.wait_send()
    swap3.wait_send()
    swap_u.wait_send()
    swap_w.wait_send()
    share_u.wait()
    share_w.wait()
    for i, j in used_f:
        ring_f(i, j).wait_send()
    for i, j in used_r:
        ring_r(i, j).wait_send()

    def settle(b, carry):
        core_copy(b).wait_send()
        return carry

    lax.fori_loop(0, yh_n * x_n, settle, 0)


def grams_of(sections, shards, x0, g16, down, up, mine_u, base):
    x_n = 4
    yh_n = shards // (2 * x_n)
    rows, width = x0.shape
    rank = up.shape[0]
    height = mine_u.shape[0]
    cut = rank // 2
    vm = pl.BlockSpec(memory_space=pltpu.VMEM)
    dma = pltpu.SemaphoreType.DMA

    def buf(*lead):
        return pltpu.VMEM(lead + (2 * rank,), bf16)

    return pl.pallas_call(
        functools.partial(gram_kernel, yh_n, x_n, sections),
        out_shape=(
            jax.ShapeDtypeStruct((3, rows // 2, 2 * rank), f32),
            jax.ShapeDtypeStruct((rows // 2, rank), f32),
            jax.ShapeDtypeStruct((yh_n, x_n, 2, rank, 4 * rank), bf16),
            jax.ShapeDtypeStruct((rank, width // 2), bf16),
            jax.ShapeDtypeStruct((width // 2, rank), bf16),
        ),
        in_specs=[vm] * 6,
        out_specs=(vm,) * 5,
        scratch_shapes=[
            pltpu.VMEM((sections // 2, 2, height, rank), bf16),
            buf(yh_n * x_n, 2, rank), buf(yh_n * x_n, rank), buf(yh_n, x_n, rank),
            buf(x_n - 1, yh_n, cut), buf(x_n, cut), buf(yh_n, cut), buf(cut),
            buf(x_n, cut), buf(x_n - 1, cut), buf(rank), buf(rank),
            pltpu.VMEM((rank, 4 * rank), bf16),
            pltpu.VMEM((3, rows, rank), f32), pltpu.VMEM((3, rows // 2, rank), f32),
            dma((14,)), dma((sections // 2,)), dma((sections // 2,)),
            dma((sections // 2,)), dma((sections // 2,)),
            dma((yh_n * x_n,)), dma((yh_n * x_n,)),
            dma((yh_n * (x_n - 1),)), dma((yh_n * (x_n - 1),)), dma((x_n,)), dma((x_n,)), dma((4,)),
            dma((x_n - 1,)), dma((x_n - 1,)),
            dma((x_n,)), dma((x_n,)), dma((2 * x_n,)), dma((2 * x_n,)), dma((x_n,)), dma((x_n,)),
        ],
        compiler_params=pltpu.CompilerParams(
            collective_id=3, has_side_effects=True, vmem_limit_bytes=48 * 1024 * 1024),
    )(x0, g16, down, up, mine_u, base)


def reduce_kernel(yh_n, x_n, sections, x1, g1, u_s, q_s, up, base, own, nxt,
                  part, rc, sums, rax, rby, sa, ray, sb, rbx, gs, nw,
                  c_send, c_recv, ax_send, ax_recv, by_send, by_recv, s_sem, bx_send, bx_recv,
                  own_send, own_recv, oc_send, oc_recv, nx_send, nx_recv, ny_send, ny_recv,
                  nc_send, nc_recv):
    d = lax.axis_index("dp")
    s = lax.axis_index("section")
    yh = d // (2 * x_n)
    x = lax.rem(d // 2, x_n)
    core = lax.rem(d, 2)
    rows = base.shape[0]
    cut = rows // 2

    def place(y_, x_, c_):
        return {"dp": (y_ * x_n + x_) * 2 + c_}

    def xp(i):
        return lax.rem(x + i, x_n)

    other_core = place(yh, x, 1 - core)
    other_y = place(1 - yh, x, core)
    up_section = lax.rem(s + 1, sections)
    down_section = lax.rem(s + sections - 1, sections)

    def copy(src, dst, send, recv, where):
        return pltpu.make_async_remote_copy(src_ref=src, dst_ref=dst, send_sem=send, recv_sem=recv,
                                            device_id=where, device_id_type=MESH)

    barrier = pltpu.get_barrier_semaphore()
    peers = [other_core, other_y, {"section": up_section}, {"section": down_section}]
    peers += [place(yh, xp(i), core) for i in range(1, x_n)]
    for where in peers:
        pl.semaphore_signal(barrier, inc=1, device_id=where, device_id_type=MESH)
    pl.semaphore_wait(barrier, len(peers))

    def core_copy(b):
        return copy(part.at[b, 1 - core], rc.at[b], c_send.at[b], c_recv.at[b], other_core)

    def terms(b, carry):
        cols = pl.ds(pl.multiple_of(b * 2 * rows, 128), 2 * rows)
        u = u_s[...]
        before = (x1[:, cols].astype(f32) - dot_nn(u, up[:, cols])).astype(bf16)
        g_down = dot_tn(before, q_s[...]).astype(bf16)
        g_up = dot_tn(g1[:, cols], u).astype(bf16)
        rank = u.shape[1]
        for half in range(2):
            part[b, half, :, 0:rank] = g_down[half * rows:(half + 1) * rows]
            part[b, half, :, rank:2 * rank] = g_up[half * rows:(half + 1) * rows]
        core_copy(b).start()

        @pl.when(b > 0)
        def _():
            collect(b - 1)
        return carry

    def collect(b):
        block_sum(b, yh_n, x_n, core_copy, part, rc, sums, rax, rby,
                  ax_send, ax_recv, by_send, by_recv)

    blocks = yh_n * x_n
    lax.fori_loop(0, blocks, terms, 0)
    collect(blocks - 1)

    total_a, total_b = scatter_sum(yh_n, x_n, sums, rax, rby, sa, ray, sb, rbx,
                                   ax_send, ax_recv, by_send, by_recv, s_sem, bx_send, bx_recv)
    gs[0:cut] = total_a.astype(bf16)
    gs[cut:rows] = total_b.astype(bf16)
    nw[...] = (base[...].astype(f32) - learn_rate * gs[...].astype(f32)).astype(bf16)

    has_next = s < sections - 1
    next_copy = copy(nw, nxt.at[yh, x, core], s_sem.at[4], s_sem.at[5], {"section": down_section})
    own_y = copy(gs, own.at[yh, x, core], s_sem.at[6], s_sem.at[7], other_y)
    own_y.start()

    @pl.when(s > 0)
    def _():
        next_copy.start()

    own[yh, x, core] = gs[...]

    def own_x(i):
        return copy(own.at[:, x, core], own.at[:, x, core], own_send.at[i - 1], own_recv.at[i - 1],
                    place(yh, xp(i), core))

    def own_c(i):
        spot = own.at[:, xp(i), core]
        return copy(spot, spot, oc_send.at[i], oc_recv.at[i], other_core)

    def nxt_x(i):
        spot = nxt.at[yh, x, core]
        return copy(spot, spot, nx_send.at[i - 1], nx_recv.at[i - 1], place(yh, xp(i), core))

    def nxt_y(i):
        spot = nxt.at[yh, xp(i), core]
        return copy(spot, spot, ny_send.at[i], ny_recv.at[i], other_y)

    def nxt_c(i):
        spot = nxt.at[:, xp(i), core]
        return copy(spot, spot, nc_send.at[i], nc_recv.at[i], other_core)

    @pl.when(has_next)
    def _():
        next_copy.wait_recv()
        for i in range(1, x_n):
            nxt_x(i).start()
        nxt_y(0).start()

    own_y.wait_recv()

    @pl.when(has_next)
    def _():
        for i in range(1, x_n):
            nxt_x(i).wait_send()

    for i in range(1, x_n):
        own_x(i).start()
    own_c(0).start()

    @pl.when(has_next)
    def _():
        for i in range(1, x_n):
            nxt_x(x_n - i).wait_recv()
            nxt_y(i).start()

    for i in range(1, x_n):
        own_x(x_n - i).wait_recv()
        own_c(i).start()

    @pl.when(has_next)
    def _():
        for i in range(x_n):
            nxt_y(i).wait_recv()
            nxt_c(i).start()
        for i in range(x_n):
            nxt_c(i).wait()
            nxt_y(i).wait_send()

    for i in range(x_n):
        own_c(i).wait()
    for i in range(1, x_n):
        own_x(i).wait_send()
    own_y.wait_send()

    @pl.when(s > 0)
    def _():
        next_copy.wait_send()

    def settle(b, carry):
        core_copy(b).wait_send()
        return carry

    lax.fori_loop(0, blocks, settle, 0)


def reduce_gather(sections, shards, x1, g1, u_s, q_s, up, base):
    x_n = 4
    yh_n = shards // (2 * x_n)
    rows, cols = base.shape
    cut = rows // 2
    vm = pl.BlockSpec(memory_space=pltpu.VMEM)
    dma = pltpu.SemaphoreType.DMA
    full = jax.ShapeDtypeStruct((yh_n, x_n, 2, rows, cols), bf16)

    def buf(*lead):
        return pltpu.VMEM(lead + (cols,), bf16)

    return pl.pallas_call(
        functools.partial(reduce_kernel, yh_n, x_n, sections),
        out_shape=(full, full),
        in_specs=[vm] * 6,
        out_specs=(vm, vm),
        scratch_shapes=[
            buf(yh_n * x_n, 2, rows), buf(yh_n * x_n, rows), buf(yh_n, x_n, rows),
            buf(x_n - 1, yh_n, cut), buf(x_n, cut), buf(yh_n, cut), buf(cut),
            buf(x_n, cut), buf(x_n - 1, cut), buf(rows), buf(rows),
            dma((yh_n * x_n,)), dma((yh_n * x_n,)),
            dma((yh_n * (x_n - 1),)), dma((yh_n * (x_n - 1),)), dma((x_n,)), dma((x_n,)), dma((8,)),
            dma((x_n - 1,)), dma((x_n - 1,)), dma((x_n - 1,)), dma((x_n - 1,)),
            dma((x_n,)), dma((x_n,)), dma((x_n - 1,)), dma((x_n - 1,)), dma((x_n,)), dma((x_n,)),
            dma((x_n,)), dma((x_n,)),
        ],
        compiler_params=pltpu.CompilerParams(
            collective_id=2, has_side_effects=True, vmem_limit_bytes=52 * 1024 * 1024),
    )(x1, g1, u_s, q_s, up, base)


def finish_kernel(sections, own, nxt, x1, grad_down, grad_up, advance):
    last = lax.axis_index("section") == sections - 1
    rows, width = x1.shape
    rank = grad_down.shape[1]
    step = 896
    count = width // step

    def first(b, carry):
        pre, norm = carry
        here = pl.ds(pl.multiple_of(b * step, 128), step)
        block = own[here, :]
        grad_down[here, :] = block[:, 0:rank]
        grad_up[:, here] = block[:, rank:2 * rank].astype(f32).T.astype(bf16)
        x = x1[:, here]
        values = x.astype(f32)
        pre = pre + dot_nn(x, nxt[here, 0:rank])
        return pre, norm + jnp.sum(values * values, axis=1, keepdims=True)

    pre, norm = lax.fori_loop(
        0, count, first, (jnp.zeros((rows, rank), f32), jnp.zeros((rows, 1), f32)))
    value, unused = gelu_pair(pre * lax.rsqrt(norm * (1.0 / width) + eps))
    value = value.astype(bf16)

    def second(b, carry):
        here = pl.ds(pl.multiple_of(b * step, 128), step)
        bump = dot_nt(value, nxt[here, rank:2 * rank])
        advance[:, here] = (x1[:, here].astype(f32) + jnp.where(last, 0.0, bump)).astype(bf16)
        return carry

    lax.fori_loop(0, count, second, 0)


def finish(sections, own, nxt, x1):
    rows, width = x1.shape
    rank = own.shape[1] // 2
    vm = pl.BlockSpec(memory_space=pltpu.VMEM)
    return pl.pallas_call(
        functools.partial(finish_kernel, sections),
        out_shape=(
            jax.ShapeDtypeStruct((width, rank), bf16),
            jax.ShapeDtypeStruct((rank, width), bf16),
            jax.ShapeDtypeStruct((rows, width), bf16),
        ),
        in_specs=[vm] * 3,
        out_specs=(vm,) * 3,
        compiler_params=pltpu.CompilerParams(vmem_limit_bytes=48 * 1024 * 1024),
    )(own, nxt, x1)


def per_device(inputs, cotangent, w_down, w_up):
    down = w_down[0]
    upward = w_up[0]
    micro, batch_rows, width = inputs.shape
    rank = down.shape[1]
    rows = micro * batch_rows
    sections = lax.axis_size("section")
    shards = lax.axis_size("dp")
    part = width // shards
    d = lax.axis_index("dp")
    x0 = inputs.reshape(rows, width)
    g16 = cotangent.reshape(rows, width)
    up_t = upward.T

    mine_u = lax.dynamic_slice_in_dim(up_t, d * part, part, 0)
    mine_w = lax.dynamic_slice_in_dim(down, d * part, part, 0)
    base = jnp.concatenate([mine_w, mine_u], axis=1)
    pyh, n0, grams, upart, wpart = grams_of(sections, shards, x0, g16, down, upward, mine_u, base)
    grams = grams.reshape(sections // 2, 2 * rank, 4 * rank)
    x1, g1, u_s, q_s = recurrence(sections, pyh, n0, grams, x0, g16, upward, down, upart, wpart)
    own, nxt = reduce_gather(sections, shards, x1, g1, u_s, q_s, upward, base)
    wide = (width, 2 * rank)
    grad_down, grad_up, advance = finish(sections, own.reshape(wide), nxt.reshape(wide), x1)
    return (grad_down[None], grad_up[None], advance.reshape(1, micro, batch_rows, width))


def solution(mesh):
    in_specs = (
        P(None, "dp", None),
        P(None, "dp", None),
        P("section", None, None),
        P("section", None, None),
    )
    out_specs = (P("section", None, None), P("section", None, None), P("section", None, "dp", None))
    return jax.shard_map(
        per_device, mesh=mesh, in_specs=in_specs, out_specs=out_specs, check_vma=False
    )
```

```python
import functools

import jax
import jax.numpy as jnp
from jax import lax
from jax.experimental import pallas as pl
from jax.experimental.pallas import tpu as pltpu
from jax.sharding import PartitionSpec as P

MESH = pl.DeviceIdType.MESH
eps = 1e-05
learn_rate = 0.05
f32 = jnp.float32
bf16 = jnp.bfloat16


def dot_nn(a, b):
    return jnp.dot(a, b, preferred_element_type=f32)


def dot_tn(a, b):
    return lax.dot_general(a, b, (((0,), (0,)), ((), ())), preferred_element_type=f32)


def dot_nt(a, b):
    return lax.dot_general(a, b, (((1,), (1,)), ((), ())), preferred_element_type=f32)


def gelu_pair(a):
    c = 0.7978845608028654
    inner = c * (a + 0.044715 * a * a * a)
    th = jnp.tanh(inner)
    value = 0.5 * a * (1.0 + th)
    slope = 0.5 * (1.0 + th) + 0.5 * a * (1.0 - th * th) * c * (1.0 + 3 * 0.044715 * a * a)
    return value, slope


def recurrence_kernel(sections, chunks, per, yh_n, x_n,
                      pyh, n0, nn, x0, g16, up, wd, upart, wpart, mine_u,
                      xout, own_w, own_u, nxt_u, bump_u,
                      ul, ql, qp, mb, ys, nl, nsend, acc, hacc, slope, act, rinv, uf, qs, cpair,
                      xin, xkeep, xgive, gin, gkeep, ggive, xpass,
                      gout, us, qv, xb, nacc, part, rc, sums, rax, rby, sa, ray, sb, rbx,
                      gw, gu, nw, ub,
                      u_send, u_recv, q_send, q_recv, m_send, m_recv, e_sem,
                      c_send, c_recv, g_send, g_recv,
                      b_send, b_recv, h_send, h_recv, p_send, p_recv,
                      k_send, k_recv, ax_send, ax_recv, by_send, by_recv, s_sem, bx_send, bx_recv,
                      wx_sem, wy_sem, wc_sem, vx_sem, vc_sem, nx_sem, ny_sem, nc_sem):
    s = lax.axis_index("section")
    yh, x, core = dp_place(x_n)
    planes = sections // 2
    rows, width = x0.shape
    some = rows // 2
    rank = up.shape[0]
    half = width // 2
    piece = half // chunks
    trips = chunks // per
    z = s // 2
    ylo = lax.rem(s, 2)
    first = ylo == 0
    partner = {"section": s + 1 - 2 * ylo}
    head = slice(0, rank)
    tail = slice(rank, 2 * rank)
    mine = pl.ds(ylo * some, some)
    theirs = pl.ds((1 - ylo) * some, some)

    def plane(i):
        return {"section": 2 * i + ylo}

    def peer(offset):
        return lax.rem(z + offset, planes)

    barrier = pltpu.get_barrier_semaphore()
    for o in range(1, planes):
        pl.semaphore_signal(barrier, inc=1, device_id=plane(peer(o)), device_id_type=MESH)

    def place(y_, x_, c_):
        return {"dp": (y_ * x_n + x_) * 2 + c_}

    def xp(i):
        return lax.rem(x + i, x_n)

    other_core = place(yh, x, 1 - core)
    other_y = place(1 - yh, x, core)
    beyond = {"section": lax.rem(s + sections - 1 + 2 * ylo, sections)}
    others = [partner, beyond, other_core, other_y] + [place(yh, xp(i), core) for i in range(1, x_n)]
    for where in others:
        pl.semaphore_signal(barrier, inc=1, device_id=where, device_id_type=MESH)
    pl.semaphore_wait(barrier, planes - 1 + len(others))

    eye = (lax.broadcasted_iota(jnp.int32, (some, rank), 0)
           == lax.broadcasted_iota(jnp.int32, (some, rank), 1)).astype(f32)

    def to_row(col):
        return jnp.sum(eye * col, axis=0, keepdims=True)

    def to_col(row):
        return jnp.sum(eye * row, axis=1, keepdims=True)

    def columns(base, c):
        return pl.ds(pl.multiple_of(base + c * piece, 128), piece)

    def x_copy(c):
        return remote(xkeep.at[:, columns(0, c)], xin.at[:, columns(0, c)],
                      c_send.at[c], c_recv.at[c], plane(peer(1)))

    def b_copy(c):
        return remote(gkeep.at[:, columns(0, c)], gin.at[:, columns(0, c)],
                      b_send.at[c], b_recv.at[c], plane(peer(planes - 1)))

    def give_copy(c):
        return remote(xgive.at[:, columns(0, c)], xout.at[:, columns(ylo * half, c)],
                      g_send.at[c], g_recv.at[c], partner)

    def give_arrived(c):
        return remote(xgive.at[:, columns(0, c)], xout.at[:, columns((1 - ylo) * half, c)],
                      g_send.at[c], g_recv.at[c], partner)

    def pass_copy(c):
        return remote(xpass.at[:, columns(0, c)], xb.at[:, columns(ylo * half, c)],
                      p_send.at[c], p_recv.at[c], partner)

    def pass_arrived(c):
        return remote(xpass.at[:, columns(0, c)], xb.at[:, columns((1 - ylo) * half, c)],
                      p_send.at[c], p_recv.at[c], partner)

    def h_copy(c):
        return remote(ggive.at[:, columns(0, c)], gout.at[:, columns(ylo * half, c)],
                      h_send.at[c], h_recv.at[c], partner)

    def h_arrived(c):
        return remote(ggive.at[:, columns(0, c)], gout.at[:, columns((1 - ylo) * half, c)],
                      h_send.at[c], h_recv.at[c], partner)

    def near_copy(k, part, sem):
        spot = ul.at[k, :, part]
        return remote(spot, spot, e_sem.at[2 * sem], e_sem.at[2 * sem + 1], plane(peer(1)))

    def n_copy():
        return remote(nsend, nl, e_sem.at[4], e_sem.at[5], plane(peer(1)))

    def uf_copy():
        return remote(ul.at[z], uf.at[mine], e_sem.at[6], e_sem.at[7], partner)

    def uf_arrived():
        return remote(ul.at[z], uf.at[theirs], e_sem.at[6], e_sem.at[7], partner)

    def qp_copy():
        return remote(ql.at[z], qp, e_sem.at[8], e_sem.at[9], partner)

    def u_copy(o):
        return remote(ul.at[z], ul.at[z], u_send.at[o], u_recv.at[z], plane(peer(o)))

    def u_arrived(k):
        return remote(ul.at[k], ul.at[k], u_send.at[0], u_recv.at[k], plane(peer(1)))

    def q_copy(j):
        return remote(ql.at[z], ql.at[z], q_send.at[j], q_recv.at[z], plane(j))

    def q_arrived(k):
        return remote(ql.at[k], ql.at[k], q_send.at[0], q_recv.at[k], plane(peer(1)))

    def m_copy(j):
        return remote(nn.at[j, :, 0:2 * rank], mb.at[z], m_send.at[j], m_recv.at[z], plane(j))

    def m_arrived(k):
        return remote(mb.at[k], mb.at[k], m_send.at[0], m_recv.at[k], plane(peer(1)))

    acc[:, 0:2 * rank] = pyh[0]
    acc[:, 2 * rank:4 * rank] = pyh[1]
    hacc[...] = pyh[2]

    def start_m(j, carry):
        m_copy(j).start()
        return carry

    lax.fori_loop(0, z, start_m, 0)

    def chain(c):
        @pl.when(z > 0)
        def _():
            x_copy(c).wait_recv()

        here = columns(ylo * half, c)
        there = columns(0, c)
        start = jnp.where(z > 0, xin[:, there], x0[:, here]).astype(f32)
        ours = up[:, here]
        other = upart[:, there]
        x_a = (start + dot_nn(uf[:, head], jnp.where(first, ours, other))).astype(bf16)
        x_b = (x_a.astype(f32) + dot_nn(uf[:, tail], jnp.where(first, other, ours))).astype(bf16)
        xkeep[:, there] = x_b

        @pl.when(z < planes - 1)
        def _():
            x_copy(c).start()

        xgive[:, there] = jnp.where(first, x_b, x_a)
        give_copy(c).start()
        xout[:, here] = jnp.where(first, x_a, x_b)
        start = start.astype(bf16)
        xpass[:, there] = jnp.where(first, x_a, start)
        pass_copy(c).start()
        xb[:, here] = jnp.where(first, start, x_a)

    def chain_back(c):
        @pl.when(z < planes - 1)
        def _():
            b_copy(c).wait_recv()

        here = columns(ylo * half, c)
        there = columns(0, c)
        ours = wd[here, :]
        other = wpart[there, :]
        g_b = jnp.where(z < planes - 1, gin[:, there], g16[:, here])
        x_a = jnp.where(z > 0, xin[:, there], x0[:, here]).astype(f32)
        x_b = jnp.where(first, xout[:, here], xgive[:, there]).astype(f32)
        g_a = (g_b.astype(f32) + dot_nt(qs[:, tail], jnp.where(first, other, ours))
               - cpair[1, :, 0:1] * x_b).astype(bf16)
        g_0 = (g_a.astype(f32) + dot_nt(qs[:, head], jnp.where(first, ours, other))
               - cpair[0, :, 0:1] * x_a).astype(bf16)

        @pl.when(z > 0)
        def _():
            gkeep[:, there] = g_0
            b_copy(c).start()

        ggive[:, there] = jnp.where(first, g_b, g_a)
        h_copy(c).start()
        gout[:, here] = jnp.where(first, g_a, g_b)

    def forward_own():
        @pl.when(z > 0)
        def _():
            n_copy().wait_recv()

        norm_a = jnp.where(z > 0, to_col(nl[0:1, :]), n0[:, 0:1])
        scale_a = lax.rsqrt(norm_a * (1.0 / width) + eps)
        pre_a = acc[:, 0:rank] * scale_a
        value_a, slope_a = gelu_pair(pre_a)
        u_a = value_a.astype(bf16)
        ul[z, :, head] = u_a

        @pl.when(z < planes - 1)
        def _():
            near_copy(z, head, 0).start()

        step = dot_nn(u_a, nn[z, 0:rank, rank:4 * rank])
        y_a = acc[:, 2 * rank:3 * rank]
        norm_b = norm_a + jnp.sum(u_a.astype(f32) * (2.0 * y_a + step[:, rank:2 * rank]),
                                  axis=1, keepdims=True)
        scale_b = lax.rsqrt(norm_b * (1.0 / width) + eps)
        pre_b = (acc[:, rank:2 * rank] + step[:, 0:rank]) * scale_b
        value_b, slope_b = gelu_pair(pre_b)
        u_b = value_b.astype(bf16)
        ul[z, :, tail] = u_b

        @pl.when(z < planes - 1)
        def _():
            near_copy(z, tail, 1).start()

        y_b = acc[:, 2 * rank:4 * rank] + step[:, rank:3 * rank]
        more = dot_nn(u_b, nn[z, rank:2 * rank, 2 * rank:4 * rank])
        norm_c = norm_b + jnp.sum(
            u_b.astype(f32) * (2.0 * y_b[:, rank:2 * rank] + more[:, rank:2 * rank]),
            axis=1, keepdims=True)

        @pl.when(z < planes - 1)
        def _():
            nsend[...] = jnp.broadcast_to(to_row(norm_c), nsend.shape)
            n_copy().start()

        uf_copy().start()
        for o in range(2, planes):
            u_copy(o).start()

        @pl.when(z == planes - 1)
        def _():
            u_copy(1).start()

        uf[mine, :] = ul[z]
        ys[2 * z + 1] = y_b
        acc[:, 2 * rank:4 * rank] = y_b + more
        act[:, head] = pre_a
        act[:, tail] = pre_b
        slope[:, head] = slope_a
        slope[:, tail] = slope_b
        rinv[0] = jnp.broadcast_to(scale_a, (some, rank))
        rinv[1] = jnp.broadcast_to(scale_b, (some, rank))

    def c_of(stat):
        line = stat[0:1, :].astype(f32) + stat[1:2, :].astype(f32)
        return to_col(line[:, head]), to_col(line[:, tail])

    def backward_own():
        scale_b = rinv[1]
        q_b = hacc[:, tail] * slope[:, tail]
        low_b = (q_b * scale_b).astype(bf16)
        mix_b = jnp.sum(q_b * act[:, tail], axis=1, keepdims=True) * (1.0 / width)
        c_b = mix_b * scale_b[:, 0:1] * scale_b[:, 0:1]
        h_a = hacc[:, head] + dot_nt(low_b, nn[z, 0:rank, rank:2 * rank]) - c_b * ys[2 * z + 1, :, head]
        scale_a = rinv[0]
        q_a = h_a * slope[:, head]
        mix_a = jnp.sum(q_a * act[:, head], axis=1, keepdims=True) * (1.0 / width)
        c_a = mix_a * scale_a[:, 0:1] * scale_a[:, 0:1]
        ql[z, 0:some, head] = (q_a * scale_a).astype(bf16)
        ql[z, 0:some, tail] = low_b
        spot = lax.broadcasted_iota(jnp.int32, (16, rank), 0)
        for part, col in ((head, c_a), (tail, c_b)):
            line = to_row(col)
            high = line.astype(bf16).astype(f32)
            ql[z, some:some + 16, part] = jnp.where(
                spot == 0, high, jnp.where(spot == 1, line - high, 0.0)).astype(bf16)

        def send(i, carry):
            q_copy(z - 1 - i).start()
            return carry

        lax.fori_loop(0, z, send, 0)
        qp_copy().start()

    shard = mine_u.shape[0]
    nacc[...] = jnp.zeros_like(nacc)

    def core_copy(b):
        return remote(part.at[b, 1 - core], rc.at[b], k_send.at[b], k_recv.at[b], other_core)

    def collect(b):
        block_sum(b, yh_n, x_n, core_copy, part, rc, sums, rax, rby,
                  ax_send, ax_recv, by_send, by_recv)

    def terms(b):
        cols = pl.ds(pl.multiple_of(b * 2 * shard, 128), 2 * shard)
        u = us[...]
        before = xb[:, cols]
        wide = before.astype(f32)
        nacc[...] += jnp.broadcast_to(jnp.sum(wide * wide, axis=1, keepdims=True), nacc.shape)
        g_down = dot_tn(before, qv[...]).astype(bf16)
        g_up = dot_tn(gout[:, cols], u).astype(bf16)
        for i in range(2):
            part[b, i, :, head] = g_down[i * shard:(i + 1) * shard]
            part[b, i, :, tail] = g_up[i * shard:(i + 1) * shard]
        core_copy(b).start()

    def tick(t, carry):
        k = t - 1
        sent = (k >= 0) & (k < planes)
        near = sent & (k == z - 1)

        @pl.when(sent & (k != z) & (k != z - 1))
        def _():
            u_arrived(k).wait_recv()

        @pl.when(near)
        def _():
            near_copy(k, head, 0).wait_recv()
            acc[...] += dot_nn(ul[k, :, head], nn[k, 0:rank, :])
            near_copy(k, tail, 1).wait_recv()
            acc[...] += dot_nn(ul[k, :, tail], nn[k, rank:2 * rank, :])

        @pl.when(sent & (k < z - 1))
        def _():
            acc[...] += dot_nn(ul[k], nn[k])

        @pl.when(t == z)
        def _():
            forward_own()

        @pl.when(sent & (k > z))
        def _():
            before = acc[:, 2 * rank:4 * rank]
            ys[2 * k] = before
            between = before + dot_nn(ul[k, :, head], nn[k, 0:rank, 2 * rank:4 * rank])
            ys[2 * k + 1] = between
            acc[:, 2 * rank:4 * rank] = between + dot_nn(
                ul[k, :, tail], nn[k, rank:2 * rank, 2 * rank:4 * rank])

        r = 2 * planes - t

        @pl.when((r < planes) & (r > z))
        def _():
            m_arrived(r).wait_recv()
            q_arrived(r).wait_recv()
            c_a, c_b = c_of(ql[r, some:some + 16, :])
            hacc[...] += (dot_nt(ql[r, 0:some, :], mb[r]) - c_a * ys[2 * r] - c_b * ys[2 * r + 1])

        @pl.when(t == 2 * planes - 1 - z)
        def _():
            backward_own()

        p = t - (z + 1)

        @pl.when((p >= 0) & (p < trips))
        def _():
            @pl.when(p == 0)
            def _():
                uf_arrived().wait_recv()
            for j in range(per):
                chain(per * p + j)

        b = t - (2 * planes - z)

        @pl.when((b >= 0) & (b < trips))
        def _():
            @pl.when(b == 0)
            def _():
                qp_copy().wait_recv()
                qs[mine, :] = ql[z, 0:some, :]
                qs[theirs, :] = qp[0:some, :]
                for where, stat in ((mine, ql[z, some:some + 16, :]), (theirs, qp[some:some + 16, :])):
                    c_a, c_b = c_of(stat)
                    cpair[0, where, :] = jnp.broadcast_to(c_a, (some, rank))
                    cpair[1, where, :] = jnp.broadcast_to(c_b, (some, rank))
                us[...] = jnp.where(first, uf[:, head], uf[:, tail])
                qv[...] = jnp.where(first, qs[:, head], qs[:, tail])
            for j in range(per):
                chain_back(per * b + j)
            terms(ylo * trips + b)

        @pl.when((b >= 1) & (b <= trips))
        def _():
            collect(ylo * trips + b - 1)

            def landed(j, carry):
                c = per * (b - 1) + j
                give_arrived(c).wait_recv()
                pass_arrived(c).wait_recv()
                h_arrived(c).wait_recv()
                return carry

            lax.fori_loop(0, per, landed, 0)
            terms((1 - ylo) * trips + b - 1)

        @pl.when((b >= 2) & (b <= trips))
        def _():
            collect((1 - ylo) * trips + b - 2)

        return carry

    lax.fori_loop(0, 2 * planes + trips + 1, tick, 0)
    collect((1 - ylo) * trips + trips - 1)

    total_a, total_b = scatter_sum(yh_n, x_n, sums, rax, rby, sa, ray, sb, rbx,
                                   ax_send, ax_recv, by_send, by_recv, s_sem, bx_send, bx_recv)
    cut = shard // 2
    gw[0:cut] = total_a[:, head].astype(bf16)
    gw[cut:shard] = total_b[:, head].astype(bf16)
    gu[0:cut] = total_a[:, tail].astype(bf16)
    gu[cut:shard] = total_b[:, tail].astype(bf16)
    has_next = s < sections - 1
    down_section = {"section": lax.rem(s + sections - 1, sections)}

    def pair_of(sems, i):
        return sems.at[2 * i], sems.at[2 * i + 1]

    def w_x(i):
        return remote(gw, own_w.at[yh, x, core], *pair_of(wx_sem, i), place(yh, xp(i), core))

    def w_y(i):
        spot = own_w.at[yh, xp(i), core]
        return remote(gw if i == 0 else spot, spot, *pair_of(wy_sem, i), other_y)

    def w_c(i):
        spot = own_w.at[:, xp(i), core]
        return remote(spot, spot, *pair_of(wc_sem, i), other_core)

    v_y = remote(gu, own_u.at[yh, x, core], *pair_of(vx_sem, 0), other_y)

    def v_x(i):
        spot = own_u.at[:, x, core]
        return remote(spot, spot, *pair_of(vx_sem, i), place(yh, xp(i), core))

    def v_c(i):
        spot = own_u.at[:, xp(i), core]
        return remote(spot, spot, *pair_of(vc_sem, i), other_core)

    next_copy = remote(nw, nxt_u.at[yh, x, core], *pair_of(nx_sem, 0), down_section)
    bump_copy = remote(ub, bump_u, *pair_of(nx_sem, x_n), down_section)

    def n_x(i):
        spot = nxt_u.at[yh, x, core]
        return remote(spot, spot, *pair_of(nx_sem, i), place(yh, xp(i), core))

    def n_y(i):
        spot = nxt_u.at[yh, xp(i), core]
        return remote(spot, spot, *pair_of(ny_sem, i), other_y)

    def n_c(i):
        spot = nxt_u.at[:, xp(i), core]
        return remote(spot, spot, *pair_of(nc_sem, i), other_core)

    for i in range(1, x_n):
        w_x(i).start()
    v_y.start()
    w_y(0).start()

    @pl.when(s > 0)
    def _():
        nw[...] = (mine_u[...].astype(f32) - learn_rate * gu[...].astype(f32)).astype(bf16)
        next_copy.start()

    own_w[yh, x, core] = gw[...]
    own_u[yh, x, core] = gu[...]
    v_y.wait_recv()
    for i in range(1, x_n):
        w_x(x_n - i).wait_recv()
        w_y(i).start()
    for i in range(1, x_n):
        v_x(i).start()
    v_c(0).start()

    @pl.when(has_next)
    def _():
        next_copy.wait_recv()
        for i in range(1, x_n):
            n_x(i).start()
        n_y(0).start()

    for i in range(x_n):
        w_y(i).wait_recv()
        w_c(i).start()

    @pl.when(has_next)
    def _():
        for i in range(1, x_n):
            n_x(x_n - i).wait_recv()
            n_y(i).start()

    for i in range(1, x_n):
        v_x(x_n - i).wait_recv()
        v_c(i).start()
    for i in range(x_n):
        w_c(i).wait()

    @pl.when(s > 0)
    def _():
        def ahead(b, pre):
            y_ = b // x_n
            x_ = lax.rem(b, x_n)
            cols = pl.ds(pl.multiple_of(b * 2 * shard, 128), 2 * shard)
            both = jnp.concatenate([own_w[y_, x_, 0], own_w[y_, x_, 1]], axis=0)
            fresh = wd[cols, :].astype(f32) - learn_rate * both.astype(f32)
            return pre + dot_nn(xb[:, cols], fresh.astype(bf16))

        pre = lax.fori_loop(0, yh_n * x_n, ahead, jnp.zeros((rows, rank), f32))
        value, unused = gelu_pair(pre * lax.rsqrt(nacc[...] * (1.0 / width) + eps))
        ub[...] = value.astype(bf16)
        bump_copy.start()

    @pl.when(has_next)
    def _():
        for i in range(x_n):
            n_y(i).wait_recv()
            n_c(i).start()
        for i in range(x_n):
            n_c(i).wait()
            n_y(i).wait_send()
        for i in range(1, x_n):
            n_x(i).wait_send()
        bump_copy.wait_recv()

    for i in range(x_n):
        v_c(i).wait()
        w_y(i).wait_send()
    for i in range(1, x_n):
        w_x(i).wait_send()
        v_x(i).wait_send()
    v_y.wait_send()

    @pl.when(s > 0)
    def _():
        next_copy.wait_send()
        bump_copy.wait_send()

    def core_settle(b, carry):
        core_copy(b).wait_send()
        return carry

    lax.fori_loop(0, yh_n * x_n, core_settle, 0)

    def finish(c, carry):
        @pl.when(z < planes - 1)
        def _():
            x_copy(c).wait_send()
        give_copy(c).wait_send()
        pass_copy(c).wait_send()

        @pl.when(z > 0)
        def _():
            b_copy(c).wait_send()
        h_copy(c).wait_send()
        return carry

    lax.fori_loop(0, chunks, finish, 0)
    for o in range(2, planes):
        u_copy(o).wait_send()

    @pl.when(z == planes - 1)
    def _():
        u_copy(1).wait_send()

    @pl.when(z < planes - 1)
    def _():
        near_copy(z, head, 0).wait_send()
        near_copy(z, tail, 1).wait_send()
        n_copy().wait_send()

    def settle(j, carry):
        q_copy(j).wait_send()
        m_copy(j).wait_send()
        return carry

    lax.fori_loop(0, z, settle, 0)
    uf_copy().wait_send()
    qp_copy().wait_send()


def recurrence(sections, shards, pyh, n0, nn, x0, g16, up, wd, upart, wpart, mine_u):
    rows, width = x0.shape
    rank = up.shape[0]
    half = width // 2
    some = rows // 2
    planes = sections // 2
    chunks = 28
    per = 7
    x_n = 4
    yh_n = shards // (2 * x_n)
    shard = mine_u.shape[0]
    cut = shard // 2
    blocks = yh_n * x_n
    vm = pl.BlockSpec(memory_space=pltpu.VMEM)
    dma = pltpu.SemaphoreType.DMA
    sq = (rows, rank)
    two = (some, 2 * rank)
    strip = pltpu.VMEM((rows, half), bf16)
    full = jax.ShapeDtypeStruct((yh_n, x_n, 2, shard, rank), bf16)

    def buf(*lead):
        return pltpu.VMEM(lead + (2 * rank,), bf16)

    return pl.pallas_call(
        functools.partial(recurrence_kernel, sections, chunks, per, yh_n, x_n),
        out_shape=(jax.ShapeDtypeStruct((rows, width), bf16), full, full, full,
                   jax.ShapeDtypeStruct(sq, bf16)),
        in_specs=[vm] * 10,
        out_specs=(vm,) * 5,
        scratch_shapes=[
            pltpu.VMEM((planes,) + two, bf16),
            pltpu.VMEM((planes, some + 16, 2 * rank), bf16),
            pltpu.VMEM((some + 16, 2 * rank), bf16),
            pltpu.VMEM((planes, 2 * rank, 2 * rank), bf16),
            pltpu.VMEM((sections,) + two, f32),
            pltpu.VMEM((8, rank), f32),
            pltpu.VMEM((8, rank), f32),
            pltpu.VMEM((some, 4 * rank), f32),
            pltpu.VMEM(two, f32), pltpu.VMEM(two, f32), pltpu.VMEM(two, f32),
            pltpu.VMEM((2, some, rank), f32),
            pltpu.VMEM((rows, 2 * rank), bf16),
            pltpu.VMEM((rows, 2 * rank), bf16),
            pltpu.VMEM((2,) + sq, f32),
            strip, strip, strip, strip, strip, strip, strip,
            pltpu.VMEM((rows, width), bf16),
            pltpu.VMEM(sq, bf16), pltpu.VMEM(sq, bf16),
            pltpu.VMEM((rows, width), bf16), pltpu.VMEM(sq, f32),
            buf(blocks, 2, shard), buf(blocks, shard), buf(yh_n, x_n, shard),
            buf(x_n - 1, yh_n, cut), buf(x_n, cut), buf(yh_n, cut), buf(cut),
            buf(x_n, cut), buf(x_n - 1, cut),
            pltpu.VMEM((shard, rank), bf16), pltpu.VMEM((shard, rank), bf16),
            pltpu.VMEM((shard, rank), bf16), pltpu.VMEM(sq, bf16),
        ] + [dma((planes,))] * 6 + [dma((10,))] + [dma((chunks,))] * 10 + [
            dma((blocks,)), dma((blocks,)),
            dma((yh_n * (x_n - 1),)), dma((yh_n * (x_n - 1),)), dma((x_n,)), dma((x_n,)), dma((2,)),
            dma((x_n - 1,)), dma((x_n - 1,)),
            dma((2 * x_n,)), dma((2 * x_n,)), dma((2 * x_n,)), dma((2 * x_n,)), dma((2 * x_n,)),
            dma((2 * x_n + 2,)), dma((2 * x_n,)), dma((2 * x_n,)),
        ],
        compiler_params=pltpu.CompilerParams(
            collective_id=1, has_side_effects=True, vmem_limit_bytes=56 * 1024 * 1024),
    )(pyh, n0, nn, x0, g16, up, wd, upart, wpart, mine_u)


def dp_place(x_n):
    d = lax.axis_index("dp")
    return d // (2 * x_n), lax.rem(d // 2, x_n), lax.rem(d, 2)


def remote(src, dst, send, recv, where):
    return pltpu.make_async_remote_copy(src_ref=src, dst_ref=dst, send_sem=send, recv_sem=recv,
                                        device_id=where, device_id_type=MESH)


def block_sum(b, yh_n, x_n, core_copy, part, rc, sums, rax, rby, ax_send, ax_recv, by_send, by_recv):
    yh, x, core = dp_place(x_n)
    cut = sums.shape[2] // 2
    y_ = b // x_n
    x_ = lax.rem(b, x_n)
    core_copy(b).wait_recv()
    sums[y_, x_] = (part[b, core].astype(f32) + rc[b].astype(f32)).astype(bf16)
    turn = lax.rem(x_ - x + x_n, x_n)

    @pl.when(turn != 0)
    def _():
        sem = (turn - 1) * yh_n + y_
        remote(sums.at[y_, x_, 0:cut], rax.at[turn - 1, y_], ax_send.at[sem], ax_recv.at[sem],
               {"dp": (yh * x_n + x_) * 2 + core}).start()

    @pl.when(y_ != yh)
    def _():
        remote(sums.at[y_, x_, cut:2 * cut], rby.at[x_], by_send.at[x_], by_recv.at[x_],
               {"dp": (y_ * x_n + x) * 2 + core}).start()


def scatter_sum(yh_n, x_n, sums, rax, rby, sa, ray, sb, rbx,
                ax_send, ax_recv, by_send, by_recv, s_sem, bx_send, bx_recv):
    yh, x, core = dp_place(x_n)
    rows = sums.shape[2]
    cut = rows // 2

    def place(y_, x_, c_):
        return {"dp": (y_ * x_n + x_) * 2 + c_}

    def xp(i):
        return lax.rem(x + i, x_n)

    other_y = place(1 - yh, x, core)

    def ax_copy(i, y_):
        sem = (i - 1) * yh_n + y_
        return remote(sums.at[y_, xp(i), 0:cut], rax.at[i - 1, y_], ax_send.at[sem], ax_recv.at[sem],
                      place(yh, xp(i), core))

    def by_copy(x_):
        return remote(sums.at[1 - yh, x_, cut:rows], rby.at[x_], by_send.at[x_], by_recv.at[x_], other_y)

    def bx_copy(i):
        return remote(sb.at[xp(i)], rbx.at[i - 1], bx_send.at[i - 1], bx_recv.at[i - 1],
                      place(yh, xp(i), core))

    ay_copy = remote(sa.at[1 - yh], ray, s_sem.at[0], s_sem.at[1], other_y)

    for i in range(x_n):
        x_ = xp(i)
        by_copy(x_).wait_recv()
        sb[x_] = (sums[yh, x_, cut:rows].astype(f32) + rby[x_].astype(f32)).astype(bf16)
        if i > 0:
            bx_copy(i).start()
    for y_ in range(yh_n):
        total = sums[y_, x, 0:cut].astype(f32)
        for i in range(1, x_n):
            ax_copy(i, y_).wait_recv()
            total = total + rax[i - 1, y_].astype(f32)
        sa[y_] = total.astype(bf16)
    ay_copy.start()
    total_b = sb[x].astype(f32)
    for i in range(1, x_n):
        bx_copy(i).wait_recv()
        total_b = total_b + rbx[i - 1].astype(f32)
    ay_copy.wait_recv()
    total_a = sa[yh].astype(f32) + ray[...].astype(f32)
    for i in range(1, x_n):
        for y_ in range(yh_n):
            ax_copy(i, y_).wait_send()
        bx_copy(i).wait_send()
    for x_ in range(x_n):
        by_copy(x_).wait_send()
    ay_copy.wait_send()
    return total_a, total_b


def gram_kernel(yh_n, x_n, sections, x0, g16, down, up, mine_u, base, pyh, n0, out, upart, wpart,
                allu, part, rc, sums, rax, rby, sa, ray, sb, rbx, gs, gp, two, mine3, theirs3,
                z_sem, f_send, f_recv, r_send, r_recv,
                c_send, c_recv, ax_send, ax_recv, by_send, by_recv, s_sem, bx_send, bx_recv,
                ga_send, ga_recv, gb_send, gb_recv, gc_send, gc_recv):
    yh, x, core = dp_place(x_n)
    s = lax.axis_index("section")
    z_n = sections // 2
    z = s // 2
    ylo = lax.rem(s, 2)
    rank = up.shape[0]
    rows = rank
    cut = rows // 2

    def place(y_, x_, c_):
        return {"dp": (y_ * x_n + x_) * 2 + c_}

    def xp(i):
        return lax.rem(x + i, x_n)

    def zp(i):
        return lax.rem(z + i, z_n)

    other_core = place(yh, x, 1 - core)
    other_y = place(1 - yh, x, core)
    partner = {"section": s + 1 - 2 * ylo}
    after = {"section": 2 * zp(1) + ylo}
    before = {"section": 2 * zp(z_n - 1) + ylo}

    barrier = pltpu.get_barrier_semaphore()
    peers = [other_core, other_y, partner, after, before]
    peers += [place(yh, xp(i), core) for i in range(1, x_n)]
    for where in peers:
        pl.semaphore_signal(barrier, inc=1, device_id=where, device_id_type=MESH)
    pl.semaphore_wait(barrier, len(peers))

    pair = remote(mine_u, allu.at[z, ylo], z_sem.at[0], z_sem.at[1], partner)

    def products(z_):
        for y_ in range(2):
            part[z_, y_] = dot_tn(allu[z_, y_], base[...]).astype(bf16)

    def core_copy(b):
        return remote(part.at[b, 1 - core], rc.at[b], c_send.at[b], c_recv.at[b], other_core)

    hops = z_n // 2

    def column(j):
        return ylo if j == 0 else 1 - ylo

    def ring_f(i, j):
        spot = allu.at[zp(z_n + 1 - i), column(j)]
        src = mine_u if (i == 1 and j == 0) else spot
        sem = 2 * (i - 1) + j
        return remote(src, spot, f_send.at[sem], f_recv.at[sem], after)

    def ring_r(i, j):
        spot = allu.at[zp(i - 1), column(j)]
        src = mine_u if (i == 1 and j == 0) else spot
        sem = 2 * (i - 1) + j
        return remote(src, spot, r_send.at[sem], r_recv.at[sem], before)

    used_f = [(i, j) for i in range(1, hops + 1) for j in range(2) if i < hops or j == 0]
    used_r = [(i, j) for i in range(1, hops + 1) for j in range(2) if i < hops or j == 1]

    pair.start()
    ring_f(1, 0).start()
    ring_r(1, 0).start()
    allu[z, ylo] = mine_u[...]
    pair.wait_recv()
    ring_f(1, 1).start()
    ring_r(1, 1).start()

    half = x0.shape[1] // 2
    quarter = half // 2
    far = pl.ds(pl.multiple_of((1 - ylo) * half + core * quarter, 128), quarter)
    near = pl.ds(pl.multiple_of(core * quarter, 128), quarter)
    swap_u = remote(up.at[:, far], upart.at[:, near], z_sem.at[6], z_sem.at[7], partner)
    swap_w = remote(down.at[far, :], wpart.at[near, :], z_sem.at[8], z_sem.at[9], partner)
    share_u = remote(upart.at[:, near], upart.at[:, near], z_sem.at[10], z_sem.at[11], other_core)
    share_w = remote(wpart.at[near, :], wpart.at[near, :], z_sem.at[12], z_sem.at[13], other_core)
    swap_u.start()
    swap_w.start()

    u = up[...]
    w = down[...]
    values = x0[...]
    token_half = x0.shape[0] // 2
    keep = pl.ds(ylo * token_half, token_half)
    give = pl.ds((1 - ylo) * token_half, token_half)
    mine3[0] = dot_nn(values, w)
    mine3[1] = dot_nt(values, u)
    mine3[2] = dot_nt(g16[...], u)
    swap3 = remote(mine3.at[:, give], theirs3, z_sem.at[2], z_sem.at[3], partner)
    swap3.start()
    wide = x0[keep, :].astype(f32)
    n0[...] = jnp.broadcast_to(jnp.sum(wide * wide, axis=1, keepdims=True), n0.shape)

    def collect(b):
        block_sum(b, yh_n, x_n, core_copy, part, rc, sums, rax, rby,
                  ax_send, ax_recv, by_send, by_recv)

    products(z)
    core_copy(z).start()
    for i in range(1, hops + 1):
        for j in range(2):
            if (i, j) in used_f:
                ring_f(i, j).wait_recv()
                if (i + 1, j) in used_f:
                    ring_f(i + 1, j).start()
            if (i, j) in used_r:
                ring_r(i, j).wait_recv()
                if (i + 1, j) in used_r:
                    ring_r(i + 1, j).start()
        products(zp(z_n - i))
        core_copy(zp(z_n - i)).start()
        if i == 1:
            collect(z)
        else:
            collect(zp(i - 1))
        if i < hops:
            products(zp(i))
            core_copy(zp(i)).start()
        collect(zp(z_n - i))

    swap_u.wait_recv()
    share_u.start()
    swap_w.wait_recv()
    share_w.start()
    total_a, total_b = scatter_sum(yh_n, x_n, sums, rax, rby, sa, ray, sb, rbx,
                                   ax_send, ax_recv, by_send, by_recv, s_sem, bx_send, bx_recv)
    gs[0:cut] = total_a.astype(bf16)
    gs[cut:rows] = total_b.astype(bf16)
    swap = remote(gs, gp, z_sem.at[4], z_sem.at[5], partner)
    swap.start()

    def lanes(base, which):
        return pl.ds(pl.multiple_of(base + which * rank, 128), rank)

    swap3.wait_recv()
    pyh[:, :, lanes(0, ylo)] = mine3[:, keep]
    pyh[:, :, lanes(0, 1 - ylo)] = theirs3[...]
    two[:, lanes(0, ylo)] = gs[:, 0:rank]
    two[:, lanes(2 * rank, ylo)] = gs[:, rank:2 * rank]
    swap.wait_recv()
    two[:, lanes(0, 1 - ylo)] = gp[:, 0:rank]
    two[:, lanes(2 * rank, 1 - ylo)] = gp[:, rank:2 * rank]
    out[yh, x, core] = two[...]

    low = pl.ds(0, cut)
    high = pl.ds(cut, cut)

    def spread(src, spot, sems, i, where):
        return remote(src, spot, sems[0].at[i], sems[1].at[i], where)

    ga = (ga_send, ga_recv)
    gb = (gb_send, gb_recv)
    a_y = spread(two.at[low], out.at[yh, x, core, low], ga, 0, other_y)

    def a_x(i):
        spot = out.at[:, x, core, low]
        return spread(spot, spot, ga, i, place(yh, xp(i), core))

    def b_x(i):
        return spread(two.at[high], out.at[yh, x, core, high], gb, i - 1, place(yh, xp(i), core))

    def b_y(i):
        spot = out.at[yh, xp(i), core, high]
        return spread(spot, spot, gb, x_n - 1 + i, other_y)

    def all_c(i):
        spot = out.at[:, xp(i), core]
        return remote(spot, spot, gc_send.at[i], gc_recv.at[i], other_core)

    a_y.start()
    for i in range(1, x_n):
        b_x(i).start()
    b_y(0).start()
    a_y.wait_recv()
    for i in range(1, x_n):
        a_x(i).start()
    for i in range(1, x_n):
        b_x(x_n - i).wait_recv()
        b_y(i).start()
    b_y(0).wait_recv()
    all_c(0).start()
    for i in range(1, x_n):
        a_x(x_n - i).wait_recv()
        b_y(i).wait_recv()
        all_c(i).start()
    for i in range(x_n):
        all_c(i).wait()
        b_y(i).wait_send()
    for i in range(1, x_n):
        a_x(i).wait_send()
        b_x(i).wait_send()
    a_y.wait_send()
    pair.wait_send()
    swap.wait_send()
    swap3.wait_send()
    swap_u.wait_send()
    swap_w.wait_send()
    share_u.wait()
    share_w.wait()
    for i, j in used_f:
        ring_f(i, j).wait_send()
    for i, j in used_r:
        ring_r(i, j).wait_send()

    def settle(b, carry):
        core_copy(b).wait_send()
        return carry

    lax.fori_loop(0, yh_n * x_n, settle, 0)


def grams_of(sections, shards, x0, g16, down, up, mine_u, base):
    x_n = 4
    yh_n = shards // (2 * x_n)
    rows, width = x0.shape
    rank = up.shape[0]
    height = mine_u.shape[0]
    cut = rank // 2
    vm = pl.BlockSpec(memory_space=pltpu.VMEM)
    dma = pltpu.SemaphoreType.DMA

    def buf(*lead):
        return pltpu.VMEM(lead + (2 * rank,), bf16)

    return pl.pallas_call(
        functools.partial(gram_kernel, yh_n, x_n, sections),
        out_shape=(
            jax.ShapeDtypeStruct((3, rows // 2, 2 * rank), f32),
            jax.ShapeDtypeStruct((rows // 2, rank), f32),
            jax.ShapeDtypeStruct((yh_n, x_n, 2, rank, 4 * rank), bf16),
            jax.ShapeDtypeStruct((rank, width // 2), bf16),
            jax.ShapeDtypeStruct((width // 2, rank), bf16),
        ),
        in_specs=[vm] * 6,
        out_specs=(vm,) * 5,
        scratch_shapes=[
            pltpu.VMEM((sections // 2, 2, height, rank), bf16),
            buf(yh_n * x_n, 2, rank), buf(yh_n * x_n, rank), buf(yh_n, x_n, rank),
            buf(x_n - 1, yh_n, cut), buf(x_n, cut), buf(yh_n, cut), buf(cut),
            buf(x_n, cut), buf(x_n - 1, cut), buf(rank), buf(rank),
            pltpu.VMEM((rank, 4 * rank), bf16),
            pltpu.VMEM((3, rows, rank), f32), pltpu.VMEM((3, rows // 2, rank), f32),
            dma((14,)), dma((sections // 2,)), dma((sections // 2,)),
            dma((sections // 2,)), dma((sections // 2,)),
            dma((yh_n * x_n,)), dma((yh_n * x_n,)),
            dma((yh_n * (x_n - 1),)), dma((yh_n * (x_n - 1),)), dma((x_n,)), dma((x_n,)), dma((4,)),
            dma((x_n - 1,)), dma((x_n - 1,)),
            dma((x_n,)), dma((x_n,)), dma((2 * x_n,)), dma((2 * x_n,)), dma((x_n,)), dma((x_n,)),
        ],
        compiler_params=pltpu.CompilerParams(
            collective_id=3, has_side_effects=True, vmem_limit_bytes=48 * 1024 * 1024),
    )(x0, g16, down, up, mine_u, base)


def finish_kernel(sections, own_w, own_u, nxt_u, bump_u, x1, grad_down, grad_up, advance):
    last = lax.axis_index("section") == sections - 1
    grad_down[...] = own_w[...]
    grad_up[...] = own_u[...].astype(f32).T.astype(bf16)
    bump = dot_nt(bump_u[...], nxt_u[...])
    advance[...] = (x1[...].astype(f32) + jnp.where(last, 0.0, bump)).astype(bf16)


def finish(sections, own_w, own_u, nxt_u, bump_u, x1):
    rows, width = x1.shape
    rank = own_w.shape[1]
    step = width // 4
    tall = pl.BlockSpec((step, rank), lambda i: (i, 0))
    flat = pl.BlockSpec((rows, step), lambda i: (0, i))
    return pl.pallas_call(
        functools.partial(finish_kernel, sections),
        grid=(width // step,),
        out_shape=(
            jax.ShapeDtypeStruct((width, rank), bf16),
            jax.ShapeDtypeStruct((rank, width), bf16),
            jax.ShapeDtypeStruct((rows, width), bf16),
        ),
        in_specs=[tall, tall, tall, pl.BlockSpec((rows, rank), lambda i: (0, 0)), flat],
        out_specs=(tall, flat, flat),
        compiler_params=pltpu.CompilerParams(vmem_limit_bytes=32 * 1024 * 1024),
    )(own_w, own_u, nxt_u, bump_u, x1)


def per_device(inputs, cotangent, w_down, w_up):
    down = w_down[0]
    upward = w_up[0]
    micro, batch_rows, width = inputs.shape
    rank = down.shape[1]
    rows = micro * batch_rows
    sections = lax.axis_size("section")
    shards = lax.axis_size("dp")
    part = width // shards
    d = lax.axis_index("dp")
    x0 = inputs.reshape(rows, width)
    g16 = cotangent.reshape(rows, width)
    up_t = upward.T

    mine_u = lax.dynamic_slice_in_dim(up_t, d * part, part, 0)
    mine_w = lax.dynamic_slice_in_dim(down, d * part, part, 0)
    base = jnp.concatenate([mine_w, mine_u], axis=1)
    pyh, n0, grams, upart, wpart = grams_of(sections, shards, x0, g16, down, upward, mine_u, base)
    grams = grams.reshape(sections // 2, 2 * rank, 4 * rank)
    x1, own_w, own_u, nxt_u, bump_u = recurrence(
        sections, shards, pyh, n0, grams, x0, g16, upward, down, upart, wpart, mine_u)
    tall = (width, rank)
    grad_down, grad_up, advance = finish(
        sections, own_w.reshape(tall), own_u.reshape(tall), nxt_u.reshape(tall), bump_u, x1)
    return (grad_down[None], grad_up[None], advance.reshape(1, micro, batch_rows, width))


def solution(mesh):
    in_specs = (
        P(None, "dp", None),
        P(None, "dp", None),
        P("section", None, None),
        P("section", None, None),
    )
    out_specs = (P("section", None, None), P("section", None, None), P("section", None, "dp", None))
    return jax.shard_map(
        per_device, mesh=mesh, in_specs=in_specs, out_specs=out_specs, check_vma=False
    )
```

```python
import functools

import jax
import jax.numpy as jnp
from jax import lax
from jax.experimental import pallas as pl
from jax.experimental.pallas import tpu as pltpu
from jax.sharding import PartitionSpec as P

MESH = pl.DeviceIdType.MESH
eps = 1e-05
learn_rate = 0.05
f32 = jnp.float32
bf16 = jnp.bfloat16


def dot_nn(a, b):
    return jnp.dot(a, b, preferred_element_type=f32)


def dot_tn(a, b):
    return lax.dot_general(a, b, (((0,), (0,)), ((), ())), preferred_element_type=f32)


def dot_nt(a, b):
    return lax.dot_general(a, b, (((1,), (1,)), ((), ())), preferred_element_type=f32)


def gelu_pair(a):
    c = 0.7978845608028654
    inner = c * (a + 0.044715 * a * a * a)
    th = jnp.tanh(inner)
    value = 0.5 * a * (1.0 + th)
    slope = 0.5 * (1.0 + th) + 0.5 * a * (1.0 - th * th) * c * (1.0 + 3 * 0.044715 * a * a)
    return value, slope


def recurrence_kernel(sections, chunks, per, yh_n, x_n,
                      pyh, n0, nn, x0, g16, up, wd, upart, wpart, mine_u,
                      xout, own_w, own_u, nxt_u, bump_u,
                      ul, ql, qp, ys, nl, nsend, acc, hacc, slope, act, rinv, uf, qs, cpair,
                      xin, xkeep, xgive, gin, gkeep, ggive, xpass, delta,
                      gout, us, qv, xb, nacc, part, rc, sums, rax, rby, sa, ray, sb, rbx,
                      gw, gu, nw, ub,
                      u_send, u_recv, q_send, q_recv, e_sem,
                      c_send, c_recv, g_send, g_recv,
                      b_send, b_recv, h_send, h_recv, p_send, p_recv,
                      k_send, k_recv, ax_send, ax_recv, by_send, by_recv, s_sem, bx_send, bx_recv,
                      wx_sem, wy_sem, wc_sem, vx_sem, vc_sem, nx_sem, ny_sem, nc_sem):
    s = lax.axis_index("section")
    yh, x, core = dp_place(x_n)
    planes = sections // 2
    rows, width = x0.shape
    some = rows // 2
    rank = up.shape[0]
    half = width // 2
    piece = half // chunks
    trips = chunks // per
    z = s // 2
    ylo = lax.rem(s, 2)
    first = ylo == 0
    partner = {"section": s + 1 - 2 * ylo}
    head = slice(0, rank)
    tail = slice(rank, 2 * rank)
    mine = pl.ds(ylo * some, some)
    theirs = pl.ds((1 - ylo) * some, some)

    def plane(i):
        return {"section": 2 * i + ylo}

    def peer(offset):
        return lax.rem(z + offset, planes)

    barrier = pltpu.get_barrier_semaphore()
    for o in range(1, planes):
        pl.semaphore_signal(barrier, inc=1, device_id=plane(peer(o)), device_id_type=MESH)

    def place(y_, x_, c_):
        return {"dp": (y_ * x_n + x_) * 2 + c_}

    def xp(i):
        return lax.rem(x + i, x_n)

    other_core = place(yh, x, 1 - core)
    other_y = place(1 - yh, x, core)
    beyond = {"section": lax.rem(s + sections - 1 + 2 * ylo, sections)}
    others = [partner, beyond, other_core, other_y] + [place(yh, xp(i), core) for i in range(1, x_n)]
    for where in others:
        pl.semaphore_signal(barrier, inc=1, device_id=where, device_id_type=MESH)
    pl.semaphore_wait(barrier, planes - 1 + len(others))

    eye = (lax.broadcasted_iota(jnp.int32, (some, rank), 0)
           == lax.broadcasted_iota(jnp.int32, (some, rank), 1)).astype(f32)

    def to_row(col):
        return jnp.sum(eye * col, axis=0, keepdims=True)

    def to_col(row):
        return jnp.sum(eye * row, axis=1, keepdims=True)

    def columns(base, c):
        return pl.ds(pl.multiple_of(base + c * piece, 128), piece)

    def x_copy(c):
        return remote(xkeep.at[:, columns(0, c)], xin.at[:, columns(0, c)],
                      c_send.at[c], c_recv.at[c], plane(peer(1)))

    def b_copy(c):
        return remote(gkeep.at[:, columns(0, c)], gin.at[:, columns(0, c)],
                      b_send.at[c], b_recv.at[c], plane(peer(planes - 1)))

    def give_copy(c):
        return remote(xgive.at[:, columns(0, c)], xout.at[:, columns(ylo * half, c)],
                      g_send.at[c], g_recv.at[c], partner)

    def give_arrived(c):
        return remote(xgive.at[:, columns(0, c)], xout.at[:, columns((1 - ylo) * half, c)],
                      g_send.at[c], g_recv.at[c], partner)

    def pass_copy(c):
        return remote(xpass.at[:, columns(0, c)], xb.at[:, columns(ylo * half, c)],
                      p_send.at[c], p_recv.at[c], partner)

    def pass_arrived(c):
        return remote(xpass.at[:, columns(0, c)], xb.at[:, columns((1 - ylo) * half, c)],
                      p_send.at[c], p_recv.at[c], partner)

    def h_copy(c):
        return remote(ggive.at[:, columns(0, c)], gout.at[:, columns(ylo * half, c)],
                      h_send.at[c], h_recv.at[c], partner)

    def h_arrived(c):
        return remote(ggive.at[:, columns(0, c)], gout.at[:, columns((1 - ylo) * half, c)],
                      h_send.at[c], h_recv.at[c], partner)

    def near_copy(k, part, sem):
        spot = ul.at[k, :, part]
        return remote(spot, spot, e_sem.at[2 * sem], e_sem.at[2 * sem + 1], plane(peer(1)))

    def n_copy():
        return remote(nsend, nl, e_sem.at[4], e_sem.at[5], plane(peer(1)))

    def uf_copy():
        return remote(ul.at[z], uf.at[mine], e_sem.at[6], e_sem.at[7], partner)

    def uf_arrived():
        return remote(ul.at[z], uf.at[theirs], e_sem.at[6], e_sem.at[7], partner)

    def qp_copy():
        return remote(ql.at[z], qp, e_sem.at[8], e_sem.at[9], partner)

    def u_copy(o):
        return remote(ul.at[z], ul.at[z], u_send.at[o], u_recv.at[z], plane(peer(o)))

    def u_arrived(k):
        return remote(ul.at[k], ul.at[k], u_send.at[0], u_recv.at[k], plane(peer(1)))

    def q_copy(j):
        return remote(ql.at[z], ql.at[z], q_send.at[j], q_recv.at[z], plane(j))

    def q_arrived(k):
        return remote(ql.at[k], ql.at[k], q_send.at[0], q_recv.at[k], plane(peer(1)))

    acc[:, 0:2 * rank] = pyh[0]
    acc[:, 2 * rank:4 * rank] = pyh[1]
    hacc[...] = pyh[2]

    batch = per * piece

    def wide_columns(base, p):
        return pl.ds(pl.multiple_of(base + p * batch, 128), batch)

    def chain(p):
        ours = up[:, wide_columns(ylo * half, p)]
        other = upart[:, wide_columns(0, p)]
        grow = dot_nn(uf[:, head], jnp.where(first, ours, other))
        delta[0] = grow
        delta[1] = grow + dot_nn(uf[:, tail], jnp.where(first, other, ours))
        for j in range(per):
            c = per * p + j

            @pl.when(z > 0)
            def _():
                x_copy(c).wait_recv()

            here = columns(ylo * half, c)
            there = columns(0, c)
            lane = slice(j * piece, (j + 1) * piece)
            start = jnp.where(z > 0, xin[:, there], x0[:, here])
            x_a = (start.astype(f32) + delta[0, :, lane]).astype(bf16)
            x_b = (start.astype(f32) + delta[1, :, lane]).astype(bf16)
            xkeep[:, there] = x_b

            @pl.when(z < planes - 1)
            def _():
                x_copy(c).start()

            xpass[:, there] = jnp.where(first, x_a, start)
            pass_copy(c).start()
            xgive[:, there] = jnp.where(first, x_b, x_a)
            xout[:, here] = jnp.where(first, x_a, x_b)
            xb[:, here] = jnp.where(first, start, x_a)

    def chain_back(p):
        here = wide_columns(ylo * half, p)
        there = wide_columns(0, p)
        ours = wd[here, :]
        other = wpart[there, :]
        x_a = jnp.where(first, xb[:, here], xpass[:, there]).astype(f32)
        x_b = jnp.where(first, xpass[:, there], xb[:, here]).astype(f32)
        grow = dot_nt(qs[:, tail], jnp.where(first, other, ours)) - cpair[1, :, 0:1] * x_b
        delta[0] = grow
        delta[1] = (grow + dot_nt(qs[:, head], jnp.where(first, ours, other))
                    - cpair[0, :, 0:1] * x_a)
        for j in range(per):
            c = per * p + j

            @pl.when(z < planes - 1)
            def _():
                b_copy(c).wait_recv()

            here = columns(ylo * half, c)
            there = columns(0, c)
            lane = slice(j * piece, (j + 1) * piece)
            g_b = jnp.where(z < planes - 1, gin[:, there], g16[:, here])
            g_a = (g_b.astype(f32) + delta[0, :, lane]).astype(bf16)

            @pl.when(z > 0)
            def _():
                gkeep[:, there] = (g_b.astype(f32) + delta[1, :, lane]).astype(bf16)
                b_copy(c).start()

            ggive[:, there] = jnp.where(first, g_b, g_a)
            h_copy(c).start()
            gout[:, here] = jnp.where(first, g_a, g_b)

    def forward_own():
        @pl.when(z > 0)
        def _():
            n_copy().wait_recv()

        norm_a = jnp.where(z > 0, to_col(nl[0:1, :]), n0[:, 0:1])
        scale_a = lax.rsqrt(norm_a * (1.0 / width) + eps)
        pre_a = acc[:, 0:rank] * scale_a
        value_a, slope_a = gelu_pair(pre_a)
        u_a = value_a.astype(bf16)
        ul[z, :, head] = u_a

        @pl.when(z < planes - 1)
        def _():
            near_copy(z, head, 0).start()

        step = dot_nn(u_a, nn[z, 0:rank, rank:4 * rank])
        y_a = acc[:, 2 * rank:3 * rank]
        norm_b = norm_a + jnp.sum(u_a.astype(f32) * (2.0 * y_a + step[:, rank:2 * rank]),
                                  axis=1, keepdims=True)
        scale_b = lax.rsqrt(norm_b * (1.0 / width) + eps)
        pre_b = (acc[:, rank:2 * rank] + step[:, 0:rank]) * scale_b
        value_b, slope_b = gelu_pair(pre_b)
        u_b = value_b.astype(bf16)
        ul[z, :, tail] = u_b

        @pl.when(z < planes - 1)
        def _():
            near_copy(z, tail, 1).start()

        y_b = acc[:, 2 * rank:4 * rank] + step[:, rank:3 * rank]
        more = dot_nn(u_b, nn[z, rank:2 * rank, 2 * rank:4 * rank])
        norm_c = norm_b + jnp.sum(
            u_b.astype(f32) * (2.0 * y_b[:, rank:2 * rank] + more[:, rank:2 * rank]),
            axis=1, keepdims=True)

        @pl.when(z < planes - 1)
        def _():
            nsend[...] = jnp.broadcast_to(to_row(norm_c), nsend.shape)
            n_copy().start()

        uf_copy().start()
        for o in range(2, planes):
            u_copy(o).start()

        @pl.when(z == planes - 1)
        def _():
            u_copy(1).start()

        uf[mine, :] = ul[z]
        ys[2 * z + 1] = y_b
        acc[:, 2 * rank:4 * rank] = y_b + more
        act[:, head] = pre_a
        act[:, tail] = pre_b
        slope[:, head] = slope_a
        slope[:, tail] = slope_b
        rinv[0] = jnp.broadcast_to(scale_a, (some, rank))
        rinv[1] = jnp.broadcast_to(scale_b, (some, rank))

    def c_of(stat):
        line = stat[0:1, :].astype(f32) + stat[1:2, :].astype(f32)
        return to_col(line[:, head]), to_col(line[:, tail])

    def backward_own():
        scale_b = rinv[1]
        q_b = hacc[:, tail] * slope[:, tail]
        low_b = (q_b * scale_b).astype(bf16)
        mix_b = jnp.sum(q_b * act[:, tail], axis=1, keepdims=True) * (1.0 / width)
        c_b = mix_b * scale_b[:, 0:1] * scale_b[:, 0:1]
        h_a = hacc[:, head] + dot_nt(low_b, nn[z, 0:rank, rank:2 * rank]) - c_b * ys[2 * z + 1, :, head]
        scale_a = rinv[0]
        q_a = h_a * slope[:, head]
        mix_a = jnp.sum(q_a * act[:, head], axis=1, keepdims=True) * (1.0 / width)
        c_a = mix_a * scale_a[:, 0:1] * scale_a[:, 0:1]
        ql[z, 0:some, head] = (q_a * scale_a).astype(bf16)
        ql[z, 0:some, tail] = low_b
        spot = lax.broadcasted_iota(jnp.int32, (16, rank), 0)
        for part, col in ((head, c_a), (tail, c_b)):
            line = to_row(col)
            high = line.astype(bf16).astype(f32)
            ql[z, some:some + 16, part] = jnp.where(
                spot == 0, high, jnp.where(spot == 1, line - high, 0.0)).astype(bf16)

        def send(i, carry):
            q_copy(z - 1 - i).start()
            return carry

        lax.fori_loop(0, z, send, 0)
        qp_copy().start()

    shard = mine_u.shape[0]
    nacc[...] = jnp.zeros_like(nacc)

    def core_copy(b):
        return remote(part.at[b, 1 - core], rc.at[b], k_send.at[b], k_recv.at[b], other_core)

    def collect(b):
        block_sum(b, yh_n, x_n, core_copy, part, rc, sums, rax, rby,
                  ax_send, ax_recv, by_send, by_recv)

    def terms(b):
        cols = pl.ds(pl.multiple_of(b * 2 * shard, 128), 2 * shard)
        u = us[...]
        before = xb[:, cols]
        wide = before.astype(f32)
        nacc[...] += jnp.broadcast_to(jnp.sum(wide * wide, axis=1, keepdims=True), nacc.shape)
        g_down = dot_tn(before, qv[...]).astype(bf16)
        g_up = dot_tn(gout[:, cols], u).astype(bf16)
        for i in range(2):
            part[b, i, :, head] = g_down[i * shard:(i + 1) * shard]
            part[b, i, :, tail] = g_up[i * shard:(i + 1) * shard]
        core_copy(b).start()

    def tick(t, carry):
        k = t - 1
        sent = (k >= 0) & (k < planes)
        near = sent & (k == z - 1)

        @pl.when(sent & (k != z) & (k != z - 1))
        def _():
            u_arrived(k).wait_recv()

        @pl.when(near)
        def _():
            near_copy(k, head, 0).wait_recv()
            acc[...] += dot_nn(ul[k, :, head], nn[k, 0:rank, :])
            near_copy(k, tail, 1).wait_recv()
            acc[...] += dot_nn(ul[k, :, tail], nn[k, rank:2 * rank, :])

        @pl.when(sent & (k < z - 1))
        def _():
            acc[...] += dot_nn(ul[k], nn[k])

        @pl.when(t == z)
        def _():
            forward_own()

        @pl.when(sent & (k > z))
        def _():
            before = acc[:, 2 * rank:4 * rank]
            ys[2 * k] = before
            between = before + dot_nn(ul[k, :, head], nn[k, 0:rank, 2 * rank:4 * rank])
            ys[2 * k + 1] = between
            acc[:, 2 * rank:4 * rank] = between + dot_nn(
                ul[k, :, tail], nn[k, rank:2 * rank, 2 * rank:4 * rank])

        r = 2 * planes - t

        @pl.when((r < planes) & (r > z))
        def _():
            q_arrived(r).wait_recv()
            c_a, c_b = c_of(ql[r, some:some + 16, :])
            hacc[...] += (dot_nn(ql[r, 0:some, :], nn[r, :, 0:2 * rank]) - c_a * ys[2 * r] - c_b * ys[2 * r + 1])

        @pl.when(t == 2 * planes - 1 - z)
        def _():
            backward_own()

        p = t - (z + 1)

        @pl.when((p >= 0) & (p < trips))
        def _():
            @pl.when(p == 0)
            def _():
                uf_arrived().wait_recv()
            chain(p)

        q = t - (z + 1 + trips)

        @pl.when((q >= 0) & (q < chunks // 4))
        def _():
            for j in range(4):
                give_copy(4 * q + j).start()

        b = t - (2 * planes - z)

        @pl.when((b >= 0) & (b < trips))
        def _():
            @pl.when(b == 0)
            def _():
                qp_copy().wait_recv()
                qs[mine, :] = ql[z, 0:some, :]
                qs[theirs, :] = qp[0:some, :]
                for where, stat in ((mine, ql[z, some:some + 16, :]), (theirs, qp[some:some + 16, :])):
                    c_a, c_b = c_of(stat)
                    cpair[0, where, :] = jnp.broadcast_to(c_a, (some, rank))
                    cpair[1, where, :] = jnp.broadcast_to(c_b, (some, rank))
                us[...] = jnp.where(first, uf[:, head], uf[:, tail])
                qv[...] = jnp.where(first, qs[:, head], qs[:, tail])
            chain_back(b)
            terms(ylo * trips + b)

        @pl.when((b >= 1) & (b <= trips))
        def _():
            collect(ylo * trips + b - 1)

            def landed(j, carry):
                c = per * (b - 1) + j
                pass_arrived(c).wait_recv()
                h_arrived(c).wait_recv()
                return carry

            lax.fori_loop(0, per, landed, 0)
            terms((1 - ylo) * trips + b - 1)

        @pl.when((b >= 2) & (b <= trips))
        def _():
            collect((1 - ylo) * trips + b - 2)

        return carry

    lax.fori_loop(0, 2 * planes + trips + 1, tick, 0)
    collect((1 - ylo) * trips + trips - 1)

    total_a, total_b = scatter_sum(yh_n, x_n, sums, rax, rby, sa, ray, sb, rbx,
                                   ax_send, ax_recv, by_send, by_recv, s_sem, bx_send, bx_recv)
    cut = shard // 2
    gw[0:cut] = total_a[:, head].astype(bf16)
    gw[cut:shard] = total_b[:, head].astype(bf16)
    gu[0:cut] = total_a[:, tail].astype(bf16)
    gu[cut:shard] = total_b[:, tail].astype(bf16)
    has_next = s < sections - 1
    down_section = {"section": lax.rem(s + sections - 1, sections)}

    def pair_of(sems, i):
        return sems.at[2 * i], sems.at[2 * i + 1]

    def w_x(i):
        return remote(gw, own_w.at[yh, x, core], *pair_of(wx_sem, i), place(yh, xp(i), core))

    def w_y(i):
        spot = own_w.at[yh, xp(i), core]
        return remote(gw if i == 0 else spot, spot, *pair_of(wy_sem, i), other_y)

    def w_c(i):
        spot = own_w.at[:, xp(i), core]
        return remote(spot, spot, *pair_of(wc_sem, i), other_core)

    v_y = remote(gu, own_u.at[yh, x, core], *pair_of(vx_sem, 0), other_y)

    def v_x(i):
        spot = own_u.at[:, x, core]
        return remote(spot, spot, *pair_of(vx_sem, i), place(yh, xp(i), core))

    def v_c(i):
        spot = own_u.at[:, xp(i), core]
        return remote(spot, spot, *pair_of(vc_sem, i), other_core)

    next_copy = remote(nw, nxt_u.at[yh, x, core], *pair_of(nx_sem, 0), down_section)
    bump_copy = remote(ub, bump_u, *pair_of(nx_sem, x_n), down_section)

    def n_x(i):
        spot = nxt_u.at[yh, x, core]
        return remote(spot, spot, *pair_of(nx_sem, i), place(yh, xp(i), core))

    def n_y(i):
        spot = nxt_u.at[yh, xp(i), core]
        return remote(spot, spot, *pair_of(ny_sem, i), other_y)

    def n_c(i):
        spot = nxt_u.at[:, xp(i), core]
        return remote(spot, spot, *pair_of(nc_sem, i), other_core)

    for i in range(1, x_n):
        w_x(i).start()
    v_y.start()
    w_y(0).start()

    @pl.when(s > 0)
    def _():
        nw[...] = (mine_u[...].astype(f32) - learn_rate * gu[...].astype(f32)).astype(bf16)
        next_copy.start()

    own_w[yh, x, core] = gw[...]
    own_u[yh, x, core] = gu[...]
    v_y.wait_recv()
    for i in range(1, x_n):
        w_x(x_n - i).wait_recv()
        w_y(i).start()
    for i in range(1, x_n):
        v_x(i).start()
    v_c(0).start()

    @pl.when(has_next)
    def _():
        next_copy.wait_recv()
        for i in range(1, x_n):
            n_x(i).start()
        n_y(0).start()

    for i in range(x_n):
        w_y(i).wait_recv()
        w_c(i).start()

    @pl.when(has_next)
    def _():
        for i in range(1, x_n):
            n_x(x_n - i).wait_recv()
            n_y(i).start()

    for i in range(1, x_n):
        v_x(x_n - i).wait_recv()
        v_c(i).start()
    for i in range(x_n):
        w_c(i).wait()

    @pl.when(s > 0)
    def _():
        def ahead(b, pre):
            y_ = b // x_n
            x_ = lax.rem(b, x_n)
            cols = pl.ds(pl.multiple_of(b * 2 * shard, 128), 2 * shard)
            both = jnp.concatenate([own_w[y_, x_, 0], own_w[y_, x_, 1]], axis=0)
            fresh = wd[cols, :].astype(f32) - learn_rate * both.astype(f32)
            return pre + dot_nn(xb[:, cols], fresh.astype(bf16))

        pre = lax.fori_loop(0, yh_n * x_n, ahead, jnp.zeros((rows, rank), f32))
        value, unused = gelu_pair(pre * lax.rsqrt(nacc[...] * (1.0 / width) + eps))
        ub[...] = value.astype(bf16)
        bump_copy.start()

    @pl.when(has_next)
    def _():
        for i in range(x_n):
            n_y(i).wait_recv()
            n_c(i).start()
        for i in range(x_n):
            n_c(i).wait()
            n_y(i).wait_send()
        for i in range(1, x_n):
            n_x(i).wait_send()
        bump_copy.wait_recv()

    for i in range(x_n):
        v_c(i).wait()
        w_y(i).wait_send()
    for i in range(1, x_n):
        w_x(i).wait_send()
        v_x(i).wait_send()
    v_y.wait_send()

    @pl.when(s > 0)
    def _():
        next_copy.wait_send()
        bump_copy.wait_send()

    def core_settle(b, carry):
        core_copy(b).wait_send()
        return carry

    lax.fori_loop(0, yh_n * x_n, core_settle, 0)

    def finish(c, carry):
        @pl.when(z < planes - 1)
        def _():
            x_copy(c).wait_send()
        give_copy(c).wait_send()
        give_arrived(c).wait_recv()
        pass_copy(c).wait_send()

        @pl.when(z > 0)
        def _():
            b_copy(c).wait_send()
        h_copy(c).wait_send()
        return carry

    lax.fori_loop(0, chunks, finish, 0)
    for o in range(2, planes):
        u_copy(o).wait_send()

    @pl.when(z == planes - 1)
    def _():
        u_copy(1).wait_send()

    @pl.when(z < planes - 1)
    def _():
        near_copy(z, head, 0).wait_send()
        near_copy(z, tail, 1).wait_send()
        n_copy().wait_send()

    def settle(j, carry):
        q_copy(j).wait_send()
        return carry

    lax.fori_loop(0, z, settle, 0)
    uf_copy().wait_send()
    qp_copy().wait_send()


def recurrence(sections, shards, pyh, n0, nn, x0, g16, up, wd, upart, wpart, mine_u):
    rows, width = x0.shape
    rank = up.shape[0]
    half = width // 2
    some = rows // 2
    planes = sections // 2
    chunks = 28
    per = 7
    x_n = 4
    yh_n = shards // (2 * x_n)
    shard = mine_u.shape[0]
    cut = shard // 2
    blocks = yh_n * x_n
    vm = pl.BlockSpec(memory_space=pltpu.VMEM)
    dma = pltpu.SemaphoreType.DMA
    sq = (rows, rank)
    two = (some, 2 * rank)
    strip = pltpu.VMEM((rows, half), bf16)
    full = jax.ShapeDtypeStruct((yh_n, x_n, 2, shard, rank), bf16)

    def buf(*lead):
        return pltpu.VMEM(lead + (2 * rank,), bf16)

    return pl.pallas_call(
        functools.partial(recurrence_kernel, sections, chunks, per, yh_n, x_n),
        out_shape=(jax.ShapeDtypeStruct((rows, width), bf16), full, full, full,
                   jax.ShapeDtypeStruct(sq, bf16)),
        in_specs=[vm] * 10,
        out_specs=(vm,) * 5,
        scratch_shapes=[
            pltpu.VMEM((planes,) + two, bf16),
            pltpu.VMEM((planes, some + 16, 2 * rank), bf16),
            pltpu.VMEM((some + 16, 2 * rank), bf16),
            pltpu.VMEM((sections,) + two, f32),
            pltpu.VMEM((8, rank), f32),
            pltpu.VMEM((8, rank), f32),
            pltpu.VMEM((some, 4 * rank), f32),
            pltpu.VMEM(two, f32), pltpu.VMEM(two, f32), pltpu.VMEM(two, f32),
            pltpu.VMEM((2, some, rank), f32),
            pltpu.VMEM((rows, 2 * rank), bf16),
            pltpu.VMEM((rows, 2 * rank), bf16),
            pltpu.VMEM((2,) + sq, f32),
            strip, strip, strip, strip, strip, strip, strip,
            pltpu.VMEM((2, rows, half * per // chunks), f32),
            pltpu.VMEM((rows, width), bf16),
            pltpu.VMEM(sq, bf16), pltpu.VMEM(sq, bf16),
            pltpu.VMEM((rows, width), bf16), pltpu.VMEM(sq, f32),
            buf(blocks, 2, shard), buf(blocks, shard), buf(yh_n, x_n, shard),
            buf(x_n - 1, yh_n, cut), buf(x_n, cut), buf(yh_n, cut), buf(cut),
            buf(x_n, cut), buf(x_n - 1, cut),
            pltpu.VMEM((shard, rank), bf16), pltpu.VMEM((shard, rank), bf16),
            pltpu.VMEM((shard, rank), bf16), pltpu.VMEM(sq, bf16),
        ] + [dma((planes,))] * 4 + [dma((10,))] + [dma((chunks,))] * 10 + [
            dma((blocks,)), dma((blocks,)),
            dma((yh_n * (x_n - 1),)), dma((yh_n * (x_n - 1),)), dma((x_n,)), dma((x_n,)), dma((2,)),
            dma((x_n - 1,)), dma((x_n - 1,)),
            dma((2 * x_n,)), dma((2 * x_n,)), dma((2 * x_n,)), dma((2 * x_n,)), dma((2 * x_n,)),
            dma((2 * x_n + 2,)), dma((2 * x_n,)), dma((2 * x_n,)),
        ],
        compiler_params=pltpu.CompilerParams(
            collective_id=1, has_side_effects=True, vmem_limit_bytes=56 * 1024 * 1024),
    )(pyh, n0, nn, x0, g16, up, wd, upart, wpart, mine_u)


def dp_place(x_n):
    d = lax.axis_index("dp")
    return d // (2 * x_n), lax.rem(d // 2, x_n), lax.rem(d, 2)


def remote(src, dst, send, recv, where):
    return pltpu.make_async_remote_copy(src_ref=src, dst_ref=dst, send_sem=send, recv_sem=recv,
                                        device_id=where, device_id_type=MESH)


def block_sum(b, yh_n, x_n, core_copy, part, rc, sums, rax, rby, ax_send, ax_recv, by_send, by_recv):
    yh, x, core = dp_place(x_n)
    cut = sums.shape[2] // 2
    y_ = b // x_n
    x_ = lax.rem(b, x_n)
    core_copy(b).wait_recv()
    sums[y_, x_] = (part[b, core].astype(f32) + rc[b].astype(f32)).astype(bf16)
    turn = lax.rem(x_ - x + x_n, x_n)

    @pl.when(turn != 0)
    def _():
        sem = (turn - 1) * yh_n + y_
        remote(sums.at[y_, x_, 0:cut], rax.at[turn - 1, y_], ax_send.at[sem], ax_recv.at[sem],
               {"dp": (yh * x_n + x_) * 2 + core}).start()

    @pl.when(y_ != yh)
    def _():
        remote(sums.at[y_, x_, cut:2 * cut], rby.at[x_], by_send.at[x_], by_recv.at[x_],
               {"dp": (y_ * x_n + x) * 2 + core}).start()


def scatter_sum(yh_n, x_n, sums, rax, rby, sa, ray, sb, rbx,
                ax_send, ax_recv, by_send, by_recv, s_sem, bx_send, bx_recv):
    yh, x, core = dp_place(x_n)
    rows = sums.shape[2]
    cut = rows // 2

    def place(y_, x_, c_):
        return {"dp": (y_ * x_n + x_) * 2 + c_}

    def xp(i):
        return lax.rem(x + i, x_n)

    other_y = place(1 - yh, x, core)

    def ax_copy(i, y_):
        sem = (i - 1) * yh_n + y_
        return remote(sums.at[y_, xp(i), 0:cut], rax.at[i - 1, y_], ax_send.at[sem], ax_recv.at[sem],
                      place(yh, xp(i), core))

    def by_copy(x_):
        return remote(sums.at[1 - yh, x_, cut:rows], rby.at[x_], by_send.at[x_], by_recv.at[x_], other_y)

    def bx_copy(i):
        return remote(sb.at[xp(i)], rbx.at[i - 1], bx_send.at[i - 1], bx_recv.at[i - 1],
                      place(yh, xp(i), core))

    ay_copy = remote(sa.at[1 - yh], ray, s_sem.at[0], s_sem.at[1], other_y)

    for i in range(x_n):
        x_ = xp(i)
        by_copy(x_).wait_recv()
        sb[x_] = (sums[yh, x_, cut:rows].astype(f32) + rby[x_].astype(f32)).astype(bf16)
        if i > 0:
            bx_copy(i).start()
    for y_ in range(yh_n):
        total = sums[y_, x, 0:cut].astype(f32)
        for i in range(1, x_n):
            ax_copy(i, y_).wait_recv()
            total = total + rax[i - 1, y_].astype(f32)
        sa[y_] = total.astype(bf16)
    ay_copy.start()
    total_b = sb[x].astype(f32)
    for i in range(1, x_n):
        bx_copy(i).wait_recv()
        total_b = total_b + rbx[i - 1].astype(f32)
    ay_copy.wait_recv()
    total_a = sa[yh].astype(f32) + ray[...].astype(f32)
    for i in range(1, x_n):
        for y_ in range(yh_n):
            ax_copy(i, y_).wait_send()
        bx_copy(i).wait_send()
    for x_ in range(x_n):
        by_copy(x_).wait_send()
    ay_copy.wait_send()
    return total_a, total_b


def gram_kernel(yh_n, x_n, sections, x0, g16, down, up, mine_u, base, pyh, n0, out, upart, wpart,
                allu, part, rc, sums, rax, rby, sa, ray, sb, rbx, gs, gp, two, mine3, theirs3, flip, turned,
                z_sem, f_send, f_recv, r_send, r_recv,
                c_send, c_recv, ax_send, ax_recv, by_send, by_recv, s_sem, bx_send, bx_recv,
                ga_send, ga_recv, gb_send, gb_recv, gc_send, gc_recv, t_sem):
    yh, x, core = dp_place(x_n)
    s = lax.axis_index("section")
    z_n = sections // 2
    z = s // 2
    ylo = lax.rem(s, 2)
    rank = up.shape[0]
    rows = rank
    cut = rows // 2

    def place(y_, x_, c_):
        return {"dp": (y_ * x_n + x_) * 2 + c_}

    def xp(i):
        return lax.rem(x + i, x_n)

    def zp(i):
        return lax.rem(z + i, z_n)

    other_core = place(yh, x, 1 - core)
    other_y = place(1 - yh, x, core)
    partner = {"section": s + 1 - 2 * ylo}
    after = {"section": 2 * zp(1) + ylo}
    before = {"section": 2 * zp(z_n - 1) + ylo}

    barrier = pltpu.get_barrier_semaphore()
    peers = [other_core, other_y, partner, after, before]
    peers += [place(yh, xp(i), core) for i in range(1, x_n)]
    for where in peers:
        pl.semaphore_signal(barrier, inc=1, device_id=where, device_id_type=MESH)
    d = lax.axis_index("dp")
    above = d // 2 < z
    below = d // 2 > z
    mirror = [{"section": 2 * (d // 2) + i, "dp": s} for i in range(2)]

    @pl.when(below)
    def _():
        for i in range(2):
            pl.semaphore_signal(barrier, inc=1, device_id={"section": d, "dp": 2 * z + i},
                                device_id_type=MESH)

    pl.semaphore_wait(barrier, len(peers) + 2 * above.astype(jnp.int32))

    def flip_copy(i):
        k = lax.rem(d, 2)
        return remote(flip, turned.at[k], t_sem.at[i], t_sem.at[2 + k], mirror[i])

    def flip_arrived(i):
        return remote(flip, turned.at[i], t_sem.at[0], t_sem.at[2 + i], mirror[0])

    pair = remote(mine_u, allu.at[z, ylo], z_sem.at[0], z_sem.at[1], partner)

    def products(z_):
        for y_ in range(2):
            part[z_, y_] = dot_tn(allu[z_, y_], base[...]).astype(bf16)

    def core_copy(b):
        return remote(part.at[b, 1 - core], rc.at[b], c_send.at[b], c_recv.at[b], other_core)

    hops = z_n // 2

    def column(j):
        return ylo if j == 0 else 1 - ylo

    def ring_f(i, j):
        spot = allu.at[zp(z_n + 1 - i), column(j)]
        src = mine_u if (i == 1 and j == 0) else spot
        sem = 2 * (i - 1) + j
        return remote(src, spot, f_send.at[sem], f_recv.at[sem], after)

    def ring_r(i, j):
        spot = allu.at[zp(i - 1), column(j)]
        src = mine_u if (i == 1 and j == 0) else spot
        sem = 2 * (i - 1) + j
        return remote(src, spot, r_send.at[sem], r_recv.at[sem], before)

    used_f = [(i, j) for i in range(1, hops + 1) for j in range(2) if i < hops or j == 0]
    used_r = [(i, j) for i in range(1, hops + 1) for j in range(2) if i < hops or j == 1]

    pair.start()
    ring_f(1, 0).start()
    ring_r(1, 0).start()
    allu[z, ylo] = mine_u[...]
    pair.wait_recv()
    ring_f(1, 1).start()
    ring_r(1, 1).start()

    half = x0.shape[1] // 2
    quarter = half // 2
    far = pl.ds(pl.multiple_of((1 - ylo) * half + core * quarter, 128), quarter)
    near = pl.ds(pl.multiple_of(core * quarter, 128), quarter)
    swap_u = remote(up.at[:, far], upart.at[:, near], z_sem.at[6], z_sem.at[7], partner)
    swap_w = remote(down.at[far, :], wpart.at[near, :], z_sem.at[8], z_sem.at[9], partner)
    share_u = remote(upart.at[:, near], upart.at[:, near], z_sem.at[10], z_sem.at[11], other_core)
    share_w = remote(wpart.at[near, :], wpart.at[near, :], z_sem.at[12], z_sem.at[13], other_core)
    swap_u.start()
    swap_w.start()

    u = up[...]
    w = down[...]
    values = x0[...]
    token_half = x0.shape[0] // 2
    keep = pl.ds(ylo * token_half, token_half)
    give = pl.ds((1 - ylo) * token_half, token_half)
    mine3[0] = dot_nn(values, w)
    mine3[1] = dot_nt(values, u)
    mine3[2] = dot_nt(g16[...], u)
    swap3 = remote(mine3.at[:, give], theirs3, z_sem.at[2], z_sem.at[3], partner)
    swap3.start()
    wide = x0[keep, :].astype(f32)
    n0[...] = jnp.broadcast_to(jnp.sum(wide * wide, axis=1, keepdims=True), n0.shape)

    def collect(b):
        block_sum(b, yh_n, x_n, core_copy, part, rc, sums, rax, rby,
                  ax_send, ax_recv, by_send, by_recv)

    products(z)
    core_copy(z).start()
    for i in range(1, hops + 1):
        for j in range(2):
            if (i, j) in used_f:
                ring_f(i, j).wait_recv()
                if (i + 1, j) in used_f:
                    ring_f(i + 1, j).start()
            if (i, j) in used_r:
                ring_r(i, j).wait_recv()
                if (i + 1, j) in used_r:
                    ring_r(i + 1, j).start()
        products(zp(z_n - i))
        core_copy(zp(z_n - i)).start()
        if i == 1:
            collect(z)
        else:
            collect(zp(i - 1))
        if i < hops:
            products(zp(i))
            core_copy(zp(i)).start()
        collect(zp(z_n - i))

    swap_u.wait_recv()
    share_u.start()
    swap_w.wait_recv()
    share_w.start()
    total_a, total_b = scatter_sum(yh_n, x_n, sums, rax, rby, sa, ray, sb, rbx,
                                   ax_send, ax_recv, by_send, by_recv, s_sem, bx_send, bx_recv)
    gs[0:cut] = total_a.astype(bf16)
    gs[cut:rows] = total_b.astype(bf16)
    swap = remote(gs, gp, z_sem.at[4], z_sem.at[5], partner)
    swap.start()

    @pl.when(above)
    def _():
        flip[...] = gs[:, 0:rank].astype(f32).T.astype(bf16)
        for i in range(2):
            flip_copy(i).start()

    def lanes(base, which):
        return pl.ds(pl.multiple_of(base + which * rank, 128), rank)

    swap3.wait_recv()
    pyh[:, :, lanes(0, ylo)] = mine3[:, keep]
    pyh[:, :, lanes(0, 1 - ylo)] = theirs3[...]
    two[:, lanes(0, ylo)] = gs[:, 0:rank]
    two[:, lanes(2 * rank, ylo)] = gs[:, rank:2 * rank]
    swap.wait_recv()
    two[:, lanes(0, 1 - ylo)] = gp[:, 0:rank]
    two[:, lanes(2 * rank, 1 - ylo)] = gp[:, rank:2 * rank]

    @pl.when(below)
    def _():
        for i in range(2):
            flip_arrived(i).wait_recv()
            two[:, i * rank:(i + 1) * rank] = turned[i]
    out[yh, x, core] = two[...]

    low = pl.ds(0, cut)
    high = pl.ds(cut, cut)

    def spread(src, spot, sems, i, where):
        return remote(src, spot, sems[0].at[i], sems[1].at[i], where)

    ga = (ga_send, ga_recv)
    gb = (gb_send, gb_recv)
    a_y = spread(two.at[low], out.at[yh, x, core, low], ga, 0, other_y)

    def a_x(i):
        spot = out.at[:, x, core, low]
        return spread(spot, spot, ga, i, place(yh, xp(i), core))

    def b_x(i):
        return spread(two.at[high], out.at[yh, x, core, high], gb, i - 1, place(yh, xp(i), core))

    def b_y(i):
        spot = out.at[yh, xp(i), core, high]
        return spread(spot, spot, gb, x_n - 1 + i, other_y)

    def all_c(i):
        spot = out.at[:, xp(i), core]
        return remote(spot, spot, gc_send.at[i], gc_recv.at[i], other_core)

    a_y.start()
    for i in range(1, x_n):
        b_x(i).start()
    b_y(0).start()
    a_y.wait_recv()
    for i in range(1, x_n):
        a_x(i).start()
    for i in range(1, x_n):
        b_x(x_n - i).wait_recv()
        b_y(i).start()
    b_y(0).wait_recv()
    all_c(0).start()
    for i in range(1, x_n):
        a_x(x_n - i).wait_recv()
        b_y(i).wait_recv()
        all_c(i).start()
    for i in range(x_n):
        all_c(i).wait()
        b_y(i).wait_send()
    for i in range(1, x_n):
        a_x(i).wait_send()
        b_x(i).wait_send()
    a_y.wait_send()
    pair.wait_send()
    swap.wait_send()
    swap3.wait_send()

    @pl.when(above)
    def _():
        for i in range(2):
            flip_copy(i).wait_send()
    swap_u.wait_send()
    swap_w.wait_send()
    share_u.wait()
    share_w.wait()
    for i, j in used_f:
        ring_f(i, j).wait_send()
    for i, j in used_r:
        ring_r(i, j).wait_send()

    def settle(b, carry):
        core_copy(b).wait_send()
        return carry

    lax.fori_loop(0, yh_n * x_n, settle, 0)


def grams_of(sections, shards, x0, g16, down, up, mine_u, base):
    x_n = 4
    yh_n = shards // (2 * x_n)
    rows, width = x0.shape
    rank = up.shape[0]
    height = mine_u.shape[0]
    cut = rank // 2
    vm = pl.BlockSpec(memory_space=pltpu.VMEM)
    dma = pltpu.SemaphoreType.DMA

    def buf(*lead):
        return pltpu.VMEM(lead + (2 * rank,), bf16)

    return pl.pallas_call(
        functools.partial(gram_kernel, yh_n, x_n, sections),
        out_shape=(
            jax.ShapeDtypeStruct((3, rows // 2, 2 * rank), f32),
            jax.ShapeDtypeStruct((rows // 2, rank), f32),
            jax.ShapeDtypeStruct((yh_n, x_n, 2, rank, 4 * rank), bf16),
            jax.ShapeDtypeStruct((rank, width // 2), bf16),
            jax.ShapeDtypeStruct((width // 2, rank), bf16),
        ),
        in_specs=[vm] * 6,
        out_specs=(vm,) * 5,
        scratch_shapes=[
            pltpu.VMEM((sections // 2, 2, height, rank), bf16),
            buf(yh_n * x_n, 2, rank), buf(yh_n * x_n, rank), buf(yh_n, x_n, rank),
            buf(x_n - 1, yh_n, cut), buf(x_n, cut), buf(yh_n, cut), buf(cut),
            buf(x_n, cut), buf(x_n - 1, cut), buf(rank), buf(rank),
            pltpu.VMEM((rank, 4 * rank), bf16),
            pltpu.VMEM((3, rows, rank), f32), pltpu.VMEM((3, rows // 2, rank), f32),
            pltpu.VMEM((rank, rank), bf16), pltpu.VMEM((2, rank, rank), bf16),
            dma((14,)), dma((sections // 2,)), dma((sections // 2,)),
            dma((sections // 2,)), dma((sections // 2,)),
            dma((yh_n * x_n,)), dma((yh_n * x_n,)),
            dma((yh_n * (x_n - 1),)), dma((yh_n * (x_n - 1),)), dma((x_n,)), dma((x_n,)), dma((4,)),
            dma((x_n - 1,)), dma((x_n - 1,)),
            dma((x_n,)), dma((x_n,)), dma((2 * x_n,)), dma((2 * x_n,)), dma((x_n,)), dma((x_n,)), dma((4,)),
        ],
        compiler_params=pltpu.CompilerParams(
            collective_id=3, has_side_effects=True, vmem_limit_bytes=48 * 1024 * 1024),
    )(x0, g16, down, up, mine_u, base)


def finish_kernel(sections, own_w, own_u, nxt_u, bump_u, x1, grad_down, grad_up, advance):
    last = lax.axis_index("section") == sections - 1
    grad_down[...] = own_w[...]
    grad_up[...] = own_u[...].astype(f32).T.astype(bf16)
    bump = dot_nt(bump_u[...], nxt_u[...])
    advance[...] = (x1[...].astype(f32) + jnp.where(last, 0.0, bump)).astype(bf16)


def finish(sections, own_w, own_u, nxt_u, bump_u, x1):
    rows, width = x1.shape
    rank = own_w.shape[1]
    step = width // 4
    tall = pl.BlockSpec((step, rank), lambda i: (i, 0))
    flat = pl.BlockSpec((rows, step), lambda i: (0, i))
    return pl.pallas_call(
        functools.partial(finish_kernel, sections),
        grid=(width // step,),
        out_shape=(
            jax.ShapeDtypeStruct((width, rank), bf16),
            jax.ShapeDtypeStruct((rank, width), bf16),
            jax.ShapeDtypeStruct((rows, width), bf16),
        ),
        in_specs=[tall, tall, tall, pl.BlockSpec((rows, rank), lambda i: (0, 0)), flat],
        out_specs=(tall, flat, flat),
        compiler_params=pltpu.CompilerParams(vmem_limit_bytes=32 * 1024 * 1024),
    )(own_w, own_u, nxt_u, bump_u, x1)


def per_device(inputs, cotangent, w_down, w_up):
    down = w_down[0]
    upward = w_up[0]
    micro, batch_rows, width = inputs.shape
    rank = down.shape[1]
    rows = micro * batch_rows
    sections = lax.axis_size("section")
    shards = lax.axis_size("dp")
    part = width // shards
    d = lax.axis_index("dp")
    x0 = inputs.reshape(rows, width)
    g16 = cotangent.reshape(rows, width)
    up_t = upward.T

    mine_u = lax.dynamic_slice_in_dim(up_t, d * part, part, 0)
    mine_w = lax.dynamic_slice_in_dim(down, d * part, part, 0)
    base = jnp.concatenate([mine_w, mine_u], axis=1)
    pyh, n0, grams, upart, wpart = grams_of(sections, shards, x0, g16, down, upward, mine_u, base)
    grams = grams.reshape(sections // 2, 2 * rank, 4 * rank)
    x1, own_w, own_u, nxt_u, bump_u = recurrence(
        sections, shards, pyh, n0, grams, x0, g16, upward, down, upart, wpart, mine_u)
    tall = (width, rank)
    grad_down, grad_up, advance = finish(
        sections, own_w.reshape(tall), own_u.reshape(tall), nxt_u.reshape(tall), bump_u, x1)
    return (grad_down[None], grad_up[None], advance.reshape(1, micro, batch_rows, width))


def solution(mesh):
    in_specs = (
        P(None, "dp", None),
        P(None, "dp", None),
        P("section", None, None),
        P("section", None, None),
    )
    out_specs = (P("section", None, None), P("section", None, None), P("section", None, "dp", None))
    return jax.shard_map(
        per_device, mesh=mesh, in_specs=in_specs, out_specs=out_specs, check_vma=False
    )
```

```python
import functools

import jax
import jax.numpy as jnp
from jax import lax
from jax.experimental import pallas as pl
from jax.experimental.pallas import tpu as pltpu
from jax.sharding import PartitionSpec as P

MESH = pl.DeviceIdType.MESH
eps = 1e-05
learn_rate = 0.05
f32 = jnp.float32
bf16 = jnp.bfloat16


def dot_nn(a, b):
    return jnp.dot(a, b, preferred_element_type=f32)


def dot_tn(a, b):
    return lax.dot_general(a, b, (((0,), (0,)), ((), ())), preferred_element_type=f32)


def dot_nt(a, b):
    return lax.dot_general(a, b, (((1,), (1,)), ((), ())), preferred_element_type=f32)


def gelu_pair(a):
    c = 0.7978845608028654
    inner = c * (a + 0.044715 * a * a * a)
    th = jnp.tanh(inner)
    value = 0.5 * a * (1.0 + th)
    slope = 0.5 * (1.0 + th) + 0.5 * a * (1.0 - th * th) * c * (1.0 + 3 * 0.044715 * a * a)
    return value, slope


def recurrence_kernel(sections, chunks, per, yh_n, x_n,
                      pyh, n0, nn, x0_far, g16_far, up_far, wd_far, upart_far, wpart_far, mine_u,
                      xout, own_w, own_u, nxt_u, bump_u,
                      ul, ql, qp, ys, nl, nsend, acc, hacc, slope, act, rinv, uf, qs, cpair,
                      xin, xkeep, xgive, gin, gkeep, ggive, xpass, delta,
                      gout, us, qv, xb, nacc, part, rc, sums, rax, rby, sa, ray, sb, rbx,
                      gw, gu, nw, ub, x0, g16, up, wd, upart, wpart, l_sem,
                      u_send, u_recv, q_send, q_recv, e_sem,
                      c_send, c_recv, g_send, g_recv,
                      b_send, b_recv, h_send, h_recv, p_send, p_recv,
                      k_send, k_recv, ax_send, ax_recv, by_send, by_recv, s_sem, bx_send, bx_recv,
                      wx_sem, wy_sem, wc_sem, vx_sem, vc_sem, nx_sem, ny_sem, nc_sem):
    loads = [pltpu.make_async_copy(far, near, l_sem.at[i]) for i, (far, near) in enumerate((
        (up_far, up), (upart_far, upart), (x0_far, x0),
        (wd_far, wd), (wpart_far, wpart), (g16_far, g16)))]
    for load in loads:
        load.start()
    s = lax.axis_index("section")
    yh, x, core = dp_place(x_n)
    planes = sections // 2
    rows, width = x0.shape
    some = rows // 2
    rank = up.shape[0]
    half = width // 2
    piece = half // chunks
    trips = chunks // per
    z = s // 2
    ylo = lax.rem(s, 2)
    first = ylo == 0
    partner = {"section": s + 1 - 2 * ylo}
    head = slice(0, rank)
    tail = slice(rank, 2 * rank)
    mine = pl.ds(ylo * some, some)
    theirs = pl.ds((1 - ylo) * some, some)

    def plane(i):
        return {"section": 2 * i + ylo}

    def peer(offset):
        return lax.rem(z + offset, planes)

    barrier = pltpu.get_barrier_semaphore()
    for o in range(1, planes):
        pl.semaphore_signal(barrier, inc=1, device_id=plane(peer(o)), device_id_type=MESH)

    def place(y_, x_, c_):
        return {"dp": (y_ * x_n + x_) * 2 + c_}

    def xp(i):
        return lax.rem(x + i, x_n)

    other_core = place(yh, x, 1 - core)
    other_y = place(1 - yh, x, core)
    beyond = {"section": lax.rem(s + sections - 1 + 2 * ylo, sections)}
    others = [partner, beyond, other_core, other_y] + [place(yh, xp(i), core) for i in range(1, x_n)]
    for where in others:
        pl.semaphore_signal(barrier, inc=1, device_id=where, device_id_type=MESH)
    pl.semaphore_wait(barrier, planes - 1 + len(others))

    eye = (lax.broadcasted_iota(jnp.int32, (some, rank), 0)
           == lax.broadcasted_iota(jnp.int32, (some, rank), 1)).astype(f32)

    def to_row(col):
        return jnp.sum(eye * col, axis=0, keepdims=True)

    def to_col(row):
        return jnp.sum(eye * row, axis=1, keepdims=True)

    def columns(base, c):
        return pl.ds(pl.multiple_of(base + c * piece, 128), piece)

    def x_copy(c):
        return remote(xkeep.at[:, columns(0, c)], xin.at[:, columns(0, c)],
                      c_send.at[c], c_recv.at[c], plane(peer(1)))

    def b_copy(c):
        return remote(gkeep.at[:, columns(0, c)], gin.at[:, columns(0, c)],
                      b_send.at[c], b_recv.at[c], plane(peer(planes - 1)))

    def give_copy(c):
        return remote(xgive.at[:, columns(0, c)], xout.at[:, columns(ylo * half, c)],
                      g_send.at[c], g_recv.at[c], partner)

    def give_arrived(c):
        return remote(xgive.at[:, columns(0, c)], xout.at[:, columns((1 - ylo) * half, c)],
                      g_send.at[c], g_recv.at[c], partner)

    def pass_copy(c):
        return remote(xpass.at[:, columns(0, c)], xb.at[:, columns(ylo * half, c)],
                      p_send.at[c], p_recv.at[c], partner)

    def pass_arrived(c):
        return remote(xpass.at[:, columns(0, c)], xb.at[:, columns((1 - ylo) * half, c)],
                      p_send.at[c], p_recv.at[c], partner)

    def h_copy(c):
        return remote(ggive.at[:, columns(0, c)], gout.at[:, columns(ylo * half, c)],
                      h_send.at[c], h_recv.at[c], partner)

    def h_arrived(c):
        return remote(ggive.at[:, columns(0, c)], gout.at[:, columns((1 - ylo) * half, c)],
                      h_send.at[c], h_recv.at[c], partner)

    def near_copy(k, part, sem):
        spot = ul.at[k, :, part]
        return remote(spot, spot, e_sem.at[2 * sem], e_sem.at[2 * sem + 1], plane(peer(1)))

    def n_copy():
        return remote(nsend, nl, e_sem.at[4], e_sem.at[5], plane(peer(1)))

    def uf_copy():
        return remote(ul.at[z], uf.at[mine], e_sem.at[6], e_sem.at[7], partner)

    def uf_arrived():
        return remote(ul.at[z], uf.at[theirs], e_sem.at[6], e_sem.at[7], partner)

    def qp_copy():
        return remote(ql.at[z], qp, e_sem.at[8], e_sem.at[9], partner)

    def u_copy(o):
        return remote(ul.at[z], ul.at[z], u_send.at[o], u_recv.at[z], plane(peer(o)))

    def u_arrived(k):
        return remote(ul.at[k], ul.at[k], u_send.at[0], u_recv.at[k], plane(peer(1)))

    def q_copy(j):
        return remote(ql.at[z], ql.at[z], q_send.at[j], q_recv.at[z], plane(j))

    def q_arrived(k):
        return remote(ql.at[k], ql.at[k], q_send.at[0], q_recv.at[k], plane(peer(1)))

    acc[:, 0:2 * rank] = pyh[0]
    acc[:, 2 * rank:4 * rank] = pyh[1]
    hacc[...] = pyh[2]

    batch = per * piece

    def wide_columns(base, p):
        return pl.ds(pl.multiple_of(base + p * batch, 128), batch)

    def chain(p):
        ours = up[:, wide_columns(ylo * half, p)]
        other = upart[:, wide_columns(0, p)]
        grow = dot_nn(uf[:, head], jnp.where(first, ours, other))
        delta[0] = grow
        delta[1] = grow + dot_nn(uf[:, tail], jnp.where(first, other, ours))
        for j in range(per):
            c = per * p + j

            @pl.when(z > 0)
            def _():
                x_copy(c).wait_recv()

            here = columns(ylo * half, c)
            there = columns(0, c)
            lane = slice(j * piece, (j + 1) * piece)
            start = jnp.where(z > 0, xin[:, there], x0[:, here])
            x_a = (start.astype(f32) + delta[0, :, lane]).astype(bf16)
            x_b = (start.astype(f32) + delta[1, :, lane]).astype(bf16)
            xkeep[:, there] = x_b

            @pl.when(z < planes - 1)
            def _():
                x_copy(c).start()

            xpass[:, there] = jnp.where(first, x_a, start)
            pass_copy(c).start()
            xgive[:, there] = jnp.where(first, x_b, x_a)
            xout[:, here] = jnp.where(first, x_a, x_b)
            xb[:, here] = jnp.where(first, start, x_a)

    def chain_back(p):
        here = wide_columns(ylo * half, p)
        there = wide_columns(0, p)
        ours = wd[here, :]
        other = wpart[there, :]
        x_a = jnp.where(first, xb[:, here], xpass[:, there]).astype(f32)
        x_b = jnp.where(first, xpass[:, there], xb[:, here]).astype(f32)
        grow = dot_nt(qs[:, tail], jnp.where(first, other, ours)) - cpair[1, :, 0:1] * x_b
        delta[0] = grow
        delta[1] = (grow + dot_nt(qs[:, head], jnp.where(first, ours, other))
                    - cpair[0, :, 0:1] * x_a)
        for j in range(per):
            c = per * p + j

            @pl.when(z < planes - 1)
            def _():
                b_copy(c).wait_recv()

            here = columns(ylo * half, c)
            there = columns(0, c)
            lane = slice(j * piece, (j + 1) * piece)
            g_b = jnp.where(z < planes - 1, gin[:, there], g16[:, here])
            g_a = (g_b.astype(f32) + delta[0, :, lane]).astype(bf16)

            @pl.when(z > 0)
            def _():
                gkeep[:, there] = (g_b.astype(f32) + delta[1, :, lane]).astype(bf16)
                b_copy(c).start()

            ggive[:, there] = jnp.where(first, g_b, g_a)
            h_copy(c).start()
            gout[:, here] = jnp.where(first, g_a, g_b)

    def forward_own():
        @pl.when(z > 0)
        def _():
            n_copy().wait_recv()

        norm_a = jnp.where(z > 0, to_col(nl[0:1, :]), n0[:, 0:1])
        scale_a = lax.rsqrt(norm_a * (1.0 / width) + eps)
        pre_a = acc[:, 0:rank] * scale_a
        value_a, slope_a = gelu_pair(pre_a)
        u_a = value_a.astype(bf16)
        ul[z, :, head] = u_a

        @pl.when(z < planes - 1)
        def _():
            near_copy(z, head, 0).start()

        step = dot_nn(u_a, nn[z, 0:rank, rank:4 * rank])
        y_a = acc[:, 2 * rank:3 * rank]
        norm_b = norm_a + jnp.sum(u_a.astype(f32) * (2.0 * y_a + step[:, rank:2 * rank]),
                                  axis=1, keepdims=True)
        scale_b = lax.rsqrt(norm_b * (1.0 / width) + eps)
        pre_b = (acc[:, rank:2 * rank] + step[:, 0:rank]) * scale_b
        value_b, slope_b = gelu_pair(pre_b)
        u_b = value_b.astype(bf16)
        ul[z, :, tail] = u_b

        @pl.when(z < planes - 1)
        def _():
            near_copy(z, tail, 1).start()

        y_b = acc[:, 2 * rank:4 * rank] + step[:, rank:3 * rank]
        more = dot_nn(u_b, nn[z, rank:2 * rank, 2 * rank:4 * rank])
        norm_c = norm_b + jnp.sum(
            u_b.astype(f32) * (2.0 * y_b[:, rank:2 * rank] + more[:, rank:2 * rank]),
            axis=1, keepdims=True)

        @pl.when(z < planes - 1)
        def _():
            nsend[...] = jnp.broadcast_to(to_row(norm_c), nsend.shape)
            n_copy().start()

        uf_copy().start()
        for o in range(2, planes):
            u_copy(o).start()

        @pl.when(z == planes - 1)
        def _():
            u_copy(1).start()

        uf[mine, :] = ul[z]
        ys[2 * z + 1] = y_b
        acc[:, 2 * rank:4 * rank] = y_b + more
        act[:, head] = pre_a
        act[:, tail] = pre_b
        slope[:, head] = slope_a
        slope[:, tail] = slope_b
        rinv[0] = jnp.broadcast_to(scale_a, (some, rank))
        rinv[1] = jnp.broadcast_to(scale_b, (some, rank))

    def c_of(stat):
        line = stat[0:1, :].astype(f32) + stat[1:2, :].astype(f32)
        return to_col(line[:, head]), to_col(line[:, tail])

    def backward_own():
        scale_b = rinv[1]
        q_b = hacc[:, tail] * slope[:, tail]
        low_b = (q_b * scale_b).astype(bf16)
        mix_b = jnp.sum(q_b * act[:, tail], axis=1, keepdims=True) * (1.0 / width)
        c_b = mix_b * scale_b[:, 0:1] * scale_b[:, 0:1]
        h_a = hacc[:, head] + dot_nt(low_b, nn[z, 0:rank, rank:2 * rank]) - c_b * ys[2 * z + 1, :, head]
        scale_a = rinv[0]
        q_a = h_a * slope[:, head]
        mix_a = jnp.sum(q_a * act[:, head], axis=1, keepdims=True) * (1.0 / width)
        c_a = mix_a * scale_a[:, 0:1] * scale_a[:, 0:1]
        ql[z, 0:some, head] = (q_a * scale_a).astype(bf16)
        ql[z, 0:some, tail] = low_b
        spot = lax.broadcasted_iota(jnp.int32, (16, rank), 0)
        for part, col in ((head, c_a), (tail, c_b)):
            line = to_row(col)
            high = line.astype(bf16).astype(f32)
            ql[z, some:some + 16, part] = jnp.where(
                spot == 0, high, jnp.where(spot == 1, line - high, 0.0)).astype(bf16)

        def send(i, carry):
            q_copy(z - 1 - i).start()
            return carry

        lax.fori_loop(0, z, send, 0)
        qp_copy().start()

    shard = mine_u.shape[0]
    nacc[...] = jnp.zeros_like(nacc)

    def core_copy(b):
        return remote(part.at[b, 1 - core], rc.at[b], k_send.at[b], k_recv.at[b], other_core)

    def collect(b):
        block_sum(b, yh_n, x_n, core_copy, part, rc, sums, rax, rby,
                  ax_send, ax_recv, by_send, by_recv)

    def terms(b):
        cols = pl.ds(pl.multiple_of(b * 2 * shard, 128), 2 * shard)
        u = us[...]
        before = xb[:, cols]
        wide = before.astype(f32)
        nacc[...] += jnp.broadcast_to(jnp.sum(wide * wide, axis=1, keepdims=True), nacc.shape)
        g_down = dot_tn(before, qv[...]).astype(bf16)
        g_up = dot_tn(gout[:, cols], u).astype(bf16)
        for i in range(2):
            part[b, i, :, head] = g_down[i * shard:(i + 1) * shard]
            part[b, i, :, tail] = g_up[i * shard:(i + 1) * shard]
        core_copy(b).start()

    def tick(t, carry):
        k = t - 1
        sent = (k >= 0) & (k < planes)
        near = sent & (k == z - 1)

        @pl.when(sent & (k != z) & (k != z - 1))
        def _():
            u_arrived(k).wait_recv()

        @pl.when(near)
        def _():
            near_copy(k, head, 0).wait_recv()
            acc[...] += dot_nn(ul[k, :, head], nn[k, 0:rank, :])
            near_copy(k, tail, 1).wait_recv()
            acc[...] += dot_nn(ul[k, :, tail], nn[k, rank:2 * rank, :])

        @pl.when(sent & (k < z - 1))
        def _():
            acc[...] += dot_nn(ul[k], nn[k])

        @pl.when(t == z)
        def _():
            forward_own()

        @pl.when(sent & (k > z))
        def _():
            before = acc[:, 2 * rank:4 * rank]
            ys[2 * k] = before
            between = before + dot_nn(ul[k, :, head], nn[k, 0:rank, 2 * rank:4 * rank])
            ys[2 * k + 1] = between
            acc[:, 2 * rank:4 * rank] = between + dot_nn(
                ul[k, :, tail], nn[k, rank:2 * rank, 2 * rank:4 * rank])

        r = 2 * planes - t

        @pl.when((r < planes) & (r > z))
        def _():
            q_arrived(r).wait_recv()
            c_a, c_b = c_of(ql[r, some:some + 16, :])
            hacc[...] += (dot_nn(ql[r, 0:some, :], nn[r, :, 0:2 * rank]) - c_a * ys[2 * r] - c_b * ys[2 * r + 1])

        @pl.when(t == 2 * planes - 1 - z)
        def _():
            backward_own()

        p = t - (z + 1)

        @pl.when((p >= 0) & (p < trips))
        def _():
            @pl.when(p == 0)
            def _():
                for load in loads[:3]:
                    load.wait()
                uf_arrived().wait_recv()
            chain(p)

        q = t - (z + 1 + trips)

        @pl.when((q >= 0) & (q < chunks // 4))
        def _():
            for j in range(4):
                give_copy(4 * q + j).start()

        b = t - (2 * planes - z)

        @pl.when((b >= 0) & (b < trips))
        def _():
            @pl.when(b == 0)
            def _():
                for load in loads[3:]:
                    load.wait()
                qp_copy().wait_recv()
                qs[mine, :] = ql[z, 0:some, :]
                qs[theirs, :] = qp[0:some, :]
                for where, stat in ((mine, ql[z, some:some + 16, :]), (theirs, qp[some:some + 16, :])):
                    c_a, c_b = c_of(stat)
                    cpair[0, where, :] = jnp.broadcast_to(c_a, (some, rank))
                    cpair[1, where, :] = jnp.broadcast_to(c_b, (some, rank))
                us[...] = jnp.where(first, uf[:, head], uf[:, tail])
                qv[...] = jnp.where(first, qs[:, head], qs[:, tail])
            chain_back(b)
            terms(ylo * trips + b)

        @pl.when((b >= 1) & (b <= trips))
        def _():
            collect(ylo * trips + b - 1)

            def landed(j, carry):
                c = per * (b - 1) + j
                pass_arrived(c).wait_recv()
                h_arrived(c).wait_recv()
                return carry

            lax.fori_loop(0, per, landed, 0)
            terms((1 - ylo) * trips + b - 1)

        @pl.when((b >= 2) & (b <= trips))
        def _():
            collect((1 - ylo) * trips + b - 2)

        return carry

    lax.fori_loop(0, 2 * planes + trips + 1, tick, 0)
    collect((1 - ylo) * trips + trips - 1)

    total_a, total_b = scatter_sum(yh_n, x_n, sums, rax, rby, sa, ray, sb, rbx,
                                   ax_send, ax_recv, by_send, by_recv, s_sem, bx_send, bx_recv)
    cut = shard // 2
    gw[0:cut] = total_a[:, head].astype(bf16)
    gw[cut:shard] = total_b[:, head].astype(bf16)
    gu[0:cut] = total_a[:, tail].astype(bf16)
    gu[cut:shard] = total_b[:, tail].astype(bf16)
    has_next = s < sections - 1
    down_section = {"section": lax.rem(s + sections - 1, sections)}

    def pair_of(sems, i):
        return sems.at[2 * i], sems.at[2 * i + 1]

    def w_x(i):
        return remote(gw, own_w.at[yh, x, core], *pair_of(wx_sem, i), place(yh, xp(i), core))

    def w_y(i):
        spot = own_w.at[yh, xp(i), core]
        return remote(gw if i == 0 else spot, spot, *pair_of(wy_sem, i), other_y)

    def w_c(i):
        spot = own_w.at[:, xp(i), core]
        return remote(spot, spot, *pair_of(wc_sem, i), other_core)

    v_y = remote(gu, own_u.at[yh, x, core], *pair_of(vx_sem, 0), other_y)

    def v_x(i):
        spot = own_u.at[:, x, core]
        return remote(spot, spot, *pair_of(vx_sem, i), place(yh, xp(i), core))

    def v_c(i):
        spot = own_u.at[:, xp(i), core]
        return remote(spot, spot, *pair_of(vc_sem, i), other_core)

    next_copy = remote(nw, nxt_u.at[yh, x, core], *pair_of(nx_sem, 0), down_section)
    bump_copy = remote(ub, bump_u, *pair_of(nx_sem, x_n), down_section)

    def n_x(i):
        spot = nxt_u.at[yh, x, core]
        return remote(spot, spot, *pair_of(nx_sem, i), place(yh, xp(i), core))

    def n_y(i):
        spot = nxt_u.at[yh, xp(i), core]
        return remote(spot, spot, *pair_of(ny_sem, i), other_y)

    def n_c(i):
        spot = nxt_u.at[:, xp(i), core]
        return remote(spot, spot, *pair_of(nc_sem, i), other_core)

    for i in range(1, x_n):
        w_x(i).start()
    v_y.start()
    w_y(0).start()

    @pl.when(s > 0)
    def _():
        nw[...] = (mine_u[...].astype(f32) - learn_rate * gu[...].astype(f32)).astype(bf16)
        next_copy.start()

    own_w[yh, x, core] = gw[...]
    own_u[yh, x, core] = gu[...]
    v_y.wait_recv()
    for i in range(1, x_n):
        w_x(x_n - i).wait_recv()
        w_y(i).start()
    for i in range(1, x_n):
        v_x(i).start()
    v_c(0).start()

    @pl.when(has_next)
    def _():
        next_copy.wait_recv()
        for i in range(1, x_n):
            n_x(i).start()
        n_y(0).start()

    for i in range(x_n):
        w_y(i).wait_recv()
        w_c(i).start()

    @pl.when(has_next)
    def _():
        for i in range(1, x_n):
            n_x(x_n - i).wait_recv()
            n_y(i).start()

    for i in range(1, x_n):
        v_x(x_n - i).wait_recv()
        v_c(i).start()
    for i in range(x_n):
        w_c(i).wait()

    @pl.when(s > 0)
    def _():
        def ahead(b, pre):
            y_ = b // x_n
            x_ = lax.rem(b, x_n)
            cols = pl.ds(pl.multiple_of(b * 2 * shard, 128), 2 * shard)
            both = jnp.concatenate([own_w[y_, x_, 0], own_w[y_, x_, 1]], axis=0)
            fresh = wd[cols, :].astype(f32) - learn_rate * both.astype(f32)
            return pre + dot_nn(xb[:, cols], fresh.astype(bf16))

        pre = lax.fori_loop(0, yh_n * x_n, ahead, jnp.zeros((rows, rank), f32))
        value, unused = gelu_pair(pre * lax.rsqrt(nacc[...] * (1.0 / width) + eps))
        ub[...] = value.astype(bf16)
        bump_copy.start()

    @pl.when(has_next)
    def _():
        for i in range(x_n):
            n_y(i).wait_recv()
            n_c(i).start()
        for i in range(x_n):
            n_c(i).wait()
            n_y(i).wait_send()
        for i in range(1, x_n):
            n_x(i).wait_send()
        bump_copy.wait_recv()

    for i in range(x_n):
        v_c(i).wait()
        w_y(i).wait_send()
    for i in range(1, x_n):
        w_x(i).wait_send()
        v_x(i).wait_send()
    v_y.wait_send()

    @pl.when(s > 0)
    def _():
        next_copy.wait_send()
        bump_copy.wait_send()

    def core_settle(b, carry):
        core_copy(b).wait_send()
        return carry

    lax.fori_loop(0, yh_n * x_n, core_settle, 0)

    def finish(c, carry):
        @pl.when(z < planes - 1)
        def _():
            x_copy(c).wait_send()
        give_copy(c).wait_send()
        give_arrived(c).wait_recv()
        pass_copy(c).wait_send()

        @pl.when(z > 0)
        def _():
            b_copy(c).wait_send()
        h_copy(c).wait_send()
        return carry

    lax.fori_loop(0, chunks, finish, 0)
    for o in range(2, planes):
        u_copy(o).wait_send()

    @pl.when(z == planes - 1)
    def _():
        u_copy(1).wait_send()

    @pl.when(z < planes - 1)
    def _():
        near_copy(z, head, 0).wait_send()
        near_copy(z, tail, 1).wait_send()
        n_copy().wait_send()

    def settle(j, carry):
        q_copy(j).wait_send()
        return carry

    lax.fori_loop(0, z, settle, 0)
    uf_copy().wait_send()
    qp_copy().wait_send()


def recurrence(sections, shards, pyh, n0, nn, x0, g16, up, wd, upart, wpart, mine_u):
    rows, width = x0.shape
    rank = up.shape[0]
    half = width // 2
    some = rows // 2
    planes = sections // 2
    chunks = 28
    per = 7
    x_n = 4
    yh_n = shards // (2 * x_n)
    shard = mine_u.shape[0]
    cut = shard // 2
    blocks = yh_n * x_n
    vm = pl.BlockSpec(memory_space=pltpu.VMEM)
    dma = pltpu.SemaphoreType.DMA
    sq = (rows, rank)
    two = (some, 2 * rank)
    strip = pltpu.VMEM((rows, half), bf16)
    full = jax.ShapeDtypeStruct((yh_n, x_n, 2, shard, rank), bf16)

    def buf(*lead):
        return pltpu.VMEM(lead + (2 * rank,), bf16)

    return pl.pallas_call(
        functools.partial(recurrence_kernel, sections, chunks, per, yh_n, x_n),
        out_shape=(jax.ShapeDtypeStruct((rows, width), bf16), full, full, full,
                   jax.ShapeDtypeStruct(sq, bf16)),
        in_specs=[vm] * 3 + [pl.BlockSpec(memory_space=pl.ANY)] * 6 + [vm],
        out_specs=(vm,) * 5,
        scratch_shapes=[
            pltpu.VMEM((planes,) + two, bf16),
            pltpu.VMEM((planes, some + 16, 2 * rank), bf16),
            pltpu.VMEM((some + 16, 2 * rank), bf16),
            pltpu.VMEM((sections,) + two, f32),
            pltpu.VMEM((8, rank), f32),
            pltpu.VMEM((8, rank), f32),
            pltpu.VMEM((some, 4 * rank), f32),
            pltpu.VMEM(two, f32), pltpu.VMEM(two, f32), pltpu.VMEM(two, f32),
            pltpu.VMEM((2, some, rank), f32),
            pltpu.VMEM((rows, 2 * rank), bf16),
            pltpu.VMEM((rows, 2 * rank), bf16),
            pltpu.VMEM((2,) + sq, f32),
            strip, strip, strip, strip, strip, strip, strip,
            pltpu.VMEM((2, rows, half * per // chunks), f32),
            pltpu.VMEM((rows, width), bf16),
            pltpu.VMEM(sq, bf16), pltpu.VMEM(sq, bf16),
            pltpu.VMEM((rows, width), bf16), pltpu.VMEM(sq, f32),
            buf(blocks, 2, shard), buf(blocks, shard), buf(yh_n, x_n, shard),
            buf(x_n - 1, yh_n, cut), buf(x_n, cut), buf(yh_n, cut), buf(cut),
            buf(x_n, cut), buf(x_n - 1, cut),
            pltpu.VMEM((shard, rank), bf16), pltpu.VMEM((shard, rank), bf16),
            pltpu.VMEM((shard, rank), bf16), pltpu.VMEM(sq, bf16),
            pltpu.VMEM((rows, width), bf16), pltpu.VMEM((rows, width), bf16),
            pltpu.VMEM((rank, width), bf16), pltpu.VMEM((width, rank), bf16),
            pltpu.VMEM((rank, half), bf16), pltpu.VMEM((half, rank), bf16), dma((6,)),
        ] + [dma((planes,))] * 4 + [dma((10,))] + [dma((chunks,))] * 10 + [
            dma((blocks,)), dma((blocks,)),
            dma((yh_n * (x_n - 1),)), dma((yh_n * (x_n - 1),)), dma((x_n,)), dma((x_n,)), dma((2,)),
            dma((x_n - 1,)), dma((x_n - 1,)),
            dma((2 * x_n,)), dma((2 * x_n,)), dma((2 * x_n,)), dma((2 * x_n,)), dma((2 * x_n,)),
            dma((2 * x_n + 2,)), dma((2 * x_n,)), dma((2 * x_n,)),
        ],
        compiler_params=pltpu.CompilerParams(
            collective_id=1, has_side_effects=True, vmem_limit_bytes=60 * 1024 * 1024),
    )(pyh, n0, nn, x0, g16, up, wd, upart, wpart, mine_u)


def dp_place(x_n):
    d = lax.axis_index("dp")
    return d // (2 * x_n), lax.rem(d // 2, x_n), lax.rem(d, 2)


def remote(src, dst, send, recv, where):
    return pltpu.make_async_remote_copy(src_ref=src, dst_ref=dst, send_sem=send, recv_sem=recv,
                                        device_id=where, device_id_type=MESH)


def block_sum(b, yh_n, x_n, core_copy, part, rc, sums, rax, rby, ax_send, ax_recv, by_send, by_recv):
    yh, x, core = dp_place(x_n)
    cut = sums.shape[2] // 2
    y_ = b // x_n
    x_ = lax.rem(b, x_n)
    core_copy(b).wait_recv()
    sums[y_, x_] = (part[b, core].astype(f32) + rc[b].astype(f32)).astype(bf16)
    turn = lax.rem(x_ - x + x_n, x_n)

    @pl.when(turn != 0)
    def _():
        sem = (turn - 1) * yh_n + y_
        remote(sums.at[y_, x_, 0:cut], rax.at[turn - 1, y_], ax_send.at[sem], ax_recv.at[sem],
               {"dp": (yh * x_n + x_) * 2 + core}).start()

    @pl.when(y_ != yh)
    def _():
        remote(sums.at[y_, x_, cut:2 * cut], rby.at[x_], by_send.at[x_], by_recv.at[x_],
               {"dp": (y_ * x_n + x) * 2 + core}).start()


def scatter_sum(yh_n, x_n, sums, rax, rby, sa, ray, sb, rbx,
                ax_send, ax_recv, by_send, by_recv, s_sem, bx_send, bx_recv):
    yh, x, core = dp_place(x_n)
    rows = sums.shape[2]
    cut = rows // 2

    def place(y_, x_, c_):
        return {"dp": (y_ * x_n + x_) * 2 + c_}

    def xp(i):
        return lax.rem(x + i, x_n)

    other_y = place(1 - yh, x, core)

    def ax_copy(i, y_):
        sem = (i - 1) * yh_n + y_
        return remote(sums.at[y_, xp(i), 0:cut], rax.at[i - 1, y_], ax_send.at[sem], ax_recv.at[sem],
                      place(yh, xp(i), core))

    def by_copy(x_):
        return remote(sums.at[1 - yh, x_, cut:rows], rby.at[x_], by_send.at[x_], by_recv.at[x_], other_y)

    def bx_copy(i):
        return remote(sb.at[xp(i)], rbx.at[i - 1], bx_send.at[i - 1], bx_recv.at[i - 1],
                      place(yh, xp(i), core))

    ay_copy = remote(sa.at[1 - yh], ray, s_sem.at[0], s_sem.at[1], other_y)

    for i in range(x_n):
        x_ = xp(i)
        by_copy(x_).wait_recv()
        sb[x_] = (sums[yh, x_, cut:rows].astype(f32) + rby[x_].astype(f32)).astype(bf16)
        if i > 0:
            bx_copy(i).start()
    for y_ in range(yh_n):
        total = sums[y_, x, 0:cut].astype(f32)
        for i in range(1, x_n):
            ax_copy(i, y_).wait_recv()
            total = total + rax[i - 1, y_].astype(f32)
        sa[y_] = total.astype(bf16)
    ay_copy.start()
    total_b = sb[x].astype(f32)
    for i in range(1, x_n):
        bx_copy(i).wait_recv()
        total_b = total_b + rbx[i - 1].astype(f32)
    ay_copy.wait_recv()
    total_a = sa[yh].astype(f32) + ray[...].astype(f32)
    for i in range(1, x_n):
        for y_ in range(yh_n):
            ax_copy(i, y_).wait_send()
        bx_copy(i).wait_send()
    for x_ in range(x_n):
        by_copy(x_).wait_send()
    ay_copy.wait_send()
    return total_a, total_b


def gram_kernel(yh_n, x_n, sections, x0_far, g16_far, down_far, up_far, mine_u, base, pyh, n0, out, upart, wpart,
                allu, part, rc, sums, rax, rby, sa, ray, sb, rbx, gs, gp, two, mine3, theirs3, flip, turned,
                x0, g16, down, up, l_sem,
                z_sem, f_send, f_recv, r_send, r_recv,
                c_send, c_recv, ax_send, ax_recv, by_send, by_recv, s_sem, bx_send, bx_recv,
                ga_send, ga_recv, gb_send, gb_recv, gc_send, gc_recv, t_sem):
    loads = [pltpu.make_async_copy(far, near, l_sem.at[i]) for i, (far, near) in enumerate((
        (up_far, up), (down_far, down), (x0_far, x0), (g16_far, g16)))]
    for load in loads:
        load.start()
    yh, x, core = dp_place(x_n)
    s = lax.axis_index("section")
    z_n = sections // 2
    z = s // 2
    ylo = lax.rem(s, 2)
    rank = up.shape[0]
    rows = rank
    cut = rows // 2

    def place(y_, x_, c_):
        return {"dp": (y_ * x_n + x_) * 2 + c_}

    def xp(i):
        return lax.rem(x + i, x_n)

    def zp(i):
        return lax.rem(z + i, z_n)

    other_core = place(yh, x, 1 - core)
    other_y = place(1 - yh, x, core)
    partner = {"section": s + 1 - 2 * ylo}
    after = {"section": 2 * zp(1) + ylo}
    before = {"section": 2 * zp(z_n - 1) + ylo}

    barrier = pltpu.get_barrier_semaphore()
    peers = [other_core, other_y, partner, after, before]
    peers += [place(yh, xp(i), core) for i in range(1, x_n)]
    for where in peers:
        pl.semaphore_signal(barrier, inc=1, device_id=where, device_id_type=MESH)
    d = lax.axis_index("dp")
    above = d // 2 < z
    below = d // 2 > z
    mirror = [{"section": 2 * (d // 2) + i, "dp": s} for i in range(2)]

    @pl.when(below)
    def _():
        for i in range(2):
            pl.semaphore_signal(barrier, inc=1, device_id={"section": d, "dp": 2 * z + i},
                                device_id_type=MESH)

    pl.semaphore_wait(barrier, len(peers) + 2 * above.astype(jnp.int32))

    def flip_copy(i):
        k = lax.rem(d, 2)
        return remote(flip, turned.at[k], t_sem.at[i], t_sem.at[2 + k], mirror[i])

    def flip_arrived(i):
        return remote(flip, turned.at[i], t_sem.at[0], t_sem.at[2 + i], mirror[0])

    pair = remote(mine_u, allu.at[z, ylo], z_sem.at[0], z_sem.at[1], partner)

    def products(z_):
        for y_ in range(2):
            part[z_, y_] = dot_tn(allu[z_, y_], base[...]).astype(bf16)

    def core_copy(b):
        return remote(part.at[b, 1 - core], rc.at[b], c_send.at[b], c_recv.at[b], other_core)

    hops = z_n // 2

    def column(j):
        return ylo if j == 0 else 1 - ylo

    def ring_f(i, j):
        spot = allu.at[zp(z_n + 1 - i), column(j)]
        src = mine_u if (i == 1 and j == 0) else spot
        sem = 2 * (i - 1) + j
        return remote(src, spot, f_send.at[sem], f_recv.at[sem], after)

    def ring_r(i, j):
        spot = allu.at[zp(i - 1), column(j)]
        src = mine_u if (i == 1 and j == 0) else spot
        sem = 2 * (i - 1) + j
        return remote(src, spot, r_send.at[sem], r_recv.at[sem], before)

    used_f = [(i, j) for i in range(1, hops + 1) for j in range(2) if i < hops or j == 0]
    used_r = [(i, j) for i in range(1, hops + 1) for j in range(2) if i < hops or j == 1]

    pair.start()
    ring_f(1, 0).start()
    ring_r(1, 0).start()
    allu[z, ylo] = mine_u[...]
    pair.wait_recv()
    ring_f(1, 1).start()
    ring_r(1, 1).start()

    half = x0.shape[1] // 2
    quarter = half // 2
    far = pl.ds(pl.multiple_of((1 - ylo) * half + core * quarter, 128), quarter)
    near = pl.ds(pl.multiple_of(core * quarter, 128), quarter)
    swap_u = remote(up.at[:, far], upart.at[:, near], z_sem.at[6], z_sem.at[7], partner)
    swap_w = remote(down.at[far, :], wpart.at[near, :], z_sem.at[8], z_sem.at[9], partner)
    share_u = remote(upart.at[:, near], upart.at[:, near], z_sem.at[10], z_sem.at[11], other_core)
    share_w = remote(wpart.at[near, :], wpart.at[near, :], z_sem.at[12], z_sem.at[13], other_core)
    for load in loads:
        load.wait()
    swap_u.start()
    swap_w.start()

    u = up[...]
    w = down[...]
    values = x0[...]
    token_half = x0.shape[0] // 2
    keep = pl.ds(ylo * token_half, token_half)
    give = pl.ds((1 - ylo) * token_half, token_half)
    mine3[0] = dot_nn(values, w)
    mine3[1] = dot_nt(values, u)
    mine3[2] = dot_nt(g16[...], u)
    swap3 = remote(mine3.at[:, give], theirs3, z_sem.at[2], z_sem.at[3], partner)
    swap3.start()
    wide = x0[keep, :].astype(f32)
    n0[...] = jnp.broadcast_to(jnp.sum(wide * wide, axis=1, keepdims=True), n0.shape)

    def collect(b):
        block_sum(b, yh_n, x_n, core_copy, part, rc, sums, rax, rby,
                  ax_send, ax_recv, by_send, by_recv)

    products(z)
    core_copy(z).start()
    for i in range(1, hops + 1):
        for j in range(2):
            if (i, j) in used_f:
                ring_f(i, j).wait_recv()
                if (i + 1, j) in used_f:
                    ring_f(i + 1, j).start()
            if (i, j) in used_r:
                ring_r(i, j).wait_recv()
                if (i + 1, j) in used_r:
                    ring_r(i + 1, j).start()
        products(zp(z_n - i))
        core_copy(zp(z_n - i)).start()
        if i == 1:
            collect(z)
        else:
            collect(zp(i - 1))
        if i < hops:
            products(zp(i))
            core_copy(zp(i)).start()
        collect(zp(z_n - i))

    swap_u.wait_recv()
    share_u.start()
    swap_w.wait_recv()
    share_w.start()
    total_a, total_b = scatter_sum(yh_n, x_n, sums, rax, rby, sa, ray, sb, rbx,
                                   ax_send, ax_recv, by_send, by_recv, s_sem, bx_send, bx_recv)
    gs[0:cut] = total_a.astype(bf16)
    gs[cut:rows] = total_b.astype(bf16)
    swap = remote(gs, gp, z_sem.at[4], z_sem.at[5], partner)
    swap.start()

    @pl.when(above)
    def _():
        flip[...] = gs[:, 0:rank].astype(f32).T.astype(bf16)
        for i in range(2):
            flip_copy(i).start()

    def lanes(base, which):
        return pl.ds(pl.multiple_of(base + which * rank, 128), rank)

    swap3.wait_recv()
    pyh[:, :, lanes(0, ylo)] = mine3[:, keep]
    pyh[:, :, lanes(0, 1 - ylo)] = theirs3[...]
    two[:, lanes(0, ylo)] = gs[:, 0:rank]
    two[:, lanes(2 * rank, ylo)] = gs[:, rank:2 * rank]
    swap.wait_recv()
    two[:, lanes(0, 1 - ylo)] = gp[:, 0:rank]
    two[:, lanes(2 * rank, 1 - ylo)] = gp[:, rank:2 * rank]

    @pl.when(below)
    def _():
        for i in range(2):
            flip_arrived(i).wait_recv()
            two[:, i * rank:(i + 1) * rank] = turned[i]
    out[yh, x, core] = two[...]

    low = pl.ds(0, cut)
    high = pl.ds(cut, cut)

    def spread(src, spot, sems, i, where):
        return remote(src, spot, sems[0].at[i], sems[1].at[i], where)

    ga = (ga_send, ga_recv)
    gb = (gb_send, gb_recv)
    a_y = spread(two.at[low], out.at[yh, x, core, low], ga, 0, other_y)

    def a_x(i):
        spot = out.at[:, x, core, low]
        return spread(spot, spot, ga, i, place(yh, xp(i), core))

    def b_x(i):
        return spread(two.at[high], out.at[yh, x, core, high], gb, i - 1, place(yh, xp(i), core))

    def b_y(i):
        spot = out.at[yh, xp(i), core, high]
        return spread(spot, spot, gb, x_n - 1 + i, other_y)

    def all_c(i):
        spot = out.at[:, xp(i), core]
        return remote(spot, spot, gc_send.at[i], gc_recv.at[i], other_core)

    a_y.start()
    for i in range(1, x_n):
        b_x(i).start()
    b_y(0).start()
    a_y.wait_recv()
    for i in range(1, x_n):
        a_x(i).start()
    for i in range(1, x_n):
        b_x(x_n - i).wait_recv()
        b_y(i).start()
    b_y(0).wait_recv()
    all_c(0).start()
    for i in range(1, x_n):
        a_x(x_n - i).wait_recv()
        b_y(i).wait_recv()
        all_c(i).start()
    for i in range(x_n):
        all_c(i).wait()
        b_y(i).wait_send()
    for i in range(1, x_n):
        a_x(i).wait_send()
        b_x(i).wait_send()
    a_y.wait_send()
    pair.wait_send()
    swap.wait_send()
    swap3.wait_send()

    @pl.when(above)
    def _():
        for i in range(2):
            flip_copy(i).wait_send()
    swap_u.wait_send()
    swap_w.wait_send()
    share_u.wait()
    share_w.wait()
    for i, j in used_f:
        ring_f(i, j).wait_send()
    for i, j in used_r:
        ring_r(i, j).wait_send()

    def settle(b, carry):
        core_copy(b).wait_send()
        return carry

    lax.fori_loop(0, yh_n * x_n, settle, 0)


def grams_of(sections, shards, x0, g16, down, up, mine_u, base):
    x_n = 4
    yh_n = shards // (2 * x_n)
    rows, width = x0.shape
    rank = up.shape[0]
    height = mine_u.shape[0]
    cut = rank // 2
    vm = pl.BlockSpec(memory_space=pltpu.VMEM)
    dma = pltpu.SemaphoreType.DMA

    def buf(*lead):
        return pltpu.VMEM(lead + (2 * rank,), bf16)

    return pl.pallas_call(
        functools.partial(gram_kernel, yh_n, x_n, sections),
        out_shape=(
            jax.ShapeDtypeStruct((3, rows // 2, 2 * rank), f32),
            jax.ShapeDtypeStruct((rows // 2, rank), f32),
            jax.ShapeDtypeStruct((yh_n, x_n, 2, rank, 4 * rank), bf16),
            jax.ShapeDtypeStruct((rank, width // 2), bf16),
            jax.ShapeDtypeStruct((width // 2, rank), bf16),
        ),
        in_specs=[pl.BlockSpec(memory_space=pl.ANY)] * 4 + [vm] * 2,
        out_specs=(vm,) * 5,
        scratch_shapes=[
            pltpu.VMEM((sections // 2, 2, height, rank), bf16),
            buf(yh_n * x_n, 2, rank), buf(yh_n * x_n, rank), buf(yh_n, x_n, rank),
            buf(x_n - 1, yh_n, cut), buf(x_n, cut), buf(yh_n, cut), buf(cut),
            buf(x_n, cut), buf(x_n - 1, cut), buf(rank), buf(rank),
            pltpu.VMEM((rank, 4 * rank), bf16),
            pltpu.VMEM((3, rows, rank), f32), pltpu.VMEM((3, rows // 2, rank), f32),
            pltpu.VMEM((rank, rank), bf16), pltpu.VMEM((2, rank, rank), bf16),
            pltpu.VMEM((rows, width), bf16), pltpu.VMEM((rows, width), bf16),
            pltpu.VMEM((width, rank), bf16), pltpu.VMEM((rank, width), bf16), dma((4,)),
            dma((14,)), dma((sections // 2,)), dma((sections // 2,)),
            dma((sections // 2,)), dma((sections // 2,)),
            dma((yh_n * x_n,)), dma((yh_n * x_n,)),
            dma((yh_n * (x_n - 1),)), dma((yh_n * (x_n - 1),)), dma((x_n,)), dma((x_n,)), dma((4,)),
            dma((x_n - 1,)), dma((x_n - 1,)),
            dma((x_n,)), dma((x_n,)), dma((2 * x_n,)), dma((2 * x_n,)), dma((x_n,)), dma((x_n,)), dma((4,)),
        ],
        compiler_params=pltpu.CompilerParams(
            collective_id=3, has_side_effects=True, vmem_limit_bytes=60 * 1024 * 1024),
    )(x0, g16, down, up, mine_u, base)


def finish_kernel(sections, own_w, own_u, nxt_u, bump_u, x1, grad_down, grad_up, advance):
    last = lax.axis_index("section") == sections - 1
    grad_down[...] = own_w[...]
    grad_up[...] = own_u[...].astype(f32).T.astype(bf16)
    bump = dot_nt(bump_u[...], nxt_u[...])
    advance[...] = (x1[...].astype(f32) + jnp.where(last, 0.0, bump)).astype(bf16)


def finish(sections, own_w, own_u, nxt_u, bump_u, x1):
    rows, width = x1.shape
    rank = own_w.shape[1]
    step = width // 4
    tall = pl.BlockSpec((step, rank), lambda i: (i, 0))
    flat = pl.BlockSpec((rows, step), lambda i: (0, i))
    return pl.pallas_call(
        functools.partial(finish_kernel, sections),
        grid=(width // step,),
        out_shape=(
            jax.ShapeDtypeStruct((width, rank), bf16),
            jax.ShapeDtypeStruct((rank, width), bf16),
            jax.ShapeDtypeStruct((rows, width), bf16),
        ),
        in_specs=[tall, tall, tall, pl.BlockSpec((rows, rank), lambda i: (0, 0)), flat],
        out_specs=(tall, flat, flat),
        compiler_params=pltpu.CompilerParams(vmem_limit_bytes=60 * 1024 * 1024),
    )(own_w, own_u, nxt_u, bump_u, x1)


def per_device(inputs, cotangent, w_down, w_up):
    down = w_down[0]
    upward = w_up[0]
    micro, batch_rows, width = inputs.shape
    rank = down.shape[1]
    rows = micro * batch_rows
    sections = lax.axis_size("section")
    shards = lax.axis_size("dp")
    part = width // shards
    d = lax.axis_index("dp")
    x0 = inputs.reshape(rows, width)
    g16 = cotangent.reshape(rows, width)
    up_t = upward.T

    mine_u = lax.dynamic_slice_in_dim(up_t, d * part, part, 0)
    mine_w = lax.dynamic_slice_in_dim(down, d * part, part, 0)
    base = jnp.concatenate([mine_w, mine_u], axis=1)
    pyh, n0, grams, upart, wpart = grams_of(sections, shards, x0, g16, down, upward, mine_u, base)
    grams = grams.reshape(sections // 2, 2 * rank, 4 * rank)
    x1, own_w, own_u, nxt_u, bump_u = recurrence(
        sections, shards, pyh, n0, grams, x0, g16, upward, down, upart, wpart, mine_u)
    tall = (width, rank)
    grad_down, grad_up, advance = finish(
        sections, own_w.reshape(tall), own_u.reshape(tall), nxt_u.reshape(tall), bump_u, x1)
    return (grad_down[None], grad_up[None], advance.reshape(1, micro, batch_rows, width))


def solution(mesh):
    in_specs = (
        P(None, "dp", None),
        P(None, "dp", None),
        P("section", None, None),
        P("section", None, None),
    )
    out_specs = (P("section", None, None), P("section", None, None), P("section", None, "dp", None))
    return jax.shard_map(
        per_device, mesh=mesh, in_specs=in_specs, out_specs=out_specs, check_vma=False
    )
```

```python
import functools

import jax
import jax.numpy as jnp
from jax import lax
from jax.experimental import pallas as pl
from jax.experimental.pallas import tpu as pltpu
from jax.sharding import PartitionSpec as P

MESH = pl.DeviceIdType.MESH
eps = 1e-05
learn_rate = 0.05
f32 = jnp.float32
bf16 = jnp.bfloat16


def dot_nn(a, b):
    return jnp.dot(a, b, preferred_element_type=f32)


def dot_tn(a, b):
    return lax.dot_general(a, b, (((0,), (0,)), ((), ())), preferred_element_type=f32)


def dot_nt(a, b):
    return lax.dot_general(a, b, (((1,), (1,)), ((), ())), preferred_element_type=f32)


def gelu_pair(a):
    c = 0.7978845608028654
    inner = c * (a + 0.044715 * a * a * a)
    th = jnp.tanh(inner)
    value = 0.5 * a * (1.0 + th)
    slope = 0.5 * (1.0 + th) + 0.5 * a * (1.0 - th * th) * c * (1.0 + 3 * 0.044715 * a * a)
    return value, slope


def recurrence_kernel(sections, chunks, per, yh_n, x_n,
                      pyh, n0, nn, x0_far, g16_far, up_far, wd_far, upart_far, wpart_far, mine_u,
                      xout_far, own_w_far, own_u, nxt_u, bump_u,
                      ul, ql, qp, ys, nl, nsend, acc, hacc, slope, act, rinv, uf, qs, cpair,
                      xin, xkeep, xgive, gin, gkeep, ggive, xpass, delta,
                      gout, us, qv, xb, nacc, part, rc, sums, rax, rby, sa, ray, sb, rbx,
                      gw, gu, nw, ub, x0, g16, up, wd, upart, wpart, xout, own_w, l_sem,
                      u_send, u_recv, q_send, q_recv, e_sem,
                      c_send, c_recv, g_send, g_recv,
                      b_send, b_recv, h_send, h_recv, p_send, p_recv,
                      k_send, k_recv, ax_send, ax_recv, by_send, by_recv, s_sem, bx_send, bx_recv,
                      wx_sem, wy_sem, wc_sem, vx_sem, vc_sem, nx_sem, ny_sem, nc_sem):
    loads = [pltpu.make_async_copy(far, near, l_sem.at[i]) for i, (far, near) in enumerate((
        (up_far, up), (upart_far, upart), (x0_far, x0),
        (wd_far, wd), (wpart_far, wpart), (g16_far, g16)))]
    for load in loads:
        load.start()
    s = lax.axis_index("section")
    yh, x, core = dp_place(x_n)
    planes = sections // 2
    rows, width = x0.shape
    some = rows // 2
    rank = up.shape[0]
    half = width // 2
    piece = half // chunks
    trips = chunks // per
    z = s // 2
    ylo = lax.rem(s, 2)
    first = ylo == 0
    partner = {"section": s + 1 - 2 * ylo}
    head = slice(0, rank)
    tail = slice(rank, 2 * rank)
    mine = pl.ds(ylo * some, some)
    theirs = pl.ds((1 - ylo) * some, some)

    def plane(i):
        return {"section": 2 * i + ylo}

    def peer(offset):
        return lax.rem(z + offset, planes)

    barrier = pltpu.get_barrier_semaphore()
    for o in range(1, planes):
        pl.semaphore_signal(barrier, inc=1, device_id=plane(peer(o)), device_id_type=MESH)

    def place(y_, x_, c_):
        return {"dp": (y_ * x_n + x_) * 2 + c_}

    def xp(i):
        return lax.rem(x + i, x_n)

    other_core = place(yh, x, 1 - core)
    other_y = place(1 - yh, x, core)
    beyond = {"section": lax.rem(s + sections - 1 + 2 * ylo, sections)}
    others = [partner, beyond, other_core, other_y] + [place(yh, xp(i), core) for i in range(1, x_n)]
    for where in others:
        pl.semaphore_signal(barrier, inc=1, device_id=where, device_id_type=MESH)
    pl.semaphore_wait(barrier, planes - 1 + len(others))

    eye = (lax.broadcasted_iota(jnp.int32, (some, rank), 0)
           == lax.broadcasted_iota(jnp.int32, (some, rank), 1)).astype(f32)

    def to_row(col):
        return jnp.sum(eye * col, axis=0, keepdims=True)

    def to_col(row):
        return jnp.sum(eye * row, axis=1, keepdims=True)

    def columns(base, c):
        return pl.ds(pl.multiple_of(base + c * piece, 128), piece)

    def x_copy(c):
        return remote(xkeep.at[:, columns(0, c)], xin.at[:, columns(0, c)],
                      c_send.at[c], c_recv.at[c], plane(peer(1)))

    def b_copy(c):
        return remote(gkeep.at[:, columns(0, c)], gin.at[:, columns(0, c)],
                      b_send.at[c], b_recv.at[c], plane(peer(planes - 1)))

    def give_copy(c):
        return remote(xgive.at[:, columns(0, c)], xout.at[:, columns(ylo * half, c)],
                      g_send.at[c], g_recv.at[c], partner)

    def give_arrived(c):
        return remote(xgive.at[:, columns(0, c)], xout.at[:, columns((1 - ylo) * half, c)],
                      g_send.at[c], g_recv.at[c], partner)

    def pass_copy(c):
        return remote(xpass.at[:, columns(0, c)], xb.at[:, columns(ylo * half, c)],
                      p_send.at[c], p_recv.at[c], partner)

    def pass_arrived(c):
        return remote(xpass.at[:, columns(0, c)], xb.at[:, columns((1 - ylo) * half, c)],
                      p_send.at[c], p_recv.at[c], partner)

    def h_copy(c):
        return remote(ggive.at[:, columns(0, c)], gout.at[:, columns(ylo * half, c)],
                      h_send.at[c], h_recv.at[c], partner)

    def h_arrived(c):
        return remote(ggive.at[:, columns(0, c)], gout.at[:, columns((1 - ylo) * half, c)],
                      h_send.at[c], h_recv.at[c], partner)

    def near_copy(k, part, sem):
        spot = ul.at[k, :, part]
        return remote(spot, spot, e_sem.at[2 * sem], e_sem.at[2 * sem + 1], plane(peer(1)))

    def n_copy():
        return remote(nsend, nl, e_sem.at[4], e_sem.at[5], plane(peer(1)))

    def uf_copy():
        return remote(ul.at[z], uf.at[mine], e_sem.at[6], e_sem.at[7], partner)

    def uf_arrived():
        return remote(ul.at[z], uf.at[theirs], e_sem.at[6], e_sem.at[7], partner)

    def qp_copy():
        return remote(ql.at[z], qp, e_sem.at[8], e_sem.at[9], partner)

    def u_copy(o):
        return remote(ul.at[z], ul.at[z], u_send.at[o], u_recv.at[z], plane(peer(o)))

    def u_arrived(k):
        return remote(ul.at[k], ul.at[k], u_send.at[0], u_recv.at[k], plane(peer(1)))

    def q_copy(j):
        return remote(ql.at[z], ql.at[z], q_send.at[j], q_recv.at[z], plane(j))

    def q_arrived(k):
        return remote(ql.at[k], ql.at[k], q_send.at[0], q_recv.at[k], plane(peer(1)))

    acc[:, 0:2 * rank] = pyh[0]
    acc[:, 2 * rank:4 * rank] = pyh[1]
    hacc[...] = pyh[2]

    batch = per * piece

    def wide_columns(base, p):
        return pl.ds(pl.multiple_of(base + p * batch, 128), batch)

    def chain(p):
        ours = up[:, wide_columns(ylo * half, p)]
        other = upart[:, wide_columns(0, p)]
        grow = dot_nn(uf[:, head], jnp.where(first, ours, other))
        delta[0] = grow
        delta[1] = grow + dot_nn(uf[:, tail], jnp.where(first, other, ours))
        for j in range(per):
            c = per * p + j

            @pl.when(z > 0)
            def _():
                x_copy(c).wait_recv()

            here = columns(ylo * half, c)
            there = columns(0, c)
            lane = slice(j * piece, (j + 1) * piece)
            start = jnp.where(z > 0, xin[:, there], x0[:, here])
            x_a = (start.astype(f32) + delta[0, :, lane]).astype(bf16)
            x_b = (start.astype(f32) + delta[1, :, lane]).astype(bf16)
            xkeep[:, there] = x_b

            @pl.when(z < planes - 1)
            def _():
                x_copy(c).start()

            xpass[:, there] = jnp.where(first, x_a, start)
            pass_copy(c).start()
            xgive[:, there] = jnp.where(first, x_b, x_a)
            xout[:, here] = jnp.where(first, x_a, x_b)
            xb[:, here] = jnp.where(first, start, x_a)

    def chain_back(p):
        here = wide_columns(ylo * half, p)
        there = wide_columns(0, p)
        ours = wd[here, :]
        other = wpart[there, :]
        x_a = jnp.where(first, xb[:, here], xpass[:, there]).astype(f32)
        x_b = jnp.where(first, xpass[:, there], xb[:, here]).astype(f32)
        grow = dot_nt(qs[:, tail], jnp.where(first, other, ours)) - cpair[1, :, 0:1] * x_b
        delta[0] = grow
        delta[1] = (grow + dot_nt(qs[:, head], jnp.where(first, ours, other))
                    - cpair[0, :, 0:1] * x_a)
        for j in range(per):
            c = per * p + j

            @pl.when(z < planes - 1)
            def _():
                b_copy(c).wait_recv()

            here = columns(ylo * half, c)
            there = columns(0, c)
            lane = slice(j * piece, (j + 1) * piece)
            g_b = jnp.where(z < planes - 1, gin[:, there], g16[:, here])
            g_a = (g_b.astype(f32) + delta[0, :, lane]).astype(bf16)

            @pl.when(z > 0)
            def _():
                gkeep[:, there] = (g_b.astype(f32) + delta[1, :, lane]).astype(bf16)
                b_copy(c).start()

            ggive[:, there] = jnp.where(first, g_b, g_a)
            h_copy(c).start()
            gout[:, here] = jnp.where(first, g_a, g_b)

    def forward_own():
        @pl.when(z > 0)
        def _():
            n_copy().wait_recv()

        norm_a = jnp.where(z > 0, to_col(nl[0:1, :]), n0[:, 0:1])
        scale_a = lax.rsqrt(norm_a * (1.0 / width) + eps)
        pre_a = acc[:, 0:rank] * scale_a
        value_a, slope_a = gelu_pair(pre_a)
        u_a = value_a.astype(bf16)
        ul[z, :, head] = u_a

        @pl.when(z < planes - 1)
        def _():
            near_copy(z, head, 0).start()

        step = dot_nn(u_a, nn[z, 0:rank, rank:4 * rank])
        y_a = acc[:, 2 * rank:3 * rank]
        norm_b = norm_a + jnp.sum(u_a.astype(f32) * (2.0 * y_a + step[:, rank:2 * rank]),
                                  axis=1, keepdims=True)
        scale_b = lax.rsqrt(norm_b * (1.0 / width) + eps)
        pre_b = (acc[:, rank:2 * rank] + step[:, 0:rank]) * scale_b
        value_b, slope_b = gelu_pair(pre_b)
        u_b = value_b.astype(bf16)
        ul[z, :, tail] = u_b

        @pl.when(z < planes - 1)
        def _():
            near_copy(z, tail, 1).start()

        y_b = acc[:, 2 * rank:4 * rank] + step[:, rank:3 * rank]
        more = dot_nn(u_b, nn[z, rank:2 * rank, 2 * rank:4 * rank])
        norm_c = norm_b + jnp.sum(
            u_b.astype(f32) * (2.0 * y_b[:, rank:2 * rank] + more[:, rank:2 * rank]),
            axis=1, keepdims=True)

        @pl.when(z < planes - 1)
        def _():
            nsend[...] = jnp.broadcast_to(to_row(norm_c), nsend.shape)
            n_copy().start()

        uf_copy().start()
        for o in range(2, planes):
            u_copy(o).start()

        @pl.when(z == planes - 1)
        def _():
            u_copy(1).start()

        uf[mine, :] = ul[z]
        ys[2 * z + 1] = y_b
        acc[:, 2 * rank:4 * rank] = y_b + more
        act[:, head] = pre_a
        act[:, tail] = pre_b
        slope[:, head] = slope_a
        slope[:, tail] = slope_b
        rinv[0] = jnp.broadcast_to(scale_a, (some, rank))
        rinv[1] = jnp.broadcast_to(scale_b, (some, rank))

    def c_of(stat):
        line = stat[0:1, :].astype(f32) + stat[1:2, :].astype(f32)
        return to_col(line[:, head]), to_col(line[:, tail])

    def backward_own():
        scale_b = rinv[1]
        q_b = hacc[:, tail] * slope[:, tail]
        low_b = (q_b * scale_b).astype(bf16)
        mix_b = jnp.sum(q_b * act[:, tail], axis=1, keepdims=True) * (1.0 / width)
        c_b = mix_b * scale_b[:, 0:1] * scale_b[:, 0:1]
        h_a = hacc[:, head] + dot_nt(low_b, nn[z, 0:rank, rank:2 * rank]) - c_b * ys[2 * z + 1, :, head]
        scale_a = rinv[0]
        q_a = h_a * slope[:, head]
        mix_a = jnp.sum(q_a * act[:, head], axis=1, keepdims=True) * (1.0 / width)
        c_a = mix_a * scale_a[:, 0:1] * scale_a[:, 0:1]
        ql[z, 0:some, head] = (q_a * scale_a).astype(bf16)
        ql[z, 0:some, tail] = low_b
        spot = lax.broadcasted_iota(jnp.int32, (16, rank), 0)
        for part, col in ((head, c_a), (tail, c_b)):
            line = to_row(col)
            high = line.astype(bf16).astype(f32)
            ql[z, some:some + 16, part] = jnp.where(
                spot == 0, high, jnp.where(spot == 1, line - high, 0.0)).astype(bf16)

        def send(i, carry):
            q_copy(z - 1 - i).start()
            return carry

        lax.fori_loop(0, z, send, 0)
        qp_copy().start()

    shard = mine_u.shape[0]
    nacc[...] = jnp.zeros_like(nacc)

    def core_copy(b):
        return remote(part.at[b, 1 - core], rc.at[b], k_send.at[b], k_recv.at[b], other_core)

    def collect(b):
        block_sum(b, yh_n, x_n, core_copy, part, rc, sums, rax, rby,
                  ax_send, ax_recv, by_send, by_recv)

    def terms(b):
        cols = pl.ds(pl.multiple_of(b * 2 * shard, 128), 2 * shard)
        u = us[...]
        before = xb[:, cols]
        wide = before.astype(f32)
        nacc[...] += jnp.broadcast_to(jnp.sum(wide * wide, axis=1, keepdims=True), nacc.shape)
        g_down = dot_tn(before, qv[...]).astype(bf16)
        g_up = dot_tn(gout[:, cols], u).astype(bf16)
        for i in range(2):
            part[b, i, :, head] = g_down[i * shard:(i + 1) * shard]
            part[b, i, :, tail] = g_up[i * shard:(i + 1) * shard]
        core_copy(b).start()

    def tick(t, carry):
        k = t - 1
        sent = (k >= 0) & (k < planes)
        near = sent & (k == z - 1)

        @pl.when(sent & (k != z) & (k != z - 1))
        def _():
            u_arrived(k).wait_recv()

        @pl.when(near)
        def _():
            near_copy(k, head, 0).wait_recv()
            acc[...] += dot_nn(ul[k, :, head], nn[k, 0:rank, :])
            near_copy(k, tail, 1).wait_recv()
            acc[...] += dot_nn(ul[k, :, tail], nn[k, rank:2 * rank, :])

        @pl.when(sent & (k < z - 1))
        def _():
            acc[...] += dot_nn(ul[k], nn[k])

        @pl.when(t == z)
        def _():
            forward_own()

        @pl.when(sent & (k > z))
        def _():
            before = acc[:, 2 * rank:4 * rank]
            ys[2 * k] = before
            between = before + dot_nn(ul[k, :, head], nn[k, 0:rank, 2 * rank:4 * rank])
            ys[2 * k + 1] = between
            acc[:, 2 * rank:4 * rank] = between + dot_nn(
                ul[k, :, tail], nn[k, rank:2 * rank, 2 * rank:4 * rank])

        r = 2 * planes - t

        @pl.when((r < planes) & (r > z))
        def _():
            q_arrived(r).wait_recv()
            c_a, c_b = c_of(ql[r, some:some + 16, :])
            hacc[...] += (dot_nn(ql[r, 0:some, :], nn[r, :, 0:2 * rank]) - c_a * ys[2 * r] - c_b * ys[2 * r + 1])

        @pl.when(t == 2 * planes - 1 - z)
        def _():
            backward_own()

        p = t - (z + 1)

        @pl.when((p >= 0) & (p < trips))
        def _():
            @pl.when(p == 0)
            def _():
                for load in loads[:3]:
                    load.wait()
                uf_arrived().wait_recv()
            chain(p)

        q = t - (z + 1 + trips)

        @pl.when((q >= 0) & (q < chunks // 4))
        def _():
            for j in range(4):
                give_copy(4 * q + j).start()

        b = t - (2 * planes - z)

        @pl.when((b >= 0) & (b < trips))
        def _():
            @pl.when(b == 0)
            def _():
                for load in loads[3:]:
                    load.wait()
                qp_copy().wait_recv()
                qs[mine, :] = ql[z, 0:some, :]
                qs[theirs, :] = qp[0:some, :]
                for where, stat in ((mine, ql[z, some:some + 16, :]), (theirs, qp[some:some + 16, :])):
                    c_a, c_b = c_of(stat)
                    cpair[0, where, :] = jnp.broadcast_to(c_a, (some, rank))
                    cpair[1, where, :] = jnp.broadcast_to(c_b, (some, rank))
                us[...] = jnp.where(first, uf[:, head], uf[:, tail])
                qv[...] = jnp.where(first, qs[:, head], qs[:, tail])
            chain_back(b)
            terms(ylo * trips + b)

        @pl.when((b >= 1) & (b <= trips))
        def _():
            collect(ylo * trips + b - 1)

            def landed(j, carry):
                c = per * (b - 1) + j
                pass_arrived(c).wait_recv()
                h_arrived(c).wait_recv()
                return carry

            lax.fori_loop(0, per, landed, 0)
            terms((1 - ylo) * trips + b - 1)

        @pl.when((b >= 2) & (b <= trips))
        def _():
            collect((1 - ylo) * trips + b - 2)

        return carry

    lax.fori_loop(0, 2 * planes + trips + 1, tick, 0)
    collect((1 - ylo) * trips + trips - 1)

    def landed_x(c, carry):
        give_arrived(c).wait_recv()
        return carry

    lax.fori_loop(0, chunks, landed_x, 0)
    save_x = pltpu.make_async_copy(xout, xout_far, l_sem.at[6])
    save_x.start()
    total_a, total_b = scatter_sum(yh_n, x_n, sums, rax, rby, sa, ray, sb, rbx,
                                   ax_send, ax_recv, by_send, by_recv, s_sem, bx_send, bx_recv)
    cut = shard // 2
    gw[0:cut] = total_a[:, head].astype(bf16)
    gw[cut:shard] = total_b[:, head].astype(bf16)
    gu[0:cut] = total_a[:, tail].astype(bf16)
    gu[cut:shard] = total_b[:, tail].astype(bf16)
    has_next = s < sections - 1
    down_section = {"section": lax.rem(s + sections - 1, sections)}

    def pair_of(sems, i):
        return sems.at[2 * i], sems.at[2 * i + 1]

    def w_x(i):
        return remote(gw, own_w.at[yh, x, core], *pair_of(wx_sem, i), place(yh, xp(i), core))

    def w_y(i):
        spot = own_w.at[yh, xp(i), core]
        return remote(gw if i == 0 else spot, spot, *pair_of(wy_sem, i), other_y)

    def w_c(i):
        spot = own_w.at[:, xp(i), core]
        return remote(spot, spot, *pair_of(wc_sem, i), other_core)

    v_y = remote(gu, own_u.at[yh, x, core], *pair_of(vx_sem, 0), other_y)

    def v_x(i):
        spot = own_u.at[:, x, core]
        return remote(spot, spot, *pair_of(vx_sem, i), place(yh, xp(i), core))

    def v_c(i):
        spot = own_u.at[:, xp(i), core]
        return remote(spot, spot, *pair_of(vc_sem, i), other_core)

    next_copy = remote(nw, nxt_u.at[yh, x, core], *pair_of(nx_sem, 0), down_section)
    bump_copy = remote(ub, bump_u, *pair_of(nx_sem, x_n), down_section)

    def n_x(i):
        spot = nxt_u.at[yh, x, core]
        return remote(spot, spot, *pair_of(nx_sem, i), place(yh, xp(i), core))

    def n_y(i):
        spot = nxt_u.at[yh, xp(i), core]
        return remote(spot, spot, *pair_of(ny_sem, i), other_y)

    def n_c(i):
        spot = nxt_u.at[:, xp(i), core]
        return remote(spot, spot, *pair_of(nc_sem, i), other_core)

    for i in range(1, x_n):
        w_x(i).start()
    v_y.start()
    w_y(0).start()

    @pl.when(s > 0)
    def _():
        nw[...] = (mine_u[...].astype(f32) - learn_rate * gu[...].astype(f32)).astype(bf16)
        next_copy.start()

    own_w[yh, x, core] = gw[...]
    own_u[yh, x, core] = gu[...]
    @pl.when(has_next)
    def _():
        next_copy.wait_recv()
        for i in range(1, x_n):
            n_x(i).start()

    for i in range(1, x_n):
        w_x(x_n - i).wait_recv()
        w_y(i).start()

    @pl.when(has_next)
    def _():
        n_y(0).start()
        for i in range(1, x_n):
            n_x(i).wait_send()

    v_y.wait_recv()
    for i in range(1, x_n):
        v_x(i).start()
    v_c(0).start()

    for i in range(x_n):
        w_y(i).wait_recv()
        w_c(i).start()

    @pl.when(has_next)
    def _():
        for i in range(1, x_n):
            n_x(x_n - i).wait_recv()
            n_y(i).start()

    for i in range(1, x_n):
        v_x(x_n - i).wait_recv()
        v_c(i).start()
    for i in range(x_n):
        w_c(i).wait()
    save_w = pltpu.make_async_copy(own_w, own_w_far, l_sem.at[7])
    save_w.start()

    @pl.when(s > 0)
    def _():
        def ahead(b, pre):
            y_ = b // x_n
            x_ = lax.rem(b, x_n)
            cols = pl.ds(pl.multiple_of(b * 2 * shard, 128), 2 * shard)
            both = jnp.concatenate([own_w[y_, x_, 0], own_w[y_, x_, 1]], axis=0)
            fresh = wd[cols, :].astype(f32) - learn_rate * both.astype(f32)
            return pre + dot_nn(xb[:, cols], fresh.astype(bf16))

        pre = lax.fori_loop(0, yh_n * x_n, ahead, jnp.zeros((rows, rank), f32))
        value, unused = gelu_pair(pre * lax.rsqrt(nacc[...] * (1.0 / width) + eps))
        ub[...] = value.astype(bf16)
        bump_copy.start()

    @pl.when(has_next)
    def _():
        for i in range(x_n):
            n_y(i).wait_recv()
            n_c(i).start()
        for i in range(x_n):
            n_c(i).wait()
            n_y(i).wait_send()
        bump_copy.wait_recv()

    for i in range(x_n):
        v_c(i).wait()
        w_y(i).wait_send()
    for i in range(1, x_n):
        w_x(i).wait_send()
        v_x(i).wait_send()
    v_y.wait_send()

    @pl.when(s > 0)
    def _():
        next_copy.wait_send()
        bump_copy.wait_send()

    def core_settle(b, carry):
        core_copy(b).wait_send()
        return carry

    lax.fori_loop(0, yh_n * x_n, core_settle, 0)
    save_x.wait()
    save_w.wait()

    def finish(c, carry):
        @pl.when(z < planes - 1)
        def _():
            x_copy(c).wait_send()
        give_copy(c).wait_send()
        pass_copy(c).wait_send()

        @pl.when(z > 0)
        def _():
            b_copy(c).wait_send()
        h_copy(c).wait_send()
        return carry

    lax.fori_loop(0, chunks, finish, 0)
    for o in range(2, planes):
        u_copy(o).wait_send()

    @pl.when(z == planes - 1)
    def _():
        u_copy(1).wait_send()

    @pl.when(z < planes - 1)
    def _():
        near_copy(z, head, 0).wait_send()
        near_copy(z, tail, 1).wait_send()
        n_copy().wait_send()

    def settle(j, carry):
        q_copy(j).wait_send()
        return carry

    lax.fori_loop(0, z, settle, 0)
    uf_copy().wait_send()
    qp_copy().wait_send()


def recurrence(sections, shards, pyh, n0, nn, x0, g16, up, wd, upart, wpart, mine_u):
    rows, width = x0.shape
    rank = up.shape[0]
    half = width // 2
    some = rows // 2
    planes = sections // 2
    chunks = 28
    per = 7
    x_n = 4
    yh_n = shards // (2 * x_n)
    shard = mine_u.shape[0]
    cut = shard // 2
    blocks = yh_n * x_n
    vm = pl.BlockSpec(memory_space=pltpu.VMEM)
    dma = pltpu.SemaphoreType.DMA
    sq = (rows, rank)
    two = (some, 2 * rank)
    strip = pltpu.VMEM((rows, half), bf16)
    full = jax.ShapeDtypeStruct((yh_n, x_n, 2, shard, rank), bf16)

    def buf(*lead):
        return pltpu.VMEM(lead + (2 * rank,), bf16)

    return pl.pallas_call(
        functools.partial(recurrence_kernel, sections, chunks, per, yh_n, x_n),
        out_shape=(jax.ShapeDtypeStruct((rows, width), bf16), full, full, full,
                   jax.ShapeDtypeStruct(sq, bf16)),
        in_specs=[vm] * 3 + [pl.BlockSpec(memory_space=pl.ANY)] * 6 + [vm],
        out_specs=(pl.BlockSpec(memory_space=pl.ANY),) * 2 + (vm,) * 3,
        scratch_shapes=[
            pltpu.VMEM((planes,) + two, bf16),
            pltpu.VMEM((planes, some + 16, 2 * rank), bf16),
            pltpu.VMEM((some + 16, 2 * rank), bf16),
            pltpu.VMEM((sections,) + two, f32),
            pltpu.VMEM((8, rank), f32),
            pltpu.VMEM((8, rank), f32),
            pltpu.VMEM((some, 4 * rank), f32),
            pltpu.VMEM(two, f32), pltpu.VMEM(two, f32), pltpu.VMEM(two, f32),
            pltpu.VMEM((2, some, rank), f32),
            pltpu.VMEM((rows, 2 * rank), bf16),
            pltpu.VMEM((rows, 2 * rank), bf16),
            pltpu.VMEM((2,) + sq, f32),
            strip, strip, strip, strip, strip, strip, strip,
            pltpu.VMEM((2, rows, half * per // chunks), f32),
            pltpu.VMEM((rows, width), bf16),
            pltpu.VMEM(sq, bf16), pltpu.VMEM(sq, bf16),
            pltpu.VMEM((rows, width), bf16), pltpu.VMEM(sq, f32),
            buf(blocks, 2, shard), buf(blocks, shard), buf(yh_n, x_n, shard),
            buf(x_n - 1, yh_n, cut), buf(x_n, cut), buf(yh_n, cut), buf(cut),
            buf(x_n, cut), buf(x_n - 1, cut),
            pltpu.VMEM((shard, rank), bf16), pltpu.VMEM((shard, rank), bf16),
            pltpu.VMEM((shard, rank), bf16), pltpu.VMEM(sq, bf16),
            pltpu.VMEM((rows, width), bf16), pltpu.VMEM((rows, width), bf16),
            pltpu.VMEM((rank, width), bf16), pltpu.VMEM((width, rank), bf16),
            pltpu.VMEM((rank, half), bf16), pltpu.VMEM((half, rank), bf16),
            pltpu.VMEM((rows, width), bf16), pltpu.VMEM((yh_n, x_n, 2, shard, rank), bf16), dma((8,)),
        ] + [dma((planes,))] * 4 + [dma((10,))] + [dma((chunks,))] * 10 + [
            dma((blocks,)), dma((blocks,)),
            dma((yh_n * (x_n - 1),)), dma((yh_n * (x_n - 1),)), dma((x_n,)), dma((x_n,)), dma((2,)),
            dma((x_n - 1,)), dma((x_n - 1,)),
            dma((2 * x_n,)), dma((2 * x_n,)), dma((2 * x_n,)), dma((2 * x_n,)), dma((2 * x_n,)),
            dma((2 * x_n + 2,)), dma((2 * x_n,)), dma((2 * x_n,)),
        ],
        compiler_params=pltpu.CompilerParams(
            collective_id=1, has_side_effects=True, vmem_limit_bytes=60 * 1024 * 1024),
    )(pyh, n0, nn, x0, g16, up, wd, upart, wpart, mine_u)


def dp_place(x_n):
    d = lax.axis_index("dp")
    return d // (2 * x_n), lax.rem(d // 2, x_n), lax.rem(d, 2)


def remote(src, dst, send, recv, where):
    return pltpu.make_async_remote_copy(src_ref=src, dst_ref=dst, send_sem=send, recv_sem=recv,
                                        device_id=where, device_id_type=MESH)


def block_sum(b, yh_n, x_n, core_copy, part, rc, sums, rax, rby, ax_send, ax_recv, by_send, by_recv):
    yh, x, core = dp_place(x_n)
    cut = sums.shape[2] // 2
    y_ = b // x_n
    x_ = lax.rem(b, x_n)
    core_copy(b).wait_recv()
    sums[y_, x_] = (part[b, core].astype(f32) + rc[b].astype(f32)).astype(bf16)
    turn = lax.rem(x_ - x + x_n, x_n)

    @pl.when(turn != 0)
    def _():
        sem = (turn - 1) * yh_n + y_
        remote(sums.at[y_, x_, 0:cut], rax.at[turn - 1, y_], ax_send.at[sem], ax_recv.at[sem],
               {"dp": (yh * x_n + x_) * 2 + core}).start()

    @pl.when(y_ != yh)
    def _():
        remote(sums.at[y_, x_, cut:2 * cut], rby.at[x_], by_send.at[x_], by_recv.at[x_],
               {"dp": (y_ * x_n + x) * 2 + core}).start()


def scatter_sum(yh_n, x_n, sums, rax, rby, sa, ray, sb, rbx,
                ax_send, ax_recv, by_send, by_recv, s_sem, bx_send, bx_recv):
    yh, x, core = dp_place(x_n)
    rows = sums.shape[2]
    cut = rows // 2

    def place(y_, x_, c_):
        return {"dp": (y_ * x_n + x_) * 2 + c_}

    def xp(i):
        return lax.rem(x + i, x_n)

    other_y = place(1 - yh, x, core)

    def ax_copy(i, y_):
        sem = (i - 1) * yh_n + y_
        return remote(sums.at[y_, xp(i), 0:cut], rax.at[i - 1, y_], ax_send.at[sem], ax_recv.at[sem],
                      place(yh, xp(i), core))

    def by_copy(x_):
        return remote(sums.at[1 - yh, x_, cut:rows], rby.at[x_], by_send.at[x_], by_recv.at[x_], other_y)

    def bx_copy(i):
        return remote(sb.at[xp(i)], rbx.at[i - 1], bx_send.at[i - 1], bx_recv.at[i - 1],
                      place(yh, xp(i), core))

    ay_copy = remote(sa.at[1 - yh], ray, s_sem.at[0], s_sem.at[1], other_y)

    for i in range(x_n):
        x_ = xp(i)
        by_copy(x_).wait_recv()
        sb[x_] = (sums[yh, x_, cut:rows].astype(f32) + rby[x_].astype(f32)).astype(bf16)
        if i > 0:
            bx_copy(i).start()
    for y_ in range(yh_n):
        total = sums[y_, x, 0:cut].astype(f32)
        for i in range(1, x_n):
            ax_copy(i, y_).wait_recv()
            total = total + rax[i - 1, y_].astype(f32)
        sa[y_] = total.astype(bf16)
    ay_copy.start()
    total_b = sb[x].astype(f32)
    for i in range(1, x_n):
        bx_copy(i).wait_recv()
        total_b = total_b + rbx[i - 1].astype(f32)
    ay_copy.wait_recv()
    total_a = sa[yh].astype(f32) + ray[...].astype(f32)
    for i in range(1, x_n):
        for y_ in range(yh_n):
            ax_copy(i, y_).wait_send()
        bx_copy(i).wait_send()
    for x_ in range(x_n):
        by_copy(x_).wait_send()
    ay_copy.wait_send()
    return total_a, total_b


def gram_kernel(yh_n, x_n, sections, x0_far, g16_far, down_far, up_far, mine_u, base, pyh, n0, out, upart, wpart,
                allu, part, rc, sums, rax, rby, sa, ray, sb, rbx, gs, gp, two, mine3, theirs3, flip, turned,
                x0, g16, down, up, l_sem,
                z_sem, f_send, f_recv, r_send, r_recv,
                c_send, c_recv, ax_send, ax_recv, by_send, by_recv, s_sem, bx_send, bx_recv,
                ga_send, ga_recv, gb_send, gb_recv, gc_send, gc_recv, t_sem):
    loads = [pltpu.make_async_copy(far, near, l_sem.at[i]) for i, (far, near) in enumerate((
        (up_far, up), (down_far, down), (x0_far, x0), (g16_far, g16)))]
    for load in loads:
        load.start()
    yh, x, core = dp_place(x_n)
    s = lax.axis_index("section")
    z_n = sections // 2
    z = s // 2
    ylo = lax.rem(s, 2)
    rank = up.shape[0]
    rows = rank
    cut = rows // 2

    def place(y_, x_, c_):
        return {"dp": (y_ * x_n + x_) * 2 + c_}

    def xp(i):
        return lax.rem(x + i, x_n)

    def zp(i):
        return lax.rem(z + i, z_n)

    other_core = place(yh, x, 1 - core)
    other_y = place(1 - yh, x, core)
    partner = {"section": s + 1 - 2 * ylo}
    after = {"section": 2 * zp(1) + ylo}
    before = {"section": 2 * zp(z_n - 1) + ylo}

    barrier = pltpu.get_barrier_semaphore()
    peers = [other_core, other_y, partner, after, before]
    peers += [place(yh, xp(i), core) for i in range(1, x_n)]
    for where in peers:
        pl.semaphore_signal(barrier, inc=1, device_id=where, device_id_type=MESH)
    d = lax.axis_index("dp")
    above = d // 2 < z
    below = d // 2 > z
    mirror = [{"section": 2 * (d // 2) + i, "dp": s} for i in range(2)]

    @pl.when(below)
    def _():
        for i in range(2):
            pl.semaphore_signal(barrier, inc=1, device_id={"section": d, "dp": 2 * z + i},
                                device_id_type=MESH)

    pl.semaphore_wait(barrier, len(peers) + 2 * above.astype(jnp.int32))

    def flip_copy(i):
        k = lax.rem(d, 2)
        return remote(flip, turned.at[k], t_sem.at[i], t_sem.at[2 + k], mirror[i])

    def flip_arrived(i):
        return remote(flip, turned.at[i], t_sem.at[0], t_sem.at[2 + i], mirror[0])

    pair = remote(mine_u, allu.at[z, ylo], z_sem.at[0], z_sem.at[1], partner)

    def products(z_):
        for y_ in range(2):
            part[z_, y_] = dot_tn(allu[z_, y_], base[...]).astype(bf16)

    def core_copy(b):
        return remote(part.at[b, 1 - core], rc.at[b], c_send.at[b], c_recv.at[b], other_core)

    hops = z_n // 2

    def column(j):
        return ylo if j == 0 else 1 - ylo

    def ring_f(i, j):
        spot = allu.at[zp(z_n + 1 - i), column(j)]
        src = mine_u if (i == 1 and j == 0) else spot
        sem = 2 * (i - 1) + j
        return remote(src, spot, f_send.at[sem], f_recv.at[sem], after)

    def ring_r(i, j):
        spot = allu.at[zp(i - 1), column(j)]
        src = mine_u if (i == 1 and j == 0) else spot
        sem = 2 * (i - 1) + j
        return remote(src, spot, r_send.at[sem], r_recv.at[sem], before)

    used_f = [(i, j) for i in range(1, hops + 1) for j in range(2) if i < hops or j == 0]
    used_r = [(i, j) for i in range(1, hops + 1) for j in range(2) if i < hops or j == 1]

    pair.start()
    ring_f(1, 0).start()
    ring_r(1, 0).start()
    allu[z, ylo] = mine_u[...]
    pair.wait_recv()
    ring_f(1, 1).start()
    ring_r(1, 1).start()

    half = x0.shape[1] // 2
    quarter = half // 2
    far = pl.ds(pl.multiple_of((1 - ylo) * half + core * quarter, 128), quarter)
    near = pl.ds(pl.multiple_of(core * quarter, 128), quarter)
    swap_u = remote(up.at[:, far], upart.at[:, near], z_sem.at[6], z_sem.at[7], partner)
    swap_w = remote(down.at[far, :], wpart.at[near, :], z_sem.at[8], z_sem.at[9], partner)
    share_u = remote(upart.at[:, near], upart.at[:, near], z_sem.at[10], z_sem.at[11], other_core)
    share_w = remote(wpart.at[near, :], wpart.at[near, :], z_sem.at[12], z_sem.at[13], other_core)
    for load in loads:
        load.wait()
    swap_u.start()
    swap_w.start()

    u = up[...]
    w = down[...]
    values = x0[...]
    token_half = x0.shape[0] // 2
    keep = pl.ds(ylo * token_half, token_half)
    give = pl.ds((1 - ylo) * token_half, token_half)
    mine3[0] = dot_nn(values, w)
    mine3[1] = dot_nt(values, u)
    mine3[2] = dot_nt(g16[...], u)
    swap3 = remote(mine3.at[:, give], theirs3, z_sem.at[2], z_sem.at[3], partner)
    swap3.start()
    wide = x0[keep, :].astype(f32)
    n0[...] = jnp.broadcast_to(jnp.sum(wide * wide, axis=1, keepdims=True), n0.shape)

    def collect(b):
        block_sum(b, yh_n, x_n, core_copy, part, rc, sums, rax, rby,
                  ax_send, ax_recv, by_send, by_recv)

    products(z)
    core_copy(z).start()
    for i in range(1, hops + 1):
        for j in range(2):
            if (i, j) in used_f:
                ring_f(i, j).wait_recv()
                if (i + 1, j) in used_f:
                    ring_f(i + 1, j).start()
            if (i, j) in used_r:
                ring_r(i, j).wait_recv()
                if (i + 1, j) in used_r:
                    ring_r(i + 1, j).start()
        products(zp(z_n - i))
        core_copy(zp(z_n - i)).start()
        if i == 1:
            collect(z)
        else:
            collect(zp(i - 1))
        if i < hops:
            products(zp(i))
            core_copy(zp(i)).start()
        collect(zp(z_n - i))

    swap_u.wait_recv()
    share_u.start()
    swap_w.wait_recv()
    share_w.start()
    total_a, total_b = scatter_sum(yh_n, x_n, sums, rax, rby, sa, ray, sb, rbx,
                                   ax_send, ax_recv, by_send, by_recv, s_sem, bx_send, bx_recv)
    gs[0:cut] = total_a.astype(bf16)
    gs[cut:rows] = total_b.astype(bf16)
    swap = remote(gs, gp, z_sem.at[4], z_sem.at[5], partner)
    swap.start()

    @pl.when(above)
    def _():
        flip[...] = gs[:, 0:rank].astype(f32).T.astype(bf16)
        for i in range(2):
            flip_copy(i).start()

    def lanes(base, which):
        return pl.ds(pl.multiple_of(base + which * rank, 128), rank)

    swap3.wait_recv()
    pyh[:, :, lanes(0, ylo)] = mine3[:, keep]
    pyh[:, :, lanes(0, 1 - ylo)] = theirs3[...]
    two[:, lanes(0, ylo)] = gs[:, 0:rank]
    two[:, lanes(2 * rank, ylo)] = gs[:, rank:2 * rank]
    swap.wait_recv()
    two[:, lanes(0, 1 - ylo)] = gp[:, 0:rank]
    two[:, lanes(2 * rank, 1 - ylo)] = gp[:, rank:2 * rank]

    @pl.when(below)
    def _():
        for i in range(2):
            flip_arrived(i).wait_recv()
            two[:, i * rank:(i + 1) * rank] = turned[i]
    out[yh, x, core] = two[...]

    low = pl.ds(0, cut)
    high = pl.ds(cut, cut)

    def spread(src, spot, sems, i, where):
        return remote(src, spot, sems[0].at[i], sems[1].at[i], where)

    ga = (ga_send, ga_recv)
    gb = (gb_send, gb_recv)
    a_y = spread(two.at[low], out.at[yh, x, core, low], ga, 0, other_y)

    def a_x(i):
        spot = out.at[:, x, core, low]
        return spread(spot, spot, ga, i, place(yh, xp(i), core))

    def b_x(i):
        return spread(two.at[high], out.at[yh, x, core, high], gb, i - 1, place(yh, xp(i), core))

    def b_y(i):
        spot = out.at[yh, xp(i), core, high]
        return spread(spot, spot, gb, x_n - 1 + i, other_y)

    def all_c(i):
        spot = out.at[:, xp(i), core]
        return remote(spot, spot, gc_send.at[i], gc_recv.at[i], other_core)

    a_y.start()
    for i in range(1, x_n):
        b_x(i).start()
    b_y(0).start()
    a_y.wait_recv()
    for i in range(1, x_n):
        a_x(i).start()
    for i in range(1, x_n):
        b_x(x_n - i).wait_recv()
        b_y(i).start()
    b_y(0).wait_recv()
    all_c(0).start()
    for i in range(1, x_n):
        a_x(x_n - i).wait_recv()
        b_y(i).wait_recv()
        all_c(i).start()
    for i in range(x_n):
        all_c(i).wait()
        b_y(i).wait_send()
    for i in range(1, x_n):
        a_x(i).wait_send()
        b_x(i).wait_send()
    a_y.wait_send()
    pair.wait_send()
    swap.wait_send()
    swap3.wait_send()

    @pl.when(above)
    def _():
        for i in range(2):
            flip_copy(i).wait_send()
    swap_u.wait_send()
    swap_w.wait_send()
    share_u.wait()
    share_w.wait()
    for i, j in used_f:
        ring_f(i, j).wait_send()
    for i, j in used_r:
        ring_r(i, j).wait_send()

    def settle(b, carry):
        core_copy(b).wait_send()
        return carry

    lax.fori_loop(0, yh_n * x_n, settle, 0)


def grams_of(sections, shards, x0, g16, down, up, mine_u, base):
    x_n = 4
    yh_n = shards // (2 * x_n)
    rows, width = x0.shape
    rank = up.shape[0]
    height = mine_u.shape[0]
    cut = rank // 2
    vm = pl.BlockSpec(memory_space=pltpu.VMEM)
    dma = pltpu.SemaphoreType.DMA

    def buf(*lead):
        return pltpu.VMEM(lead + (2 * rank,), bf16)

    return pl.pallas_call(
        functools.partial(gram_kernel, yh_n, x_n, sections),
        out_shape=(
            jax.ShapeDtypeStruct((3, rows // 2, 2 * rank), f32),
            jax.ShapeDtypeStruct((rows // 2, rank), f32),
            jax.ShapeDtypeStruct((yh_n, x_n, 2, rank, 4 * rank), bf16),
            jax.ShapeDtypeStruct((rank, width // 2), bf16),
            jax.ShapeDtypeStruct((width // 2, rank), bf16),
        ),
        in_specs=[pl.BlockSpec(memory_space=pl.ANY)] * 4 + [vm] * 2,
        out_specs=(vm,) * 5,
        scratch_shapes=[
            pltpu.VMEM((sections // 2, 2, height, rank), bf16),
            buf(yh_n * x_n, 2, rank), buf(yh_n * x_n, rank), buf(yh_n, x_n, rank),
            buf(x_n - 1, yh_n, cut), buf(x_n, cut), buf(yh_n, cut), buf(cut),
            buf(x_n, cut), buf(x_n - 1, cut), buf(rank), buf(rank),
            pltpu.VMEM((rank, 4 * rank), bf16),
            pltpu.VMEM((3, rows, rank), f32), pltpu.VMEM((3, rows // 2, rank), f32),
            pltpu.VMEM((rank, rank), bf16), pltpu.VMEM((2, rank, rank), bf16),
            pltpu.VMEM((rows, width), bf16), pltpu.VMEM((rows, width), bf16),
            pltpu.VMEM((width, rank), bf16), pltpu.VMEM((rank, width), bf16), dma((4,)),
            dma((14,)), dma((sections // 2,)), dma((sections // 2,)),
            dma((sections // 2,)), dma((sections // 2,)),
            dma((yh_n * x_n,)), dma((yh_n * x_n,)),
            dma((yh_n * (x_n - 1),)), dma((yh_n * (x_n - 1),)), dma((x_n,)), dma((x_n,)), dma((4,)),
            dma((x_n - 1,)), dma((x_n - 1,)),
            dma((x_n,)), dma((x_n,)), dma((2 * x_n,)), dma((2 * x_n,)), dma((x_n,)), dma((x_n,)), dma((4,)),
        ],
        compiler_params=pltpu.CompilerParams(
            collective_id=3, has_side_effects=True, vmem_limit_bytes=60 * 1024 * 1024),
    )(x0, g16, down, up, mine_u, base)


def finish_kernel(sections, own_w, own_u, nxt_u, bump_u, x1, grad_down, grad_up, advance):
    last = lax.axis_index("section") == sections - 1
    grad_down[...] = own_w[...]
    grad_up[...] = own_u[...].astype(f32).T.astype(bf16)
    bump = dot_nt(bump_u[...], nxt_u[...])
    advance[...] = (x1[...].astype(f32) + jnp.where(last, 0.0, bump)).astype(bf16)


def finish(sections, own_w, own_u, nxt_u, bump_u, x1):
    rows, width = x1.shape
    rank = own_w.shape[1]
    step = width // 8
    tall = pl.BlockSpec((step, rank), lambda i: (i, 0))
    flat = pl.BlockSpec((rows, step), lambda i: (0, i))
    return pl.pallas_call(
        functools.partial(finish_kernel, sections),
        grid=(width // step,),
        out_shape=(
            jax.ShapeDtypeStruct((width, rank), bf16),
            jax.ShapeDtypeStruct((rank, width), bf16),
            jax.ShapeDtypeStruct((rows, width), bf16),
        ),
        in_specs=[tall, tall, tall, pl.BlockSpec((rows, rank), lambda i: (0, 0)), flat],
        out_specs=(tall, flat, flat),
        compiler_params=pltpu.CompilerParams(vmem_limit_bytes=60 * 1024 * 1024),
    )(own_w, own_u, nxt_u, bump_u, x1)


def per_device(inputs, cotangent, w_down, w_up):
    down = w_down[0]
    upward = w_up[0]
    micro, batch_rows, width = inputs.shape
    rank = down.shape[1]
    rows = micro * batch_rows
    sections = lax.axis_size("section")
    shards = lax.axis_size("dp")
    part = width // shards
    d = lax.axis_index("dp")
    x0 = inputs.reshape(rows, width)
    g16 = cotangent.reshape(rows, width)
    up_t = upward.T

    mine_u = lax.dynamic_slice_in_dim(up_t, d * part, part, 0)
    mine_w = lax.dynamic_slice_in_dim(down, d * part, part, 0)
    base = jnp.concatenate([mine_w, mine_u], axis=1)
    pyh, n0, grams, upart, wpart = grams_of(sections, shards, x0, g16, down, upward, mine_u, base)
    grams = grams.reshape(sections // 2, 2 * rank, 4 * rank)
    x1, own_w, own_u, nxt_u, bump_u = recurrence(
        sections, shards, pyh, n0, grams, x0, g16, upward, down, upart, wpart, mine_u)
    tall = (width, rank)
    grad_down, grad_up, advance = finish(
        sections, own_w.reshape(tall), own_u.reshape(tall), nxt_u.reshape(tall), bump_u, x1)
    return (grad_down[None], grad_up[None], advance.reshape(1, micro, batch_rows, width))


def solution(mesh):
    in_specs = (
        P(None, "dp", None),
        P(None, "dp", None),
        P("section", None, None),
        P("section", None, None),
    )
    out_specs = (P("section", None, None), P("section", None, None), P("section", None, "dp", None))
    return jax.shard_map(
        per_device, mesh=mesh, in_specs=in_specs, out_specs=out_specs, check_vma=False
    )
```

```python
import functools

import jax
import jax.numpy as jnp
from jax import lax
from jax.experimental import pallas as pl
from jax.experimental.pallas import tpu as pltpu
from jax.sharding import PartitionSpec as P

MESH = pl.DeviceIdType.MESH
eps = 1e-05
learn_rate = 0.05
f32 = jnp.float32
bf16 = jnp.bfloat16


def dot_nn(a, b):
    return jnp.dot(a, b, preferred_element_type=f32)


def dot_tn(a, b):
    return lax.dot_general(a, b, (((0,), (0,)), ((), ())), preferred_element_type=f32)


def dot_nt(a, b):
    return lax.dot_general(a, b, (((1,), (1,)), ((), ())), preferred_element_type=f32)


def gelu_pair(a):
    c = 0.7978845608028654
    inner = c * (a + 0.044715 * a * a * a)
    th = jnp.tanh(inner)
    value = 0.5 * a * (1.0 + th)
    slope = 0.5 * (1.0 + th) + 0.5 * a * (1.0 - th * th) * c * (1.0 + 3 * 0.044715 * a * a)
    return value, slope


def recurrence_kernel(sections, chunks, per, yh_n, x_n,
                      pyh, n0, nn, x0_far, g16_far, up_far, wd_far, upart_far, wpart_far, mine_u,
                      xout_far, own_w_far, own_u, nxt_u, bump_u,
                      ul, ql, qp, ys, nl, nsend, acc, hacc, slope, act, rinv, uf, qs, cpair,
                      xin, xkeep, xgive, gin, gkeep, ggive, xpass, delta,
                      gout, us, qv, xb, nacc, part, rc, sums, rax, rby, sa, ray, sb, rbx,
                      gw, gu, nw, ub, x0, g16, up, wd, upart, wpart, xout, own_w, l_sem,
                      u_send, u_recv, q_send, q_recv, e_sem,
                      c_send, c_recv, g_send, g_recv,
                      b_send, b_recv, h_send, h_recv, p_send, p_recv,
                      k_send, k_recv, ax_send, ax_recv, by_send, by_recv, s_sem, bx_send, bx_recv,
                      wx_sem, wy_sem, wc_sem, vx_sem, vc_sem, nx_sem, ny_sem, nc_sem):
    loads = [pltpu.make_async_copy(far, near, l_sem.at[i]) for i, (far, near) in enumerate((
        (up_far, up), (upart_far, upart), (x0_far, x0),
        (wd_far, wd), (wpart_far, wpart), (g16_far, g16)))]
    for load in loads:
        load.start()
    s = lax.axis_index("section")
    yh, x, core = dp_place(x_n)
    planes = sections // 2
    rows, width = x0.shape
    some = rows // 2
    rank = up.shape[0]
    half = width // 2
    piece = half // chunks
    trips = chunks // per
    z = s // 2
    ylo = lax.rem(s, 2)
    first = ylo == 0
    partner = {"section": s + 1 - 2 * ylo}
    head = slice(0, rank)
    tail = slice(rank, 2 * rank)
    mine = pl.ds(ylo * some, some)
    theirs = pl.ds((1 - ylo) * some, some)

    def plane(i):
        return {"section": 2 * i + ylo}

    def peer(offset):
        return lax.rem(z + offset, planes)

    barrier = pltpu.get_barrier_semaphore()
    for o in range(1, planes):
        pl.semaphore_signal(barrier, inc=1, device_id=plane(peer(o)), device_id_type=MESH)

    def place(y_, x_, c_):
        return {"dp": (y_ * x_n + x_) * 2 + c_}

    def xp(i):
        return lax.rem(x + i, x_n)

    other_core = place(yh, x, 1 - core)
    other_y = place(1 - yh, x, core)
    beyond = {"section": lax.rem(s + sections - 1 + 2 * ylo, sections)}
    others = [partner, beyond, other_core, other_y] + [place(yh, xp(i), core) for i in range(1, x_n)]
    for where in others:
        pl.semaphore_signal(barrier, inc=1, device_id=where, device_id_type=MESH)
    pl.semaphore_wait(barrier, planes - 1 + len(others))

    eye = (lax.broadcasted_iota(jnp.int32, (some, rank), 0)
           == lax.broadcasted_iota(jnp.int32, (some, rank), 1)).astype(f32)

    def to_row(col):
        return jnp.sum(eye * col, axis=0, keepdims=True)

    def to_col(row):
        return jnp.sum(eye * row, axis=1, keepdims=True)

    def columns(base, c):
        return pl.ds(pl.multiple_of(base + c * piece, 128), piece)

    def x_copy(c):
        return remote(xkeep.at[:, columns(0, c)], xin.at[:, columns(0, c)],
                      c_send.at[c], c_recv.at[c], plane(peer(1)))

    def b_copy(c):
        return remote(gkeep.at[:, columns(0, c)], gin.at[:, columns(0, c)],
                      b_send.at[c], b_recv.at[c], plane(peer(planes - 1)))

    def give_copy(c):
        return remote(xgive.at[:, columns(0, c)], xout.at[:, columns(ylo * half, c)],
                      g_send.at[c], g_recv.at[c], partner)

    def give_arrived(c):
        return remote(xgive.at[:, columns(0, c)], xout.at[:, columns((1 - ylo) * half, c)],
                      g_send.at[c], g_recv.at[c], partner)

    def pass_copy(c):
        return remote(xpass.at[:, columns(0, c)], xb.at[:, columns(ylo * half, c)],
                      p_send.at[c], p_recv.at[c], partner)

    def pass_arrived(c):
        return remote(xpass.at[:, columns(0, c)], xb.at[:, columns((1 - ylo) * half, c)],
                      p_send.at[c], p_recv.at[c], partner)

    def h_copy(c):
        return remote(ggive.at[:, columns(0, c)], gout.at[:, columns(ylo * half, c)],
                      h_send.at[c], h_recv.at[c], partner)

    def h_arrived(c):
        return remote(ggive.at[:, columns(0, c)], gout.at[:, columns((1 - ylo) * half, c)],
                      h_send.at[c], h_recv.at[c], partner)

    def near_copy(k, part, sem):
        spot = ul.at[k, :, part]
        return remote(spot, spot, e_sem.at[2 * sem], e_sem.at[2 * sem + 1], plane(peer(1)))

    def n_copy():
        return remote(nsend, nl, e_sem.at[4], e_sem.at[5], plane(peer(1)))

    def uf_copy():
        return remote(ul.at[z], uf.at[mine], e_sem.at[6], e_sem.at[7], partner)

    def uf_arrived():
        return remote(ul.at[z], uf.at[theirs], e_sem.at[6], e_sem.at[7], partner)

    def qp_copy():
        return remote(ql.at[z], qp, e_sem.at[8], e_sem.at[9], partner)

    def u_copy(o):
        return remote(ul.at[z], ul.at[z], u_send.at[o], u_recv.at[z], plane(peer(o)))

    def u_arrived(k):
        return remote(ul.at[k], ul.at[k], u_send.at[0], u_recv.at[k], plane(peer(1)))

    def q_copy(j):
        return remote(ql.at[z], ql.at[z], q_send.at[j], q_recv.at[z], plane(j))

    def q_arrived(k):
        return remote(ql.at[k], ql.at[k], q_send.at[0], q_recv.at[k], plane(peer(1)))

    acc[:, 0:2 * rank] = pyh[0]
    acc[:, 2 * rank:4 * rank] = pyh[1]
    hacc[...] = pyh[2]

    batch = per * piece

    def wide_columns(base, p):
        return pl.ds(pl.multiple_of(base + p * batch, 128), batch)

    def chain(p):
        ours = up[:, wide_columns(ylo * half, p)]
        other = upart[:, wide_columns(0, p)]
        grow = dot_nn(uf[:, head], jnp.where(first, ours, other))
        delta[0] = grow
        delta[1] = grow + dot_nn(uf[:, tail], jnp.where(first, other, ours))
        for j in range(per):
            c = per * p + j

            @pl.when(z > 0)
            def _():
                x_copy(c).wait_recv()

            here = columns(ylo * half, c)
            there = columns(0, c)
            lane = slice(j * piece, (j + 1) * piece)
            start = jnp.where(z > 0, xin[:, there], x0[:, here])
            x_a = (start.astype(f32) + delta[0, :, lane]).astype(bf16)
            x_b = (start.astype(f32) + delta[1, :, lane]).astype(bf16)
            xkeep[:, there] = x_b

            @pl.when(z < planes - 1)
            def _():
                x_copy(c).start()

            xpass[:, there] = jnp.where(first, x_a, start)
            pass_copy(c).start()
            xgive[:, there] = jnp.where(first, x_b, x_a)
            xout[:, here] = jnp.where(first, x_a, x_b)
            xb[:, here] = jnp.where(first, start, x_a)

    def chain_back(p):
        here = wide_columns(ylo * half, p)
        there = wide_columns(0, p)
        ours = wd[here, :]
        other = wpart[there, :]
        x_a = jnp.where(first, xb[:, here], xpass[:, there]).astype(f32)
        x_b = jnp.where(first, xpass[:, there], xb[:, here]).astype(f32)
        grow = dot_nt(qs[:, tail], jnp.where(first, other, ours)) - cpair[1, :, 0:1] * x_b
        delta[0] = grow
        delta[1] = (grow + dot_nt(qs[:, head], jnp.where(first, ours, other))
                    - cpair[0, :, 0:1] * x_a)
        for j in range(per):
            c = per * p + j

            @pl.when(z < planes - 1)
            def _():
                b_copy(c).wait_recv()

            here = columns(ylo * half, c)
            there = columns(0, c)
            lane = slice(j * piece, (j + 1) * piece)
            g_b = jnp.where(z < planes - 1, gin[:, there], g16[:, here])
            g_a = (g_b.astype(f32) + delta[0, :, lane]).astype(bf16)

            @pl.when(z > 0)
            def _():
                gkeep[:, there] = (g_b.astype(f32) + delta[1, :, lane]).astype(bf16)
                b_copy(c).start()

            ggive[:, there] = jnp.where(first, g_b, g_a)
            h_copy(c).start()
            gout[:, here] = jnp.where(first, g_a, g_b)

    def forward_own():
        @pl.when(z > 0)
        def _():
            n_copy().wait_recv()

        norm_a = jnp.where(z > 0, to_col(nl[0:1, :]), n0[:, 0:1])
        scale_a = lax.rsqrt(norm_a * (1.0 / width) + eps)
        pre_a = acc[:, 0:rank] * scale_a
        value_a, slope_a = gelu_pair(pre_a)
        u_a = value_a.astype(bf16)
        ul[z, :, head] = u_a

        @pl.when(z < planes - 1)
        def _():
            near_copy(z, head, 0).start()

        step = dot_nn(u_a, nn[z, 0:rank, rank:4 * rank])
        y_a = acc[:, 2 * rank:3 * rank]
        norm_b = norm_a + jnp.sum(u_a.astype(f32) * (2.0 * y_a + step[:, rank:2 * rank]),
                                  axis=1, keepdims=True)
        scale_b = lax.rsqrt(norm_b * (1.0 / width) + eps)
        pre_b = (acc[:, rank:2 * rank] + step[:, 0:rank]) * scale_b
        value_b, slope_b = gelu_pair(pre_b)
        u_b = value_b.astype(bf16)
        ul[z, :, tail] = u_b

        @pl.when(z < planes - 1)
        def _():
            near_copy(z, tail, 1).start()

        y_b = acc[:, 2 * rank:4 * rank] + step[:, rank:3 * rank]
        more = dot_nn(u_b, nn[z, rank:2 * rank, 2 * rank:4 * rank])
        norm_c = norm_b + jnp.sum(
            u_b.astype(f32) * (2.0 * y_b[:, rank:2 * rank] + more[:, rank:2 * rank]),
            axis=1, keepdims=True)

        @pl.when(z < planes - 1)
        def _():
            nsend[...] = jnp.broadcast_to(to_row(norm_c), nsend.shape)
            n_copy().start()

        uf_copy().start()
        for o in range(2, planes):
            u_copy(o).start()

        @pl.when(z == planes - 1)
        def _():
            u_copy(1).start()

        uf[mine, :] = ul[z]
        ys[2 * z + 1] = y_b
        acc[:, 2 * rank:4 * rank] = y_b + more
        act[:, head] = pre_a
        act[:, tail] = pre_b
        slope[:, head] = slope_a
        slope[:, tail] = slope_b
        rinv[0] = jnp.broadcast_to(scale_a, (some, rank))
        rinv[1] = jnp.broadcast_to(scale_b, (some, rank))

    def c_of(stat):
        line = stat[0:1, :].astype(f32) + stat[1:2, :].astype(f32)
        return to_col(line[:, head]), to_col(line[:, tail])

    def backward_own():
        scale_b = rinv[1]
        q_b = hacc[:, tail] * slope[:, tail]
        low_b = (q_b * scale_b).astype(bf16)
        mix_b = jnp.sum(q_b * act[:, tail], axis=1, keepdims=True) * (1.0 / width)
        c_b = mix_b * scale_b[:, 0:1] * scale_b[:, 0:1]
        h_a = hacc[:, head] + dot_nt(low_b, nn[z, 0:rank, rank:2 * rank]) - c_b * ys[2 * z + 1, :, head]
        scale_a = rinv[0]
        q_a = h_a * slope[:, head]
        mix_a = jnp.sum(q_a * act[:, head], axis=1, keepdims=True) * (1.0 / width)
        c_a = mix_a * scale_a[:, 0:1] * scale_a[:, 0:1]
        ql[z, 0:some, head] = (q_a * scale_a).astype(bf16)
        ql[z, 0:some, tail] = low_b
        spot = lax.broadcasted_iota(jnp.int32, (16, rank), 0)
        for part, col in ((head, c_a), (tail, c_b)):
            line = to_row(col)
            high = line.astype(bf16).astype(f32)
            ql[z, some:some + 16, part] = jnp.where(
                spot == 0, high, jnp.where(spot == 1, line - high, 0.0)).astype(bf16)

        def send(i, carry):
            q_copy(z - 1 - i).start()
            return carry

        lax.fori_loop(0, z, send, 0)
        qp_copy().start()

    shard = mine_u.shape[0]
    nacc[...] = jnp.zeros_like(nacc)

    def core_copy(b):
        return remote(part.at[b, 1 - core], rc.at[b], k_send.at[b], k_recv.at[b], other_core)

    def collect(b):
        block_sum(b, yh_n, x_n, core_copy, part, rc, sums, rax, rby,
                  ax_send, ax_recv, by_send, by_recv)

    def terms(b):
        cols = pl.ds(pl.multiple_of(b * 2 * shard, 128), 2 * shard)
        u = us[...]
        before = xb[:, cols]
        wide = before.astype(f32)
        nacc[...] += jnp.broadcast_to(jnp.sum(wide * wide, axis=1, keepdims=True), nacc.shape)
        g_down = dot_tn(before, qv[...]).astype(bf16)
        g_up = dot_tn(gout[:, cols], u).astype(bf16)
        for i in range(2):
            part[b, i, :, head] = g_down[i * shard:(i + 1) * shard]
            part[b, i, :, tail] = g_up[i * shard:(i + 1) * shard]
        core_copy(b).start()

    def tick(t, carry):
        k = t - 1
        sent = (k >= 0) & (k < planes)
        near = sent & (k == z - 1)

        @pl.when(sent & (k != z) & (k != z - 1))
        def _():
            u_arrived(k).wait_recv()

        @pl.when(near)
        def _():
            near_copy(k, head, 0).wait_recv()
            acc[...] += dot_nn(ul[k, :, head], nn[k, 0:rank, :])
            near_copy(k, tail, 1).wait_recv()
            acc[...] += dot_nn(ul[k, :, tail], nn[k, rank:2 * rank, :])

        @pl.when(sent & (k < z - 1))
        def _():
            acc[...] += dot_nn(ul[k], nn[k])

        @pl.when(t == z)
        def _():
            forward_own()

        @pl.when(sent & (k > z))
        def _():
            before = acc[:, 2 * rank:4 * rank]
            ys[2 * k] = before
            between = before + dot_nn(ul[k, :, head], nn[k, 0:rank, 2 * rank:4 * rank])
            ys[2 * k + 1] = between
            acc[:, 2 * rank:4 * rank] = between + dot_nn(
                ul[k, :, tail], nn[k, rank:2 * rank, 2 * rank:4 * rank])

        r = 2 * planes - t

        @pl.when((r < planes) & (r > z))
        def _():
            q_arrived(r).wait_recv()
            c_a, c_b = c_of(ql[r, some:some + 16, :])
            hacc[...] += (dot_nn(ql[r, 0:some, :], nn[r, :, 0:2 * rank]) - c_a * ys[2 * r] - c_b * ys[2 * r + 1])

        @pl.when(t == 2 * planes - 1 - z)
        def _():
            backward_own()

        p = t - (z + 1)

        @pl.when((p >= 0) & (p < trips))
        def _():
            @pl.when(p == 0)
            def _():
                for load in loads[:3]:
                    load.wait()
                uf_arrived().wait_recv()
            chain(p)

        q = t - (z + 1 + trips)

        @pl.when((q >= 0) & (q < chunks // 4))
        def _():
            for j in range(4):
                give_copy(4 * q + j).start()

        b = t - (2 * planes - z)

        @pl.when((b >= 0) & (b < trips))
        def _():
            @pl.when(b == 0)
            def _():
                for load in loads[3:]:
                    load.wait()
                qp_copy().wait_recv()
                qs[mine, :] = ql[z, 0:some, :]
                qs[theirs, :] = qp[0:some, :]
                for where, stat in ((mine, ql[z, some:some + 16, :]), (theirs, qp[some:some + 16, :])):
                    c_a, c_b = c_of(stat)
                    cpair[0, where, :] = jnp.broadcast_to(c_a, (some, rank))
                    cpair[1, where, :] = jnp.broadcast_to(c_b, (some, rank))
                us[...] = jnp.where(first, uf[:, head], uf[:, tail])
                qv[...] = jnp.where(first, qs[:, head], qs[:, tail])
            chain_back(b)
            terms(ylo * trips + b)

        @pl.when((b >= 1) & (b <= trips))
        def _():
            collect(ylo * trips + b - 1)

            def landed(j, carry):
                c = per * (b - 1) + j
                pass_arrived(c).wait_recv()
                h_arrived(c).wait_recv()
                return carry

            lax.fori_loop(0, per, landed, 0)
            terms((1 - ylo) * trips + b - 1)

        @pl.when((b >= 2) & (b <= trips))
        def _():
            collect((1 - ylo) * trips + b - 2)

        return carry

    lax.fori_loop(0, 2 * planes + trips + 1, tick, 0)
    collect((1 - ylo) * trips + trips - 1)

    def landed_x(c, carry):
        give_arrived(c).wait_recv()
        return carry

    lax.fori_loop(0, chunks, landed_x, 0)
    save_x = pltpu.make_async_copy(xout, xout_far, l_sem.at[6])
    save_x.start()
    total_a, total_b = scatter_sum(yh_n, x_n, sums, rax, rby, sa, ray, sb, rbx,
                                   ax_send, ax_recv, by_send, by_recv, s_sem, bx_send, bx_recv)
    cut = shard // 2
    gw[0:cut] = total_a[:, head].astype(bf16)
    gw[cut:shard] = total_b[:, head].astype(bf16)
    gu[0:cut] = total_a[:, tail].astype(bf16)
    gu[cut:shard] = total_b[:, tail].astype(bf16)
    has_next = s < sections - 1
    down_section = {"section": lax.rem(s + sections - 1, sections)}

    def pair_of(sems, i):
        return sems.at[2 * i], sems.at[2 * i + 1]

    def w_x(i):
        return remote(gw, own_w.at[yh, x, core], *pair_of(wx_sem, i), place(yh, xp(i), core))

    def w_y(i):
        spot = own_w.at[yh, xp(i), core]
        return remote(gw if i == 0 else spot, spot, *pair_of(wy_sem, i), other_y)

    def w_c(i):
        spot = own_w.at[:, xp(i), core]
        return remote(spot, spot, *pair_of(wc_sem, i), other_core)

    v_y = remote(gu, own_u.at[yh, x, core], *pair_of(vx_sem, 0), other_y)

    def v_x(i):
        spot = own_u.at[:, x, core]
        return remote(spot, spot, *pair_of(vx_sem, i), place(yh, xp(i), core))

    def v_c(i):
        spot = own_u.at[:, xp(i), core]
        return remote(spot, spot, *pair_of(vc_sem, i), other_core)

    next_copy = remote(nw, nxt_u.at[yh, x, core], *pair_of(nx_sem, 0), down_section)
    bump_copy = remote(ub, bump_u, *pair_of(nx_sem, x_n), down_section)

    def n_x(i):
        spot = nxt_u.at[yh, x, core]
        return remote(spot, spot, *pair_of(nx_sem, i), place(yh, xp(i), core))

    def n_y(i):
        spot = nxt_u.at[yh, xp(i), core]
        return remote(spot, spot, *pair_of(ny_sem, i), other_y)

    def n_c(i):
        spot = nxt_u.at[:, xp(i), core]
        return remote(spot, spot, *pair_of(nc_sem, i), other_core)

    for i in range(1, x_n):
        w_x(i).start()
    v_y.start()
    w_y(0).start()

    @pl.when(s > 0)
    def _():
        nw[...] = (mine_u[...].astype(f32) - learn_rate * gu[...].astype(f32)).astype(bf16)
        next_copy.start()

    own_w[yh, x, core] = gw[...]
    own_u[yh, x, core] = gu[...]
    @pl.when(has_next)
    def _():
        next_copy.wait_recv()
        for i in range(1, x_n):
            n_x(i).start()

    for i in range(1, x_n):
        w_x(x_n - i).wait_recv()
        w_y(i).start()

    @pl.when(has_next)
    def _():
        n_y(0).start()
        for i in range(1, x_n):
            n_x(i).wait_send()

    v_y.wait_recv()
    for i in range(1, x_n):
        v_x(i).start()
    v_c(0).start()

    for i in range(x_n):
        w_y(i).wait_recv()
        w_c(i).start()

    @pl.when(has_next)
    def _():
        for i in range(1, x_n):
            n_x(x_n - i).wait_recv()
            n_y(i).start()

    for i in range(1, x_n):
        v_x(x_n - i).wait_recv()
        v_c(i).start()
    for i in range(x_n):
        w_c(i).wait()
    save_w = pltpu.make_async_copy(own_w, own_w_far, l_sem.at[7])
    save_w.start()

    @pl.when(s > 0)
    def _():
        def ahead(b, pre):
            y_ = b // x_n
            x_ = lax.rem(b, x_n)
            cols = pl.ds(pl.multiple_of(b * 2 * shard, 128), 2 * shard)
            both = jnp.concatenate([own_w[y_, x_, 0], own_w[y_, x_, 1]], axis=0)
            fresh = wd[cols, :].astype(f32) - learn_rate * both.astype(f32)
            return pre + dot_nn(xb[:, cols], fresh.astype(bf16))

        pre = lax.fori_loop(0, yh_n * x_n, ahead, jnp.zeros((rows, rank), f32))
        value, unused = gelu_pair(pre * lax.rsqrt(nacc[...] * (1.0 / width) + eps))
        ub[...] = value.astype(bf16)
        bump_copy.start()

    @pl.when(has_next)
    def _():
        for i in range(x_n):
            n_y(i).wait_recv()
            n_c(i).start()
        for i in range(x_n):
            n_c(i).wait()
            n_y(i).wait_send()
        bump_copy.wait_recv()

    for i in range(x_n):
        v_c(i).wait()
        w_y(i).wait_send()
    for i in range(1, x_n):
        w_x(i).wait_send()
        v_x(i).wait_send()
    v_y.wait_send()

    @pl.when(s > 0)
    def _():
        next_copy.wait_send()
        bump_copy.wait_send()

    def core_settle(b, carry):
        core_copy(b).wait_send()
        return carry

    lax.fori_loop(0, yh_n * x_n, core_settle, 0)
    save_x.wait()
    save_w.wait()

    def finish(c, carry):
        @pl.when(z < planes - 1)
        def _():
            x_copy(c).wait_send()
        give_copy(c).wait_send()
        pass_copy(c).wait_send()

        @pl.when(z > 0)
        def _():
            b_copy(c).wait_send()
        h_copy(c).wait_send()
        return carry

    lax.fori_loop(0, chunks, finish, 0)
    for o in range(2, planes):
        u_copy(o).wait_send()

    @pl.when(z == planes - 1)
    def _():
        u_copy(1).wait_send()

    @pl.when(z < planes - 1)
    def _():
        near_copy(z, head, 0).wait_send()
        near_copy(z, tail, 1).wait_send()
        n_copy().wait_send()

    def settle(j, carry):
        q_copy(j).wait_send()
        return carry

    lax.fori_loop(0, z, settle, 0)
    uf_copy().wait_send()
    qp_copy().wait_send()


def recurrence(sections, shards, pyh, n0, nn, x0, g16, up, wd, upart, wpart, mine_u):
    rows, width = x0.shape
    rank = up.shape[0]
    half = width // 2
    some = rows // 2
    planes = sections // 2
    chunks = 28
    per = 7
    x_n = 4
    yh_n = shards // (2 * x_n)
    shard = mine_u.shape[0]
    cut = shard // 2
    blocks = yh_n * x_n
    vm = pl.BlockSpec(memory_space=pltpu.VMEM)
    dma = pltpu.SemaphoreType.DMA
    sq = (rows, rank)
    two = (some, 2 * rank)
    strip = pltpu.VMEM((rows, half), bf16)
    full = jax.ShapeDtypeStruct((yh_n, x_n, 2, shard, rank), bf16)

    def buf(*lead):
        return pltpu.VMEM(lead + (2 * rank,), bf16)

    return pl.pallas_call(
        functools.partial(recurrence_kernel, sections, chunks, per, yh_n, x_n),
        out_shape=(jax.ShapeDtypeStruct((rows, width), bf16), full, full, full,
                   jax.ShapeDtypeStruct(sq, bf16)),
        in_specs=[vm] * 3 + [pl.BlockSpec(memory_space=pl.ANY)] * 6 + [vm],
        out_specs=(pl.BlockSpec(memory_space=pl.ANY),) * 2 + (vm,) * 3,
        scratch_shapes=[
            pltpu.VMEM((planes,) + two, bf16),
            pltpu.VMEM((planes, some + 16, 2 * rank), bf16),
            pltpu.VMEM((some + 16, 2 * rank), bf16),
            pltpu.VMEM((sections,) + two, f32),
            pltpu.VMEM((8, rank), f32),
            pltpu.VMEM((8, rank), f32),
            pltpu.VMEM((some, 4 * rank), f32),
            pltpu.VMEM(two, f32), pltpu.VMEM(two, f32), pltpu.VMEM(two, f32),
            pltpu.VMEM((2, some, rank), f32),
            pltpu.VMEM((rows, 2 * rank), bf16),
            pltpu.VMEM((rows, 2 * rank), bf16),
            pltpu.VMEM((2,) + sq, f32),
            strip, strip, strip, strip, strip, strip, strip,
            pltpu.VMEM((2, rows, half * per // chunks), f32),
            pltpu.VMEM((rows, width), bf16),
            pltpu.VMEM(sq, bf16), pltpu.VMEM(sq, bf16),
            pltpu.VMEM((rows, width), bf16), pltpu.VMEM(sq, f32),
            buf(blocks, 2, shard), buf(blocks, shard), buf(yh_n, x_n, shard),
            buf(x_n - 1, yh_n, cut), buf(x_n, cut), buf(yh_n, cut), buf(cut),
            buf(x_n, cut), buf(x_n - 1, cut),
            pltpu.VMEM((shard, rank), bf16), pltpu.VMEM((shard, rank), bf16),
            pltpu.VMEM((shard, rank), bf16), pltpu.VMEM(sq, bf16),
            pltpu.VMEM((rows, width), bf16), pltpu.VMEM((rows, width), bf16),
            pltpu.VMEM((rank, width), bf16), pltpu.VMEM((width, rank), bf16),
            pltpu.VMEM((rank, half), bf16), pltpu.VMEM((half, rank), bf16),
            pltpu.VMEM((rows, width), bf16), pltpu.VMEM((yh_n, x_n, 2, shard, rank), bf16), dma((8,)),
        ] + [dma((planes,))] * 4 + [dma((10,))] + [dma((chunks,))] * 10 + [
            dma((blocks,)), dma((blocks,)),
            dma((yh_n * (x_n - 1),)), dma((yh_n * (x_n - 1),)), dma((x_n,)), dma((x_n,)), dma((2,)),
            dma((x_n - 1,)), dma((x_n - 1,)),
            dma((2 * x_n,)), dma((2 * x_n,)), dma((2 * x_n,)), dma((2 * x_n,)), dma((2 * x_n,)),
            dma((2 * x_n + 2,)), dma((2 * x_n,)), dma((2 * x_n,)),
        ],
        compiler_params=pltpu.CompilerParams(
            collective_id=1, has_side_effects=True, vmem_limit_bytes=60 * 1024 * 1024),
    )(pyh, n0, nn, x0, g16, up, wd, upart, wpart, mine_u)


def dp_place(x_n):
    d = lax.axis_index("dp")
    return d // (2 * x_n), lax.rem(d // 2, x_n), lax.rem(d, 2)


def remote(src, dst, send, recv, where):
    return pltpu.make_async_remote_copy(src_ref=src, dst_ref=dst, send_sem=send, recv_sem=recv,
                                        device_id=where, device_id_type=MESH)


def block_sum(b, yh_n, x_n, core_copy, part, rc, sums, rax, rby, ax_send, ax_recv, by_send, by_recv):
    yh, x, core = dp_place(x_n)
    cut = sums.shape[2] // 2
    y_ = b // x_n
    x_ = lax.rem(b, x_n)
    core_copy(b).wait_recv()
    sums[y_, x_] = (part[b, core].astype(f32) + rc[b].astype(f32)).astype(bf16)
    turn = lax.rem(x_ - x + x_n, x_n)

    @pl.when(turn != 0)
    def _():
        sem = (turn - 1) * yh_n + y_
        remote(sums.at[y_, x_, 0:cut], rax.at[turn - 1, y_], ax_send.at[sem], ax_recv.at[sem],
               {"dp": (yh * x_n + x_) * 2 + core}).start()

    @pl.when(y_ != yh)
    def _():
        remote(sums.at[y_, x_, cut:2 * cut], rby.at[x_], by_send.at[x_], by_recv.at[x_],
               {"dp": (y_ * x_n + x) * 2 + core}).start()


def scatter_sum(yh_n, x_n, sums, rax, rby, sa, ray, sb, rbx,
                ax_send, ax_recv, by_send, by_recv, s_sem, bx_send, bx_recv):
    yh, x, core = dp_place(x_n)
    rows = sums.shape[2]
    cut = rows // 2

    def place(y_, x_, c_):
        return {"dp": (y_ * x_n + x_) * 2 + c_}

    def xp(i):
        return lax.rem(x + i, x_n)

    other_y = place(1 - yh, x, core)

    def ax_copy(i, y_):
        sem = (i - 1) * yh_n + y_
        return remote(sums.at[y_, xp(i), 0:cut], rax.at[i - 1, y_], ax_send.at[sem], ax_recv.at[sem],
                      place(yh, xp(i), core))

    def by_copy(x_):
        return remote(sums.at[1 - yh, x_, cut:rows], rby.at[x_], by_send.at[x_], by_recv.at[x_], other_y)

    def bx_copy(i):
        return remote(sb.at[xp(i)], rbx.at[i - 1], bx_send.at[i - 1], bx_recv.at[i - 1],
                      place(yh, xp(i), core))

    ay_copy = remote(sa.at[1 - yh], ray, s_sem.at[0], s_sem.at[1], other_y)

    for i in range(x_n):
        x_ = xp(i)
        by_copy(x_).wait_recv()
        sb[x_] = (sums[yh, x_, cut:rows].astype(f32) + rby[x_].astype(f32)).astype(bf16)
        if i > 0:
            bx_copy(i).start()
    for y_ in range(yh_n):
        total = sums[y_, x, 0:cut].astype(f32)
        for i in range(1, x_n):
            ax_copy(i, y_).wait_recv()
            total = total + rax[i - 1, y_].astype(f32)
        sa[y_] = total.astype(bf16)
    ay_copy.start()
    total_b = sb[x].astype(f32)
    for i in range(1, x_n):
        bx_copy(i).wait_recv()
        total_b = total_b + rbx[i - 1].astype(f32)
    ay_copy.wait_recv()
    total_a = sa[yh].astype(f32) + ray[...].astype(f32)
    for i in range(1, x_n):
        for y_ in range(yh_n):
            ax_copy(i, y_).wait_send()
        bx_copy(i).wait_send()
    for x_ in range(x_n):
        by_copy(x_).wait_send()
    ay_copy.wait_send()
    return total_a, total_b


def gram_kernel(yh_n, x_n, sections, x0_far, g16_far, down_far, up_far, mine_u, pyh, n0, out, upart, wpart,
                allu, part, rc, sums, rax, rby, sa, ray, sb, rbx, gs, gp, two, mine3, theirs3, flip, turned,
                x0, g16, down, up, base, mine_w, l_sem,
                z_sem, f_send, f_recv, r_send, r_recv,
                c_send, c_recv, ax_send, ax_recv, by_send, by_recv, s_sem, bx_send, bx_recv,
                ga_send, ga_recv, gb_send, gb_recv, gc_send, gc_recv, t_sem):
    loads = [pltpu.make_async_copy(far, near, l_sem.at[i]) for i, (far, near) in enumerate((
        (up_far, up), (down_far, down), (x0_far, x0), (g16_far, g16)))]
    height = mine_u.shape[0]
    own_rows = pl.ds(pl.multiple_of(lax.axis_index("dp") * height, 64), height)
    load_w = pltpu.make_async_copy(down_far.at[own_rows, :], mine_w, l_sem.at[4])
    load_w.start()
    for load in loads:
        load.start()
    yh, x, core = dp_place(x_n)
    s = lax.axis_index("section")
    z_n = sections // 2
    z = s // 2
    ylo = lax.rem(s, 2)
    rank = up.shape[0]
    rows = rank
    cut = rows // 2

    def place(y_, x_, c_):
        return {"dp": (y_ * x_n + x_) * 2 + c_}

    def xp(i):
        return lax.rem(x + i, x_n)

    def zp(i):
        return lax.rem(z + i, z_n)

    other_core = place(yh, x, 1 - core)
    other_y = place(1 - yh, x, core)
    partner = {"section": s + 1 - 2 * ylo}
    after = {"section": 2 * zp(1) + ylo}
    before = {"section": 2 * zp(z_n - 1) + ylo}

    barrier = pltpu.get_barrier_semaphore()
    peers = [other_core, other_y, partner, after, before]
    peers += [place(yh, xp(i), core) for i in range(1, x_n)]
    for where in peers:
        pl.semaphore_signal(barrier, inc=1, device_id=where, device_id_type=MESH)
    d = lax.axis_index("dp")
    above = d // 2 < z
    below = d // 2 > z
    mirror = [{"section": 2 * (d // 2) + i, "dp": s} for i in range(2)]

    @pl.when(below)
    def _():
        for i in range(2):
            pl.semaphore_signal(barrier, inc=1, device_id={"section": d, "dp": 2 * z + i},
                                device_id_type=MESH)

    pl.semaphore_wait(barrier, len(peers) + 2 * above.astype(jnp.int32))

    def flip_copy(i):
        k = lax.rem(d, 2)
        return remote(flip, turned.at[k], t_sem.at[i], t_sem.at[2 + k], mirror[i])

    def flip_arrived(i):
        return remote(flip, turned.at[i], t_sem.at[0], t_sem.at[2 + i], mirror[0])

    pair = remote(mine_u, allu.at[z, ylo], z_sem.at[0], z_sem.at[1], partner)

    def products(z_):
        for y_ in range(2):
            part[z_, y_] = dot_tn(allu[z_, y_], base[...]).astype(bf16)

    def core_copy(b):
        return remote(part.at[b, 1 - core], rc.at[b], c_send.at[b], c_recv.at[b], other_core)

    hops = z_n // 2

    def column(j):
        return ylo if j == 0 else 1 - ylo

    def ring_f(i, j):
        spot = allu.at[zp(z_n + 1 - i), column(j)]
        src = mine_u if (i == 1 and j == 0) else spot
        sem = 2 * (i - 1) + j
        return remote(src, spot, f_send.at[sem], f_recv.at[sem], after)

    def ring_r(i, j):
        spot = allu.at[zp(i - 1), column(j)]
        src = mine_u if (i == 1 and j == 0) else spot
        sem = 2 * (i - 1) + j
        return remote(src, spot, r_send.at[sem], r_recv.at[sem], before)

    used_f = [(i, j) for i in range(1, hops + 1) for j in range(2) if i < hops or j == 0]
    used_r = [(i, j) for i in range(1, hops + 1) for j in range(2) if i < hops or j == 1]

    pair.start()
    ring_f(1, 0).start()
    ring_r(1, 0).start()
    allu[z, ylo] = mine_u[...]
    pair.wait_recv()
    ring_f(1, 1).start()
    ring_r(1, 1).start()

    half = x0.shape[1] // 2
    quarter = half // 2
    far = pl.ds(pl.multiple_of((1 - ylo) * half + core * quarter, 128), quarter)
    near = pl.ds(pl.multiple_of(core * quarter, 128), quarter)
    swap_u = remote(up.at[:, far], upart.at[:, near], z_sem.at[6], z_sem.at[7], partner)
    swap_w = remote(down.at[far, :], wpart.at[near, :], z_sem.at[8], z_sem.at[9], partner)
    share_u = remote(upart.at[:, near], upart.at[:, near], z_sem.at[10], z_sem.at[11], other_core)
    share_w = remote(wpart.at[near, :], wpart.at[near, :], z_sem.at[12], z_sem.at[13], other_core)
    token_half = x0.shape[0] // 2
    keep = pl.ds(ylo * token_half, token_half)
    give = pl.ds((1 - ylo) * token_half, token_half)
    swap3 = remote(mine3.at[:, give], theirs3, z_sem.at[2], z_sem.at[3], partner)

    def project(i):
        if i == 1:
            for load in loads[2:]:
                load.wait()
            mine3[0] = dot_nn(x0[...], down[...])
            mine3[1] = dot_nt(x0[...], up[...])
        elif i == 2:
            mine3[2] = dot_nt(g16[...], up[...])
            swap3.start()
            wide = x0[keep, :].astype(f32)
            n0[...] = jnp.broadcast_to(jnp.sum(wide * wide, axis=1, keepdims=True), n0.shape)

    def collect(b):
        block_sum(b, yh_n, x_n, core_copy, part, rc, sums, rax, rby,
                  ax_send, ax_recv, by_send, by_recv)

    for load in loads[:2]:
        load.wait()
    swap_u.start()
    swap_w.start()
    load_w.wait()
    base[:, 0:rank] = mine_w[...]
    base[:, rank:2 * rank] = mine_u[...]
    products(z)
    core_copy(z).start()
    for i in range(1, hops + 1):
        for j in range(2):
            if (i, j) in used_f:
                ring_f(i, j).wait_recv()
                if (i + 1, j) in used_f:
                    ring_f(i + 1, j).start()
            if (i, j) in used_r:
                ring_r(i, j).wait_recv()
                if (i + 1, j) in used_r:
                    ring_r(i + 1, j).start()
        if i < hops:
            project(i)
        products(zp(z_n - i))
        core_copy(zp(z_n - i)).start()
        if i == 1:
            collect(z)
        else:
            collect(zp(i - 1))
        if i < hops:
            products(zp(i))
            core_copy(zp(i)).start()
        collect(zp(z_n - i))

    swap_u.wait_recv()
    share_u.start()
    swap_w.wait_recv()
    share_w.start()
    total_a, total_b = scatter_sum(yh_n, x_n, sums, rax, rby, sa, ray, sb, rbx,
                                   ax_send, ax_recv, by_send, by_recv, s_sem, bx_send, bx_recv)
    gs[0:cut] = total_a.astype(bf16)
    gs[cut:rows] = total_b.astype(bf16)
    swap = remote(gs, gp, z_sem.at[4], z_sem.at[5], partner)
    swap.start()

    @pl.when(above)
    def _():
        flip[...] = gs[:, 0:rank].astype(f32).T.astype(bf16)
        for i in range(2):
            flip_copy(i).start()

    def lanes(base, which):
        return pl.ds(pl.multiple_of(base + which * rank, 128), rank)

    swap3.wait_recv()
    pyh[:, :, lanes(0, ylo)] = mine3[:, keep]
    pyh[:, :, lanes(0, 1 - ylo)] = theirs3[...]
    two[:, lanes(0, ylo)] = gs[:, 0:rank]
    two[:, lanes(2 * rank, ylo)] = gs[:, rank:2 * rank]
    swap.wait_recv()
    two[:, lanes(0, 1 - ylo)] = gp[:, 0:rank]
    two[:, lanes(2 * rank, 1 - ylo)] = gp[:, rank:2 * rank]

    @pl.when(below)
    def _():
        for i in range(2):
            flip_arrived(i).wait_recv()
            two[:, i * rank:(i + 1) * rank] = turned[i]
    out[yh, x, core] = two[...]

    low = pl.ds(0, cut)
    high = pl.ds(cut, cut)

    def spread(src, spot, sems, i, where):
        return remote(src, spot, sems[0].at[i], sems[1].at[i], where)

    ga = (ga_send, ga_recv)
    gb = (gb_send, gb_recv)
    a_y = spread(two.at[low], out.at[yh, x, core, low], ga, 0, other_y)

    def a_x(i):
        spot = out.at[:, x, core, low]
        return spread(spot, spot, ga, i, place(yh, xp(i), core))

    def b_x(i):
        return spread(two.at[high], out.at[yh, x, core, high], gb, i - 1, place(yh, xp(i), core))

    def b_y(i):
        spot = out.at[yh, xp(i), core, high]
        return spread(spot, spot, gb, x_n - 1 + i, other_y)

    def all_c(i):
        spot = out.at[:, xp(i), core]
        return remote(spot, spot, gc_send.at[i], gc_recv.at[i], other_core)

    a_y.start()
    for i in range(1, x_n):
        b_x(i).start()
    b_y(0).start()
    a_y.wait_recv()
    for i in range(1, x_n):
        a_x(i).start()
    for i in range(1, x_n):
        b_x(x_n - i).wait_recv()
        b_y(i).start()
    b_y(0).wait_recv()
    all_c(0).start()
    for i in range(1, x_n):
        a_x(x_n - i).wait_recv()
        b_y(i).wait_recv()
        all_c(i).start()
    for i in range(x_n):
        all_c(i).wait()
        b_y(i).wait_send()
    for i in range(1, x_n):
        a_x(i).wait_send()
        b_x(i).wait_send()
    a_y.wait_send()
    pair.wait_send()
    swap.wait_send()
    swap3.wait_send()

    @pl.when(above)
    def _():
        for i in range(2):
            flip_copy(i).wait_send()
    swap_u.wait_send()
    swap_w.wait_send()
    share_u.wait()
    share_w.wait()
    for i, j in used_f:
        ring_f(i, j).wait_send()
    for i, j in used_r:
        ring_r(i, j).wait_send()

    def settle(b, carry):
        core_copy(b).wait_send()
        return carry

    lax.fori_loop(0, yh_n * x_n, settle, 0)


def grams_of(sections, shards, x0, g16, down, up, mine_u):
    x_n = 4
    yh_n = shards // (2 * x_n)
    rows, width = x0.shape
    rank = up.shape[0]
    height = mine_u.shape[0]
    cut = rank // 2
    vm = pl.BlockSpec(memory_space=pltpu.VMEM)
    dma = pltpu.SemaphoreType.DMA

    def buf(*lead):
        return pltpu.VMEM(lead + (2 * rank,), bf16)

    return pl.pallas_call(
        functools.partial(gram_kernel, yh_n, x_n, sections),
        out_shape=(
            jax.ShapeDtypeStruct((3, rows // 2, 2 * rank), f32),
            jax.ShapeDtypeStruct((rows // 2, rank), f32),
            jax.ShapeDtypeStruct((yh_n, x_n, 2, rank, 4 * rank), bf16),
            jax.ShapeDtypeStruct((rank, width // 2), bf16),
            jax.ShapeDtypeStruct((width // 2, rank), bf16),
        ),
        in_specs=[pl.BlockSpec(memory_space=pl.ANY)] * 4 + [vm],
        out_specs=(vm,) * 5,
        scratch_shapes=[
            pltpu.VMEM((sections // 2, 2, height, rank), bf16),
            buf(yh_n * x_n, 2, rank), buf(yh_n * x_n, rank), buf(yh_n, x_n, rank),
            buf(x_n - 1, yh_n, cut), buf(x_n, cut), buf(yh_n, cut), buf(cut),
            buf(x_n, cut), buf(x_n - 1, cut), buf(rank), buf(rank),
            pltpu.VMEM((rank, 4 * rank), bf16),
            pltpu.VMEM((3, rows, rank), f32), pltpu.VMEM((3, rows // 2, rank), f32),
            pltpu.VMEM((rank, rank), bf16), pltpu.VMEM((2, rank, rank), bf16),
            pltpu.VMEM((rows, width), bf16), pltpu.VMEM((rows, width), bf16),
            pltpu.VMEM((width, rank), bf16), pltpu.VMEM((rank, width), bf16),
            pltpu.VMEM((height, 2 * rank), bf16), pltpu.VMEM((height, rank), bf16), dma((5,)),
            dma((14,)), dma((sections // 2,)), dma((sections // 2,)),
            dma((sections // 2,)), dma((sections // 2,)),
            dma((yh_n * x_n,)), dma((yh_n * x_n,)),
            dma((yh_n * (x_n - 1),)), dma((yh_n * (x_n - 1),)), dma((x_n,)), dma((x_n,)), dma((4,)),
            dma((x_n - 1,)), dma((x_n - 1,)),
            dma((x_n,)), dma((x_n,)), dma((2 * x_n,)), dma((2 * x_n,)), dma((x_n,)), dma((x_n,)), dma((4,)),
        ],
        compiler_params=pltpu.CompilerParams(
            collective_id=3, has_side_effects=True, vmem_limit_bytes=60 * 1024 * 1024),
    )(x0, g16, down, up, mine_u)


def finish_kernel(sections, own_w, own_u, nxt_u, bump_u, x1, grad_down, grad_up, advance):
    last = lax.axis_index("section") == sections - 1
    grad_down[...] = own_w[...]
    grad_up[...] = own_u[...].astype(f32).T.astype(bf16)
    bump = dot_nt(bump_u[...], nxt_u[...])
    advance[...] = (x1[...].astype(f32) + jnp.where(last, 0.0, bump)).astype(bf16)


def finish(sections, own_w, own_u, nxt_u, bump_u, x1):
    rows, width = x1.shape
    rank = own_w.shape[1]
    step = width // 8
    tall = pl.BlockSpec((step, rank), lambda i: (i, 0))
    flat = pl.BlockSpec((rows, step), lambda i: (0, i))
    return pl.pallas_call(
        functools.partial(finish_kernel, sections),
        grid=(width // step,),
        out_shape=(
            jax.ShapeDtypeStruct((width, rank), bf16),
            jax.ShapeDtypeStruct((rank, width), bf16),
            jax.ShapeDtypeStruct((rows, width), bf16),
        ),
        in_specs=[tall, tall, tall, pl.BlockSpec((rows, rank), lambda i: (0, 0)), flat],
        out_specs=(tall, flat, flat),
        compiler_params=pltpu.CompilerParams(vmem_limit_bytes=60 * 1024 * 1024),
    )(own_w, own_u, nxt_u, bump_u, x1)


def per_device(inputs, cotangent, w_down, w_up):
    down = w_down[0]
    upward = w_up[0]
    micro, batch_rows, width = inputs.shape
    rank = down.shape[1]
    rows = micro * batch_rows
    sections = lax.axis_size("section")
    shards = lax.axis_size("dp")
    part = width // shards
    d = lax.axis_index("dp")
    x0 = inputs.reshape(rows, width)
    g16 = cotangent.reshape(rows, width)
    up_t = upward.T

    mine_u = lax.dynamic_slice_in_dim(up_t, d * part, part, 0)
    pyh, n0, grams, upart, wpart = grams_of(sections, shards, x0, g16, down, upward, mine_u)
    grams = grams.reshape(sections // 2, 2 * rank, 4 * rank)
    x1, own_w, own_u, nxt_u, bump_u = recurrence(
        sections, shards, pyh, n0, grams, x0, g16, upward, down, upart, wpart, mine_u)
    tall = (width, rank)
    grad_down, grad_up, advance = finish(
        sections, own_w.reshape(tall), own_u.reshape(tall), nxt_u.reshape(tall), bump_u, x1)
    return (grad_down[None], grad_up[None], advance.reshape(1, micro, batch_rows, width))


def solution(mesh):
    in_specs = (
        P(None, "dp", None),
        P(None, "dp", None),
        P("section", None, None),
        P("section", None, None),
    )
    out_specs = (P("section", None, None), P("section", None, None), P("section", None, "dp", None))
    return jax.shard_map(
        per_device, mesh=mesh, in_specs=in_specs, out_specs=out_specs, check_vma=False
    )
```

```python
import functools

import jax
import jax.numpy as jnp
from jax import lax
from jax.experimental import pallas as pl
from jax.experimental.pallas import tpu as pltpu
from jax.sharding import PartitionSpec as P

MESH = pl.DeviceIdType.MESH
eps = 1e-05
learn_rate = 0.05
f32 = jnp.float32
bf16 = jnp.bfloat16


def dot_nn(a, b):
    return jnp.dot(a, b, preferred_element_type=f32)


def dot_tn(a, b):
    return lax.dot_general(a, b, (((0,), (0,)), ((), ())), preferred_element_type=f32)


def dot_nt(a, b):
    return lax.dot_general(a, b, (((1,), (1,)), ((), ())), preferred_element_type=f32)


def gelu_pair(a):
    c = 0.7978845608028654
    inner = c * (a + 0.044715 * a * a * a)
    th = jnp.tanh(inner)
    value = 0.5 * a * (1.0 + th)
    slope = 0.5 * (1.0 + th) + 0.5 * a * (1.0 - th * th) * c * (1.0 + 3 * 0.044715 * a * a)
    return value, slope


def recurrence_kernel(sections, chunks, per, yh_n, x_n,
                      pyh, n0, nn, x0_far, g16_far, up_far, wd_far, upart_far, wpart_far, mine_u,
                      xout_far, own_w_far, own_u, nxt_u, bump_u,
                      ul, ql, qp, ys, nl, nsend, acc, hacc, slope, act, rinv, uf, qs, cpair,
                      xin, xkeep, xgive, gin, gkeep, ggive, xpass, delta,
                      gout, us, qv, xb, nacc, part, rc, sums, rax, rby, sa, ray, sb, rbx,
                      gw, gu, nw, ub, x0, g16, up, wd, upart, wpart, xout, own_w, l_sem,
                      u_send, u_recv, q_send, q_recv, e_sem,
                      c_send, c_recv, g_send, g_recv,
                      b_send, b_recv, h_send, h_recv, p_send, p_recv,
                      k_send, k_recv, ax_send, ax_recv, by_send, by_recv, s_sem, bx_send, bx_recv,
                      wx_sem, wy_sem, wc_sem, vx_sem, vc_sem, nx_sem, ny_sem, nc_sem):
    loads = [pltpu.make_async_copy(far, near, l_sem.at[i]) for i, (far, near) in enumerate((
        (up_far, up), (upart_far, upart), (x0_far, x0),
        (wd_far, wd), (wpart_far, wpart), (g16_far, g16)))]
    for load in loads:
        load.start()
    s = lax.axis_index("section")
    yh, x, core = dp_place(x_n)
    planes = sections // 2
    rows, width = x0.shape
    some = rows // 2
    rank = up.shape[0]
    half = width // 2
    piece = half // chunks
    trips = chunks // per
    z = s // 2
    ylo = lax.rem(s, 2)
    first = ylo == 0
    partner = {"section": s + 1 - 2 * ylo}
    head = slice(0, rank)
    tail = slice(rank, 2 * rank)
    mine = pl.ds(ylo * some, some)
    theirs = pl.ds((1 - ylo) * some, some)

    def plane(i):
        return {"section": 2 * i + ylo}

    def peer(offset):
        return lax.rem(z + offset, planes)

    barrier = pltpu.get_barrier_semaphore()
    for o in range(1, planes):
        pl.semaphore_signal(barrier, inc=1, device_id=plane(peer(o)), device_id_type=MESH)

    def place(y_, x_, c_):
        return {"dp": (y_ * x_n + x_) * 2 + c_}

    def xp(i):
        return lax.rem(x + i, x_n)

    other_core = place(yh, x, 1 - core)
    other_y = place(1 - yh, x, core)
    beyond = {"section": lax.rem(s + sections - 1 + 2 * ylo, sections)}
    others = [partner, beyond, other_core, other_y] + [place(yh, xp(i), core) for i in range(1, x_n)]
    for where in others:
        pl.semaphore_signal(barrier, inc=1, device_id=where, device_id_type=MESH)
    pl.semaphore_wait(barrier, planes - 1 + len(others))

    eye = (lax.broadcasted_iota(jnp.int32, (some, rank), 0)
           == lax.broadcasted_iota(jnp.int32, (some, rank), 1)).astype(f32)

    def to_row(col):
        return jnp.sum(eye * col, axis=0, keepdims=True)

    def to_col(row):
        return jnp.sum(eye * row, axis=1, keepdims=True)

    def columns(base, c):
        return pl.ds(pl.multiple_of(base + c * piece, 128), piece)

    def x_copy(c):
        return remote(xkeep.at[:, columns(0, c)], xin.at[:, columns(0, c)],
                      c_send.at[c], c_recv.at[c], plane(peer(1)))

    def b_copy(c):
        return remote(gkeep.at[:, columns(0, c)], gin.at[:, columns(0, c)],
                      b_send.at[c], b_recv.at[c], plane(peer(planes - 1)))

    def give_copy(c):
        return remote(xgive.at[:, columns(0, c)], xout.at[:, columns(ylo * half, c)],
                      g_send.at[c], g_recv.at[c], partner)

    def give_arrived(c):
        return remote(xgive.at[:, columns(0, c)], xout.at[:, columns((1 - ylo) * half, c)],
                      g_send.at[c], g_recv.at[c], partner)

    def pass_copy(c):
        return remote(xpass.at[:, columns(0, c)], xb.at[:, columns(ylo * half, c)],
                      p_send.at[c], p_recv.at[c], partner)

    def pass_arrived(c):
        return remote(xpass.at[:, columns(0, c)], xb.at[:, columns((1 - ylo) * half, c)],
                      p_send.at[c], p_recv.at[c], partner)

    def h_copy(c):
        return remote(ggive.at[:, columns(0, c)], gout.at[:, columns(ylo * half, c)],
                      h_send.at[c], h_recv.at[c], partner)

    def h_arrived(c):
        return remote(ggive.at[:, columns(0, c)], gout.at[:, columns((1 - ylo) * half, c)],
                      h_send.at[c], h_recv.at[c], partner)

    def near_copy(k, part, sem):
        spot = ul.at[k, :, part]
        return remote(spot, spot, e_sem.at[2 * sem], e_sem.at[2 * sem + 1], plane(peer(1)))

    def n_copy():
        return remote(nsend, nl, e_sem.at[4], e_sem.at[5], plane(peer(1)))

    def uf_copy():
        return remote(ul.at[z], uf.at[mine], e_sem.at[6], e_sem.at[7], partner)

    def uf_arrived():
        return remote(ul.at[z], uf.at[theirs], e_sem.at[6], e_sem.at[7], partner)

    def qp_copy():
        return remote(ql.at[z], qp, e_sem.at[8], e_sem.at[9], partner)

    def u_copy(o):
        return remote(ul.at[z], ul.at[z], u_send.at[o], u_recv.at[z], plane(peer(o)))

    def u_arrived(k):
        return remote(ul.at[k], ul.at[k], u_send.at[0], u_recv.at[k], plane(peer(1)))

    def q_copy(j):
        return remote(ql.at[z], ql.at[z], q_send.at[j], q_recv.at[z], plane(j))

    def q_arrived(k):
        return remote(ql.at[k], ql.at[k], q_send.at[0], q_recv.at[k], plane(peer(1)))

    acc[:, 0:2 * rank] = pyh[0]
    acc[:, 2 * rank:4 * rank] = pyh[1]
    hacc[...] = pyh[2]

    batch = per * piece

    def wide_columns(base, p):
        return pl.ds(pl.multiple_of(base + p * batch, 128), batch)

    def chain(p):
        ours = up[:, wide_columns(ylo * half, p)]
        other = upart[:, wide_columns(0, p)]
        grow = dot_nn(uf[:, head], jnp.where(first, ours, other))
        delta[0] = grow
        delta[1] = grow + dot_nn(uf[:, tail], jnp.where(first, other, ours))
        for j in range(per):
            c = per * p + j

            @pl.when(z > 0)
            def _():
                x_copy(c).wait_recv()

            here = columns(ylo * half, c)
            there = columns(0, c)
            lane = slice(j * piece, (j + 1) * piece)
            start = jnp.where(z > 0, xin[:, there], x0[:, here])
            x_a = (start.astype(f32) + delta[0, :, lane]).astype(bf16)
            x_b = (start.astype(f32) + delta[1, :, lane]).astype(bf16)
            xkeep[:, there] = x_b

            @pl.when(z < planes - 1)
            def _():
                x_copy(c).start()

            xpass[:, there] = jnp.where(first, x_a, start)
            pass_copy(c).start()
            xgive[:, there] = jnp.where(first, x_b, x_a)
            xout[:, here] = jnp.where(first, x_a, x_b)
            xb[:, here] = jnp.where(first, start, x_a)

    def chain_back(p):
        here = wide_columns(ylo * half, p)
        there = wide_columns(0, p)
        ours = wd[here, :]
        other = wpart[there, :]
        x_a = jnp.where(first, xb[:, here], xpass[:, there]).astype(f32)
        x_b = jnp.where(first, xpass[:, there], xb[:, here]).astype(f32)
        grow = dot_nt(qs[:, tail], jnp.where(first, other, ours)) - cpair[1, :, 0:1] * x_b
        delta[0] = grow
        delta[1] = (grow + dot_nt(qs[:, head], jnp.where(first, ours, other))
                    - cpair[0, :, 0:1] * x_a)
        for j in range(per):
            c = per * p + j

            @pl.when(z < planes - 1)
            def _():
                b_copy(c).wait_recv()

            here = columns(ylo * half, c)
            there = columns(0, c)
            lane = slice(j * piece, (j + 1) * piece)
            g_b = jnp.where(z < planes - 1, gin[:, there], g16[:, here])
            g_a = (g_b.astype(f32) + delta[0, :, lane]).astype(bf16)

            @pl.when(z > 0)
            def _():
                gkeep[:, there] = (g_b.astype(f32) + delta[1, :, lane]).astype(bf16)
                b_copy(c).start()

            ggive[:, there] = jnp.where(first, g_b, g_a)
            h_copy(c).start()
            gout[:, here] = jnp.where(first, g_a, g_b)

    def forward_own():
        @pl.when(z > 0)
        def _():
            n_copy().wait_recv()

        norm_a = jnp.where(z > 0, to_col(nl[0:1, :]), n0[:, 0:1])
        scale_a = lax.rsqrt(norm_a * (1.0 / width) + eps)
        pre_a = acc[:, 0:rank] * scale_a
        value_a, slope_a = gelu_pair(pre_a)
        u_a = value_a.astype(bf16)
        ul[z, :, head] = u_a

        @pl.when(z < planes - 1)
        def _():
            near_copy(z, head, 0).start()

        step = dot_nn(u_a, nn[z, 0:rank, rank:4 * rank])
        y_a = acc[:, 2 * rank:3 * rank]
        norm_b = norm_a + jnp.sum(u_a.astype(f32) * (2.0 * y_a + step[:, rank:2 * rank]),
                                  axis=1, keepdims=True)
        scale_b = lax.rsqrt(norm_b * (1.0 / width) + eps)
        pre_b = (acc[:, rank:2 * rank] + step[:, 0:rank]) * scale_b
        value_b, slope_b = gelu_pair(pre_b)
        u_b = value_b.astype(bf16)
        ul[z, :, tail] = u_b

        @pl.when(z < planes - 1)
        def _():
            near_copy(z, tail, 1).start()

        y_b = acc[:, 2 * rank:4 * rank] + step[:, rank:3 * rank]
        more = dot_nn(u_b, nn[z, rank:2 * rank, 2 * rank:4 * rank])
        norm_c = norm_b + jnp.sum(
            u_b.astype(f32) * (2.0 * y_b[:, rank:2 * rank] + more[:, rank:2 * rank]),
            axis=1, keepdims=True)

        @pl.when(z < planes - 1)
        def _():
            nsend[...] = jnp.broadcast_to(to_row(norm_c), nsend.shape)
            n_copy().start()

        uf_copy().start()
        for o in range(2, planes):
            u_copy(o).start()

        @pl.when(z == planes - 1)
        def _():
            u_copy(1).start()

        uf[mine, :] = ul[z]
        ys[2 * z + 1] = y_b
        acc[:, 2 * rank:4 * rank] = y_b + more
        act[:, head] = pre_a
        act[:, tail] = pre_b
        slope[:, head] = slope_a
        slope[:, tail] = slope_b
        rinv[0] = jnp.broadcast_to(scale_a, (some, rank))
        rinv[1] = jnp.broadcast_to(scale_b, (some, rank))

    def c_of(stat):
        line = stat[0:1, :].astype(f32) + stat[1:2, :].astype(f32)
        return to_col(line[:, head]), to_col(line[:, tail])

    def backward_own():
        scale_b = rinv[1]
        q_b = hacc[:, tail] * slope[:, tail]
        low_b = (q_b * scale_b).astype(bf16)
        mix_b = jnp.sum(q_b * act[:, tail], axis=1, keepdims=True) * (1.0 / width)
        c_b = mix_b * scale_b[:, 0:1] * scale_b[:, 0:1]
        h_a = hacc[:, head] + dot_nt(low_b, nn[z, 0:rank, rank:2 * rank]) - c_b * ys[2 * z + 1, :, head]
        scale_a = rinv[0]
        q_a = h_a * slope[:, head]
        mix_a = jnp.sum(q_a * act[:, head], axis=1, keepdims=True) * (1.0 / width)
        c_a = mix_a * scale_a[:, 0:1] * scale_a[:, 0:1]
        ql[z, 0:some, head] = (q_a * scale_a).astype(bf16)
        ql[z, 0:some, tail] = low_b
        spot = lax.broadcasted_iota(jnp.int32, (16, rank), 0)
        for part, col in ((head, c_a), (tail, c_b)):
            line = to_row(col)
            high = line.astype(bf16).astype(f32)
            ql[z, some:some + 16, part] = jnp.where(
                spot == 0, high, jnp.where(spot == 1, line - high, 0.0)).astype(bf16)

        def send(i, carry):
            q_copy(z - 1 - i).start()
            return carry

        lax.fori_loop(0, z, send, 0)
        qp_copy().start()

    shard = mine_u.shape[0]
    nacc[...] = jnp.zeros_like(nacc)

    def core_copy(b):
        return remote(part.at[b, 1 - core], rc.at[b], k_send.at[b], k_recv.at[b], other_core)

    def collect(b):
        block_sum(b, yh_n, x_n, core_copy, part, rc, sums, rax, rby,
                  ax_send, ax_recv, by_send, by_recv)

    def terms(b):
        cols = pl.ds(pl.multiple_of(b * 2 * shard, 128), 2 * shard)
        u = us[...]
        before = xb[:, cols]
        wide = before.astype(f32)
        nacc[...] += jnp.broadcast_to(jnp.sum(wide * wide, axis=1, keepdims=True), nacc.shape)
        g_down = dot_tn(before, qv[...]).astype(bf16)
        g_up = dot_tn(gout[:, cols], u).astype(bf16)
        for i in range(2):
            part[b, i, :, head] = g_down[i * shard:(i + 1) * shard]
            part[b, i, :, tail] = g_up[i * shard:(i + 1) * shard]
        core_copy(b).start()

    def tick(t, carry):
        k = t - 1
        sent = (k >= 0) & (k < planes)
        near = sent & (k == z - 1)

        @pl.when(sent & (k != z) & (k != z - 1))
        def _():
            u_arrived(k).wait_recv()

        @pl.when(near)
        def _():
            near_copy(k, head, 0).wait_recv()
            acc[...] += dot_nn(ul[k, :, head], nn[k, 0:rank, :])
            near_copy(k, tail, 1).wait_recv()
            acc[...] += dot_nn(ul[k, :, tail], nn[k, rank:2 * rank, :])

        @pl.when(sent & (k < z - 1))
        def _():
            acc[...] += dot_nn(ul[k], nn[k])

        @pl.when(t == z)
        def _():
            forward_own()

        @pl.when(sent & (k > z))
        def _():
            before = acc[:, 2 * rank:4 * rank]
            ys[2 * k] = before
            between = before + dot_nn(ul[k, :, head], nn[k, 0:rank, 2 * rank:4 * rank])
            ys[2 * k + 1] = between
            acc[:, 2 * rank:4 * rank] = between + dot_nn(
                ul[k, :, tail], nn[k, rank:2 * rank, 2 * rank:4 * rank])

        r = 2 * planes - t

        @pl.when((r < planes) & (r > z))
        def _():
            q_arrived(r).wait_recv()
            c_a, c_b = c_of(ql[r, some:some + 16, :])
            hacc[...] += (dot_nn(ql[r, 0:some, :], nn[r, :, 0:2 * rank]) - c_a * ys[2 * r] - c_b * ys[2 * r + 1])

        @pl.when(t == 2 * planes - 1 - z)
        def _():
            backward_own()

        p = t - (z + 1)

        @pl.when((p >= 0) & (p < trips))
        def _():
            @pl.when(p == 0)
            def _():
                for load in loads[:3]:
                    load.wait()
                uf_arrived().wait_recv()
            chain(p)

        q = t - (z + 1 + trips)

        @pl.when((q >= 0) & (q < chunks // 4))
        def _():
            for j in range(4):
                give_copy(4 * q + j).start()

        b = t - (2 * planes - z)

        @pl.when((b >= 0) & (b < trips))
        def _():
            @pl.when(b == 0)
            def _():
                for load in loads[3:]:
                    load.wait()
                qp_copy().wait_recv()
                qs[mine, :] = ql[z, 0:some, :]
                qs[theirs, :] = qp[0:some, :]
                for where, stat in ((mine, ql[z, some:some + 16, :]), (theirs, qp[some:some + 16, :])):
                    c_a, c_b = c_of(stat)
                    cpair[0, where, :] = jnp.broadcast_to(c_a, (some, rank))
                    cpair[1, where, :] = jnp.broadcast_to(c_b, (some, rank))
                us[...] = jnp.where(first, uf[:, head], uf[:, tail])
                qv[...] = jnp.where(first, qs[:, head], qs[:, tail])
            chain_back(b)
            terms(ylo * trips + b)

        @pl.when((b >= 1) & (b <= trips))
        def _():
            collect(ylo * trips + b - 1)

            def landed(j, carry):
                c = per * (b - 1) + j
                pass_arrived(c).wait_recv()
                h_arrived(c).wait_recv()
                return carry

            lax.fori_loop(0, per, landed, 0)
            terms((1 - ylo) * trips + b - 1)

        @pl.when((b >= 2) & (b <= trips))
        def _():
            collect((1 - ylo) * trips + b - 2)

        return carry

    lax.fori_loop(0, 2 * planes + trips + 1, tick, 0)
    collect((1 - ylo) * trips + trips - 1)

    def landed_x(c, carry):
        give_arrived(c).wait_recv()
        return carry

    lax.fori_loop(0, chunks, landed_x, 0)
    save_x = pltpu.make_async_copy(xout, xout_far, l_sem.at[6])
    save_x.start()
    total_a, total_b = scatter_sum(yh_n, x_n, sums, rax, rby, sa, ray, sb, rbx,
                                   ax_send, ax_recv, by_send, by_recv, s_sem, bx_send, bx_recv)
    cut = shard // 2
    gw[0:cut] = total_a[:, head].astype(bf16)
    gw[cut:shard] = total_b[:, head].astype(bf16)
    gu[0:cut] = total_a[:, tail].astype(bf16)
    gu[cut:shard] = total_b[:, tail].astype(bf16)
    has_next = s < sections - 1
    down_section = {"section": lax.rem(s + sections - 1, sections)}

    def pair_of(sems, i):
        return sems.at[2 * i], sems.at[2 * i + 1]

    def w_x(i):
        return remote(gw, own_w.at[yh, x, core], *pair_of(wx_sem, i), place(yh, xp(i), core))

    def w_y(i):
        spot = own_w.at[yh, xp(i), core]
        return remote(gw if i == 0 else spot, spot, *pair_of(wy_sem, i), other_y)

    def w_c(i):
        spot = own_w.at[:, xp(i), core]
        return remote(spot, spot, *pair_of(wc_sem, i), other_core)

    v_y = remote(gu, own_u.at[yh, x, core], *pair_of(vx_sem, 0), other_y)

    def v_x(i):
        spot = own_u.at[:, x, core]
        return remote(spot, spot, *pair_of(vx_sem, i), place(yh, xp(i), core))

    def v_c(i):
        spot = own_u.at[:, xp(i), core]
        return remote(spot, spot, *pair_of(vc_sem, i), other_core)

    next_copy = remote(nw, nxt_u.at[yh, x, core], *pair_of(nx_sem, 0), down_section)
    bump_copy = remote(ub, bump_u, *pair_of(nx_sem, x_n), down_section)

    def n_x(i):
        spot = nxt_u.at[yh, x, core]
        return remote(spot, spot, *pair_of(nx_sem, i), place(yh, xp(i), core))

    def n_y(i):
        spot = nxt_u.at[yh, xp(i), core]
        return remote(spot, spot, *pair_of(ny_sem, i), other_y)

    def n_c(i):
        spot = nxt_u.at[:, xp(i), core]
        return remote(spot, spot, *pair_of(nc_sem, i), other_core)

    for i in range(1, x_n):
        w_x(i).start()
    v_y.start()
    w_y(0).start()

    @pl.when(s > 0)
    def _():
        nw[...] = (mine_u[...].astype(f32) - learn_rate * gu[...].astype(f32)).astype(bf16)
        next_copy.start()

    own_w[yh, x, core] = gw[...]
    own_u[yh, x, core] = gu[...]
    @pl.when(has_next)
    def _():
        next_copy.wait_recv()
        for i in range(1, x_n):
            n_x(i).start()

    for i in range(1, x_n):
        w_x(x_n - i).wait_recv()
        w_y(i).start()

    @pl.when(has_next)
    def _():
        n_y(0).start()
        for i in range(1, x_n):
            n_x(i).wait_send()

    v_y.wait_recv()
    for i in range(1, x_n):
        v_x(i).start()
    v_c(0).start()

    for i in range(x_n):
        w_y(i).wait_recv()
        w_c(i).start()

    @pl.when(has_next)
    def _():
        for i in range(1, x_n):
            n_x(x_n - i).wait_recv()
            n_y(i).start()

    for i in range(1, x_n):
        v_x(x_n - i).wait_recv()
        v_c(i).start()
    for i in range(x_n):
        w_c(i).wait()
    save_w = pltpu.make_async_copy(own_w, own_w_far, l_sem.at[7])
    save_w.start()

    @pl.when(s > 0)
    def _():
        def ahead(b, pre):
            y_ = b // x_n
            x_ = lax.rem(b, x_n)
            cols = pl.ds(pl.multiple_of(b * 2 * shard, 128), 2 * shard)
            both = jnp.concatenate([own_w[y_, x_, 0], own_w[y_, x_, 1]], axis=0)
            fresh = wd[cols, :].astype(f32) - learn_rate * both.astype(f32)
            return pre + dot_nn(xb[:, cols], fresh.astype(bf16))

        pre = lax.fori_loop(0, yh_n * x_n, ahead, jnp.zeros((rows, rank), f32))
        value, unused = gelu_pair(pre * lax.rsqrt(nacc[...] * (1.0 / width) + eps))
        ub[...] = value.astype(bf16)
        bump_copy.start()

    @pl.when(has_next)
    def _():
        for i in range(x_n):
            n_y(i).wait_recv()
            n_c(i).start()
        for i in range(x_n):
            n_c(i).wait()
            n_y(i).wait_send()
        bump_copy.wait_recv()

    for i in range(x_n):
        v_c(i).wait()
        w_y(i).wait_send()
    for i in range(1, x_n):
        w_x(i).wait_send()
        v_x(i).wait_send()
    v_y.wait_send()

    @pl.when(s > 0)
    def _():
        next_copy.wait_send()
        bump_copy.wait_send()

    def core_settle(b, carry):
        core_copy(b).wait_send()
        return carry

    lax.fori_loop(0, yh_n * x_n, core_settle, 0)
    save_x.wait()
    save_w.wait()

    def finish(c, carry):
        @pl.when(z < planes - 1)
        def _():
            x_copy(c).wait_send()
        give_copy(c).wait_send()
        pass_copy(c).wait_send()

        @pl.when(z > 0)
        def _():
            b_copy(c).wait_send()
        h_copy(c).wait_send()
        return carry

    lax.fori_loop(0, chunks, finish, 0)
    for o in range(2, planes):
        u_copy(o).wait_send()

    @pl.when(z == planes - 1)
    def _():
        u_copy(1).wait_send()

    @pl.when(z < planes - 1)
    def _():
        near_copy(z, head, 0).wait_send()
        near_copy(z, tail, 1).wait_send()
        n_copy().wait_send()

    def settle(j, carry):
        q_copy(j).wait_send()
        return carry

    lax.fori_loop(0, z, settle, 0)
    uf_copy().wait_send()
    qp_copy().wait_send()


def recurrence(sections, shards, pyh, n0, nn, x0, g16, up, wd, upart, wpart, mine_u):
    rows, width = x0.shape
    rank = up.shape[0]
    half = width // 2
    some = rows // 2
    planes = sections // 2
    chunks = 28
    per = 7
    x_n = 4
    yh_n = shards // (2 * x_n)
    shard = mine_u.shape[0]
    cut = shard // 2
    blocks = yh_n * x_n
    vm = pl.BlockSpec(memory_space=pltpu.VMEM)
    dma = pltpu.SemaphoreType.DMA
    sq = (rows, rank)
    two = (some, 2 * rank)
    strip = pltpu.VMEM((rows, half), bf16)
    full = jax.ShapeDtypeStruct((yh_n, x_n, 2, shard, rank), bf16)

    def buf(*lead):
        return pltpu.VMEM(lead + (2 * rank,), bf16)

    return pl.pallas_call(
        functools.partial(recurrence_kernel, sections, chunks, per, yh_n, x_n),
        out_shape=(jax.ShapeDtypeStruct((rows, width), bf16), full, full, full,
                   jax.ShapeDtypeStruct(sq, bf16)),
        in_specs=[vm] * 3 + [pl.BlockSpec(memory_space=pl.ANY)] * 6 + [vm],
        out_specs=(pl.BlockSpec(memory_space=pl.ANY),) * 2 + (vm,) * 3,
        scratch_shapes=[
            pltpu.VMEM((planes,) + two, bf16),
            pltpu.VMEM((planes, some + 16, 2 * rank), bf16),
            pltpu.VMEM((some + 16, 2 * rank), bf16),
            pltpu.VMEM((sections,) + two, f32),
            pltpu.VMEM((8, rank), f32),
            pltpu.VMEM((8, rank), f32),
            pltpu.VMEM((some, 4 * rank), f32),
            pltpu.VMEM(two, f32), pltpu.VMEM(two, f32), pltpu.VMEM(two, f32),
            pltpu.VMEM((2, some, rank), f32),
            pltpu.VMEM((rows, 2 * rank), bf16),
            pltpu.VMEM((rows, 2 * rank), bf16),
            pltpu.VMEM((2,) + sq, f32),
            strip, strip, strip, strip, strip, strip, strip,
            pltpu.VMEM((2, rows, half * per // chunks), f32),
            pltpu.VMEM((rows, width), bf16),
            pltpu.VMEM(sq, bf16), pltpu.VMEM(sq, bf16),
            pltpu.VMEM((rows, width), bf16), pltpu.VMEM(sq, f32),
            buf(blocks, 2, shard), buf(blocks, shard), buf(yh_n, x_n, shard),
            buf(x_n - 1, yh_n, cut), buf(x_n, cut), buf(yh_n, cut), buf(cut),
            buf(x_n, cut), buf(x_n - 1, cut),
            pltpu.VMEM((shard, rank), bf16), pltpu.VMEM((shard, rank), bf16),
            pltpu.VMEM((shard, rank), bf16), pltpu.VMEM(sq, bf16),
            pltpu.VMEM((rows, width), bf16), pltpu.VMEM((rows, width), bf16),
            pltpu.VMEM((rank, width), bf16), pltpu.VMEM((width, rank), bf16),
            pltpu.VMEM((rank, half), bf16), pltpu.VMEM((half, rank), bf16),
            pltpu.VMEM((rows, width), bf16), pltpu.VMEM((yh_n, x_n, 2, shard, rank), bf16), dma((8,)),
        ] + [dma((planes,))] * 4 + [dma((10,))] + [dma((chunks,))] * 10 + [
            dma((blocks,)), dma((blocks,)),
            dma((yh_n * (x_n - 1),)), dma((yh_n * (x_n - 1),)), dma((x_n,)), dma((x_n,)), dma((2,)),
            dma((x_n - 1,)), dma((x_n - 1,)),
            dma((2 * x_n,)), dma((2 * x_n,)), dma((2 * x_n,)), dma((2 * x_n,)), dma((2 * x_n,)),
            dma((2 * x_n + 2,)), dma((2 * x_n,)), dma((2 * x_n,)),
        ],
        compiler_params=pltpu.CompilerParams(
            collective_id=1, has_side_effects=True, vmem_limit_bytes=60 * 1024 * 1024),
    )(pyh, n0, nn, x0, g16, up, wd, upart, wpart, mine_u)


def dp_place(x_n):
    d = lax.axis_index("dp")
    return d // (2 * x_n), lax.rem(d // 2, x_n), lax.rem(d, 2)


def remote(src, dst, send, recv, where):
    return pltpu.make_async_remote_copy(src_ref=src, dst_ref=dst, send_sem=send, recv_sem=recv,
                                        device_id=where, device_id_type=MESH)


def block_sum(b, yh_n, x_n, core_copy, part, rc, sums, rax, rby, ax_send, ax_recv, by_send, by_recv):
    yh, x, core = dp_place(x_n)
    cut = sums.shape[2] // 2
    y_ = b // x_n
    x_ = lax.rem(b, x_n)
    core_copy(b).wait_recv()
    sums[y_, x_] = (part[b, core].astype(f32) + rc[b].astype(f32)).astype(bf16)
    turn = lax.rem(x_ - x + x_n, x_n)

    @pl.when(turn != 0)
    def _():
        sem = (turn - 1) * yh_n + y_
        remote(sums.at[y_, x_, 0:cut], rax.at[turn - 1, y_], ax_send.at[sem], ax_recv.at[sem],
               {"dp": (yh * x_n + x_) * 2 + core}).start()

    @pl.when(y_ != yh)
    def _():
        remote(sums.at[y_, x_, cut:2 * cut], rby.at[x_], by_send.at[x_], by_recv.at[x_],
               {"dp": (y_ * x_n + x) * 2 + core}).start()


def scatter_sum(yh_n, x_n, sums, rax, rby, sa, ray, sb, rbx,
                ax_send, ax_recv, by_send, by_recv, s_sem, bx_send, bx_recv):
    yh, x, core = dp_place(x_n)
    rows = sums.shape[2]
    cut = rows // 2

    def place(y_, x_, c_):
        return {"dp": (y_ * x_n + x_) * 2 + c_}

    def xp(i):
        return lax.rem(x + i, x_n)

    other_y = place(1 - yh, x, core)

    def ax_copy(i, y_):
        sem = (i - 1) * yh_n + y_
        return remote(sums.at[y_, xp(i), 0:cut], rax.at[i - 1, y_], ax_send.at[sem], ax_recv.at[sem],
                      place(yh, xp(i), core))

    def by_copy(x_):
        return remote(sums.at[1 - yh, x_, cut:rows], rby.at[x_], by_send.at[x_], by_recv.at[x_], other_y)

    def bx_copy(i):
        return remote(sb.at[xp(i)], rbx.at[i - 1], bx_send.at[i - 1], bx_recv.at[i - 1],
                      place(yh, xp(i), core))

    ay_copy = remote(sa.at[1 - yh], ray, s_sem.at[0], s_sem.at[1], other_y)

    for i in range(x_n):
        x_ = xp(i)
        by_copy(x_).wait_recv()
        sb[x_] = (sums[yh, x_, cut:rows].astype(f32) + rby[x_].astype(f32)).astype(bf16)
        if i > 0:
            bx_copy(i).start()
    for y_ in range(yh_n):
        total = sums[y_, x, 0:cut].astype(f32)
        for i in range(1, x_n):
            ax_copy(i, y_).wait_recv()
            total = total + rax[i - 1, y_].astype(f32)
        sa[y_] = total.astype(bf16)
    ay_copy.start()
    total_b = sb[x].astype(f32)
    for i in range(1, x_n):
        bx_copy(i).wait_recv()
        total_b = total_b + rbx[i - 1].astype(f32)
    ay_copy.wait_recv()
    total_a = sa[yh].astype(f32) + ray[...].astype(f32)
    for i in range(1, x_n):
        for y_ in range(yh_n):
            ax_copy(i, y_).wait_send()
        bx_copy(i).wait_send()
    for x_ in range(x_n):
        by_copy(x_).wait_send()
    ay_copy.wait_send()
    return total_a, total_b


def gram_kernel(yh_n, x_n, sections, x0_far, g16_far, down_far, up_far, mine_u, pyh, n0, out, upart, wpart,
                allu, part, rc, sums, rax, rby, sa, ray, sb, rbx, gs, gp, two, mine3, theirs3, flip, turned,
                x0, g16, down, up, base, mine_w, l_sem,
                z_sem, f_send, f_recv, r_send, r_recv,
                c_send, c_recv, ax_send, ax_recv, by_send, by_recv, s_sem, bx_send, bx_recv,
                ga_send, ga_recv, gb_send, gb_recv, gc_send, gc_recv, t_sem):
    loads = [pltpu.make_async_copy(far, near, l_sem.at[i]) for i, (far, near) in enumerate((
        (up_far, up), (down_far, down), (x0_far, x0), (g16_far, g16)))]
    height = mine_u.shape[0]
    own_rows = pl.ds(pl.multiple_of(lax.axis_index("dp") * height, 64), height)
    load_w = pltpu.make_async_copy(down_far.at[own_rows, :], mine_w, l_sem.at[4])
    load_w.start()
    for load in loads:
        load.start()
    yh, x, core = dp_place(x_n)
    s = lax.axis_index("section")
    z_n = sections // 2
    z = s // 2
    ylo = lax.rem(s, 2)
    rank = up.shape[0]
    rows = rank
    cut = rows // 2

    def place(y_, x_, c_):
        return {"dp": (y_ * x_n + x_) * 2 + c_}

    def xp(i):
        return lax.rem(x + i, x_n)

    def zp(i):
        return lax.rem(z + i, z_n)

    other_core = place(yh, x, 1 - core)
    other_y = place(1 - yh, x, core)
    partner = {"section": s + 1 - 2 * ylo}
    after = {"section": 2 * zp(1) + ylo}
    before = {"section": 2 * zp(z_n - 1) + ylo}

    barrier = pltpu.get_barrier_semaphore()
    peers = [other_core, other_y, partner, after, before]
    peers += [place(yh, xp(i), core) for i in range(1, x_n)]
    for where in peers:
        pl.semaphore_signal(barrier, inc=1, device_id=where, device_id_type=MESH)
    d = lax.axis_index("dp")
    above = d // 2 < z
    below = d // 2 > z
    mirror = [{"section": 2 * (d // 2) + i, "dp": s} for i in range(2)]

    @pl.when(below)
    def _():
        for i in range(2):
            pl.semaphore_signal(barrier, inc=1, device_id={"section": d, "dp": 2 * z + i},
                                device_id_type=MESH)

    pl.semaphore_wait(barrier, len(peers) + 2 * above.astype(jnp.int32))

    def flip_copy(i):
        k = lax.rem(d, 2)
        return remote(flip, turned.at[k], t_sem.at[i], t_sem.at[2 + k], mirror[i])

    def flip_arrived(i):
        return remote(flip, turned.at[i], t_sem.at[0], t_sem.at[2 + i], mirror[0])

    pair = remote(mine_u, allu.at[z, ylo], z_sem.at[0], z_sem.at[1], partner)

    def products(z_):
        for y_ in range(2):
            part[z_, y_] = dot_tn(allu[z_, y_], base[...]).astype(bf16)

    def core_copy(b):
        return remote(part.at[b, 1 - core], rc.at[b], c_send.at[b], c_recv.at[b], other_core)

    hops = z_n // 2

    def column(j):
        return ylo if j == 0 else 1 - ylo

    def ring_f(i, j):
        spot = allu.at[zp(z_n + 1 - i), column(j)]
        src = mine_u if (i == 1 and j == 0) else spot
        sem = 2 * (i - 1) + j
        return remote(src, spot, f_send.at[sem], f_recv.at[sem], after)

    def ring_r(i, j):
        spot = allu.at[zp(i - 1), column(j)]
        src = mine_u if (i == 1 and j == 0) else spot
        sem = 2 * (i - 1) + j
        return remote(src, spot, r_send.at[sem], r_recv.at[sem], before)

    used_f = [(i, j) for i in range(1, hops + 1) for j in range(2) if i < hops or j == 0]
    used_r = [(i, j) for i in range(1, hops + 1) for j in range(2) if i < hops or j == 1]

    pair.start()
    ring_f(1, 0).start()
    ring_r(1, 0).start()
    allu[z, ylo] = mine_u[...]
    pair.wait_recv()
    ring_f(1, 1).start()
    ring_r(1, 1).start()

    half = x0.shape[1] // 2
    quarter = half // 2
    far = pl.ds(pl.multiple_of((1 - ylo) * half + core * quarter, 128), quarter)
    near = pl.ds(pl.multiple_of(core * quarter, 128), quarter)
    swap_u = remote(up.at[:, far], upart.at[:, near], z_sem.at[6], z_sem.at[7], partner)
    swap_w = remote(down.at[far, :], wpart.at[near, :], z_sem.at[8], z_sem.at[9], partner)
    share_u = remote(upart.at[:, near], upart.at[:, near], z_sem.at[10], z_sem.at[11], other_core)
    share_w = remote(wpart.at[near, :], wpart.at[near, :], z_sem.at[12], z_sem.at[13], other_core)
    token_half = x0.shape[0] // 2
    keep = pl.ds(ylo * token_half, token_half)
    give = pl.ds((1 - ylo) * token_half, token_half)
    swap3 = remote(mine3.at[:, give], theirs3, z_sem.at[2], z_sem.at[3], partner)

    def project(i):
        if i == 1:
            for load in loads[2:]:
                load.wait()
            mine3[0] = dot_nn(x0[...], down[...])
            mine3[1] = dot_nt(x0[...], up[...])
        elif i == 2:
            mine3[2] = dot_nt(g16[...], up[...])
            swap3.start()
            wide = x0[keep, :].astype(f32)
            n0[...] = jnp.broadcast_to(jnp.sum(wide * wide, axis=1, keepdims=True), n0.shape)

    def collect(b):
        block_sum(b, yh_n, x_n, core_copy, part, rc, sums, rax, rby,
                  ax_send, ax_recv, by_send, by_recv)

    for load in loads[:2]:
        load.wait()
    swap_u.start()
    swap_w.start()
    load_w.wait()
    base[:, 0:rank] = mine_w[...]
    base[:, rank:2 * rank] = mine_u[...]
    products(z)
    core_copy(z).start()
    for i in range(1, hops + 1):
        for j in range(2):
            if (i, j) in used_f:
                ring_f(i, j).wait_recv()
                if (i + 1, j) in used_f:
                    ring_f(i + 1, j).start()
            if (i, j) in used_r:
                ring_r(i, j).wait_recv()
                if (i + 1, j) in used_r:
                    ring_r(i + 1, j).start()
        if i < hops:
            project(i)
        products(zp(z_n - i))
        core_copy(zp(z_n - i)).start()
        if i == 1:
            collect(z)
        else:
            collect(zp(i - 1))
        if i < hops:
            products(zp(i))
            core_copy(zp(i)).start()
        collect(zp(z_n - i))

    swap_u.wait_recv()
    share_u.start()
    swap_w.wait_recv()
    share_w.start()
    total_a, total_b = scatter_sum(yh_n, x_n, sums, rax, rby, sa, ray, sb, rbx,
                                   ax_send, ax_recv, by_send, by_recv, s_sem, bx_send, bx_recv)
    gs[0:cut] = total_a.astype(bf16)
    gs[cut:rows] = total_b.astype(bf16)
    swap = remote(gs, gp, z_sem.at[4], z_sem.at[5], partner)
    swap.start()

    @pl.when(above)
    def _():
        flip[...] = gs[:, 0:rank].astype(f32).T.astype(bf16)
        for i in range(2):
            flip_copy(i).start()

    def lanes(base, which):
        return pl.ds(pl.multiple_of(base + which * rank, 128), rank)

    swap3.wait_recv()
    pyh[:, :, lanes(0, ylo)] = mine3[:, keep]
    pyh[:, :, lanes(0, 1 - ylo)] = theirs3[...]
    two[:, lanes(0, ylo)] = gs[:, 0:rank]
    two[:, lanes(2 * rank, ylo)] = gs[:, rank:2 * rank]
    swap.wait_recv()
    two[:, lanes(0, 1 - ylo)] = gp[:, 0:rank]
    two[:, lanes(2 * rank, 1 - ylo)] = gp[:, rank:2 * rank]

    @pl.when(below)
    def _():
        for i in range(2):
            flip_arrived(i).wait_recv()
            two[:, i * rank:(i + 1) * rank] = turned[i]
    out[yh, x, core] = two[...]

    low = pl.ds(0, cut)
    high = pl.ds(cut, cut)

    def spread(src, spot, sems, i, where):
        return remote(src, spot, sems[0].at[i], sems[1].at[i], where)

    ga = (ga_send, ga_recv)
    gb = (gb_send, gb_recv)
    a_y = spread(two.at[low], out.at[yh, x, core, low], ga, 0, other_y)

    def a_x(i):
        spot = out.at[:, x, core, low]
        return spread(spot, spot, ga, i, place(yh, xp(i), core))

    def b_x(i):
        return spread(two.at[high], out.at[yh, x, core, high], gb, i - 1, place(yh, xp(i), core))

    def b_y(i):
        spot = out.at[yh, xp(i), core, high]
        return spread(spot, spot, gb, x_n - 1 + i, other_y)

    def all_c(i):
        spot = out.at[:, xp(i), core]
        return remote(spot, spot, gc_send.at[i], gc_recv.at[i], other_core)

    a_y.start()
    for i in range(1, x_n):
        b_x(i).start()
    b_y(0).start()
    a_y.wait_recv()
    for i in range(1, x_n):
        a_x(i).start()
    for i in range(1, x_n):
        b_x(x_n - i).wait_recv()
        b_y(i).start()
    b_y(0).wait_recv()
    all_c(0).start()
    for i in range(1, x_n):
        a_x(x_n - i).wait_recv()
        b_y(i).wait_recv()
        all_c(i).start()
    for i in range(x_n):
        all_c(i).wait()
        b_y(i).wait_send()
    for i in range(1, x_n):
        a_x(i).wait_send()
        b_x(i).wait_send()
    a_y.wait_send()
    pair.wait_send()
    swap.wait_send()
    swap3.wait_send()

    @pl.when(above)
    def _():
        for i in range(2):
            flip_copy(i).wait_send()
    swap_u.wait_send()
    swap_w.wait_send()
    share_u.wait()
    share_w.wait()
    for i, j in used_f:
        ring_f(i, j).wait_send()
    for i, j in used_r:
        ring_r(i, j).wait_send()

    def settle(b, carry):
        core_copy(b).wait_send()
        return carry

    lax.fori_loop(0, yh_n * x_n, settle, 0)


def grams_of(sections, shards, x0, g16, down, up, mine_u):
    x_n = 4
    yh_n = shards // (2 * x_n)
    rows, width = x0.shape
    rank = up.shape[0]
    height = mine_u.shape[0]
    cut = rank // 2
    vm = pl.BlockSpec(memory_space=pltpu.VMEM)
    dma = pltpu.SemaphoreType.DMA

    def buf(*lead):
        return pltpu.VMEM(lead + (2 * rank,), bf16)

    return pl.pallas_call(
        functools.partial(gram_kernel, yh_n, x_n, sections),
        out_shape=(
            jax.ShapeDtypeStruct((3, rows // 2, 2 * rank), f32),
            jax.ShapeDtypeStruct((rows // 2, rank), f32),
            jax.ShapeDtypeStruct((yh_n, x_n, 2, rank, 4 * rank), bf16),
            jax.ShapeDtypeStruct((rank, width // 2), bf16),
            jax.ShapeDtypeStruct((width // 2, rank), bf16),
        ),
        in_specs=[pl.BlockSpec(memory_space=pl.ANY)] * 4 + [vm],
        out_specs=(vm,) * 3 + (pl.BlockSpec(memory_space=pl.ANY),) * 2,
        scratch_shapes=[
            pltpu.VMEM((sections // 2, 2, height, rank), bf16),
            buf(yh_n * x_n, 2, rank), buf(yh_n * x_n, rank), buf(yh_n, x_n, rank),
            buf(x_n - 1, yh_n, cut), buf(x_n, cut), buf(yh_n, cut), buf(cut),
            buf(x_n, cut), buf(x_n - 1, cut), buf(rank), buf(rank),
            pltpu.VMEM((rank, 4 * rank), bf16),
            pltpu.VMEM((3, rows, rank), f32), pltpu.VMEM((3, rows // 2, rank), f32),
            pltpu.VMEM((rank, rank), bf16), pltpu.VMEM((2, rank, rank), bf16),
            pltpu.VMEM((rows, width), bf16), pltpu.VMEM((rows, width), bf16),
            pltpu.VMEM((width, rank), bf16), pltpu.VMEM((rank, width), bf16),
            pltpu.VMEM((height, 2 * rank), bf16), pltpu.VMEM((height, rank), bf16), dma((5,)),
            dma((14,)), dma((sections // 2,)), dma((sections // 2,)),
            dma((sections // 2,)), dma((sections // 2,)),
            dma((yh_n * x_n,)), dma((yh_n * x_n,)),
            dma((yh_n * (x_n - 1),)), dma((yh_n * (x_n - 1),)), dma((x_n,)), dma((x_n,)), dma((4,)),
            dma((x_n - 1,)), dma((x_n - 1,)),
            dma((x_n,)), dma((x_n,)), dma((2 * x_n,)), dma((2 * x_n,)), dma((x_n,)), dma((x_n,)), dma((4,)),
        ],
        compiler_params=pltpu.CompilerParams(
            collective_id=3, has_side_effects=True, vmem_limit_bytes=60 * 1024 * 1024),
    )(x0, g16, down, up, mine_u)


def finish_kernel(sections, own_w, own_u, nxt_u, bump_u, x1, grad_down, grad_up, advance):
    last = lax.axis_index("section") == sections - 1
    grad_down[...] = own_w[...]
    grad_up[...] = own_u[...].astype(f32).T.astype(bf16)
    bump = dot_nt(bump_u[...], nxt_u[...])
    advance[...] = (x1[...].astype(f32) + jnp.where(last, 0.0, bump)).astype(bf16)


def finish(sections, own_w, own_u, nxt_u, bump_u, x1):
    rows, width = x1.shape
    rank = own_w.shape[1]
    step = width // 8
    tall = pl.BlockSpec((step, rank), lambda i: (i, 0))
    flat = pl.BlockSpec((rows, step), lambda i: (0, i))
    return pl.pallas_call(
        functools.partial(finish_kernel, sections),
        grid=(width // step,),
        out_shape=(
            jax.ShapeDtypeStruct((width, rank), bf16),
            jax.ShapeDtypeStruct((rank, width), bf16),
            jax.ShapeDtypeStruct((rows, width), bf16),
        ),
        in_specs=[tall, tall, tall, pl.BlockSpec((rows, rank), lambda i: (0, 0)), flat],
        out_specs=(tall, flat, flat),
        compiler_params=pltpu.CompilerParams(vmem_limit_bytes=60 * 1024 * 1024),
    )(own_w, own_u, nxt_u, bump_u, x1)


def per_device(inputs, cotangent, w_down, w_up):
    down = w_down[0]
    upward = w_up[0]
    micro, batch_rows, width = inputs.shape
    rank = down.shape[1]
    rows = micro * batch_rows
    sections = lax.axis_size("section")
    shards = lax.axis_size("dp")
    part = width // shards
    d = lax.axis_index("dp")
    x0 = inputs.reshape(rows, width)
    g16 = cotangent.reshape(rows, width)
    up_t = upward.T

    mine_u = lax.dynamic_slice_in_dim(up_t, d * part, part, 0)
    pyh, n0, grams, upart, wpart = grams_of(sections, shards, x0, g16, down, upward, mine_u)
    grams = grams.reshape(sections // 2, 2 * rank, 4 * rank)
    x1, own_w, own_u, nxt_u, bump_u = recurrence(
        sections, shards, pyh, n0, grams, x0, g16, upward, down, upart, wpart, mine_u)
    tall = (width, rank)
    grad_down, grad_up, advance = finish(
        sections, own_w.reshape(tall), own_u.reshape(tall), nxt_u.reshape(tall), bump_u, x1)
    return (grad_down[None], grad_up[None], advance.reshape(1, micro, batch_rows, width))


def solution(mesh):
    in_specs = (
        P(None, "dp", None),
        P(None, "dp", None),
        P("section", None, None),
        P("section", None, None),
    )
    out_specs = (P("section", None, None), P("section", None, None), P("section", None, "dp", None))
    return jax.shard_map(
        per_device, mesh=mesh, in_specs=in_specs, out_specs=out_specs, check_vma=False
    )
```
